32 devices in a mesh: groups: 2 (over y), wide: 4 (over z), narrow: 4 (over x, core).
Axes of the slice: x: 2, y: 2, z: 4, core: 2. Of those that a mesh axis runs over, the one named last changes fastest.
Arguments:
- inputs: bfloat16 [48, 8192], P(('groups', 'wide'), 'narrow'), parts along dimension 0, may hold values from -6 to 6
- cotangent: bfloat16 [48, 8192], P(('groups', 'wide'), 'narrow'), parts along dimension 0, may hold values from -3 to 3
- gate_weight: bfloat16 [8192, 24576], P('narrow', 'wide'), may hold values from -0.0625 to 0.0625
- up_weight: bfloat16 [8192, 24576], P('narrow', 'wide'), may hold values from -0.0625 to 0.0625
- down_weight: bfloat16 [24576, 8192], P('wide', 'narrow'), may hold values from -0.0390625 to 0.0390625
- ia3_scale: float32 [24576], P('wide'), may hold values from 0.3 to 3
- seq_ids: int32 [48], P('groups'), parts along dimension 0, may hold values from 0 to 3, as said below
Outputs:
- example_grads: float32 [8, 24576], P('groups', ('wide', 'narrow')), parts along dimension 0
- grad_norms: float32 [8], P('groups'), parts along dimension 0
- input_grad: bfloat16 [48, 8192], P(('groups', 'wide'), 'narrow'), parts along dimension 0
The draws below stay inside these ranges and needn't reach their ends.
There are 2 independent parts, one for each index of `groups`. The reference program is written for one: setup_inputs(seed, part) draws one part's arguments, and reference() takes and returns one part's arrays. A program takes and returns all parts, laid end to end along the dimension named above; an argument that names none is the same for every part. Nothing has to cross between parts.
Inputs may be any that keep to these rules, and one draw needn't show every extreme that they name: `seq_ids`: ids never fall along the tokens; every one of the 4 sequences has at least one token, and one sequence, drawn at random, has exactly 12.
All inputs are finite; a program needn't handle non-finite values.
Results may differ from the reference program's by a relative error of at most 0.0051.
Values may be sent and summed in bfloat16 or wider, within the bound.
No kernel may reach another device: no remote copies, remote signals or barrier semaphores. Data moves between devices by JAX's collectives and lax.ppermute only.
A program may use at most 192 MiB of HBM per device.

```python
import math
import jax
import jax.numpy as jnp
from jax import lax

D = 8192
FF = 24576
SEQS = 4
TOKENS = 24


def draw_seq_ids(key, part):
    key = jax.random.fold_in(key, 7)
    first_key, second_key = jax.random.split(key)
    half_tokens = TOKENS // 2
    rest_tokens = TOKENS - half_tokens
    longest = jax.random.randint(first_key, (), 0, SEQS)
    shuffled = jax.random.permutation(second_key, rest_tokens - 1) + 1
    cut_points = jnp.sort(shuffled[:SEQS - 2]).astype(jnp.int32)
    bounds = jnp.concatenate([jnp.zeros((1,), jnp.int32), cut_points, jnp.full((1,), rest_tokens, jnp.int32)])
    others = bounds[1:] - bounds[:-1]
    slots = jnp.arange(SEQS, dtype=jnp.int32)
    shifted = jnp.clip(slots - (slots > longest).astype(jnp.int32), 0, SEQS - 2)
    lengths = jnp.where(slots == longest, half_tokens, others[shifted]).astype(jnp.int32)
    ends = jnp.cumsum(lengths).astype(jnp.int32)
    positions = jnp.arange(TOKENS, dtype=jnp.int32)
    return jnp.sum((positions[:, None] >= ends[None, :-1]).astype(jnp.int32), axis=1).astype(jnp.int32)


def steps_of(own_key, dims, shards, low, high):
    loudness, own = 1.0, jax.random.fold_in(own_key, 6)
    for axis_at, parts in shards:
        draws = jnp.exp(jax.random.uniform(jax.random.fold_in(own, axis_at), (parts,), jnp.float32, low / len(shards), high / len(shards)))
        loudness = loudness * jnp.repeat(draws, dims[axis_at] // parts).reshape([-1 if axis == axis_at else 1 for axis in range(len(dims))])
    return loudness


def noise(stream_key, shape, scale, limit, shards=(), held_as=jnp.bfloat16):
    entries = scale * jax.random.normal(stream_key, shape, jnp.float32)
    if shards:
        entries = entries * steps_of(stream_key, shape, shards, -0.22, 0.18)
    return jnp.clip(entries, -limit, limit).astype(held_as)


def setup_inputs(seed: int = 0, part: int = 0) -> dict:
    key_of = jax.random.split(jax.random.key(seed), 8)
    own_keys = jax.random.split(jax.random.fold_in(key_of[7], part), 8)
    return {
        "inputs": noise(own_keys[0], (TOKENS, D), 1.0, 6.0, ((0, 4), (1, 4))),
        "cotangent": noise(own_keys[1], (TOKENS, D), 0.5, 3.0, ((0, 4), (1, 4))),
        "gate_weight": noise(key_of[2], (D, FF), D ** -0.5, 0.0625, ((0, 4), (1, 4))),
        "up_weight": noise(key_of[3], (D, FF), D ** -0.5, 0.0625, ((0, 4), (1, 4))),
        "down_weight": noise(key_of[4], (FF, D), FF ** -0.5, 0.0390625, ((0, 4), (1, 4))),
        "ia3_scale": jnp.clip(jnp.exp(math.log(3.0) - 2.3025851 * jax.random.uniform(key_of[5], (FF,), jnp.float32) ** steps_of(key_of[5], (FF,), ((0, 4),), -0.2, 0.2)), 0.3, 3.0),
        "seq_ids": draw_seq_ids(jax.random.fold_in(jax.random.fold_in(key_of[7], part), 71), part),
    }


def contract_rows(left, right):
    return lax.dot_general(left, right, (((1,), (1,)), ((), ())), preferred_element_type=jnp.float32)

def reference(inputs, cotangent, gate_weight, up_weight, down_weight, ia3_scale, seq_ids):
    gate_pre = jnp.dot(inputs, gate_weight, preferred_element_type=jnp.float32)
    up_pre = jnp.dot(inputs, up_weight, preferred_element_type=jnp.float32)
    mid_grad = contract_rows(cotangent, down_weight)
    sigmoid_gate = jax.nn.sigmoid(gate_pre)
    activation = gate_pre * sigmoid_gate
    hidden = activation * up_pre
    onehot = (seq_ids[None, :] == jnp.arange(SEQS, dtype=jnp.int32)[:, None]).astype(jnp.float32)
    example_grads = jnp.dot(onehot, hidden * mid_grad, precision=lax.Precision.HIGHEST)
    grad_norms = jnp.sqrt(lax.optimization_barrier(jnp.sum(example_grads * example_grads, axis=1)))
    scaled = ia3_scale[None, :] * mid_grad
    d_up = (scaled * activation).astype(jnp.bfloat16)
    d_gate = (scaled * up_pre * sigmoid_gate * (1.0 + gate_pre * (1.0 - sigmoid_gate))).astype(jnp.bfloat16)
    input_grad = (contract_rows(d_gate, gate_weight) + contract_rows(d_up, up_weight)).astype(jnp.bfloat16)
    return (example_grads, grad_norms, input_grad)
```

```python
import functools

import jax
import jax.numpy as jnp
from jax import lax
from jax.experimental import pallas as pl
from jax.experimental.pallas import tpu as pltpu
from jax.sharding import PartitionSpec as P

SEQS = 4
KERNEL_VMEM = 12 << 20


def contract_rows(left, right):
    return lax.dot_general(
        left, right, (((1,), (1,)), ((), ())), preferred_element_type=jnp.float32
    )


def local_grads(gate_pre, up_pre, mid_grad, scale_part):
    sigmoid_gate = jax.nn.sigmoid(gate_pre)
    activation = gate_pre * sigmoid_gate
    hidden = activation * up_pre
    scaled = scale_part * mid_grad
    d_up = (scaled * activation).astype(jnp.bfloat16)
    d_gate = (scaled * up_pre * sigmoid_gate * (1.0 + gate_pre * (1.0 - sigmoid_gate))).astype(
        jnp.bfloat16
    )
    return (hidden * mid_grad, d_gate, d_up)


def whole_block(inputs, cotangent, gate_weight, up_weight, down_weight, ia3_scale, seq_ids):
    panel_inputs = lax.all_gather(inputs, "wide", axis=0, tiled=True)
    panel_cotangent = lax.all_gather(cotangent, "wide", axis=0, tiled=True)
    gate_part = jnp.dot(panel_inputs, gate_weight, preferred_element_type=jnp.float32)
    up_part = jnp.dot(panel_inputs, up_weight, preferred_element_type=jnp.float32)
    mid_part = contract_rows(panel_cotangent, down_weight)
    quarter = gate_weight.shape[1] // lax.axis_size("narrow")
    position = lax.axis_index("narrow")
    onehot_full = (seq_ids[None, :] == jnp.arange(SEQS, dtype=jnp.int32)[:, None]).astype(
        jnp.float32
    )
    gate_pre, up_pre, mid_grad = (
        lax.psum_scatter(gate_part, "narrow", scatter_dimension=1, tiled=True),
        lax.psum_scatter(up_part, "narrow", scatter_dimension=1, tiled=True),
        lax.psum_scatter(mid_part, "narrow", scatter_dimension=1, tiled=True),
    )
    scale_part = lax.dynamic_slice_in_dim(ia3_scale, position * quarter, quarter, 0)
    product, d_gate, d_up = local_grads(gate_pre, up_pre, mid_grad, scale_part[None, :])
    example_grads = jnp.dot(onehot_full, product, precision=lax.Precision.HIGHEST)
    whole_gate, whole_up = (
        lax.all_gather(d_gate, "narrow", axis=1, tiled=True),
        lax.all_gather(d_up, "narrow", axis=1, tiled=True),
    )
    squares = lax.psum(jnp.sum(example_grads * example_grads, axis=1), ("wide", "narrow"))
    grad_norms = jnp.sqrt(squares)
    input_grad = lax.psum_scatter(
        contract_rows(whole_gate, gate_weight) + contract_rows(whole_up, up_weight),
        "wide",
        scatter_dimension=0,
        tiled=True,
    ).astype(jnp.bfloat16)
    return (example_grads, grad_norms, input_grad)


def exchange(array, axes, size, step):
    return lax.ppermute(array, axes, [(i, i ^ step) for i in range(size)])


def in_vmem(shape, dtype):
    return pltpu.VMEM(shape, dtype)


def held(array):
    return pltpu.with_memory_space_constraint(array, pltpu.VMEM)


def specs(count, space=pltpu.VMEM):
    return [pl.BlockSpec(memory_space=space)] * count


def load_kernel(strips, groups, gate, up, down, gate_held, up_held, down_held, sem):
    narrow, group = lax.axis_index("narrow"), lax.axis_index("groups")
    width = gate_held.shape[2]
    copies = []
    for s in range(strips):
        start = pl.multiple_of(((narrow ^ s) * groups + group) * width, width)
        copies.append(pltpu.make_async_copy(down.at[pl.ds(start, width), :], down_held.at[s], sem.at[0, s]))
        copies.append(pltpu.make_async_copy(gate.at[:, pl.ds(start, width)], gate_held.at[s], sem.at[1, s]))
        copies.append(pltpu.make_async_copy(up.at[:, pl.ds(start, width)], up_held.at[s], sem.at[2, s]))
    for copy in copies:
        copy.start()
    for copy in copies:
        copy.wait()


def forward_kernel(strips, peers, *refs):
    inputs, cotangent = refs[:2]
    arrived = refs[2 : 1 + peers]
    gate, up, down = refs[1 + peers : 4 + peers]
    own, sends = refs[4 + peers], refs[5 + peers : 4 + peers + strips]
    rows, cots = refs[4 + peers + strips :]
    share = inputs.shape[0]
    rows[0:share, :] = inputs[...].astype(jnp.float32)
    cots[0:share, :] = cotangent[...].astype(jnp.float32)
    for s in range(1, peers):
        both = arrived[s - 1][...].astype(jnp.float32)
        rows[s * share : (s + 1) * share, :] = both[:share]
        cots[s * share : (s + 1) * share, :] = both[share:]
    tokens, cotans = rows[...].astype(jnp.bfloat16), cots[...].astype(jnp.bfloat16)
    for s in range(strips):
        gate_part = jnp.dot(tokens, gate[s], preferred_element_type=jnp.float32)
        up_part = jnp.dot(tokens, up[s], preferred_element_type=jnp.float32)
        mid_part = contract_rows(cotans, down[s])
        target = own if s == 0 else sends[s - 1]
        for i, part in enumerate((gate_part, up_part, mid_part)):
            target[i] = part.astype(target.dtype)


def middle_kernel(strips, groups, wide, *refs):
    own, arrived = refs[0], refs[1:strips]
    scale, ids, other_ids = refs[strips : strips + 3]
    message, grads, other_grads, stage = refs[strips + 3 :]
    _, tokens, width = own.shape
    narrow, group, position = lax.axis_index("narrow"), lax.axis_index("groups"), lax.axis_index("wide")
    share = tokens // (groups * wide)
    sums = [own[i] + sum(ref[i].astype(jnp.float32) for ref in arrived) for i in range(3)]
    start = pl.multiple_of((narrow * groups + group) * width, width)
    product, d_gate, d_up = local_grads(*sums, scale[:, pl.ds(start, width)])
    message[0:tokens, :] = d_gate
    message[tokens : 2 * tokens, :] = d_up
    row = lax.broadcasted_iota(jnp.int32, (8, 128), 0)
    keys = []
    for base in range(0, tokens, 8):
        key = jnp.zeros((8, 128), jnp.int32)
        for r in range(8):
            block, j = divmod(base + r, share)
            source = ids if block < wide else other_ids
            key = jnp.where(row == r, source[(position ^ (block % wide)) * share + j], key)
        keys.append(jnp.concatenate([key] * (width // 128), axis=1))
    key = jnp.concatenate(keys, axis=0)
    half = tokens // groups
    for side, target in enumerate((grads, other_grads)):
        part, seq = product[side * half : (side + 1) * half], key[side * half : (side + 1) * half]
        for e in range(SEQS):
            total = jnp.sum(jnp.where(seq == e, part, 0.0), axis=0, keepdims=True)
            target[e : e + 1, :] = total
            stage[side * SEQS + e : side * SEQS + e + 1, :] = total * total
    squares = jnp.broadcast_to(jnp.sum(stage[...], axis=1, keepdims=True), stage.shape)
    high = squares.astype(jnp.bfloat16).astype(jnp.float32)
    message[2 * tokens :, :] = jnp.concatenate([high, squares - high], axis=0).astype(jnp.bfloat16)


def backward_kernel(strips, peers, *refs):
    messages, (gate, up) = refs[:strips], refs[strips : strips + 2]
    own, sends = refs[strips + 2], refs[strips + 3 : strips + 2 + peers]
    total, stage = refs[strips + 2 + peers :]
    tokens, features = total.shape
    tile = 512
    for start in range(0, features, tile):
        part = None
        for s in range(strips):
            for i, weight in enumerate((gate, up)):
                term = contract_rows(
                    messages[s][i * tokens : (i + 1) * tokens, :], weight[s, start : start + tile, :]
                )
                part = term if part is None else part + term
        total[:, start : start + tile] = part
    squares = sum(message[2 * tokens :, 0:128].astype(jnp.float32) for message in messages)
    squares = squares[0:8] + squares[8:16]
    high = squares.astype(jnp.bfloat16).astype(jnp.float32)
    low = squares - high
    share = tokens // peers
    stage[...] = jnp.zeros_like(stage)
    for k in range(8):
        stage[6:7, k * 128 : (k + 1) * 128] = high[k : k + 1]
        stage[7:8, k * 128 : (k + 1) * 128] = low[k : k + 1]
    for s in range(peers):
        stage[0:share, :] = total[s * share : (s + 1) * share, :]
        target = own if s == 0 else sends[s - 1]
        target[...] = stage[...].astype(target.dtype)


def last_kernel(peers, wide, *refs):
    blocks = refs[:peers]
    grads, other = refs[peers : peers + 2]
    input_grad, example_grads, norms = refs[peers + 2 :]
    share, width = input_grad.shape[0], grads.shape[1]
    group = lax.axis_index("groups")
    total = jnp.zeros(blocks[0].shape, jnp.float32)
    squares = jnp.zeros((1, SEQS * 128), jnp.float32)
    for s, block in enumerate(blocks):
        values = block[...].astype(jnp.float32)
        total = total + values
        first = SEQS * 128 * (s // wide)
        squares = squares + values[6:7, first : first + SEQS * 128] + values[7:8, first : first + SEQS * 128]
    input_grad[...] = total[0:share].astype(jnp.bfloat16)
    roots = jnp.sqrt(squares)
    for e in range(SEQS):
        norms[e] = jnp.max(roots[:, e * 128 : (e + 1) * 128])
    example_grads[:, pl.ds(pl.multiple_of(group * width, width), width)] = grads[...]
    example_grads[:, pl.ds(pl.multiple_of((1 - group) * width, width), width)] = other[...]


def shared(inputs, cotangent, gate_weight, up_weight, down_weight, ia3_scale, seq_ids):
    groups, wide, strips = lax.axis_size("groups"), lax.axis_size("wide"), lax.axis_size("narrow")
    peers = groups * wide
    share, features = inputs.shape
    hidden = gate_weight.shape[1]
    width = hidden // (strips * groups)
    tokens = share * peers
    f32, bf16 = jnp.float32, jnp.bfloat16
    params = pltpu.CompilerParams(vmem_limit_bytes=KERNEL_VMEM)

    both = jnp.concatenate([inputs, cotangent], axis=0)
    arrived = [exchange(both, ("groups", "wide"), peers, s) for s in range(1, peers)]
    other_ids = exchange(seq_ids, "groups", groups, 1)

    weight_bytes = 3 * strips * features * width * 2
    gate, up, down = pl.pallas_call(
        functools.partial(load_kernel, strips, groups),
        out_shape=[
            in_vmem((strips, features, width), bf16),
            in_vmem((strips, features, width), bf16),
            in_vmem((strips, width, features), bf16),
        ],
        in_specs=specs(3, pl.ANY),
        out_specs=specs(3),
        scratch_shapes=[pltpu.SemaphoreType.DMA((3, strips))],
        compiler_params=params,
        cost_estimate=pl.CostEstimate(flops=0, bytes_accessed=2 * weight_bytes, transcendentals=0),
        name="load_weights",
    )(gate_weight, up_weight, down_weight)

    partials = pl.pallas_call(
        functools.partial(forward_kernel, strips, peers),
        out_shape=[in_vmem((3, tokens, width), f32)] + [in_vmem((3, tokens, width), bf16)] * (strips - 1),
        in_specs=specs(4 + peers),
        out_specs=specs(strips),
        scratch_shapes=[pltpu.VMEM((tokens, features), f32)] * 2,
        compiler_params=params,
        cost_estimate=pl.CostEstimate(
            flops=2 * tokens * weight_bytes // 2, bytes_accessed=weight_bytes, transcendentals=0
        ),
        name="forward",
    )(inputs, cotangent, *arrived, held(gate), held(up), held(down))
    terms = [exchange(partials[s], "narrow", strips, s) for s in range(1, strips)]

    message, grads, other_grads = pl.pallas_call(
        functools.partial(middle_kernel, strips, groups, wide),
        out_shape=[
            in_vmem((2 * tokens + 16, width), bf16),
            in_vmem((SEQS, width), f32),
            in_vmem((SEQS, width), f32),
        ],
        in_specs=specs(strips + 1) + specs(2, pltpu.SMEM),
        out_specs=specs(3),
        scratch_shapes=[pltpu.VMEM((groups * SEQS, width), f32)],
        compiler_params=params,
        name="middle",
    )(partials[0], *terms, ia3_scale[None, :], seq_ids, other_ids)
    messages = [message] + [exchange(message, "narrow", strips, s) for s in range(1, strips)]
    other_part = exchange(other_grads, "groups", groups, 1)

    blocks = pl.pallas_call(
        functools.partial(backward_kernel, strips, peers),
        out_shape=[in_vmem((8, features), f32)] + [in_vmem((8, features), bf16)] * (peers - 1),
        in_specs=specs(strips + 2),
        out_specs=specs(peers),
        scratch_shapes=[pltpu.VMEM((tokens, features), f32), pltpu.VMEM((8, features), f32)],
        compiler_params=params,
        cost_estimate=pl.CostEstimate(
            flops=2 * tokens * weight_bytes // 3, bytes_accessed=weight_bytes * 2 // 3, transcendentals=0
        ),
        name="backward",
    )(*messages, held(gate), held(up))
    blocks = [blocks[0]] + [exchange(blocks[s], ("groups", "wide"), peers, s) for s in range(1, peers)]

    input_grad, example_grads, norms = pl.pallas_call(
        functools.partial(last_kernel, peers, wide),
        out_shape=[
            jax.ShapeDtypeStruct((share, features), bf16),
            jax.ShapeDtypeStruct((SEQS, groups * width), f32),
            jax.ShapeDtypeStruct((SEQS,), f32),
        ],
        in_specs=specs(peers + 2),
        out_specs=specs(2) + specs(1, pltpu.SMEM),
        compiler_params=params,
        name="last",
    )(*blocks, grads, other_part)
    return (example_grads, norms, input_grad)


def power_of_two(number):
    return number & (number - 1) == 0


def local(inputs, cotangent, gate_weight, up_weight, down_weight, ia3_scale, seq_ids):
    groups, wide, narrow = lax.axis_size("groups"), lax.axis_size("wide"), lax.axis_size("narrow")
    share, (features, hidden) = inputs.shape[0], gate_weight.shape
    fits = (
        groups == 2
        and power_of_two(wide)
        and power_of_two(narrow)
        and hidden % (narrow * groups * 256) == 0
        and features % 512 == 0
        and features >= 2 * SEQS * 128
        and share <= 6
        and (share * wide) % 8 == 0
        and (share * wide * groups) % 16 == 0
        and 3 * features * hidden // groups * 2 <= 40 << 20
    )
    plan = shared if fits else whole_block
    return plan(inputs, cotangent, gate_weight, up_weight, down_weight, ia3_scale, seq_ids)


def solution(mesh):
    return jax.shard_map(
        local,
        mesh=mesh,
        in_specs=(
            P(("groups", "wide"), "narrow"),
            P(("groups", "wide"), "narrow"),
            P("narrow", "wide"),
            P("narrow", "wide"),
            P("wide", "narrow"),
            P("wide"),
            P("groups"),
        ),
        out_specs=(P("groups", ("wide", "narrow")), P("groups"), P(("groups", "wide"), "narrow")),
        check_vma=False,
    )
```

```python
import functools

import jax
import jax.numpy as jnp
from jax import lax
from jax.experimental import pallas as pl
from jax.experimental.pallas import tpu as pltpu
from jax.sharding import PartitionSpec as P

SEQS = 4
KERNEL_VMEM = 12 << 20


def contract_rows(left, right):
    return lax.dot_general(
        left, right, (((1,), (1,)), ((), ())), preferred_element_type=jnp.float32
    )


def local_grads(gate_pre, up_pre, mid_grad, scale_part):
    sigmoid_gate = jax.nn.sigmoid(gate_pre)
    activation = gate_pre * sigmoid_gate
    hidden = activation * up_pre
    scaled = scale_part * mid_grad
    d_up = (scaled * activation).astype(jnp.bfloat16)
    d_gate = (scaled * up_pre * sigmoid_gate * (1.0 + gate_pre * (1.0 - sigmoid_gate))).astype(
        jnp.bfloat16
    )
    return (hidden * mid_grad, d_gate, d_up)


def whole_block(inputs, cotangent, gate_weight, up_weight, down_weight, ia3_scale, seq_ids):
    panel_inputs = lax.all_gather(inputs, "wide", axis=0, tiled=True)
    panel_cotangent = lax.all_gather(cotangent, "wide", axis=0, tiled=True)
    gate_part = jnp.dot(panel_inputs, gate_weight, preferred_element_type=jnp.float32)
    up_part = jnp.dot(panel_inputs, up_weight, preferred_element_type=jnp.float32)
    mid_part = contract_rows(panel_cotangent, down_weight)
    quarter = gate_weight.shape[1] // lax.axis_size("narrow")
    position = lax.axis_index("narrow")
    onehot_full = (seq_ids[None, :] == jnp.arange(SEQS, dtype=jnp.int32)[:, None]).astype(
        jnp.float32
    )
    gate_pre, up_pre, mid_grad = (
        lax.psum_scatter(gate_part, "narrow", scatter_dimension=1, tiled=True),
        lax.psum_scatter(up_part, "narrow", scatter_dimension=1, tiled=True),
        lax.psum_scatter(mid_part, "narrow", scatter_dimension=1, tiled=True),
    )
    scale_part = lax.dynamic_slice_in_dim(ia3_scale, position * quarter, quarter, 0)
    product, d_gate, d_up = local_grads(gate_pre, up_pre, mid_grad, scale_part[None, :])
    example_grads = jnp.dot(onehot_full, product, precision=lax.Precision.HIGHEST)
    whole_gate, whole_up = (
        lax.all_gather(d_gate, "narrow", axis=1, tiled=True),
        lax.all_gather(d_up, "narrow", axis=1, tiled=True),
    )
    squares = lax.psum(jnp.sum(example_grads * example_grads, axis=1), ("wide", "narrow"))
    grad_norms = jnp.sqrt(squares)
    input_grad = lax.psum_scatter(
        contract_rows(whole_gate, gate_weight) + contract_rows(whole_up, up_weight),
        "wide",
        scatter_dimension=0,
        tiled=True,
    ).astype(jnp.bfloat16)
    return (example_grads, grad_norms, input_grad)


def exchange(array, axes, size, step):
    return lax.ppermute(array, axes, [(i, i ^ step) for i in range(size)])


def in_vmem(shape, dtype):
    return pltpu.VMEM(shape, dtype)


def held(array):
    return pltpu.with_memory_space_constraint(array, pltpu.VMEM)


def specs(count, space=pltpu.VMEM):
    return [pl.BlockSpec(memory_space=space)] * count


def load_kernel(strips, groups, gate, up, down, gate_held, up_held, down_held, sem):
    narrow, group = lax.axis_index("narrow"), lax.axis_index("groups")
    width = gate_held.shape[2]
    copies = []
    for s in range(strips):
        start = pl.multiple_of(((narrow ^ s) * groups + group) * width, width)
        copies.append(pltpu.make_async_copy(down.at[pl.ds(start, width), :], down_held.at[s], sem.at[0, s]))
        copies.append(pltpu.make_async_copy(gate.at[:, pl.ds(start, width)], gate_held.at[s], sem.at[1, s]))
        copies.append(pltpu.make_async_copy(up.at[:, pl.ds(start, width)], up_held.at[s], sem.at[2, s]))
    for copy in copies:
        copy.start()
    for copy in copies:
        copy.wait()


def forward_kernel(strips, peers, arrived, gate, up, down, own, sends, rows, cots):
    narrow = lax.axis_index("narrow")
    share = arrived.shape[1] // 2
    for p in range(peers):
        both = arrived[p].astype(jnp.float32)
        rows[p * share : (p + 1) * share, :] = both[:share]
        cots[p * share : (p + 1) * share, :] = both[share:]
    tokens, cotans = rows[...].astype(jnp.bfloat16), cots[...].astype(jnp.bfloat16)
    for s in range(strips):
        gate_part = jnp.dot(tokens, gate[s], preferred_element_type=jnp.float32)
        up_part = jnp.dot(tokens, up[s], preferred_element_type=jnp.float32)
        mid_part = contract_rows(cotans, down[s])
        for i, part in enumerate((gate_part, up_part, mid_part)):
            if s == 0:
                own[i] = part
            sends[narrow ^ s, i] = part.astype(sends.dtype)


def middle_kernel(strips, groups, wide, own, arrived, scale, ids, other_ids, gate, up, message, grads, other_grads, stage):
    del gate, up
    _, tokens, width = own.shape
    narrow, group = lax.axis_index("narrow"), lax.axis_index("groups")
    sums = []
    for i in range(3):
        total = own[i]
        for s in range(1, strips):
            total = total + arrived[narrow ^ s, i].astype(jnp.float32)
        sums.append(total)
    start = pl.multiple_of((narrow * groups + group) * width, width)
    product, d_gate, d_up = local_grads(*sums, scale[:, pl.ds(start, width)])
    row = lax.broadcasted_iota(jnp.int32, (8, 128), 0)
    half = tokens // groups
    keys = []
    for base in range(0, tokens, 8):
        key = jnp.zeros((8, 128), jnp.int32)
        side, offset = divmod(base, half)
        for r in range(8):
            value = jnp.where(group == side, ids[offset + r], other_ids[offset + r])
            key = jnp.where(row == r, value, key)
        keys.append(jnp.concatenate([key] * (width // 128), axis=1))
    key = jnp.concatenate(keys, axis=0)
    for side in range(groups):
        part, seq = product[side * half : (side + 1) * half], key[side * half : (side + 1) * half]
        for e in range(SEQS):
            total = jnp.sum(jnp.where(seq == e, part, 0.0), axis=0, keepdims=True)
            stage[side * SEQS + e : side * SEQS + e + 1, :] = total
    every = stage[...]
    first, second = every[:SEQS], every[SEQS:]
    grads[...] = jnp.where(group == 0, first, second)
    other_grads[...] = jnp.where(group == 0, second, first)
    squares = jnp.broadcast_to(jnp.sum(every * every, axis=1, keepdims=True), every.shape)
    high = squares.astype(jnp.bfloat16).astype(jnp.float32)
    tail = jnp.concatenate([high, squares - high], axis=0).astype(jnp.bfloat16)
    for s in range(strips):
        message[s, 0:tokens, :] = d_gate
        message[s, tokens : 2 * tokens, :] = d_up
        message[s, 2 * tokens :, :] = tail


def backward_kernel(strips, groups, wide, messages, gate, up, own, sends, total, stage):
    tokens, features = total.shape
    peers = groups * wide
    narrow = lax.axis_index("narrow")
    peer = lax.axis_index("groups") * wide + lax.axis_index("wide")
    tile = 512
    for start in range(0, features, tile):
        part = None
        for s in range(strips):
            for i, weight in enumerate((gate, up)):
                term = contract_rows(
                    messages[narrow ^ s, i * tokens : (i + 1) * tokens, :], weight[s, start : start + tile, :]
                )
                part = term if part is None else part + term
        total[:, start : start + tile] = part
    squares = sum(messages[s, 2 * tokens :, 0:128].astype(jnp.float32) for s in range(strips))
    squares = squares[0:8] + squares[8:16]
    high = squares.astype(jnp.bfloat16).astype(jnp.float32)
    low = squares - high
    share = tokens // peers
    for p in range(peers):
        stage[p, 0:share, :] = total[p * share : (p + 1) * share, :]
        stage[p, 6:8, :] = jnp.zeros((2, features), jnp.float32)
        for k in range(8):
            stage[p, 6:7, k * 128 : (k + 1) * 128] = high[k : k + 1]
            stage[p, 7:8, k * 128 : (k + 1) * 128] = low[k : k + 1]
        sends[p] = stage[p].astype(jnp.bfloat16)
    own[...] = stage[peer]


def last_kernel(groups, wide, own, blocks, grads, other, input_grad, example_grads, norms):
    peers = groups * wide
    share, width = input_grad.shape[0], grads.shape[1]
    group = lax.axis_index("groups")
    peer = group * wide + lax.axis_index("wide")
    total = own[...]
    for s in range(1, peers):
        total = total + blocks[peer ^ s].astype(jnp.float32)
    input_grad[...] = total[0:share].astype(jnp.bfloat16)
    lanes = SEQS * 128
    squares = total[6:7] + total[7:8]
    squares = jnp.where(group == 0, squares[:, 0:lanes], squares[:, lanes : 2 * lanes])
    roots = jnp.sqrt(squares)
    for e in range(SEQS):
        norms[e] = jnp.max(roots[:, e * 128 : (e + 1) * 128])
    example_grads[:, pl.ds(pl.multiple_of(group * width, width), width)] = grads[...]
    example_grads[:, pl.ds(pl.multiple_of((1 - group) * width, width), width)] = other[...]


def swap_blocks(array, axes):
    return lax.all_to_all(array, axes, 0, 0, tiled=True)


def shared(inputs, cotangent, gate_weight, up_weight, down_weight, ia3_scale, seq_ids):
    groups, wide, strips = lax.axis_size("groups"), lax.axis_size("wide"), lax.axis_size("narrow")
    peers = groups * wide
    share, features = inputs.shape
    hidden = gate_weight.shape[1]
    width = hidden // (strips * groups)
    tokens = share * peers
    f32, bf16 = jnp.float32, jnp.bfloat16
    params = pltpu.CompilerParams(vmem_limit_bytes=KERNEL_VMEM)

    both = jnp.concatenate([inputs, cotangent], axis=0)
    arrived = swap_blocks(jnp.broadcast_to(both[None], (peers,) + both.shape), ("groups", "wide"))
    other_ids = exchange(seq_ids, "groups", groups, 1)

    weight_bytes = 3 * strips * features * width * 2
    gate, up, down = pl.pallas_call(
        functools.partial(load_kernel, strips, groups),
        out_shape=[
            in_vmem((strips, features, width), bf16),
            in_vmem((strips, features, width), bf16),
            in_vmem((strips, width, features), bf16),
        ],
        in_specs=specs(3, pl.ANY),
        out_specs=specs(3),
        scratch_shapes=[pltpu.SemaphoreType.DMA((3, strips))],
        compiler_params=params,
        cost_estimate=pl.CostEstimate(flops=0, bytes_accessed=2 * weight_bytes, transcendentals=0),
        name="load_weights",
    )(gate_weight, up_weight, down_weight)

    own_part, parts = pl.pallas_call(
        functools.partial(forward_kernel, strips, peers),
        out_shape=[in_vmem((3, tokens, width), f32), in_vmem((strips, 3, tokens, width), bf16)],
        in_specs=specs(4),
        out_specs=specs(2),
        scratch_shapes=[pltpu.VMEM((tokens, features), f32)] * 2,
        compiler_params=params,
        cost_estimate=pl.CostEstimate(
            flops=2 * tokens * weight_bytes // 2, bytes_accessed=weight_bytes, transcendentals=0
        ),
        name="forward",
    )(arrived, held(gate), held(up), held(down))
    terms = swap_blocks(parts, "narrow")

    message, grads, other_grads = pl.pallas_call(
        functools.partial(middle_kernel, strips, groups, wide),
        out_shape=[
            in_vmem((strips, 2 * tokens + 16, width), bf16),
            in_vmem((SEQS, width), f32),
            in_vmem((SEQS, width), f32),
        ],
        in_specs=specs(3) + specs(2, pltpu.SMEM) + specs(2),
        out_specs=specs(3),
        scratch_shapes=[pltpu.VMEM((groups * SEQS, width), f32)],
        compiler_params=params,
        name="middle",
    )(own_part, terms, ia3_scale[None, :], seq_ids, other_ids, held(gate), held(up))
    messages = swap_blocks(message, "narrow")
    other_part = exchange(other_grads, "groups", groups, 1)

    own_block, blocks = pl.pallas_call(
        functools.partial(backward_kernel, strips, groups, wide),
        out_shape=[in_vmem((8, features), f32), in_vmem((peers, 8, features), bf16)],
        in_specs=specs(3),
        out_specs=specs(2),
        scratch_shapes=[pltpu.VMEM((tokens, features), f32), pltpu.VMEM((peers, 8, features), f32)],
        compiler_params=params,
        cost_estimate=pl.CostEstimate(
            flops=2 * tokens * weight_bytes // 3, bytes_accessed=weight_bytes * 2 // 3, transcendentals=0
        ),
        name="backward",
    )(messages, held(gate), held(up))
    blocks = swap_blocks(blocks, ("groups", "wide"))

    input_grad, example_grads, norms = pl.pallas_call(
        functools.partial(last_kernel, groups, wide),
        out_shape=[
            jax.ShapeDtypeStruct((share, features), bf16),
            jax.ShapeDtypeStruct((SEQS, groups * width), f32),
            jax.ShapeDtypeStruct((SEQS,), f32),
        ],
        in_specs=specs(4),
        out_specs=specs(2) + specs(1, pltpu.SMEM),
        compiler_params=params,
        name="last",
    )(own_block, blocks, grads, other_part)
    return (example_grads, norms, input_grad)


def power_of_two(number):
    return number & (number - 1) == 0


def local(inputs, cotangent, gate_weight, up_weight, down_weight, ia3_scale, seq_ids):
    groups, wide, narrow = lax.axis_size("groups"), lax.axis_size("wide"), lax.axis_size("narrow")
    share, (features, hidden) = inputs.shape[0], gate_weight.shape
    fits = (
        groups == 2
        and power_of_two(wide)
        and power_of_two(narrow)
        and hidden % (narrow * groups * 256) == 0
        and features % 512 == 0
        and features >= 2 * SEQS * 128
        and share <= 6
        and (share * wide) % 8 == 0
        and (share * wide * groups) % 16 == 0
        and 3 * features * hidden // groups * 2 <= 40 << 20
    )
    plan = shared if fits else whole_block
    return plan(inputs, cotangent, gate_weight, up_weight, down_weight, ia3_scale, seq_ids)


def solution(mesh):
    return jax.shard_map(
        local,
        mesh=mesh,
        in_specs=(
            P(("groups", "wide"), "narrow"),
            P(("groups", "wide"), "narrow"),
            P("narrow", "wide"),
            P("narrow", "wide"),
            P("wide", "narrow"),
            P("wide"),
            P("groups"),
        ),
        out_specs=(P("groups", ("wide", "narrow")), P("groups"), P(("groups", "wide"), "narrow")),
        check_vma=False,
    )
```

```python
import functools

import jax
import jax.numpy as jnp
from jax import lax
from jax.experimental import pallas as pl
from jax.experimental.pallas import tpu as pltpu
from jax.sharding import PartitionSpec as P

SEQS = 4
KERNEL_VMEM = 6 << 20


def contract_rows(left, right):
    return lax.dot_general(
        left, right, (((1,), (1,)), ((), ())), preferred_element_type=jnp.float32
    )


def local_grads(gate_pre, up_pre, mid_grad, scale_part):
    sigmoid_gate = jax.nn.sigmoid(gate_pre)
    activation = gate_pre * sigmoid_gate
    hidden = activation * up_pre
    scaled = scale_part * mid_grad
    d_up = (scaled * activation).astype(jnp.bfloat16)
    d_gate = (scaled * up_pre * sigmoid_gate * (1.0 + gate_pre * (1.0 - sigmoid_gate))).astype(
        jnp.bfloat16
    )
    return (hidden * mid_grad, d_gate, d_up)


def whole_block(inputs, cotangent, gate_weight, up_weight, down_weight, ia3_scale, seq_ids):
    panel_inputs = lax.all_gather(inputs, "wide", axis=0, tiled=True)
    panel_cotangent = lax.all_gather(cotangent, "wide", axis=0, tiled=True)
    gate_part = jnp.dot(panel_inputs, gate_weight, preferred_element_type=jnp.float32)
    up_part = jnp.dot(panel_inputs, up_weight, preferred_element_type=jnp.float32)
    mid_part = contract_rows(panel_cotangent, down_weight)
    quarter = gate_weight.shape[1] // lax.axis_size("narrow")
    position = lax.axis_index("narrow")
    onehot_full = (seq_ids[None, :] == jnp.arange(SEQS, dtype=jnp.int32)[:, None]).astype(
        jnp.float32
    )
    gate_pre, up_pre, mid_grad = (
        lax.psum_scatter(gate_part, "narrow", scatter_dimension=1, tiled=True),
        lax.psum_scatter(up_part, "narrow", scatter_dimension=1, tiled=True),
        lax.psum_scatter(mid_part, "narrow", scatter_dimension=1, tiled=True),
    )
    scale_part = lax.dynamic_slice_in_dim(ia3_scale, position * quarter, quarter, 0)
    product, d_gate, d_up = local_grads(gate_pre, up_pre, mid_grad, scale_part[None, :])
    example_grads = jnp.dot(onehot_full, product, precision=lax.Precision.HIGHEST)
    whole_gate, whole_up = (
        lax.all_gather(d_gate, "narrow", axis=1, tiled=True),
        lax.all_gather(d_up, "narrow", axis=1, tiled=True),
    )
    squares = lax.psum(jnp.sum(example_grads * example_grads, axis=1), ("wide", "narrow"))
    grad_norms = jnp.sqrt(squares)
    input_grad = lax.psum_scatter(
        contract_rows(whole_gate, gate_weight) + contract_rows(whole_up, up_weight),
        "wide",
        scatter_dimension=0,
        tiled=True,
    ).astype(jnp.bfloat16)
    return (example_grads, grad_norms, input_grad)


def exchange(array, axis, step):
    return lax.ppermute(array, axis, [(i, i ^ step) for i in range(lax.axis_size(axis))])


def held(array):
    return pltpu.with_memory_space_constraint(array, pltpu.VMEM)


def call(body, name, outs, args, spaces=None, scratch=(), out_spaces=None):
    spaces, out_spaces = spaces or {}, out_spaces or {}
    many = isinstance(outs, list)
    out_specs = [
        pl.BlockSpec(memory_space=out_spaces.get(i, pltpu.VMEM)) for i in range(len(outs) if many else 1)
    ]
    return pl.pallas_call(
        body,
        out_shape=outs,
        in_specs=[pl.BlockSpec(memory_space=spaces.get(i, pltpu.VMEM)) for i in range(len(args))],
        out_specs=out_specs if many else out_specs[0],
        scratch_shapes=list(scratch),
        compiler_params=pltpu.CompilerParams(vmem_limit_bytes=KERNEL_VMEM),
        cost_estimate=pl.CostEstimate(flops=1000, bytes_accessed=1000, transcendentals=0),
        name=name,
    )(*args)


def pack_kernel(inputs, cotangent, out, stage):
    share, features = inputs.shape
    half = features // 2
    for i, ref in enumerate((inputs, cotangent)):
        rows = ref[...].astype(jnp.float32)
        for j in range(2):
            stage[(2 * i + j) * share : (2 * i + j + 1) * share, :] = rows[:, j * half : (j + 1) * half]
    for k in range(out.shape[0]):
        out[k] = stage[8 * k : 8 * k + 8, :].astype(jnp.bfloat16)


def relay_kernel(share, *refs):
    blocks, ids, out = refs[:-3], refs[-3], refs[-1]
    slabs = blocks[0].shape[0]
    position = lax.axis_index("wide")
    for i, block in enumerate(blocks):
        out[i * slabs : (i + 1) * slabs] = block[...]
    row = lax.broadcasted_iota(jnp.int32, (8, 128), 0)
    keys = []
    for k in range(len(blocks) * share // 8):
        key = jnp.zeros((8, 128), jnp.int32)
        for r in range(8):
            block, j = divmod(8 * k + r, share)
            key = jnp.where(row == r, ids[(position ^ block) * share + j], key)
        keys.append(key.astype(jnp.float32))
    keys.append(jnp.zeros((8, out.shape[2] - 128 * len(keys)), jnp.float32))
    out[len(blocks) * slabs] = jnp.concatenate(keys, axis=1).astype(jnp.bfloat16)


def load_kernel(strip, groups, *refs):
    gate, up, down = refs[:3]
    gate_held, up_held, down_held, sem = refs[-4:]
    start_load(strip, groups, (gate, up, down), (gate_held, up_held, down_held), sem)()


def start_load(strip, groups, sources, targets, sem):
    width = targets[0].shape[1]
    owner = lax.axis_index("narrow") ^ strip
    start = pl.multiple_of((owner * groups + lax.axis_index("groups")) * width, width)
    gate, up, down = sources
    copies = [
        pltpu.make_async_copy(gate.at[:, pl.ds(start, width)], targets[0], sem.at[0]),
        pltpu.make_async_copy(up.at[:, pl.ds(start, width)], targets[1], sem.at[1]),
        pltpu.make_async_copy(down.at[pl.ds(start, width), :], targets[2], sem.at[2]),
    ]
    for copy in copies:
        copy.start()

    def wait():
        for copy in copies:
            copy.wait()

    return wait


def strip_parts(tokens, cotans, weights):
    gate, up, down = weights
    tokens, cotans = tokens[...], cotans[...]
    yield jnp.dot(tokens, gate[...], preferred_element_type=jnp.float32)
    yield jnp.dot(tokens, up[...], preferred_element_type=jnp.float32)
    yield contract_rows(cotans, down[...])


def first_kernel(share, *refs):
    relayed, other, gate, up, down = refs[:5]
    tokens, cotans, part, rows, cots = refs[-5:]
    slabs, half = 4 * share // 8, rows.shape[1] // 2
    count = (relayed.shape[0] - 1) // slabs
    for side, source in enumerate((relayed, other)):
        for i in range(count):
            packed = source[i * slabs : (i + 1) * slabs].astype(jnp.float32).reshape(4 * share, half)
            at = (side * count + i) * share
            for j, target in enumerate((rows, rows, cots, cots)):
                span = slice((j % 2) * half, (j % 2 + 1) * half)
                target[at : at + share, span] = packed[j * share : (j + 1) * share]
    tokens[...] = rows[...].astype(jnp.bfloat16)
    cotans[...] = cots[...].astype(jnp.bfloat16)
    forward_kernel(tokens, cotans, gate, up, down, part)


def forward_kernel(tokens, cotans, gate, up, down, out):
    for i, part in enumerate(strip_parts(tokens, cotans, (gate, up, down))):
        out[i] = part.astype(out.dtype)


def forward_add_kernel(tokens, cotans, gate, up, down, arrived, out):
    for i, part in enumerate(strip_parts(tokens, cotans, (gate, up, down))):
        out[i] = (part + arrived[i].astype(jnp.float32)).astype(out.dtype)


def forward_load_kernel(strip, groups, tokens, cotans, gate, up, down, next_gate, next_up, next_down, *refs):
    out, targets, sem = refs[-5], refs[-4:-1], refs[-1]
    wait = start_load(strip, groups, (next_gate, next_up, next_down), targets, sem)
    forward_kernel(tokens, cotans, gate, up, down, out)
    wait()


def middle_kernel(groups, *refs):
    own, arrived, crossed, scale, relayed, other_relayed = refs[:6]
    message, grads, other_grads, stage = refs[-4:]
    _, tokens, width = own.shape
    narrow, group = lax.axis_index("narrow"), lax.axis_index("groups")
    sums = [own[i] + arrived[i].astype(jnp.float32) + crossed[i].astype(jnp.float32) for i in range(3)]
    start = pl.multiple_of((narrow * groups + group) * width, width)
    product, d_gate, d_up = local_grads(*sums, scale[:, pl.ds(start, width)])
    message[0:tokens, :] = d_gate
    message[tokens : 2 * tokens, :] = d_up
    half = tokens // groups
    for side, (source, target) in enumerate(((relayed, grads), (other_relayed, other_grads))):
        marks = source[source.shape[0] - 1].astype(jnp.float32)
        seq = jnp.concatenate(
            [
                jnp.concatenate([marks[:, k * 128 : (k + 1) * 128]] * (width // 128), axis=1)
                for k in range(half // 8)
            ],
            axis=0,
        )
        part = product[side * half : (side + 1) * half]
        for e in range(SEQS):
            total = jnp.sum(jnp.where(seq == float(e), part, 0.0), axis=0, keepdims=True)
            target[e : e + 1, :] = total
            stage[side * SEQS + e : side * SEQS + e + 1, :] = total
    every = stage[...]
    squares = jnp.broadcast_to(jnp.sum(every * every, axis=1, keepdims=True), every.shape)
    high = squares.astype(jnp.bfloat16).astype(jnp.float32)
    message[2 * tokens :, :] = jnp.concatenate([high, squares - high], axis=0).astype(jnp.bfloat16)


TILE = 512


def backward_part(message, gate, up, start):
    tokens = (message.shape[0] - 16) // 2
    gate_term = contract_rows(message[0:tokens, :], gate[start : start + TILE, :])
    return gate_term + contract_rows(message[tokens : 2 * tokens, :], up[start : start + TILE, :])


def backward_first_kernel(message, gate, up, total):
    for start in range(0, total.shape[1], TILE):
        total[:, start : start + TILE] = backward_part(message, gate, up, start)


def backward_next_kernel(message, gate, up, before, total):
    for start in range(0, total.shape[1], TILE):
        total[:, start : start + TILE] = before[:, start : start + TILE] + backward_part(message, gate, up, start)


def split_high(values):
    high = values.astype(jnp.bfloat16).astype(jnp.float32)
    return high, values - high


def backward_last_kernel(message, gate, up, before, *refs):
    others, other_grads = refs[:3], refs[3]
    own, own_tail, send = refs[4:7]
    half, features = own.shape
    for start in range(0, features, TILE):
        span = slice(start, start + TILE)
        total = before[:, span] + backward_part(message, gate, up, start)
        own[:, span] = total[:half]
        for k in range(half // 8):
            send[k, :, span] = total[half + 8 * k : half + 8 * k + 8].astype(jnp.bfloat16)
    squares = sum(ref[ref.shape[0] - 16 :, 0:128].astype(jnp.float32) for ref in (message,) + others)
    high, low = split_high(squares[0:8] + squares[8:16])
    own_tail[...] = jnp.zeros_like(own_tail)
    width = other_grads.shape[1]
    for i, rows in enumerate(split_high(other_grads[...])):
        own_tail[i * SEQS : (i + 1) * SEQS, 0:width] = rows
    first = features - 8 * 128
    for k in range(8):
        span = slice(first + k * 128, first + (k + 1) * 128)
        own_tail[0:1, span] = high[k : k + 1]
        own_tail[1:2, span] = low[k : k + 1]
    send[half // 8] = own_tail[...].astype(jnp.bfloat16)


def combine_kernel(share, own, own_tail, arrived, grads, *refs):
    example_grads, own_block, sends, total = refs[0], refs[1], refs[2:-1], refs[-1]
    half, features = own.shape
    width = grads.shape[1]
    group = lax.axis_index("groups")
    slabs = half // 8
    for k in range(slabs):
        total[8 * k : 8 * k + 8, :] = own[8 * k : 8 * k + 8, :] + arrived[k].astype(jnp.float32)
    tail = arrived[slabs].astype(jnp.float32)
    other = tail[0:SEQS, 0:width] + tail[SEQS : 2 * SEQS, 0:width]
    example_grads[:, pl.ds(pl.multiple_of(group * width, width), width)] = grads[...]
    example_grads[:, pl.ds(pl.multiple_of((1 - group) * width, width), width)] = other
    first, lanes = features - 8 * 128, SEQS * 128
    here = own_tail[0:1, first : first + lanes] + own_tail[1:2, first : first + lanes]
    there = tail[0:1, first + lanes : first + 2 * lanes] + tail[1:2, first + lanes : first + 2 * lanes]
    high, low = split_high(here + there)
    for i, target in enumerate((own_block,) + tuple(sends)):
        rows = total[i * share : (i + 1) * share, :]
        if i == 0:
            target[...] = jnp.zeros_like(target)
            target[0:share, :] = rows
            target[6:7, 0:lanes] = high
            target[7:8, 0:lanes] = low
        else:
            total[half : half + share, :] = rows
            if i == 1:
                total[half + 6 : half + 8, :] = jnp.zeros((2, features), jnp.float32)
                total[half + 6 : half + 7, 0:lanes] = high
                total[half + 7 : half + 8, 0:lanes] = low
            target[...] = total[half : half + 8, :].astype(jnp.bfloat16)


def last_kernel(*refs):
    own, arrived, (input_grad, norms) = refs[0], refs[1:-2], refs[-2:]
    total = own[...] + sum(ref[...].astype(jnp.float32) for ref in arrived)
    input_grad[...] = total[0 : input_grad.shape[0]].astype(jnp.bfloat16)
    roots = jnp.sqrt(total[6:7, 0 : SEQS * 128] + total[7:8, 0 : SEQS * 128])
    for e in range(SEQS):
        norms[e] = jnp.max(roots[:, e * 128 : (e + 1) * 128])


def shared(inputs, cotangent, gate_weight, up_weight, down_weight, ia3_scale, seq_ids):
    groups, wide, strips = lax.axis_size("groups"), lax.axis_size("wide"), lax.axis_size("narrow")
    share, features = inputs.shape
    width = gate_weight.shape[1] // (strips * groups)
    half = share * wide
    tokens = half * groups
    f32, bf16 = jnp.float32, jnp.bfloat16
    slabs = 4 * share // 8
    weights = tuple(
        pltpu.with_memory_space_constraint(weight, pltpu.HBM)
        for weight in (gate_weight, up_weight, down_weight)
    )
    weight_shapes = [
        pltpu.VMEM((features, width), bf16),
        pltpu.VMEM((features, width), bf16),
        pltpu.VMEM((width, features), bf16),
    ]
    load_sem = [pltpu.SemaphoreType.DMA((3,))]

    def load(strip, after=()):
        args = weights + tuple(after)
        return call(
            functools.partial(load_kernel, strip, groups),
            f"load_{strip}",
            weight_shapes,
            args,
            {i: pltpu.HBM if i < 3 else pl.ANY for i in range(len(args))},
            load_sem,
        )

    def hold(strip):
        return [held(array) for array in kept[strip]]

    kept = {}
    packed = call(
        pack_kernel,
        "pack",
        pltpu.VMEM((slabs, 8, features // 2), bf16),
        [pltpu.with_memory_space_constraint(array, pltpu.HBM) for array in (inputs, cotangent)],
        scratch=[pltpu.VMEM((4 * share, features // 2), f32)],
    )
    blocks = [packed] + [exchange(packed, "wide", s) for s in range(1, wide)]
    kept[3] = load(3)
    relayed = call(
        functools.partial(relay_kernel, share),
        "relay",
        pltpu.VMEM((wide * slabs + 1, 8, features // 2), bf16),
        blocks + [seq_ids] + hold(3)[:1],
        {wide: pltpu.SMEM},
    )
    other_relayed = exchange(relayed, "groups", 1)
    kept[2] = load(2, [relayed])
    kept[1] = load(1, [relayed])

    tokens_all, cotans_all, diagonal = call(
        functools.partial(first_kernel, share),
        "forward_3",
        [pltpu.VMEM((tokens, features), bf16)] * 2 + [pltpu.VMEM((3, tokens, width), bf16)],
        [relayed, other_relayed] + hold(3) + hold(2)[:1] + hold(1)[:1],
        scratch=[pltpu.VMEM((tokens, features), f32)] * 2,
    )
    panel = [tokens_all, cotans_all]
    diagonal = exchange(diagonal, "narrow", 1)
    crossing = call(
        forward_add_kernel,
        "forward_2",
        pltpu.VMEM((3, tokens, width), bf16),
        panel + hold(2) + [diagonal],
    )
    crossed = exchange(crossing, "narrow", 2)
    near, *kept[0] = call(
        functools.partial(forward_load_kernel, 0, groups),
        "forward_1",
        [pltpu.VMEM((3, tokens, width), bf16)] + weight_shapes,
        panel + hold(1) + list(weights) + [held(crossing)],
        {5: pltpu.HBM, 6: pltpu.HBM, 7: pltpu.HBM},
        load_sem,
    )
    near = exchange(near, "narrow", 1)
    own_part = call(
        forward_kernel, "forward_0", pltpu.VMEM((3, tokens, width), f32), panel + hold(0)
    )

    resident = [array for s in range(strips) for array in hold(s)[:2]]
    message, grads, other_grads = call(
        functools.partial(middle_kernel, groups),
        "middle",
        [
            pltpu.VMEM((2 * tokens + 16, width), bf16),
            pltpu.VMEM((SEQS, width), f32),
            pltpu.VMEM((SEQS, width), f32),
        ],
        [own_part, near, crossed, ia3_scale[None, :], relayed, other_relayed] + resident,
        scratch=[pltpu.VMEM((groups * SEQS, width), f32)],
    )

    total = pltpu.VMEM((tokens, features), f32)
    message_1 = exchange(message, "narrow", 1)
    message_2 = exchange(message, "narrow", 2)
    sums = call(backward_first_kernel, "backward_0", total, [message] + hold(0)[:2])
    sums = call(backward_next_kernel, "backward_1", total, [message_1] + hold(1)[:2] + [sums])
    message_2, sums = lax.optimization_barrier((message_2, sums))
    message_3 = exchange(message_2, "narrow", 1)
    sums = call(backward_next_kernel, "backward_2", total, [message_2] + hold(2)[:2] + [sums])
    own, own_tail, send = call(
        backward_last_kernel,
        "backward_3",
        [
            pltpu.VMEM((half, features), f32),
            pltpu.VMEM((8, features), f32),
            pltpu.VMEM((half // 8 + 1, 8, features), bf16),
        ],
        [message_3] + hold(3)[:2] + [sums, message, message_1, message_2, other_grads],
    )
    arrived = exchange(send, "groups", 1)
    example_grads, own_block, *sends = call(
        functools.partial(combine_kernel, share),
        "combine",
        [jax.ShapeDtypeStruct((SEQS, groups * width), f32), pltpu.VMEM((8, features), f32)]
        + [pltpu.VMEM((8, features), bf16)] * (wide - 1),
        [own, own_tail, arrived, grads],
        scratch=[pltpu.VMEM((half + 8, features), f32)],
    )
    arrived = [exchange(block, "wide", s + 1) for s, block in enumerate(sends)]
    input_grad, norms = call(
        last_kernel,
        "last",
        [jax.ShapeDtypeStruct((share, features), bf16), jax.ShapeDtypeStruct((SEQS,), f32)],
        [own_block] + arrived,
        out_spaces={1: pltpu.SMEM},
    )
    return (example_grads, norms, input_grad)


def power_of_two(number):
    return number & (number - 1) == 0


def local(inputs, cotangent, gate_weight, up_weight, down_weight, ia3_scale, seq_ids):
    groups, wide, narrow = lax.axis_size("groups"), lax.axis_size("wide"), lax.axis_size("narrow")
    share, (features, hidden) = inputs.shape[0], gate_weight.shape
    width = hidden // (narrow * groups)
    fits = (
        groups == 2
        and narrow == 4
        and power_of_two(wide)
        and hidden % (narrow * groups * 256) == 0
        and features % TILE == 0
        and features >= 2048
        and width <= features - 1024
        and share <= 6
        and share % 2 == 0
        and (share * wide) % 8 == 0
        and share * wide <= 64
        and 3 * features * hidden // groups * 2 <= 40 << 20
    )
    plan = shared if fits else whole_block
    return plan(inputs, cotangent, gate_weight, up_weight, down_weight, ia3_scale, seq_ids)


def solution(mesh):
    return jax.shard_map(
        local,
        mesh=mesh,
        in_specs=(
            P(("groups", "wide"), "narrow"),
            P(("groups", "wide"), "narrow"),
            P("narrow", "wide"),
            P("narrow", "wide"),
            P("wide", "narrow"),
            P("wide"),
            P("groups"),
        ),
        out_specs=(P("groups", ("wide", "narrow")), P("groups"), P(("groups", "wide"), "narrow")),
        check_vma=False,
    )
```

```python
import functools

import jax
import jax.numpy as jnp
from jax import lax
from jax.experimental import pallas as pl
from jax.experimental.pallas import tpu as pltpu
from jax.sharding import PartitionSpec as P

SEQS = 4
KERNEL_VMEM = 6 << 20


def contract_rows(left, right):
    return lax.dot_general(
        left, right, (((1,), (1,)), ((), ())), preferred_element_type=jnp.float32
    )


def local_grads(gate_pre, up_pre, mid_grad, scale_part):
    sigmoid_gate = jax.nn.sigmoid(gate_pre)
    activation = gate_pre * sigmoid_gate
    hidden = activation * up_pre
    scaled = scale_part * mid_grad
    d_up = (scaled * activation).astype(jnp.bfloat16)
    d_gate = (scaled * up_pre * sigmoid_gate * (1.0 + gate_pre * (1.0 - sigmoid_gate))).astype(
        jnp.bfloat16
    )
    return (hidden * mid_grad, d_gate, d_up)


def whole_block(inputs, cotangent, gate_weight, up_weight, down_weight, ia3_scale, seq_ids):
    panel_inputs = lax.all_gather(inputs, "wide", axis=0, tiled=True)
    panel_cotangent = lax.all_gather(cotangent, "wide", axis=0, tiled=True)
    gate_part = jnp.dot(panel_inputs, gate_weight, preferred_element_type=jnp.float32)
    up_part = jnp.dot(panel_inputs, up_weight, preferred_element_type=jnp.float32)
    mid_part = contract_rows(panel_cotangent, down_weight)
    quarter = gate_weight.shape[1] // lax.axis_size("narrow")
    position = lax.axis_index("narrow")
    onehot_full = (seq_ids[None, :] == jnp.arange(SEQS, dtype=jnp.int32)[:, None]).astype(
        jnp.float32
    )
    gate_pre, up_pre, mid_grad = (
        lax.psum_scatter(gate_part, "narrow", scatter_dimension=1, tiled=True),
        lax.psum_scatter(up_part, "narrow", scatter_dimension=1, tiled=True),
        lax.psum_scatter(mid_part, "narrow", scatter_dimension=1, tiled=True),
    )
    scale_part = lax.dynamic_slice_in_dim(ia3_scale, position * quarter, quarter, 0)
    product, d_gate, d_up = local_grads(gate_pre, up_pre, mid_grad, scale_part[None, :])
    example_grads = jnp.dot(onehot_full, product, precision=lax.Precision.HIGHEST)
    whole_gate, whole_up = (
        lax.all_gather(d_gate, "narrow", axis=1, tiled=True),
        lax.all_gather(d_up, "narrow", axis=1, tiled=True),
    )
    squares = lax.psum(jnp.sum(example_grads * example_grads, axis=1), ("wide", "narrow"))
    grad_norms = jnp.sqrt(squares)
    input_grad = lax.psum_scatter(
        contract_rows(whole_gate, gate_weight) + contract_rows(whole_up, up_weight),
        "wide",
        scatter_dimension=0,
        tiled=True,
    ).astype(jnp.bfloat16)
    return (example_grads, grad_norms, input_grad)


def exchange(array, axis, step):
    return lax.ppermute(array, axis, [(i, i ^ step) for i in range(lax.axis_size(axis))])


def held(array):
    return pltpu.with_memory_space_constraint(array, pltpu.VMEM)


def call(body, name, outs, args, spaces=None, scratch=(), out_spaces=None):
    spaces, out_spaces = spaces or {}, out_spaces or {}
    many = isinstance(outs, list)
    out_specs = [
        pl.BlockSpec(memory_space=out_spaces.get(i, pltpu.VMEM)) for i in range(len(outs) if many else 1)
    ]
    return pl.pallas_call(
        body,
        out_shape=outs,
        in_specs=[pl.BlockSpec(memory_space=spaces.get(i, pltpu.VMEM)) for i in range(len(args))],
        out_specs=out_specs if many else out_specs[0],
        scratch_shapes=list(scratch),
        compiler_params=pltpu.CompilerParams(vmem_limit_bytes=KERNEL_VMEM),
        cost_estimate=pl.CostEstimate(flops=1000, bytes_accessed=1000, transcendentals=0),
        name=name,
    )(*args)


def pack_kernel(inputs, cotangent, out, stage):
    share, features = inputs.shape
    half = features // 2
    for i, ref in enumerate((inputs, cotangent)):
        rows = ref[...].astype(jnp.float32)
        for j in range(2):
            stage[(2 * i + j) * share : (2 * i + j + 1) * share, :] = rows[:, j * half : (j + 1) * half]
    for k in range(out.shape[0]):
        out[k] = stage[8 * k : 8 * k + 8, :].astype(jnp.bfloat16)


def relay_kernel(share, *refs):
    blocks, ids, out = refs[:-3], refs[-3], refs[-1]
    slabs = blocks[0].shape[0]
    position = lax.axis_index("wide")
    for i, block in enumerate(blocks):
        out[i * slabs : (i + 1) * slabs] = block[...]
    row = lax.broadcasted_iota(jnp.int32, (8, 128), 0)
    keys = []
    for k in range(len(blocks) * share // 8):
        key = jnp.zeros((8, 128), jnp.int32)
        for r in range(8):
            block, j = divmod(8 * k + r, share)
            key = jnp.where(row == r, ids[(position ^ block) * share + j], key)
        keys.append(key.astype(jnp.float32))
    keys.append(jnp.zeros((8, out.shape[2] - 128 * len(keys)), jnp.float32))
    out[len(blocks) * slabs] = jnp.concatenate(keys, axis=1).astype(jnp.bfloat16)


GATE, UP, DOWN = range(3)
WHOLE_STRIP = (GATE, UP, DOWN)


def start_loads(pieces, groups, sources, targets, sem):
    copies = []
    for i, (kind, strip) in enumerate(pieces):
        target = targets[i]
        width = target.shape[0 if kind == DOWN else 1]
        owner = lax.axis_index("narrow") ^ strip
        start = pl.multiple_of((owner * groups + lax.axis_index("groups")) * width, width)
        source = sources[kind]
        source = source.at[pl.ds(start, width), :] if kind == DOWN else source.at[:, pl.ds(start, width)]
        copies.append(pltpu.make_async_copy(source, target, sem.at[i]))
    for copy in copies:
        copy.start()
    return copies


def load_kernel(pieces, groups, *refs):
    count = len(pieces)
    for copy in start_loads(pieces, groups, refs[:3], refs[-1 - count : -1], refs[-1]):
        copy.wait()


def loading(body, pieces, groups, outs):
    count = len(pieces)

    def kernel(*refs):
        sources, rest = refs[:3], refs[3:]
        at = len(rest) - outs[1] - 1 - count
        targets, sem = rest[at : at + count], rest[at + count + outs[1]]
        copies = start_loads(pieces, groups, sources, targets, sem)
        body(*rest[:at], *rest[at + count : at + count + outs[1]])
        for copy in copies:
            copy.wait()

    return kernel


def strip_parts(tokens, cotans, gate, up, down, put):
    tile = 256

    @pl.loop(0, gate.shape[1] // tile)
    def _(i):
        span = pl.ds(pl.multiple_of(i * tile, tile), tile)
        put(GATE, span, jnp.dot(tokens[...], gate[:, span], preferred_element_type=jnp.float32))
        put(UP, span, jnp.dot(tokens[...], up[:, span], preferred_element_type=jnp.float32))
        put(DOWN, span, contract_rows(cotans[...], down[span, :]))


def forward_kernel(tokens, cotans, gate, up, down, out):
    def put(kind, span, part):
        out[kind, :, span] = part

    strip_parts(tokens, cotans, gate, up, down, put)


def forward_add_kernel(tokens, cotans, gate, up, down, arrived, out):
    def put(kind, span, part):
        out[kind, :, span] = (part + arrived[kind, :, span]).astype(out.dtype)

    strip_parts(tokens, cotans, gate, up, down, put)


def first_kernel(share, relayed, other, gate, up, down, *refs):
    tokens, cotans, part, rows, cots = refs[-5:]
    slabs, half = 4 * share // 8, rows.shape[1] // 2
    count = (relayed.shape[0] - 1) // slabs
    for side, source in enumerate((relayed, other)):
        for i in range(count):
            packed = source[i * slabs : (i + 1) * slabs].astype(jnp.float32).reshape(4 * share, half)
            at = (side * count + i) * share
            for j, target in enumerate((rows, rows, cots, cots)):
                span = slice((j % 2) * half, (j % 2 + 1) * half)
                target[at : at + share, span] = packed[j * share : (j + 1) * share]
    tokens[...] = rows[...].astype(jnp.bfloat16)
    cotans[...] = cots[...].astype(jnp.bfloat16)
    forward_kernel(tokens, cotans, gate, up, down, part)


def own_strip_kernel(groups, *refs):
    sources, (tokens, cotans) = refs[:3], refs[3:5]
    out, (gate, up, down), sem = refs[-5], refs[-4:-1], refs[-1]
    pieces = [(kind, 0) for kind in WHOLE_STRIP]
    copies = start_loads(pieces, groups, sources, (gate, up, down), sem)
    copies[GATE].wait()
    out[GATE] = jnp.dot(tokens[...], gate[...], preferred_element_type=jnp.float32)
    copies[UP].wait()
    out[UP] = jnp.dot(tokens[...], up[...], preferred_element_type=jnp.float32)
    copies[DOWN].wait()
    out[DOWN] = contract_rows(cotans[...], down[...])


def middle_kernel(groups, *refs):
    own, arrived, crossed, scale, relayed, other_relayed = refs[:6]
    message, grads, other_grads, stage = refs[-4:]
    _, tokens, width = own.shape
    narrow, group = lax.axis_index("narrow"), lax.axis_index("groups")
    sums = [own[i] + arrived[i] + crossed[i].astype(jnp.float32) for i in range(3)]
    start = pl.multiple_of((narrow * groups + group) * width, width)
    product, d_gate, d_up = local_grads(*sums, scale[:, pl.ds(start, width)])
    message[0:tokens, :] = d_gate
    message[tokens : 2 * tokens, :] = d_up
    half = tokens // groups
    for side, (source, target) in enumerate(((relayed, grads), (other_relayed, other_grads))):
        marks = source[source.shape[0] - 1].astype(jnp.float32)
        seq = jnp.concatenate(
            [
                jnp.concatenate([marks[:, k * 128 : (k + 1) * 128]] * (width // 128), axis=1)
                for k in range(half // 8)
            ],
            axis=0,
        )
        part = product[side * half : (side + 1) * half]
        for e in range(SEQS):
            total = jnp.sum(jnp.where(seq == float(e), part, 0.0), axis=0, keepdims=True)
            target[e : e + 1, :] = total
            stage[side * SEQS + e : side * SEQS + e + 1, :] = total
    every = stage[...]
    squares = jnp.broadcast_to(jnp.sum(every * every, axis=1, keepdims=True), every.shape)
    high = squares.astype(jnp.bfloat16).astype(jnp.float32)
    message[2 * tokens :, :] = jnp.concatenate([high, squares - high], axis=0).astype(jnp.bfloat16)


TILE = 512


def backward_part(message, gate, up, start):
    tokens = (message.shape[0] - 16) // 2
    gate_term = contract_rows(message[0:tokens, :], gate[start : start + TILE, :])
    return gate_term + contract_rows(message[tokens : 2 * tokens, :], up[start : start + TILE, :])


def backward_first_kernel(message, gate, up, total):
    for start in range(0, total.shape[1], TILE):
        total[:, start : start + TILE] = backward_part(message, gate, up, start)


def backward_next_kernel(message, gate, up, before, total):
    for start in range(0, total.shape[1], TILE):
        total[:, start : start + TILE] = before[:, start : start + TILE] + backward_part(message, gate, up, start)


def split_high(values):
    high = values.astype(jnp.bfloat16).astype(jnp.float32)
    return high, values - high


def backward_last_kernel(message, gate, up, before, *refs):
    others, other_grads = refs[:3], refs[3]
    own, own_tail, send = refs[4:7]
    half, features = own.shape
    for start in range(0, features, TILE):
        span = slice(start, start + TILE)
        total = before[:, span] + backward_part(message, gate, up, start)
        own[:, span] = total[:half]
        for k in range(half // 8):
            send[k, :, span] = total[half + 8 * k : half + 8 * k + 8].astype(jnp.bfloat16)
    squares = sum(ref[ref.shape[0] - 16 :, 0:128].astype(jnp.float32) for ref in (message,) + others)
    high, low = split_high(squares[0:8] + squares[8:16])
    own_tail[...] = jnp.zeros_like(own_tail)
    width = other_grads.shape[1]
    for i, rows in enumerate(split_high(other_grads[...])):
        own_tail[i * SEQS : (i + 1) * SEQS, 0:width] = rows
    first = features - 8 * 128
    for k in range(8):
        span = slice(first + k * 128, first + (k + 1) * 128)
        own_tail[0:1, span] = high[k : k + 1]
        own_tail[1:2, span] = low[k : k + 1]
    send[half // 8] = own_tail[...].astype(jnp.bfloat16)


def combine_kernel(share, own, own_tail, arrived, grads, *refs):
    example_grads, own_block, sends, total = refs[0], refs[1], refs[2:-1], refs[-1]
    half, features = own.shape
    width = grads.shape[1]
    group = lax.axis_index("groups")
    slabs = half // 8
    for k in range(slabs):
        total[8 * k : 8 * k + 8, :] = own[8 * k : 8 * k + 8, :] + arrived[k].astype(jnp.float32)
    tail = arrived[slabs].astype(jnp.float32)
    other = tail[0:SEQS, 0:width] + tail[SEQS : 2 * SEQS, 0:width]
    example_grads[:, pl.ds(pl.multiple_of(group * width, width), width)] = grads[...]
    example_grads[:, pl.ds(pl.multiple_of((1 - group) * width, width), width)] = other
    first, lanes = features - 8 * 128, SEQS * 128
    here = own_tail[0:1, first : first + lanes] + own_tail[1:2, first : first + lanes]
    there = tail[0:1, first + lanes : first + 2 * lanes] + tail[1:2, first + lanes : first + 2 * lanes]
    high, low = split_high(here + there)
    for i, target in enumerate((own_block,) + tuple(sends)):
        rows = total[i * share : (i + 1) * share, :]
        if i == 0:
            target[...] = jnp.zeros_like(target)
            target[0:share, :] = rows
            target[6:7, 0:lanes] = high
            target[7:8, 0:lanes] = low
        else:
            total[half : half + share, :] = rows
            if i == 1:
                total[half + 6 : half + 8, :] = jnp.zeros((2, features), jnp.float32)
                total[half + 6 : half + 7, 0:lanes] = high
                total[half + 7 : half + 8, 0:lanes] = low
            target[...] = total[half : half + 8, :].astype(jnp.bfloat16)


def last_kernel(*refs):
    own, arrived, (input_grad, norms) = refs[0], refs[1:-2], refs[-2:]
    total = own[...] + sum(ref[...].astype(jnp.float32) for ref in arrived)
    input_grad[...] = total[0 : input_grad.shape[0]].astype(jnp.bfloat16)
    roots = jnp.sqrt(total[6:7, 0 : SEQS * 128] + total[7:8, 0 : SEQS * 128])
    for e in range(SEQS):
        norms[e] = jnp.max(roots[:, e * 128 : (e + 1) * 128])


def shared(inputs, cotangent, gate_weight, up_weight, down_weight, ia3_scale, seq_ids):
    groups, wide, strips = lax.axis_size("groups"), lax.axis_size("wide"), lax.axis_size("narrow")
    share, features = inputs.shape
    width = gate_weight.shape[1] // (strips * groups)
    half = share * wide
    tokens = half * groups
    f32, bf16 = jnp.float32, jnp.bfloat16
    slabs = 4 * share // 8
    weights = tuple(
        pltpu.with_memory_space_constraint(weight, pltpu.HBM)
        for weight in (gate_weight, up_weight, down_weight)
    )
    weight_shapes = [
        pltpu.VMEM((features, width), bf16),
        pltpu.VMEM((features, width), bf16),
        pltpu.VMEM((width, features), bf16),
    ]
    kept = {}

    def load(name, pieces, after=()):
        args = weights + tuple(after)
        arrays = call(
            functools.partial(load_kernel, pieces, groups),
            name,
            [weight_shapes[kind] for kind, _ in pieces],
            args,
            {i: pltpu.HBM if i < 3 else pl.ANY for i in range(len(args))},
            [pltpu.SemaphoreType.DMA((len(pieces),))],
        )
        kept.update(zip(pieces, arrays))

    def call_loading(body, name, pieces, outs, args, scratch=()):
        made = call(
            loading(body, pieces, groups, (len(outs), len(outs) + len(scratch))),
            name,
            [weight_shapes[kind] for kind, _ in pieces] + outs,
            list(weights) + args,
            {i: pltpu.HBM for i in range(3)},
            list(scratch) + [pltpu.SemaphoreType.DMA((len(pieces),))],
        )
        kept.update(zip(pieces, made))
        return made[len(pieces) :]

    def hold(strip, kinds=WHOLE_STRIP):
        return [held(kept[kind, strip]) for kind in kinds]

    packed = call(
        pack_kernel,
        "pack",
        pltpu.VMEM((slabs, 8, features // 2), bf16),
        [pltpu.with_memory_space_constraint(array, pltpu.HBM) for array in (inputs, cotangent)],
        scratch=[pltpu.VMEM((4 * share, features // 2), f32)],
    )
    arrived = {s: exchange(packed, "wide", s) for s in reversed(range(1, wide))}
    load("load_a", [(kind, 3) for kind in WHOLE_STRIP])
    relayed = call(
        functools.partial(relay_kernel, share),
        "relay",
        pltpu.VMEM((wide * slabs + 1, 8, features // 2), bf16),
        [packed] + [arrived[s] for s in range(1, wide)] + [seq_ids] + hold(3, [GATE]),
        {wide: pltpu.SMEM},
    )
    other_relayed = exchange(relayed, "groups", 1)
    load("load_b", [(kind, 1) for kind in WHOLE_STRIP] + [(GATE, 2)], [relayed])

    part = pltpu.VMEM((3, tokens, width), f32)
    tokens_all, cotans_all, diagonal = call_loading(
        functools.partial(first_kernel, share),
        "forward_3",
        [(UP, 2)],
        [pltpu.VMEM((tokens, features), bf16)] * 2 + [part],
        [relayed, other_relayed] + hold(3) + hold(1, [GATE]),
        [pltpu.VMEM((tokens, features), f32)] * 2,
    )
    panel = [tokens_all, cotans_all]
    diagonal = exchange(diagonal, "narrow", 1)
    (near,) = call_loading(forward_kernel, "forward_1", [(DOWN, 2)], [part], panel + hold(1))
    near = exchange(near, "narrow", 1)
    crossing = call(
        forward_add_kernel,
        "forward_2",
        pltpu.VMEM((3, tokens, width), bf16),
        panel + hold(2) + [diagonal],
    )
    crossed = exchange(crossing, "narrow", 2)
    own_part, *arrays = call(
        functools.partial(own_strip_kernel, groups),
        "forward_0",
        [part] + weight_shapes,
        list(weights) + panel + [held(crossing)],
        {i: pltpu.HBM for i in range(3)},
        [pltpu.SemaphoreType.DMA((3,))],
    )
    kept.update({(kind, 0): array for kind, array in enumerate(arrays)})

    resident = [array for s in range(strips) for array in hold(s, [GATE, UP])]
    message, grads, other_grads = call(
        functools.partial(middle_kernel, groups),
        "middle",
        [
            pltpu.VMEM((2 * tokens + 16, width), bf16),
            pltpu.VMEM((SEQS, width), f32),
            pltpu.VMEM((SEQS, width), f32),
        ],
        [own_part, near, crossed, ia3_scale[None, :], relayed, other_relayed] + resident,
        scratch=[pltpu.VMEM((groups * SEQS, width), f32)],
    )

    total = pltpu.VMEM((tokens, features), f32)
    message_1 = exchange(message, "narrow", 1)
    message_2 = exchange(message, "narrow", 2)
    sums = call(backward_first_kernel, "backward_0", total, [message] + hold(0, [GATE, UP]))
    sums = call(backward_next_kernel, "backward_1", total, [message_1] + hold(1, [GATE, UP]) + [sums])
    message_2, sums = lax.optimization_barrier((message_2, sums))
    message_3 = exchange(message_2, "narrow", 1)
    sums = call(backward_next_kernel, "backward_2", total, [message_2] + hold(2, [GATE, UP]) + [sums])
    own, own_tail, send = call(
        backward_last_kernel,
        "backward_3",
        [
            pltpu.VMEM((half, features), f32),
            pltpu.VMEM((8, features), f32),
            pltpu.VMEM((half // 8 + 1, 8, features), bf16),
        ],
        [message_3] + hold(3, [GATE, UP]) + [sums, message, message_1, message_2, other_grads],
    )
    arrived = exchange(send, "groups", 1)
    example_grads, own_block, *sends = call(
        functools.partial(combine_kernel, share),
        "combine",
        [jax.ShapeDtypeStruct((SEQS, groups * width), f32), pltpu.VMEM((8, features), f32)]
        + [pltpu.VMEM((8, features), bf16)] * (wide - 1),
        [own, own_tail, arrived, grads],
        scratch=[pltpu.VMEM((half + 8, features), f32)],
    )
    arrived = [exchange(block, "wide", s + 1) for s, block in enumerate(sends)]
    input_grad, norms = call(
        last_kernel,
        "last",
        [jax.ShapeDtypeStruct((share, features), bf16), jax.ShapeDtypeStruct((SEQS,), f32)],
        [own_block] + arrived,
        out_spaces={1: pltpu.SMEM},
    )
    return (example_grads, norms, input_grad)


def power_of_two(number):
    return number & (number - 1) == 0


def local(inputs, cotangent, gate_weight, up_weight, down_weight, ia3_scale, seq_ids):
    groups, wide, narrow = lax.axis_size("groups"), lax.axis_size("wide"), lax.axis_size("narrow")
    share, (features, hidden) = inputs.shape[0], gate_weight.shape
    width = hidden // (narrow * groups)
    fits = (
        groups == 2
        and narrow == 4
        and power_of_two(wide)
        and hidden % (narrow * groups * 256) == 0
        and features % TILE == 0
        and features >= 2048
        and width <= features - 1024
        and share <= 6
        and share % 2 == 0
        and (share * wide) % 8 == 0
        and share * wide <= 64
        and 3 * features * hidden // groups * 2 <= 40 << 20
    )
    plan = shared if fits else whole_block
    return plan(inputs, cotangent, gate_weight, up_weight, down_weight, ia3_scale, seq_ids)


def solution(mesh):
    return jax.shard_map(
        local,
        mesh=mesh,
        in_specs=(
            P(("groups", "wide"), "narrow"),
            P(("groups", "wide"), "narrow"),
            P("narrow", "wide"),
            P("narrow", "wide"),
            P("wide", "narrow"),
            P("wide"),
            P("groups"),
        ),
        out_specs=(P("groups", ("wide", "narrow")), P("groups"), P(("groups", "wide"), "narrow")),
        check_vma=False,
    )
```

```python
import functools

import jax
import jax.numpy as jnp
from jax import lax
from jax.experimental import pallas as pl
from jax.experimental.pallas import tpu as pltpu
from jax.sharding import PartitionSpec as P

SEQS = 4
KERNEL_VMEM = 6 << 20


def contract_rows(left, right):
    return lax.dot_general(
        left, right, (((1,), (1,)), ((), ())), preferred_element_type=jnp.float32
    )


def local_grads(gate_pre, up_pre, mid_grad, scale_part):
    sigmoid_gate = jax.nn.sigmoid(gate_pre)
    activation = gate_pre * sigmoid_gate
    hidden = activation * up_pre
    scaled = scale_part * mid_grad
    d_up = (scaled * activation).astype(jnp.bfloat16)
    d_gate = (scaled * up_pre * sigmoid_gate * (1.0 + gate_pre * (1.0 - sigmoid_gate))).astype(
        jnp.bfloat16
    )
    return (hidden * mid_grad, d_gate, d_up)


def whole_block(inputs, cotangent, gate_weight, up_weight, down_weight, ia3_scale, seq_ids):
    panel_inputs = lax.all_gather(inputs, "wide", axis=0, tiled=True)
    panel_cotangent = lax.all_gather(cotangent, "wide", axis=0, tiled=True)
    gate_part = jnp.dot(panel_inputs, gate_weight, preferred_element_type=jnp.float32)
    up_part = jnp.dot(panel_inputs, up_weight, preferred_element_type=jnp.float32)
    mid_part = contract_rows(panel_cotangent, down_weight)
    quarter = gate_weight.shape[1] // lax.axis_size("narrow")
    position = lax.axis_index("narrow")
    onehot_full = (seq_ids[None, :] == jnp.arange(SEQS, dtype=jnp.int32)[:, None]).astype(
        jnp.float32
    )
    gate_pre, up_pre, mid_grad = (
        lax.psum_scatter(gate_part, "narrow", scatter_dimension=1, tiled=True),
        lax.psum_scatter(up_part, "narrow", scatter_dimension=1, tiled=True),
        lax.psum_scatter(mid_part, "narrow", scatter_dimension=1, tiled=True),
    )
    scale_part = lax.dynamic_slice_in_dim(ia3_scale, position * quarter, quarter, 0)
    product, d_gate, d_up = local_grads(gate_pre, up_pre, mid_grad, scale_part[None, :])
    example_grads = jnp.dot(onehot_full, product, precision=lax.Precision.HIGHEST)
    whole_gate, whole_up = (
        lax.all_gather(d_gate, "narrow", axis=1, tiled=True),
        lax.all_gather(d_up, "narrow", axis=1, tiled=True),
    )
    squares = lax.psum(jnp.sum(example_grads * example_grads, axis=1), ("wide", "narrow"))
    grad_norms = jnp.sqrt(squares)
    input_grad = lax.psum_scatter(
        contract_rows(whole_gate, gate_weight) + contract_rows(whole_up, up_weight),
        "wide",
        scatter_dimension=0,
        tiled=True,
    ).astype(jnp.bfloat16)
    return (example_grads, grad_norms, input_grad)


def exchange(array, axis, step):
    return lax.ppermute(array, axis, [(i, i ^ step) for i in range(lax.axis_size(axis))])


def held(array):
    return pltpu.with_memory_space_constraint(array, pltpu.VMEM)


def call(body, name, outs, args, spaces=None, scratch=(), out_spaces=None):
    spaces, out_spaces = spaces or {}, out_spaces or {}
    many = isinstance(outs, list)
    out_specs = [
        pl.BlockSpec(memory_space=out_spaces.get(i, pltpu.VMEM)) for i in range(len(outs) if many else 1)
    ]
    return pl.pallas_call(
        body,
        out_shape=outs,
        in_specs=[pl.BlockSpec(memory_space=spaces.get(i, pltpu.VMEM)) for i in range(len(args))],
        out_specs=out_specs if many else out_specs[0],
        scratch_shapes=list(scratch),
        compiler_params=pltpu.CompilerParams(vmem_limit_bytes=KERNEL_VMEM),
        cost_estimate=pl.CostEstimate(flops=1000, bytes_accessed=1000, transcendentals=0),
        name=name,
    )(*args)


def pack_kernel(inputs, cotangent, out, stage):
    share, features = inputs.shape
    half = features // 2
    for i, ref in enumerate((inputs, cotangent)):
        rows = ref[...].astype(jnp.float32)
        for j in range(2):
            stage[(2 * i + j) * share : (2 * i + j + 1) * share, :] = rows[:, j * half : (j + 1) * half]
    for k in range(out.shape[0]):
        out[k] = stage[8 * k : 8 * k + 8, :].astype(jnp.bfloat16)


def relay_kernel(share, *refs):
    blocks, ids, out = refs[:-3], refs[-3], refs[-1]
    slabs = blocks[0].shape[0]
    position = lax.axis_index("wide")
    for i, block in enumerate(blocks):
        out[i * slabs : (i + 1) * slabs] = block[...]
    row = lax.broadcasted_iota(jnp.int32, (8, 128), 0)
    keys = []
    for k in range(len(blocks) * share // 8):
        key = jnp.zeros((8, 128), jnp.int32)
        for r in range(8):
            block, j = divmod(8 * k + r, share)
            key = jnp.where(row == r, ids[(position ^ block) * share + j], key)
        keys.append(key.astype(jnp.float32))
    keys.append(jnp.zeros((8, out.shape[2] - 128 * len(keys)), jnp.float32))
    out[len(blocks) * slabs] = jnp.concatenate(keys, axis=1).astype(jnp.bfloat16)


GATE, UP, DOWN = range(3)
WHOLE_STRIP = (GATE, UP, DOWN)


def start_loads(pieces, groups, sources, targets, sem):
    copies = []
    for i, (kind, strip) in enumerate(pieces):
        target = targets[i]
        width = target.shape[0 if kind == DOWN else 1]
        owner = lax.axis_index("narrow") ^ strip
        start = pl.multiple_of((owner * groups + lax.axis_index("groups")) * width, width)
        source = sources[kind]
        source = source.at[pl.ds(start, width), :] if kind == DOWN else source.at[:, pl.ds(start, width)]
        copies.append(pltpu.make_async_copy(source, target, sem.at[i]))
    for copy in copies:
        copy.start()
    return copies


def load_kernel(pieces, groups, *refs):
    count = len(pieces)
    for copy in start_loads(pieces, groups, refs[:3], refs[-1 - count : -1], refs[-1]):
        copy.wait()


def loading(body, pieces, groups, outs):
    count = len(pieces)

    def kernel(*refs):
        sources, rest = refs[:3], refs[3:]
        at = len(rest) - outs[1] - 1 - count
        targets, sem = rest[at : at + count], rest[at + count + outs[1]]
        copies = start_loads(pieces, groups, sources, targets, sem)
        body(*rest[:at], *rest[at + count : at + count + outs[1]])
        for copy in copies:
            copy.wait()

    return kernel


def strip_parts(tokens, cotans, gate, up, down, put):
    tile = 256

    @pl.loop(0, gate.shape[1] // tile)
    def _(i):
        span = pl.ds(pl.multiple_of(i * tile, tile), tile)
        put(GATE, span, jnp.dot(tokens[...], gate[:, span], preferred_element_type=jnp.float32))
        put(UP, span, jnp.dot(tokens[...], up[:, span], preferred_element_type=jnp.float32))
        put(DOWN, span, contract_rows(cotans[...], down[span, :]))


def forward_kernel(tokens, cotans, gate, up, down, *refs):
    out = refs[-1]

    def put(kind, span, part):
        out[kind, :, span] = part.astype(out.dtype)

    strip_parts(tokens, cotans, gate, up, down, put)


def forward_add_kernel(tokens, cotans, gate, up, down, arrived, out):
    def put(kind, span, part):
        out[kind, :, span] = (part + arrived[kind, :, span]).astype(out.dtype)

    strip_parts(tokens, cotans, gate, up, down, put)


def first_kernel(share, relayed, other, gate, up, down, *refs):
    tokens, cotans, part, rows, cots = refs[-5:]
    slabs, half = 4 * share // 8, rows.shape[1] // 2
    count = (relayed.shape[0] - 1) // slabs
    for side, source in enumerate((relayed, other)):
        for i in range(count):
            packed = source[i * slabs : (i + 1) * slabs].astype(jnp.float32).reshape(4 * share, half)
            at = (side * count + i) * share
            for j, target in enumerate((rows, rows, cots, cots)):
                span = slice((j % 2) * half, (j % 2 + 1) * half)
                target[at : at + share, span] = packed[j * share : (j + 1) * share]
    tokens[...] = rows[...].astype(jnp.bfloat16)
    cotans[...] = cots[...].astype(jnp.bfloat16)
    forward_kernel(tokens, cotans, gate, up, down, part)


def own_strip_kernel(groups, *refs):
    sources, (tokens, cotans, gate, up) = refs[:3], refs[3:7]
    out, down, sem = refs[-3:]
    copies = start_loads([(DOWN, 0)], groups, sources, [down], sem)
    tile = 256

    @pl.loop(0, gate.shape[1] // tile)
    def _(i):
        span = pl.ds(pl.multiple_of(i * tile, tile), tile)
        out[GATE, :, span] = jnp.dot(tokens[...], gate[:, span], preferred_element_type=jnp.float32)
        out[UP, :, span] = jnp.dot(tokens[...], up[:, span], preferred_element_type=jnp.float32)

    copies[0].wait()
    out[DOWN] = contract_rows(cotans[...], down[...])


def middle_kernel(groups, *refs):
    own, arrived, crossed, scale, relayed, other_relayed = refs[:6]
    message, grads, other_grads, stage = refs[-4:]
    _, tokens, width = own.shape
    narrow, group = lax.axis_index("narrow"), lax.axis_index("groups")
    sums = [own[i] + arrived[i].astype(jnp.float32) + crossed[i].astype(jnp.float32) for i in range(3)]
    start = pl.multiple_of((narrow * groups + group) * width, width)
    product, d_gate, d_up = local_grads(*sums, scale[:, pl.ds(start, width)])
    message[0:tokens, :] = d_gate
    message[tokens : 2 * tokens, :] = d_up
    half = tokens // groups
    for side, (source, target) in enumerate(((relayed, grads), (other_relayed, other_grads))):
        marks = source[source.shape[0] - 1].astype(jnp.float32)
        seq = jnp.concatenate(
            [
                jnp.concatenate([marks[:, k * 128 : (k + 1) * 128]] * (width // 128), axis=1)
                for k in range(half // 8)
            ],
            axis=0,
        )
        part = product[side * half : (side + 1) * half]
        for e in range(SEQS):
            total = jnp.sum(jnp.where(seq == float(e), part, 0.0), axis=0, keepdims=True)
            target[e : e + 1, :] = total
            stage[side * SEQS + e : side * SEQS + e + 1, :] = total
    every = stage[...]
    squares = jnp.broadcast_to(jnp.sum(every * every, axis=1, keepdims=True), every.shape)
    high = squares.astype(jnp.bfloat16).astype(jnp.float32)
    message[2 * tokens :, :] = jnp.concatenate([high, squares - high], axis=0).astype(jnp.bfloat16)


TILE = 512


def backward_part(message, gate, up, start):
    tokens = (message.shape[0] - 16) // 2
    gate_term = contract_rows(message[0:tokens, :], gate[start : start + TILE, :])
    return gate_term + contract_rows(message[tokens : 2 * tokens, :], up[start : start + TILE, :])


def backward_first_kernel(message, gate, up, total):
    for start in range(0, total.shape[1], TILE):
        total[:, start : start + TILE] = backward_part(message, gate, up, start)


def backward_next_kernel(message, gate, up, before, total):
    for start in range(0, total.shape[1], TILE):
        total[:, start : start + TILE] = before[:, start : start + TILE] + backward_part(message, gate, up, start)


def split_high(values):
    high = values.astype(jnp.bfloat16).astype(jnp.float32)
    return high, values - high


def backward_last_kernel(message, gate, up, before, *refs):
    others, other_grads = refs[:3], refs[3]
    own, own_tail, send = refs[4:7]
    half, features = own.shape
    wide = send.shape[2]
    for start in range(0, features, TILE):
        span = slice(start, start + TILE)
        total = before[:, span] + backward_part(message, gate, up, start)
        own[:, span] = total[:half]
        at = slice(start % wide, start % wide + TILE)
        for k in range(half // 8):
            slab = start // wide * (half // 8) + k
            send[slab, :, at] = total[half + 8 * k : half + 8 * k + 8].astype(jnp.bfloat16)
    squares = sum(ref[ref.shape[0] - 16 :, 0:128].astype(jnp.float32) for ref in (message,) + others)
    high, low = split_high(squares[0:8] + squares[8:16])
    own_tail[...] = jnp.zeros_like(own_tail)
    width = other_grads.shape[1]
    for i, rows in enumerate(split_high(other_grads[...])):
        own_tail[i * SEQS : (i + 1) * SEQS, 0:width] = rows
    own_tail[:, width : width + 128] = high
    own_tail[:, width + 128 : width + 256] = low
    send[send.shape[0] - 1] = own_tail[...].astype(jnp.bfloat16)


def combine_kernel(share, own, own_tail, arrived, grads, *refs):
    example_grads, own_block, sends, total = refs[0], refs[1], refs[2:-1], refs[-1]
    half, features = own.shape
    width = grads.shape[1]
    group = lax.axis_index("groups")
    slabs, wide = half // 8, own_tail.shape[1]
    for k in range(slabs):
        for i in range(features // wide):
            span = slice(i * wide, (i + 1) * wide)
            total[8 * k : 8 * k + 8, span] = own[8 * k : 8 * k + 8, span] + arrived[i * slabs + k].astype(jnp.float32)
    tail = arrived[arrived.shape[0] - 1].astype(jnp.float32)
    other = tail[0:SEQS, 0:width] + tail[SEQS : 2 * SEQS, 0:width]
    example_grads[:, pl.ds(pl.multiple_of(group * width, width), width)] = grads[...]
    example_grads[:, pl.ds(pl.multiple_of((1 - group) * width, width), width)] = other
    lanes = SEQS * 128

    def squares(ref, first):
        rows = ref[:, width : width + 128] + ref[:, width + 128 : width + 256]
        return jnp.concatenate([rows[first + e : first + e + 1] for e in range(SEQS)], axis=1)

    here, there = squares(own_tail[...], 0), squares(tail, SEQS)
    high, low = split_high(here + there)
    for i, target in enumerate((own_block,) + tuple(sends)):
        rows = total[i * share : (i + 1) * share, :]
        if i == 0:
            target[...] = jnp.zeros_like(target)
            target[0:share, :] = rows
            target[6:7, 0:lanes] = high
            target[7:8, 0:lanes] = low
        else:
            total[half : half + share, :] = rows
            if i == 1:
                total[half + 6 : half + 8, :] = jnp.zeros((2, features), jnp.float32)
                total[half + 6 : half + 7, 0:lanes] = high
                total[half + 7 : half + 8, 0:lanes] = low
            target[...] = total[half : half + 8, :].astype(jnp.bfloat16)


def last_kernel(*refs):
    own, arrived, (input_grad, norms) = refs[0], refs[1:-2], refs[-2:]
    total = own[...] + sum(ref[...].astype(jnp.float32) for ref in arrived)
    input_grad[...] = total[0 : input_grad.shape[0]].astype(jnp.bfloat16)
    roots = jnp.sqrt(total[6:7, 0 : SEQS * 128] + total[7:8, 0 : SEQS * 128])
    for e in range(SEQS):
        norms[e] = jnp.max(roots[:, e * 128 : (e + 1) * 128])


def shared(inputs, cotangent, gate_weight, up_weight, down_weight, ia3_scale, seq_ids):
    groups, wide, strips = lax.axis_size("groups"), lax.axis_size("wide"), lax.axis_size("narrow")
    share, features = inputs.shape
    width = gate_weight.shape[1] // (strips * groups)
    half = share * wide
    tokens = half * groups
    f32, bf16 = jnp.float32, jnp.bfloat16
    slabs = 4 * share // 8
    weights = tuple(
        pltpu.with_memory_space_constraint(weight, pltpu.HBM)
        for weight in (gate_weight, up_weight, down_weight)
    )
    weight_shapes = [
        pltpu.VMEM((features, width), bf16),
        pltpu.VMEM((features, width), bf16),
        pltpu.VMEM((width, features), bf16),
    ]
    kept = {}

    def load(name, pieces, after=()):
        args = weights + tuple(after)
        arrays = call(
            functools.partial(load_kernel, pieces, groups),
            name,
            [weight_shapes[kind] for kind, _ in pieces],
            args,
            {i: pltpu.HBM if i < 3 else pl.ANY for i in range(len(args))},
            [pltpu.SemaphoreType.DMA((len(pieces),))],
        )
        kept.update(zip(pieces, arrays))

    def call_loading(body, name, pieces, outs, args, scratch=()):
        made = call(
            loading(body, pieces, groups, (len(outs), len(outs) + len(scratch))),
            name,
            [weight_shapes[kind] for kind, _ in pieces] + outs,
            list(weights) + args,
            {i: pltpu.HBM for i in range(3)},
            list(scratch) + [pltpu.SemaphoreType.DMA((len(pieces),))],
        )
        kept.update(zip(pieces, made))
        return made[len(pieces) :]

    def hold(strip, kinds=WHOLE_STRIP):
        return [held(kept[kind, strip]) for kind in kinds]

    packed = call(
        pack_kernel,
        "pack",
        pltpu.VMEM((slabs, 8, features // 2), bf16),
        [pltpu.with_memory_space_constraint(array, pltpu.HBM) for array in (inputs, cotangent)],
        scratch=[pltpu.VMEM((4 * share, features // 2), f32)],
    )
    arrived = [exchange(packed, "wide", s) for s in range(1, wide)]
    load("load_a", [(kind, 3) for kind in WHOLE_STRIP])
    relayed = call(
        functools.partial(relay_kernel, share),
        "relay",
        pltpu.VMEM((wide * slabs + 1, 8, features // 2), bf16),
        [packed] + arrived + [seq_ids] + hold(3, [GATE]),
        {wide: pltpu.SMEM},
    )
    other_relayed = exchange(relayed, "groups", 1)
    load("load_b", [(kind, 2) for kind in WHOLE_STRIP] + [(GATE, 1)], [relayed])

    part = pltpu.VMEM((3, tokens, width), f32)
    near_shape = pltpu.VMEM((3, tokens, width), bf16)
    tokens_all, cotans_all, diagonal = call_loading(
        functools.partial(first_kernel, share),
        "forward_3",
        [(UP, 1)],
        [pltpu.VMEM((tokens, features), bf16)] * 2 + [part],
        [relayed, other_relayed] + hold(3) + hold(2, [GATE]),
        [pltpu.VMEM((tokens, features), f32)] * 2,
    )
    panel = [tokens_all, cotans_all]
    diagonal = exchange(diagonal, "narrow", 1)
    (crossing,) = call_loading(
        forward_add_kernel,
        "forward_2",
        [(DOWN, 1)],
        [pltpu.VMEM((3, tokens, width), bf16)],
        panel + hold(2) + [diagonal],
    )
    crossed = exchange(crossing, "narrow", 2)
    (near,) = call_loading(
        forward_kernel, "forward_1", [(GATE, 0), (UP, 0)], [near_shape], panel + hold(1) + [held(crossing)]
    )
    near = exchange(near, "narrow", 1)
    own_part, kept[DOWN, 0] = call(
        functools.partial(own_strip_kernel, groups),
        "forward_0",
        [part, weight_shapes[DOWN]],
        list(weights) + panel + hold(0, [GATE, UP]),
        {i: pltpu.HBM for i in range(3)},
        [pltpu.SemaphoreType.DMA((1,))],
    )

    resident = [array for s in range(strips) for array in hold(s, [GATE, UP])]
    message, grads, other_grads = call(
        functools.partial(middle_kernel, groups),
        "middle",
        [
            pltpu.VMEM((2 * tokens + 16, width), bf16),
            pltpu.VMEM((SEQS, width), f32),
            pltpu.VMEM((SEQS, width), f32),
        ],
        [own_part, near, crossed, ia3_scale[None, :], relayed, other_relayed] + resident,
        scratch=[pltpu.VMEM((groups * SEQS, width), f32)],
    )

    total = pltpu.VMEM((tokens, features), f32)
    message_1 = exchange(message, "narrow", 1)
    message_2 = exchange(message, "narrow", 2)
    sums = call(backward_first_kernel, "backward_0", total, [message] + hold(0, [GATE, UP]))
    sums = call(backward_next_kernel, "backward_1", total, [message_1] + hold(1, [GATE, UP]) + [sums])
    message_2, sums = lax.optimization_barrier((message_2, sums))
    message_3 = exchange(message_2, "narrow", 1)
    sums = call(backward_next_kernel, "backward_2", total, [message_2] + hold(2, [GATE, UP]) + [sums])
    own, own_tail, send = call(
        backward_last_kernel,
        "backward_3",
        [
            pltpu.VMEM((half, features), f32),
            pltpu.VMEM((8, features // 2), f32),
            pltpu.VMEM((half // 4 + 1, 8, features // 2), bf16),
        ],
        [message_3] + hold(3, [GATE, UP]) + [sums, message, message_1, message_2, other_grads],
    )
    arrived = exchange(send, "groups", 1)
    example_grads, own_block, *sends = call(
        functools.partial(combine_kernel, share),
        "combine",
        [jax.ShapeDtypeStruct((SEQS, groups * width), f32), pltpu.VMEM((8, features), f32)]
        + [pltpu.VMEM((8, features), bf16)] * (wide - 1),
        [own, own_tail, arrived, grads],
        scratch=[pltpu.VMEM((half + 8, features), f32)],
    )
    arrived = [exchange(sends[s - 1], "wide", s) for s in reversed(range(1, wide))]
    input_grad, norms = call(
        last_kernel,
        "last",
        [jax.ShapeDtypeStruct((share, features), bf16), jax.ShapeDtypeStruct((SEQS,), f32)],
        [own_block] + arrived,
        out_spaces={1: pltpu.SMEM},
    )
    return (example_grads, norms, input_grad)


def power_of_two(number):
    return number & (number - 1) == 0


def local(inputs, cotangent, gate_weight, up_weight, down_weight, ia3_scale, seq_ids):
    groups, wide, narrow = lax.axis_size("groups"), lax.axis_size("wide"), lax.axis_size("narrow")
    share, (features, hidden) = inputs.shape[0], gate_weight.shape
    width = hidden // (narrow * groups)
    fits = (
        groups == 2
        and narrow == 4
        and power_of_two(wide)
        and hidden % (narrow * groups * 256) == 0
        and features >= 2048
        and width <= features // 2 - 256
        and features % (2 * TILE) == 0
        and share <= 6
        and share % 2 == 0
        and (share * wide) % 8 == 0
        and share * wide <= 64
        and 3 * features * hidden // groups * 2 <= 40 << 20
    )
    plan = shared if fits else whole_block
    return plan(inputs, cotangent, gate_weight, up_weight, down_weight, ia3_scale, seq_ids)


def solution(mesh):
    return jax.shard_map(
        local,
        mesh=mesh,
        in_specs=(
            P(("groups", "wide"), "narrow"),
            P(("groups", "wide"), "narrow"),
            P("narrow", "wide"),
            P("narrow", "wide"),
            P("wide", "narrow"),
            P("wide"),
            P("groups"),
        ),
        out_specs=(P("groups", ("wide", "narrow")), P("groups"), P(("groups", "wide"), "narrow")),
        check_vma=False,
    )
```

```python
from types import SimpleNamespace

import jax
import jax.numpy as jnp
from jax import lax
from jax.experimental import pallas as pl
from jax.experimental.pallas import tpu as pltpu
from jax.sharding import PartitionSpec as P

SEQS = 4
KERNEL_VMEM = 6 << 20


def contract_rows(left, right):
    return lax.dot_general(
        left, right, (((1,), (1,)), ((), ())), preferred_element_type=jnp.float32
    )


def local_grads(gate_pre, up_pre, mid_grad, scale_part):
    sigmoid_gate = jax.nn.sigmoid(gate_pre)
    activation = gate_pre * sigmoid_gate
    hidden = activation * up_pre
    scaled = scale_part * mid_grad
    d_up = (scaled * activation).astype(jnp.bfloat16)
    d_gate = (scaled * up_pre * sigmoid_gate * (1.0 + gate_pre * (1.0 - sigmoid_gate))).astype(
        jnp.bfloat16
    )
    return (hidden * mid_grad, d_gate, d_up)


def whole_block(inputs, cotangent, gate_weight, up_weight, down_weight, ia3_scale, seq_ids):
    panel_inputs = lax.all_gather(inputs, "wide", axis=0, tiled=True)
    panel_cotangent = lax.all_gather(cotangent, "wide", axis=0, tiled=True)
    gate_part = jnp.dot(panel_inputs, gate_weight, preferred_element_type=jnp.float32)
    up_part = jnp.dot(panel_inputs, up_weight, preferred_element_type=jnp.float32)
    mid_part = contract_rows(panel_cotangent, down_weight)
    quarter = gate_weight.shape[1] // lax.axis_size("narrow")
    position = lax.axis_index("narrow")
    onehot_full = (seq_ids[None, :] == jnp.arange(SEQS, dtype=jnp.int32)[:, None]).astype(
        jnp.float32
    )
    gate_pre, up_pre, mid_grad = (
        lax.psum_scatter(gate_part, "narrow", scatter_dimension=1, tiled=True),
        lax.psum_scatter(up_part, "narrow", scatter_dimension=1, tiled=True),
        lax.psum_scatter(mid_part, "narrow", scatter_dimension=1, tiled=True),
    )
    scale_part = lax.dynamic_slice_in_dim(ia3_scale, position * quarter, quarter, 0)
    product, d_gate, d_up = local_grads(gate_pre, up_pre, mid_grad, scale_part[None, :])
    example_grads = jnp.dot(onehot_full, product, precision=lax.Precision.HIGHEST)
    whole_gate, whole_up = (
        lax.all_gather(d_gate, "narrow", axis=1, tiled=True),
        lax.all_gather(d_up, "narrow", axis=1, tiled=True),
    )
    squares = lax.psum(jnp.sum(example_grads * example_grads, axis=1), ("wide", "narrow"))
    grad_norms = jnp.sqrt(squares)
    input_grad = lax.psum_scatter(
        contract_rows(whole_gate, gate_weight) + contract_rows(whole_up, up_weight),
        "wide",
        scatter_dimension=0,
        tiled=True,
    ).astype(jnp.bfloat16)
    return (example_grads, grad_norms, input_grad)


def exchange(array, axis, step):
    return lax.ppermute(array, axis, [(i, i ^ step) for i in range(lax.axis_size(axis))])


def held(array):
    return pltpu.with_memory_space_constraint(array, pltpu.VMEM)


def in_hbm(array):
    return pltpu.with_memory_space_constraint(array, pltpu.HBM)


def call(body, name, outs, ins, scratch=None, in_spaces=None, out_spaces=None):
    scratch, in_spaces, out_spaces = scratch or {}, in_spaces or {}, out_spaces or {}
    names = list(ins) + list(outs) + list(scratch)

    def kernel(*refs):
        body(SimpleNamespace(**dict(zip(names, refs))))

    arrays = pl.pallas_call(
        kernel,
        out_shape=list(outs.values()),
        in_specs=[pl.BlockSpec(memory_space=in_spaces.get(key, pltpu.VMEM)) for key in ins],
        out_specs=[pl.BlockSpec(memory_space=out_spaces.get(key, pltpu.VMEM)) for key in outs],
        scratch_shapes=list(scratch.values()),
        compiler_params=pltpu.CompilerParams(vmem_limit_bytes=KERNEL_VMEM),
        cost_estimate=pl.CostEstimate(flops=1000, bytes_accessed=1000, transcendentals=0),
        name=name,
    )(*ins.values())
    return dict(zip(outs, arrays))


GATE, UP, DOWN = "gate", "up", "down"
KINDS = (GATE, UP, DOWN)
CHUNKS = 4
TILE = 512


def piece(kind, strip):
    return f"{kind}_{strip}"


def start_loads(r, pieces, groups):
    waits = {}
    for i, (kind, strip) in enumerate(pieces):
        target, source = getattr(r, piece(kind, strip)), getattr(r, kind)
        rows, columns = target.shape
        owner = (lax.axis_index("narrow") ^ strip) * groups + lax.axis_index("groups")
        copies = []
        for c in range(CHUNKS):
            size = rows // CHUNKS
            if kind == DOWN:
                part = source.at[pl.ds(pl.multiple_of(owner * rows + c * size, size), size), :]
            else:
                part = source.at[c * size : (c + 1) * size, pl.ds(pl.multiple_of(owner * columns, columns), columns)]
            copies.append(pltpu.make_async_copy(part, target.at[c * size : (c + 1) * size, :], r.sem.at[i, c]))
        waits[kind, strip] = copies
    for copies in waits.values():
        for copy in copies:
            copy.start()

    def wait(*which):
        for key in which or list(waits):
            for copy in waits.pop(key):
                copy.wait()

    return wait


def product(r, kind, strip, span):
    weight = getattr(r, piece(kind, strip))
    if kind == DOWN:
        return contract_rows(r.cotans[...], weight[span, :])
    return jnp.dot(r.tokens[...], weight[:, span], preferred_element_type=jnp.float32)


def by_tiles(width, body):
    tile = 256

    @pl.loop(0, width // tile)
    def _(i):
        body(pl.ds(pl.multiple_of(i * tile, tile), tile))


def split_high(values):
    high = values.astype(jnp.bfloat16).astype(jnp.float32)
    return high, values - high


def shared(inputs, cotangent, gate_weight, up_weight, down_weight, ia3_scale, seq_ids):
    groups, wide, strips = lax.axis_size("groups"), lax.axis_size("wide"), lax.axis_size("narrow")
    share, features = inputs.shape
    width = gate_weight.shape[1] // (strips * groups)
    half = share * wide
    tokens = half * groups
    f32, bf16 = jnp.float32, jnp.bfloat16
    slabs, side = 4 * share // 8, features // 2
    sources = {GATE: in_hbm(gate_weight), UP: in_hbm(up_weight), DOWN: in_hbm(down_weight)}
    weight_shape = {
        GATE: pltpu.VMEM((features, width), bf16),
        UP: pltpu.VMEM((features, width), bf16),
        DOWN: pltpu.VMEM((width, features), bf16),
    }
    kept = {}

    def hold(*pieces):
        return {piece(*key): held(kept[key]) for key in pieces}

    def loading(body, name, pieces, outs, ins, scratch=None):
        def whole(r):
            wait = start_loads(r, pieces, groups)
            body(r, wait)

        made = call(
            whole,
            name,
            {**{piece(*key): weight_shape[key[0]] for key in pieces}, **outs},
            {**sources, **ins},
            {**(scratch or {}), "sem": pltpu.SemaphoreType.DMA((len(pieces), CHUNKS))},
            {kind: pltpu.HBM for kind in KINDS},
        )
        kept.update({key: made[piece(*key)] for key in pieces})
        return made

    def pack(r):
        for i, ref in enumerate((r.inputs, r.cotangent)):
            rows = ref[...].astype(f32)
            for j in range(2):
                at = (2 * i + j) * share
                r.stage[at : at + share, :] = rows[:, j * side : (j + 1) * side]
        for k in range(slabs):
            slab = r.stage[8 * k : 8 * k + 8, :].astype(bf16)
            r.packed[k] = slab
            r.marked[k] = slab
        row = lax.broadcasted_iota(jnp.int32, (8, 128), 0)
        position = lax.axis_index("wide")
        keys = []
        for k in range(half // 8):
            key = jnp.zeros((8, 128), jnp.int32)
            for i in range(8):
                block, j = divmod(8 * k + i, share)
                key = jnp.where(row == i, r.ids[(position ^ block) * share + j], key)
            keys.append(key.astype(f32))
        keys.append(jnp.zeros((8, side - 128 * len(keys)), f32))
        r.marked[slabs] = jnp.concatenate(keys, axis=1).astype(bf16)

    made = call(
        pack,
        "pack",
        {"packed": pltpu.VMEM((slabs, 8, side), bf16), "marked": pltpu.VMEM((slabs + 1, 8, side), bf16)},
        {"inputs": in_hbm(inputs), "cotangent": in_hbm(cotangent), "ids": in_hbm(seq_ids)},
        {"stage": pltpu.VMEM((4 * share, side), f32)},
        {"ids": pltpu.SMEM},
    )
    marked = made["marked"]
    blocks = [marked] + [exchange(made["packed"], "wide", s) for s in range(1, wide)]
    others = [exchange(marked, "groups", 1)]

    def only_wait(r, wait):
        wait()

    def load_a(r, wait):
        r.mark[...] = jnp.zeros_like(r.mark)
        wait()

    mark = loading(load_a, "load_a", [(kind, 3) for kind in KINDS], {"mark": pltpu.VMEM((8, 128), f32)}, {})["mark"]
    for s in reversed(range(1, wide)):
        blocks[s], mark = lax.optimization_barrier((blocks[s], mark))
        others.insert(1, exchange(blocks[s], "groups", 1))
    loading(only_wait, "load_b", [(DOWN, 2), (GATE, 2)], {}, {"after": mark})

    def forward_3_rest(r, wait):
        for i in range(groups * wide):
            packed = getattr(r, f"block_{i}")[0:slabs].astype(f32).reshape(4 * share, side)
            for j, target in enumerate((r.rows, r.rows, r.cots, r.cots)):
                span = slice((j % 2) * side, (j % 2 + 1) * side)
                target[i * share : (i + 1) * share, span] = packed[j * share : (j + 1) * share]
        r.tokens[...] = r.rows[...].astype(bf16)
        r.cotans[...] = r.cots[...].astype(bf16)

        def step(span):
            for i, kind in enumerate((GATE, UP)):
                r.part[i, :, span] = product(r, kind, 3, span)

        by_tiles(width, step)
        wait()

    panel_shape = pltpu.VMEM((tokens, features), bf16)
    made = loading(
        forward_3_rest,
        "forward_3_rest",
        [(UP, 2)],
        {"tokens": panel_shape, "cotans": panel_shape, "part": pltpu.VMEM((2, tokens, width), f32)},
        {
            **{f"block_{i}": block for i, block in enumerate(blocks + others)},
            **hold((GATE, 3), (UP, 3), (DOWN, 2)),
        },
        {"rows": pltpu.VMEM((tokens, features), f32), "cots": pltpu.VMEM((tokens, features), f32)},
    )
    tokens_in, cotans_in = {"tokens": made["tokens"]}, {"cotans": made["cotans"]}
    far_rest = exchange(made["part"], "narrow", 1)

    def forward_3_down(r, wait):
        def step(span):
            r.part[:, span] = product(r, DOWN, 3, span)

        by_tiles(width, step)
        wait()

    made = loading(
        forward_3_down,
        "forward_3_down",
        [(DOWN, 1)],
        {"part": pltpu.VMEM((tokens, width), f32)},
        {**cotans_in, **hold((DOWN, 3)), "after": held(made["part"])},
    )
    far_down = exchange(made["part"], "narrow", 1)

    def forward_2_rest(r, wait):
        def step(span):
            for i, kind in enumerate((GATE, UP)):
                r.part[i, :, span] = (product(r, kind, 2, span) + r.arrived[i, :, span]).astype(bf16)

        by_tiles(width, step)
        wait()

    made = loading(
        forward_2_rest,
        "forward_2_rest",
        [(GATE, 1)],
        {"part": pltpu.VMEM((2, tokens, width), bf16)},
        {**tokens_in, **hold((GATE, 2), (UP, 2)), "arrived": far_rest, "after": held(made["part"])},
    )

    def forward_2_down(r):
        r.part[0:2] = r.rest[...]

        def step(span):
            r.part[2, :, span] = (product(r, DOWN, 2, span) + r.arrived[:, span]).astype(bf16)

        by_tiles(width, step)

    made = call(
        forward_2_down,
        "forward_2_down",
        {"part": pltpu.VMEM((3, tokens, width), bf16)},
        {**cotans_in, **hold((DOWN, 2)), "arrived": far_down, "rest": held(made["part"])},
    )
    crossed = exchange(made["part"], "narrow", 2)

    def forward_1(r, wait):
        def step(span):
            r.part[0, :, span] = product(r, GATE, 1, span).astype(bf16)
            r.part[2, :, span] = product(r, DOWN, 1, span).astype(bf16)

        by_tiles(width, step)
        wait((UP, 1))
        r.part[1] = product(r, UP, 1, slice(None)).astype(bf16)
        wait()

    made = loading(
        forward_1,
        "forward_1",
        [(UP, 1), (GATE, 0)],
        {"part": pltpu.VMEM((3, tokens, width), bf16)},
        {**tokens_in, **cotans_in, **hold((GATE, 1), (DOWN, 1)), "after": held(made["part"])},
    )
    near = exchange(made["part"], "narrow", 1)

    def forward_0(r, wait):
        def step(span):
            r.part[0, :, span] = product(r, GATE, 0, span)

        by_tiles(width, step)
        wait((UP, 0))
        r.part[1] = product(r, UP, 0, slice(None))
        wait((DOWN, 0))
        r.part[2] = product(r, DOWN, 0, slice(None))

    made = loading(
        forward_0,
        "forward_0",
        [(UP, 0), (DOWN, 0)],
        {"part": pltpu.VMEM((3, tokens, width), f32)},
        {**tokens_in, **cotans_in, **hold((GATE, 0))},
    )
    own_part = made["part"]

    def middle(r):
        narrow, group = lax.axis_index("narrow"), lax.axis_index("groups")
        sums = [r.own[i] + r.near[i].astype(f32) + r.crossed[i].astype(f32) for i in range(3)]
        start = pl.multiple_of((narrow * groups + group) * width, width)
        contribution, d_gate, d_up = local_grads(*sums, r.scale[:, pl.ds(start, width)])
        r.message[0:tokens, :] = d_gate
        r.message[tokens : 2 * tokens, :] = d_up
        r.message_gate[0:tokens, :] = d_gate
        r.message_up[...] = d_up
        for i, (source, target) in enumerate(((r.marked, r.grads), (r.other_marked, r.other_grads))):
            marks = source[slabs].astype(f32)
            seq = jnp.concatenate(
                [
                    jnp.concatenate([marks[:, k * 128 : (k + 1) * 128]] * (width // 128), axis=1)
                    for k in range(half // 8)
                ],
                axis=0,
            )
            part = contribution[i * half : (i + 1) * half]
            for e in range(SEQS):
                total = jnp.sum(jnp.where(seq == float(e), part, 0.0), axis=0, keepdims=True)
                target[e : e + 1, :] = total
                r.stage[i * SEQS + e : i * SEQS + e + 1, :] = total
        every = r.stage[...]
        squares = jnp.broadcast_to(jnp.sum(every * every, axis=1, keepdims=True), every.shape)
        tail = jnp.concatenate(split_high(squares), axis=0).astype(bf16)
        r.message[2 * tokens :, :] = tail
        r.message_gate[tokens:, :] = tail

    resident = [(kind, s) for s in range(strips) for kind in (GATE, UP)]
    made = call(
        middle,
        "middle",
        {
            "message": pltpu.VMEM((2 * tokens + 16, width), bf16),
            "message_gate": pltpu.VMEM((tokens + 16, width), bf16),
            "message_up": pltpu.VMEM((tokens, width), bf16),
            "grads": pltpu.VMEM((SEQS, width), f32),
            "other_grads": pltpu.VMEM((SEQS, width), f32),
        },
        {
            "own": own_part,
            "near": near,
            "crossed": crossed,
            "scale": ia3_scale[None, :],
            "marked": marked,
            "other_marked": others[0],
            **hold(*resident),
        },
        {"stage": pltpu.VMEM((groups * SEQS, width), f32)},
    )
    message, grads, other_grads = made["message"], made["grads"], made["other_grads"]

    def term(r, strip, kind, grads_in, start):
        weight = getattr(r, piece(kind, strip))
        return contract_rows(grads_in, weight[start : start + TILE, :])

    total_shape = {"total": pltpu.VMEM((tokens, features), f32)}

    def both_terms(strip, before):
        def body(r):
            for start in range(0, features, TILE):
                span = slice(start, start + TILE)
                value = term(r, strip, GATE, r.message[0:tokens, :], start)
                value = value + term(r, strip, UP, r.message[tokens : 2 * tokens, :], start)
                r.total[:, span] = r.before[:, span] + value if before else value

        return body

    def one_term(strip, kind):
        def body(r):
            for start in range(0, features, TILE):
                span = slice(start, start + TILE)
                r.total[:, span] = r.before[:, span] + term(r, strip, kind, r.message[0:tokens, :], start)

        return body

    across_gate = exchange(made["message_gate"], "narrow", 2)
    across_up = exchange(made["message_up"], "narrow", 2)
    beside = exchange(message, "narrow", 1)
    sums = call(both_terms(0, False), "backward_0", total_shape, {"message": message, **hold(*resident[0:2])})
    sums = call(
        both_terms(1, True),
        "backward_1",
        total_shape,
        {"message": beside, "before": sums["total"], **hold(*resident[2:4])},
    )
    across_gate, before = lax.optimization_barrier((across_gate, sums["total"]))
    far_gate = exchange(across_gate, "narrow", 1)
    sums = call(
        one_term(2, GATE), "backward_2_gate", total_shape, {"message": across_gate, "before": before, **hold((GATE, 2))}
    )
    across_up, before = lax.optimization_barrier((across_up, sums["total"]))
    far_up = exchange(across_up, "narrow", 1)
    sums = call(
        one_term(2, UP), "backward_2_up", total_shape, {"message": across_up, "before": before, **hold((UP, 2))}
    )
    sums = call(
        one_term(3, GATE),
        "backward_3_gate",
        total_shape,
        {"message": far_gate, "before": sums["total"], **hold((GATE, 3))},
    )

    def backward_last(r):
        for start in range(0, features, TILE):
            span, at = slice(start, start + TILE), slice(start % side, start % side + TILE)
            total = r.before[:, span] + term(r, 3, UP, r.message[...], start)
            r.own[:, span] = total[:half]
            for k in range(half // 8):
                r.send[start // side * (half // 8) + k, :, at] = total[half + 8 * k : half + 8 * k + 8].astype(bf16)
        tails = (r.message_0, r.message_1, r.message_2, r.message_3)
        squares = sum(ref[ref.shape[0] - 16 :, 0:128].astype(f32) for ref in tails)
        high, low = split_high(squares[0:8] + squares[8:16])
        r.own_tail[...] = jnp.zeros_like(r.own_tail)
        for i, rows in enumerate(split_high(r.other_grads[...])):
            r.own_tail[i * SEQS : (i + 1) * SEQS, 0:width] = rows
        r.own_tail[:, width : width + 128] = high
        r.own_tail[:, width + 128 : width + 256] = low
        r.send[r.send.shape[0] - 1] = r.own_tail[...].astype(bf16)

    made = call(
        backward_last,
        "backward_3_up",
        {
            "own": pltpu.VMEM((half, features), f32),
            "own_tail": pltpu.VMEM((8, side), f32),
            "send": pltpu.VMEM((half // 4 + 1, 8, side), bf16),
        },
        {
            "message": far_up,
            "before": sums["total"],
            "message_0": message,
            "message_1": beside,
            "message_2": across_gate,
            "message_3": far_gate,
            "other_grads": other_grads,
            **hold((UP, 3)),
        },
    )

    def combine(r):
        group = lax.axis_index("groups")
        count = half // 8
        for k in range(count):
            for i in range(features // side):
                span = slice(i * side, (i + 1) * side)
                part = r.own[8 * k : 8 * k + 8, span] + r.arrived[i * count + k].astype(f32)
                r.total[8 * k : 8 * k + 8, span] = part
        tail = r.arrived[r.arrived.shape[0] - 1].astype(f32)
        other = tail[0:SEQS, 0:width] + tail[SEQS : 2 * SEQS, 0:width]
        r.example_grads[:, pl.ds(pl.multiple_of(group * width, width), width)] = r.grads[...]
        r.example_grads[:, pl.ds(pl.multiple_of((1 - group) * width, width), width)] = other
        lanes = SEQS * 128

        def squares(values, first):
            rows = values[:, width : width + 128] + values[:, width + 128 : width + 256]
            return jnp.concatenate([rows[first + e : first + e + 1] for e in range(SEQS)], axis=1)

        high, low = split_high(squares(r.own_tail[...], 0) + squares(tail, SEQS))
        r.block_0[...] = jnp.zeros_like(r.block_0)
        r.block_0[6:7, 0:lanes] = high
        r.block_0[7:8, 0:lanes] = low
        for i in range(1, wide):
            r.block_0[0:share, :] = r.total[i * share : (i + 1) * share, :]
            getattr(r, f"block_{i}")[...] = r.block_0[...].astype(bf16)
        r.block_0[0:share, :] = r.total[0:share, :]

    made = call(
        combine,
        "combine",
        {
            "example_grads": jax.ShapeDtypeStruct((SEQS, groups * width), f32),
            "block_0": pltpu.VMEM((8, features), f32),
            **{f"block_{i}": pltpu.VMEM((8, features), bf16) for i in range(1, wide)},
        },
        {
            "own": made["own"],
            "own_tail": made["own_tail"],
            "arrived": exchange(made["send"], "groups", 1),
            "grads": grads,
        },
        {"total": pltpu.VMEM((half, features), f32)},
    )

    def last(r):
        total = r.block_0[...]
        for i in range(1, wide):
            total = total + getattr(r, f"block_{i}")[...].astype(f32)
        r.input_grad[...] = total[0:share].astype(bf16)
        roots = jnp.sqrt(total[6:7, 0 : SEQS * 128] + total[7:8, 0 : SEQS * 128])
        for e in range(SEQS):
            r.norms[e] = jnp.max(roots[:, e * 128 : (e + 1) * 128])

    ends = call(
        last,
        "last",
        {"input_grad": jax.ShapeDtypeStruct((share, features), bf16), "norms": jax.ShapeDtypeStruct((SEQS,), f32)},
        {
            "block_0": made["block_0"],
            **{f"block_{i}": exchange(made[f"block_{i}"], "wide", i) for i in reversed(range(1, wide))},
        },
        out_spaces={"norms": pltpu.SMEM},
    )
    return (made["example_grads"], ends["norms"], ends["input_grad"])


def power_of_two(number):
    return number & (number - 1) == 0


def local(inputs, cotangent, gate_weight, up_weight, down_weight, ia3_scale, seq_ids):
    groups, wide, narrow = lax.axis_size("groups"), lax.axis_size("wide"), lax.axis_size("narrow")
    share, (features, hidden) = inputs.shape[0], gate_weight.shape
    width = hidden // (narrow * groups)
    fits = (
        groups == 2
        and narrow == 4
        and power_of_two(wide)
        and hidden % (narrow * groups * 256) == 0
        and features >= 2048
        and width <= features // 2 - 256
        and features % (2 * TILE) == 0
        and share <= 6
        and share % 2 == 0
        and (share * wide) % 8 == 0
        and share * wide <= 64
        and 3 * features * hidden // groups * 2 <= 40 << 20
    )
    plan = shared if fits else whole_block
    return plan(inputs, cotangent, gate_weight, up_weight, down_weight, ia3_scale, seq_ids)


def solution(mesh):
    return jax.shard_map(
        local,
        mesh=mesh,
        in_specs=(
            P(("groups", "wide"), "narrow"),
            P(("groups", "wide"), "narrow"),
            P("narrow", "wide"),
            P("narrow", "wide"),
            P("wide", "narrow"),
            P("wide"),
            P("groups"),
        ),
        out_specs=(P("groups", ("wide", "narrow")), P("groups"), P(("groups", "wide"), "narrow")),
        check_vma=False,
    )
```

```python
import functools

import jax
import jax.numpy as jnp
from jax import lax
from jax.experimental import pallas as pl
from jax.experimental.pallas import tpu as pltpu
from jax.sharding import PartitionSpec as P

SEQS = 4
KERNEL_VMEM = 6 << 20


def contract_rows(left, right):
    return lax.dot_general(
        left, right, (((1,), (1,)), ((), ())), preferred_element_type=jnp.float32
    )


def local_grads(gate_pre, up_pre, mid_grad, scale_part):
    sigmoid_gate = jax.nn.sigmoid(gate_pre)
    activation = gate_pre * sigmoid_gate
    hidden = activation * up_pre
    scaled = scale_part * mid_grad
    d_up = (scaled * activation).astype(jnp.bfloat16)
    d_gate = (scaled * up_pre * sigmoid_gate * (1.0 + gate_pre * (1.0 - sigmoid_gate))).astype(
        jnp.bfloat16
    )
    return (hidden * mid_grad, d_gate, d_up)


def whole_block(inputs, cotangent, gate_weight, up_weight, down_weight, ia3_scale, seq_ids):
    panel_inputs = lax.all_gather(inputs, "wide", axis=0, tiled=True)
    panel_cotangent = lax.all_gather(cotangent, "wide", axis=0, tiled=True)
    gate_part = jnp.dot(panel_inputs, gate_weight, preferred_element_type=jnp.float32)
    up_part = jnp.dot(panel_inputs, up_weight, preferred_element_type=jnp.float32)
    mid_part = contract_rows(panel_cotangent, down_weight)
    quarter = gate_weight.shape[1] // lax.axis_size("narrow")
    position = lax.axis_index("narrow")
    onehot_full = (seq_ids[None, :] == jnp.arange(SEQS, dtype=jnp.int32)[:, None]).astype(
        jnp.float32
    )
    gate_pre, up_pre, mid_grad = (
        lax.psum_scatter(gate_part, "narrow", scatter_dimension=1, tiled=True),
        lax.psum_scatter(up_part, "narrow", scatter_dimension=1, tiled=True),
        lax.psum_scatter(mid_part, "narrow", scatter_dimension=1, tiled=True),
    )
    scale_part = lax.dynamic_slice_in_dim(ia3_scale, position * quarter, quarter, 0)
    product, d_gate, d_up = local_grads(gate_pre, up_pre, mid_grad, scale_part[None, :])
    example_grads = jnp.dot(onehot_full, product, precision=lax.Precision.HIGHEST)
    whole_gate, whole_up = (
        lax.all_gather(d_gate, "narrow", axis=1, tiled=True),
        lax.all_gather(d_up, "narrow", axis=1, tiled=True),
    )
    squares = lax.psum(jnp.sum(example_grads * example_grads, axis=1), ("wide", "narrow"))
    grad_norms = jnp.sqrt(squares)
    input_grad = lax.psum_scatter(
        contract_rows(whole_gate, gate_weight) + contract_rows(whole_up, up_weight),
        "wide",
        scatter_dimension=0,
        tiled=True,
    ).astype(jnp.bfloat16)
    return (example_grads, grad_norms, input_grad)


def exchange(array, axis, step):
    return lax.ppermute(array, axis, [(i, i ^ step) for i in range(lax.axis_size(axis))])


def held(array):
    return pltpu.with_memory_space_constraint(array, pltpu.VMEM)


def call(body, name, outs, args, spaces=None, scratch=(), out_spaces=None):
    spaces, out_spaces = spaces or {}, out_spaces or {}
    many = isinstance(outs, list)
    out_specs = [
        pl.BlockSpec(memory_space=out_spaces.get(i, pltpu.VMEM)) for i in range(len(outs) if many else 1)
    ]
    return pl.pallas_call(
        body,
        out_shape=outs,
        in_specs=[pl.BlockSpec(memory_space=spaces.get(i, pltpu.VMEM)) for i in range(len(args))],
        out_specs=out_specs if many else out_specs[0],
        scratch_shapes=list(scratch),
        compiler_params=pltpu.CompilerParams(vmem_limit_bytes=KERNEL_VMEM),
        cost_estimate=pl.CostEstimate(flops=1000, bytes_accessed=1000, transcendentals=0),
        name=name,
    )(*args)


def pack_kernel(inputs, cotangent, out, stage):
    share, features = inputs.shape
    half = features // 2
    for i, ref in enumerate((inputs, cotangent)):
        rows = ref[...].astype(jnp.float32)
        for j in range(2):
            stage[(2 * i + j) * share : (2 * i + j + 1) * share, :] = rows[:, j * half : (j + 1) * half]
    for k in range(out.shape[0]):
        out[k] = stage[8 * k : 8 * k + 8, :].astype(jnp.bfloat16)


def relay_kernel(share, *refs):
    blocks, ids, out = refs[:-3], refs[-3], refs[-1]
    slabs = blocks[0].shape[0]
    position = lax.axis_index("wide")
    for i, block in enumerate(blocks):
        out[i * slabs : (i + 1) * slabs] = block[...]
    row = lax.broadcasted_iota(jnp.int32, (8, 128), 0)
    keys = []
    for k in range(len(blocks) * share // 8):
        key = jnp.zeros((8, 128), jnp.int32)
        for r in range(8):
            block, j = divmod(8 * k + r, share)
            key = jnp.where(row == r, ids[(position ^ block) * share + j], key)
        keys.append(key.astype(jnp.float32))
    keys.append(jnp.zeros((8, out.shape[2] - 128 * len(keys)), jnp.float32))
    out[len(blocks) * slabs] = jnp.concatenate(keys, axis=1).astype(jnp.bfloat16)


GATE, UP, DOWN = range(3)
WHOLE_STRIP = (GATE, UP, DOWN)
CHUNKS = 4


def start_loads(pieces, groups, sources, targets, sem):
    copies = []
    for i, (kind, strip) in enumerate(pieces):
        target = targets[i]
        width = target.shape[0 if kind == DOWN else 1]
        owner = lax.axis_index("narrow") ^ strip
        start = pl.multiple_of((owner * groups + lax.axis_index("groups")) * width, width)
        source = sources[kind]
        source = source.at[pl.ds(start, width), :] if kind == DOWN else source.at[:, pl.ds(start, width)]
        size = target.shape[0] // CHUNKS
        for c in range(CHUNKS):
            span = slice(c * size, (c + 1) * size)
            copies.append(pltpu.make_async_copy(source.at[span, :], target.at[span, :], sem.at[i, c]))
    for copy in copies:
        copy.start()
    return copies


def load_kernel(pieces, groups, *refs):
    count = len(pieces)
    for copy in start_loads(pieces, groups, refs[:3], refs[-1 - count : -1], refs[-1]):
        copy.wait()


def loading(body, pieces, groups, outs):
    count = len(pieces)

    def kernel(*refs):
        sources, rest = refs[:3], refs[3:]
        at = len(rest) - outs[1] - 1 - count
        targets, sem = rest[at : at + count], rest[at + count + outs[1]]
        copies = start_loads(pieces, groups, sources, targets, sem)
        body(*rest[:at], *rest[at + count : at + count + outs[1]])
        for copy in copies:
            copy.wait()

    return kernel


def strip_parts(tokens, cotans, gate, up, down, put):
    tile = 256

    @pl.loop(0, gate.shape[1] // tile)
    def _(i):
        span = pl.ds(pl.multiple_of(i * tile, tile), tile)
        put(GATE, span, jnp.dot(tokens[...], gate[:, span], preferred_element_type=jnp.float32))
        put(UP, span, jnp.dot(tokens[...], up[:, span], preferred_element_type=jnp.float32))
        put(DOWN, span, contract_rows(cotans[...], down[span, :]))


def forward_kernel(tokens, cotans, gate, up, down, *refs):
    out = refs[-1]

    def put(kind, span, part):
        out[kind, :, span] = part.astype(out.dtype)

    strip_parts(tokens, cotans, gate, up, down, put)


def forward_add_kernel(tokens, cotans, gate, up, down, arrived, out):
    def put(kind, span, part):
        out[kind, :, span] = (part + arrived[kind, :, span]).astype(out.dtype)

    strip_parts(tokens, cotans, gate, up, down, put)


def first_kernel(share, relayed, other, gate, up, down, *refs):
    tokens, cotans, part, rows, cots = refs[-5:]
    slabs, half = 4 * share // 8, rows.shape[1] // 2
    count = (relayed.shape[0] - 1) // slabs
    for side, source in enumerate((relayed, other)):
        for i in range(count):
            packed = source[i * slabs : (i + 1) * slabs].astype(jnp.float32).reshape(4 * share, half)
            at = (side * count + i) * share
            for j, target in enumerate((rows, rows, cots, cots)):
                span = slice((j % 2) * half, (j % 2 + 1) * half)
                target[at : at + share, span] = packed[j * share : (j + 1) * share]
    tokens[...] = rows[...].astype(jnp.bfloat16)
    cotans[...] = cots[...].astype(jnp.bfloat16)
    forward_kernel(tokens, cotans, gate, up, down, part)


def own_strip_kernel(groups, *refs):
    sources, (tokens, cotans, gate, up) = refs[:3], refs[3:7]
    out, down, sem = refs[-3:]
    copies = start_loads([(DOWN, 0)], groups, sources, [down], sem)
    tile = 256

    @pl.loop(0, gate.shape[1] // tile)
    def _(i):
        span = pl.ds(pl.multiple_of(i * tile, tile), tile)
        out[GATE, :, span] = jnp.dot(tokens[...], gate[:, span], preferred_element_type=jnp.float32)
        out[UP, :, span] = jnp.dot(tokens[...], up[:, span], preferred_element_type=jnp.float32)

    for copy in copies:
        copy.wait()
    out[DOWN] = contract_rows(cotans[...], down[...])


def middle_kernel(groups, *refs):
    own, arrived, crossed, scale, relayed, other_relayed = refs[:6]
    message, near_gate, near_up, grads, other_grads, stage = refs[-6:]
    _, tokens, width = own.shape
    narrow, group = lax.axis_index("narrow"), lax.axis_index("groups")
    sums = [own[i] + arrived[i].astype(jnp.float32) + crossed[i].astype(jnp.float32) for i in range(3)]
    start = pl.multiple_of((narrow * groups + group) * width, width)
    product, d_gate, d_up = local_grads(*sums, scale[:, pl.ds(start, width)])
    message[0:tokens, :] = d_gate
    message[tokens : 2 * tokens, :] = d_up
    near_gate[0:tokens, :] = d_gate
    near_up[...] = d_up
    half = tokens // groups
    for side, (source, target) in enumerate(((relayed, grads), (other_relayed, other_grads))):
        marks = source[source.shape[0] - 1].astype(jnp.float32)
        seq = jnp.concatenate(
            [
                jnp.concatenate([marks[:, k * 128 : (k + 1) * 128]] * (width // 128), axis=1)
                for k in range(half // 8)
            ],
            axis=0,
        )
        part = product[side * half : (side + 1) * half]
        for e in range(SEQS):
            total = jnp.sum(jnp.where(seq == float(e), part, 0.0), axis=0, keepdims=True)
            target[e : e + 1, :] = total
            stage[side * SEQS + e : side * SEQS + e + 1, :] = total
    every = stage[...]
    squares = jnp.broadcast_to(jnp.sum(every * every, axis=1, keepdims=True), every.shape)
    tail = jnp.concatenate(split_high(squares), axis=0).astype(jnp.bfloat16)
    message[2 * tokens :, :] = tail
    near_gate[tokens:, :] = tail


TILE = 512


def backward_part(grads, gate, up, start):
    d_gate, d_up = grads
    gate_term = contract_rows(gate[start : start + TILE, :], d_gate)
    return gate_term + contract_rows(up[start : start + TILE, :], d_up)


def halves(message):
    tokens = (message.shape[0] - 16) // 2
    return message[0:tokens, :], message[tokens : 2 * tokens, :]


def backward_first_kernel(message, gate, up, total):
    for start in range(0, total.shape[0], TILE):
        total[start : start + TILE, :] = backward_part(halves(message), gate, up, start)


def backward_near_kernel(d_gate, d_up, gate, up, before, total):
    tokens = d_up.shape[0]
    for start in range(0, total.shape[0], TILE):
        part = backward_part((d_gate[0:tokens, :], d_up[...]), gate, up, start)
        total[start : start + TILE, :] = before[start : start + TILE, :] + part


def backward_next_kernel(message, gate, up, before, total):
    for start in range(0, total.shape[0], TILE):
        part = backward_part(halves(message), gate, up, start)
        total[start : start + TILE, :] = before[start : start + TILE, :] + part


def split_high(values):
    high = values.astype(jnp.bfloat16).astype(jnp.float32)
    return high, values - high


def backward_last_kernel(message, gate, up, before, *refs):
    others, other_grads = refs[:3], refs[3]
    own, own_tail, send = refs[4:7]
    half, features = own.shape
    wide = send.shape[2]
    for start in range(0, features, TILE):
        span = slice(start, start + TILE)
        total = (before[span, :] + backward_part(halves(message), gate, up, start)).T
        own[:, span] = total[:half]
        at = slice(start % wide, start % wide + TILE)
        for k in range(half // 8):
            slab = start // wide * (half // 8) + k
            send[slab, :, at] = total[half + 8 * k : half + 8 * k + 8].astype(jnp.bfloat16)
    squares = sum(ref[ref.shape[0] - 16 :, 0:128].astype(jnp.float32) for ref in (message,) + others)
    high, low = split_high(squares[0:8] + squares[8:16])
    own_tail[...] = jnp.zeros_like(own_tail)
    width = other_grads.shape[1]
    for i, rows in enumerate(split_high(other_grads[...])):
        own_tail[i * SEQS : (i + 1) * SEQS, 0:width] = rows
    own_tail[:, width : width + 128] = high
    own_tail[:, width + 128 : width + 256] = low
    send[send.shape[0] - 1] = own_tail[...].astype(jnp.bfloat16)


def combine_kernel(share, own, own_tail, arrived, grads, *refs):
    example_grads, own_block, sends, total = refs[0], refs[1], refs[2:-1], refs[-1]
    half, features = own.shape
    width = grads.shape[1]
    group = lax.axis_index("groups")
    slabs, wide = half // 8, own_tail.shape[1]
    for k in range(slabs):
        for i in range(features // wide):
            span = slice(i * wide, (i + 1) * wide)
            total[8 * k : 8 * k + 8, span] = own[8 * k : 8 * k + 8, span] + arrived[i * slabs + k].astype(jnp.float32)
    tail = arrived[arrived.shape[0] - 1].astype(jnp.float32)
    other = tail[0:SEQS, 0:width] + tail[SEQS : 2 * SEQS, 0:width]
    example_grads[:, pl.ds(pl.multiple_of(group * width, width), width)] = grads[...]
    example_grads[:, pl.ds(pl.multiple_of((1 - group) * width, width), width)] = other
    lanes = SEQS * 128

    def squares(ref, first):
        rows = ref[:, width : width + 128] + ref[:, width + 128 : width + 256]
        return jnp.concatenate([rows[first + e : first + e + 1] for e in range(SEQS)], axis=1)

    here, there = squares(own_tail[...], 0), squares(tail, SEQS)
    high, low = split_high(here + there)
    for i, target in enumerate((own_block,) + tuple(sends)):
        rows = total[i * share : (i + 1) * share, :]
        if i == 0:
            target[...] = jnp.zeros_like(target)
            target[0:share, :] = rows
            target[6:7, 0:lanes] = high
            target[7:8, 0:lanes] = low
        else:
            total[half : half + share, :] = rows
            if i == 1:
                total[half + 6 : half + 8, :] = jnp.zeros((2, features), jnp.float32)
                total[half + 6 : half + 7, 0:lanes] = high
                total[half + 7 : half + 8, 0:lanes] = low
            target[...] = total[half : half + 8, :].astype(jnp.bfloat16)


def last_kernel(*refs):
    own, arrived, (input_grad, norms) = refs[0], refs[1:-2], refs[-2:]
    total = own[...] + sum(ref[...].astype(jnp.float32) for ref in arrived)
    input_grad[...] = total[0 : input_grad.shape[0]].astype(jnp.bfloat16)
    roots = jnp.sqrt(total[6:7, 0 : SEQS * 128] + total[7:8, 0 : SEQS * 128])
    for e in range(SEQS):
        norms[e] = jnp.max(roots[:, e * 128 : (e + 1) * 128])


def shared(inputs, cotangent, gate_weight, up_weight, down_weight, ia3_scale, seq_ids):
    groups, wide, strips = lax.axis_size("groups"), lax.axis_size("wide"), lax.axis_size("narrow")
    share, features = inputs.shape
    width = gate_weight.shape[1] // (strips * groups)
    half = share * wide
    tokens = half * groups
    f32, bf16 = jnp.float32, jnp.bfloat16
    slabs = 4 * share // 8
    weights = tuple(
        pltpu.with_memory_space_constraint(weight, pltpu.HBM)
        for weight in (gate_weight, up_weight, down_weight)
    )
    weight_shapes = [
        pltpu.VMEM((features, width), bf16),
        pltpu.VMEM((features, width), bf16),
        pltpu.VMEM((width, features), bf16),
    ]
    kept = {}

    def load(name, pieces, after=()):
        args = weights + tuple(after)
        arrays = call(
            functools.partial(load_kernel, pieces, groups),
            name,
            [weight_shapes[kind] for kind, _ in pieces],
            args,
            {i: pltpu.HBM if i < 3 else pl.ANY for i in range(len(args))},
            [pltpu.SemaphoreType.DMA((len(pieces), CHUNKS))],
        )
        kept.update(zip(pieces, arrays))

    def call_loading(body, name, pieces, outs, args, scratch=()):
        made = call(
            loading(body, pieces, groups, (len(outs), len(outs) + len(scratch))),
            name,
            [weight_shapes[kind] for kind, _ in pieces] + outs,
            list(weights) + args,
            {i: pltpu.HBM for i in range(3)},
            list(scratch) + [pltpu.SemaphoreType.DMA((len(pieces), CHUNKS))],
        )
        kept.update(zip(pieces, made))
        return made[len(pieces) :]

    def hold(strip, kinds=WHOLE_STRIP):
        return [held(kept[kind, strip]) for kind in kinds]

    packed = call(
        pack_kernel,
        "pack",
        pltpu.VMEM((slabs, 8, features // 2), bf16),
        [pltpu.with_memory_space_constraint(array, pltpu.HBM) for array in (inputs, cotangent)],
        scratch=[pltpu.VMEM((4 * share, features // 2), f32)],
    )
    arrived = [exchange(packed, "wide", s) for s in range(1, wide)]
    load("load_a", [(kind, 3) for kind in WHOLE_STRIP])
    relayed = call(
        functools.partial(relay_kernel, share),
        "relay",
        pltpu.VMEM((wide * slabs + 1, 8, features // 2), bf16),
        [packed] + arrived + [seq_ids] + hold(3, [GATE]),
        {wide: pltpu.SMEM},
    )
    other_relayed = exchange(relayed, "groups", 1)
    load("load_b", [(kind, 2) for kind in WHOLE_STRIP] + [(GATE, 1)], [relayed])

    part = pltpu.VMEM((3, tokens, width), f32)
    near_shape = pltpu.VMEM((3, tokens, width), bf16)
    tokens_all, cotans_all, diagonal = call_loading(
        functools.partial(first_kernel, share),
        "forward_3",
        [(UP, 1)],
        [pltpu.VMEM((tokens, features), bf16)] * 2 + [part],
        [relayed, other_relayed] + hold(3) + hold(2, [GATE]),
        [pltpu.VMEM((tokens, features), f32)] * 2,
    )
    panel = [tokens_all, cotans_all]
    diagonal = exchange(diagonal, "narrow", 1)
    (crossing,) = call_loading(
        forward_add_kernel,
        "forward_2",
        [(DOWN, 1)],
        [pltpu.VMEM((3, tokens, width), bf16)],
        panel + hold(2) + [diagonal],
    )
    crossed = exchange(crossing, "narrow", 2)
    (near,) = call_loading(
        forward_kernel, "forward_1", [(GATE, 0), (UP, 0)], [near_shape], panel + hold(1) + [held(crossing)]
    )
    near = exchange(near, "narrow", 1)
    own_part, kept[DOWN, 0] = call(
        functools.partial(own_strip_kernel, groups),
        "forward_0",
        [part, weight_shapes[DOWN]],
        list(weights) + panel + hold(0, [GATE, UP]),
        {i: pltpu.HBM for i in range(3)},
        [pltpu.SemaphoreType.DMA((1, CHUNKS))],
    )

    resident = [array for s in range(strips) for array in hold(s, [GATE, UP])]
    message, near_gate, near_up, grads, other_grads = call(
        functools.partial(middle_kernel, groups),
        "middle",
        [
            pltpu.VMEM((2 * tokens + 16, width), bf16),
            pltpu.VMEM((tokens + 16, width), bf16),
            pltpu.VMEM((tokens, width), bf16),
            pltpu.VMEM((SEQS, width), f32),
            pltpu.VMEM((SEQS, width), f32),
        ],
        [own_part, near, crossed, ia3_scale[None, :], relayed, other_relayed] + resident,
        scratch=[pltpu.VMEM((groups * SEQS, width), f32)],
    )

    total = pltpu.VMEM((features, tokens), f32)
    near_gate, near_up = exchange(near_gate, "narrow", 1), exchange(near_up, "narrow", 1)
    message_2 = exchange(message, "narrow", 2)
    sums = call(backward_first_kernel, "backward_0", total, [message] + hold(0, [GATE, UP]))
    sums = call(backward_near_kernel, "backward_1", total, [near_gate, near_up] + hold(1, [GATE, UP]) + [sums])
    message_2, sums = lax.optimization_barrier((message_2, sums))
    message_3 = exchange(message_2, "narrow", 1)
    sums = call(backward_next_kernel, "backward_2", total, [message_2] + hold(2, [GATE, UP]) + [sums])
    own, own_tail, send = call(
        backward_last_kernel,
        "backward_3",
        [
            pltpu.VMEM((half, features), f32),
            pltpu.VMEM((8, features // 2), f32),
            pltpu.VMEM((half // 4 + 1, 8, features // 2), bf16),
        ],
        [message_3] + hold(3, [GATE, UP]) + [sums, message, near_gate, message_2, other_grads],
    )
    arrived = exchange(send, "groups", 1)
    example_grads, own_block, *sends = call(
        functools.partial(combine_kernel, share),
        "combine",
        [jax.ShapeDtypeStruct((SEQS, groups * width), f32), pltpu.VMEM((8, features), f32)]
        + [pltpu.VMEM((8, features), bf16)] * (wide - 1),
        [own, own_tail, arrived, grads],
        scratch=[pltpu.VMEM((half + 8, features), f32)],
    )
    arrived = [exchange(sends[s - 1], "wide", s) for s in reversed(range(1, wide))]
    input_grad, norms = call(
        last_kernel,
        "last",
        [jax.ShapeDtypeStruct((share, features), bf16), jax.ShapeDtypeStruct((SEQS,), f32)],
        [own_block] + arrived,
        out_spaces={1: pltpu.SMEM},
    )
    return (example_grads, norms, input_grad)


def power_of_two(number):
    return number & (number - 1) == 0


def local(inputs, cotangent, gate_weight, up_weight, down_weight, ia3_scale, seq_ids):
    groups, wide, narrow = lax.axis_size("groups"), lax.axis_size("wide"), lax.axis_size("narrow")
    share, (features, hidden) = inputs.shape[0], gate_weight.shape
    width = hidden // (narrow * groups)
    fits = (
        groups == 2
        and narrow == 4
        and power_of_two(wide)
        and hidden % (narrow * groups * 256) == 0
        and features >= 2048
        and width <= features // 2 - 256
        and features % (2 * TILE) == 0
        and share <= 6
        and share % 2 == 0
        and (share * wide) % 8 == 0
        and share * wide <= 64
        and 3 * features * hidden // groups * 2 <= 40 << 20
    )
    plan = shared if fits else whole_block
    return plan(inputs, cotangent, gate_weight, up_weight, down_weight, ia3_scale, seq_ids)


def solution(mesh):
    return jax.shard_map(
        local,
        mesh=mesh,
        in_specs=(
            P(("groups", "wide"), "narrow"),
            P(("groups", "wide"), "narrow"),
            P("narrow", "wide"),
            P("narrow", "wide"),
            P("wide", "narrow"),
            P("wide"),
            P("groups"),
        ),
        out_specs=(P("groups", ("wide", "narrow")), P("groups"), P(("groups", "wide"), "narrow")),
        check_vma=False,
    )
```

```python
import functools

import jax
import jax.numpy as jnp
from jax import lax
from jax.experimental import pallas as pl
from jax.experimental.pallas import tpu as pltpu
from jax.sharding import PartitionSpec as P

SEQS = 4
KERNEL_VMEM = 6 << 20


def contract_rows(left, right):
    return lax.dot_general(
        left, right, (((1,), (1,)), ((), ())), preferred_element_type=jnp.float32
    )


def local_grads(gate_pre, up_pre, mid_grad, scale_part):
    sigmoid_gate = jax.nn.sigmoid(gate_pre)
    activation = gate_pre * sigmoid_gate
    hidden = activation * up_pre
    scaled = scale_part * mid_grad
    d_up = (scaled * activation).astype(jnp.bfloat16)
    d_gate = (scaled * up_pre * sigmoid_gate * (1.0 + gate_pre * (1.0 - sigmoid_gate))).astype(
        jnp.bfloat16
    )
    return (hidden * mid_grad, d_gate, d_up)


def whole_block(inputs, cotangent, gate_weight, up_weight, down_weight, ia3_scale, seq_ids):
    panel_inputs = lax.all_gather(inputs, "wide", axis=0, tiled=True)
    panel_cotangent = lax.all_gather(cotangent, "wide", axis=0, tiled=True)
    gate_part = jnp.dot(panel_inputs, gate_weight, preferred_element_type=jnp.float32)
    up_part = jnp.dot(panel_inputs, up_weight, preferred_element_type=jnp.float32)
    mid_part = contract_rows(panel_cotangent, down_weight)
    quarter = gate_weight.shape[1] // lax.axis_size("narrow")
    position = lax.axis_index("narrow")
    onehot_full = (seq_ids[None, :] == jnp.arange(SEQS, dtype=jnp.int32)[:, None]).astype(
        jnp.float32
    )
    gate_pre, up_pre, mid_grad = (
        lax.psum_scatter(gate_part, "narrow", scatter_dimension=1, tiled=True),
        lax.psum_scatter(up_part, "narrow", scatter_dimension=1, tiled=True),
        lax.psum_scatter(mid_part, "narrow", scatter_dimension=1, tiled=True),
    )
    scale_part = lax.dynamic_slice_in_dim(ia3_scale, position * quarter, quarter, 0)
    product, d_gate, d_up = local_grads(gate_pre, up_pre, mid_grad, scale_part[None, :])
    example_grads = jnp.dot(onehot_full, product, precision=lax.Precision.HIGHEST)
    whole_gate, whole_up = (
        lax.all_gather(d_gate, "narrow", axis=1, tiled=True),
        lax.all_gather(d_up, "narrow", axis=1, tiled=True),
    )
    squares = lax.psum(jnp.sum(example_grads * example_grads, axis=1), ("wide", "narrow"))
    grad_norms = jnp.sqrt(squares)
    input_grad = lax.psum_scatter(
        contract_rows(whole_gate, gate_weight) + contract_rows(whole_up, up_weight),
        "wide",
        scatter_dimension=0,
        tiled=True,
    ).astype(jnp.bfloat16)
    return (example_grads, grad_norms, input_grad)


def exchange(array, axis, step):
    return lax.ppermute(array, axis, [(i, i ^ step) for i in range(lax.axis_size(axis))])


def held(array):
    return pltpu.with_memory_space_constraint(array, pltpu.VMEM)


def call(body, name, outs, args, spaces=None, scratch=(), out_spaces=None):
    spaces, out_spaces = spaces or {}, out_spaces or {}
    many = isinstance(outs, list)
    out_specs = [
        pl.BlockSpec(memory_space=out_spaces.get(i, pltpu.VMEM)) for i in range(len(outs) if many else 1)
    ]
    return pl.pallas_call(
        body,
        out_shape=outs,
        in_specs=[pl.BlockSpec(memory_space=spaces.get(i, pltpu.VMEM)) for i in range(len(args))],
        out_specs=out_specs if many else out_specs[0],
        scratch_shapes=list(scratch),
        compiler_params=pltpu.CompilerParams(vmem_limit_bytes=KERNEL_VMEM),
        cost_estimate=pl.CostEstimate(flops=1000, bytes_accessed=1000, transcendentals=0),
        name=name,
    )(*args)


def pack_kernel(inputs, cotangent, out, stage):
    share, features = inputs.shape
    half = features // 2
    for i, ref in enumerate((inputs, cotangent)):
        rows = ref[...].astype(jnp.float32)
        for j in range(2):
            stage[(2 * i + j) * share : (2 * i + j + 1) * share, :] = rows[:, j * half : (j + 1) * half]
    for k in range(out.shape[0]):
        out[k] = stage[8 * k : 8 * k + 8, :].astype(jnp.bfloat16)


def relay_kernel(share, *refs):
    blocks, ids, out = refs[:-3], refs[-3], refs[-1]
    slabs = blocks[0].shape[0]
    position = lax.axis_index("wide")
    for i, block in enumerate(blocks):
        out[i * slabs : (i + 1) * slabs] = block[...]
    row = lax.broadcasted_iota(jnp.int32, (8, 128), 0)
    keys = []
    for k in range(len(blocks) * share // 8):
        key = jnp.zeros((8, 128), jnp.int32)
        for r in range(8):
            block, j = divmod(8 * k + r, share)
            key = jnp.where(row == r, ids[(position ^ block) * share + j], key)
        keys.append(key.astype(jnp.float32))
    keys.append(jnp.zeros((8, out.shape[2] - 128 * len(keys)), jnp.float32))
    out[len(blocks) * slabs] = jnp.concatenate(keys, axis=1).astype(jnp.bfloat16)


GATE, UP, DOWN = range(3)
WHOLE_STRIP = (GATE, UP, DOWN)
CHUNKS = 4


def start_loads(pieces, groups, sources, targets, sem):
    copies = []
    for i, (kind, strip) in enumerate(pieces):
        target = targets[i]
        width = target.shape[0 if kind == DOWN else 1]
        owner = lax.axis_index("narrow") ^ strip
        start = pl.multiple_of((owner * groups + lax.axis_index("groups")) * width, width)
        source = sources[kind]
        source = source.at[pl.ds(start, width), :] if kind == DOWN else source.at[:, pl.ds(start, width)]
        size = target.shape[0] // CHUNKS
        for c in range(CHUNKS):
            span = slice(c * size, (c + 1) * size)
            copies.append(pltpu.make_async_copy(source.at[span, :], target.at[span, :], sem.at[i, c]))
    for copy in copies:
        copy.start()
    return copies


def load_kernel(pieces, groups, *refs):
    count = len(pieces)
    for copy in start_loads(pieces, groups, refs[:3], refs[-1 - count : -1], refs[-1]):
        copy.wait()


def loading(body, pieces, groups, outs):
    count = len(pieces)

    def kernel(*refs):
        sources, rest = refs[:3], refs[3:]
        at = len(rest) - outs[1] - 1 - count
        targets, sem = rest[at : at + count], rest[at + count + outs[1]]
        copies = start_loads(pieces, groups, sources, targets, sem)
        body(*rest[:at], *rest[at + count : at + count + outs[1]])
        for copy in copies:
            copy.wait()

    return kernel


def strip_parts(tokens, cotans, gate, up, down, put):
    tile = 256

    @pl.loop(0, gate.shape[1] // tile)
    def _(i):
        span = pl.ds(pl.multiple_of(i * tile, tile), tile)
        put(GATE, span, jnp.dot(tokens[...], gate[:, span], preferred_element_type=jnp.float32))
        put(UP, span, jnp.dot(tokens[...], up[:, span], preferred_element_type=jnp.float32))
        put(DOWN, span, contract_rows(cotans[...], down[span, :]))


def forward_kernel(tokens, cotans, gate, up, down, *refs):
    out = refs[-1]

    def put(kind, span, part):
        out[kind, :, span] = part.astype(out.dtype)

    strip_parts(tokens, cotans, gate, up, down, put)


def join_kernel(own, arrived, out):
    out[...] = (own[...] + arrived[...]).astype(out.dtype)


def first_kernel(share, relayed, other, gate, up, down, *refs):
    tokens, cotans, part, rows, cots = refs[-5:]
    slabs, half = 4 * share // 8, rows.shape[1] // 2
    count = (relayed.shape[0] - 1) // slabs
    for side, source in enumerate((relayed, other)):
        for i in range(count):
            packed = source[i * slabs : (i + 1) * slabs].astype(jnp.float32).reshape(4 * share, half)
            at = (side * count + i) * share
            for j, target in enumerate((rows, rows, cots, cots)):
                span = slice((j % 2) * half, (j % 2 + 1) * half)
                target[at : at + share, span] = packed[j * share : (j + 1) * share]
    tokens[...] = rows[...].astype(jnp.bfloat16)
    cotans[...] = cots[...].astype(jnp.bfloat16)
    forward_kernel(tokens, cotans, gate, up, down, part)


def own_strip_kernel(groups, *refs):
    sources, (tokens, cotans, up, down) = refs[:3], refs[3:7]
    out, gate, sem = refs[-3:]
    copies = start_loads([(GATE, 0)], groups, sources, [gate], sem)
    tile = 256

    @pl.loop(0, up.shape[1] // tile)
    def _(i):
        span = pl.ds(pl.multiple_of(i * tile, tile), tile)
        out[UP, :, span] = jnp.dot(tokens[...], up[:, span], preferred_element_type=jnp.float32)
        out[DOWN, :, span] = contract_rows(cotans[...], down[span, :])

    for copy in copies:
        copy.wait()
    out[GATE] = jnp.dot(tokens[...], gate[...], preferred_element_type=jnp.float32)


def middle_kernel(groups, *refs):
    own, arrived, crossed, scale, relayed, other_relayed = refs[:6]
    message, near_gate, near_up, grads, other_grads, stage = refs[-6:]
    _, tokens, width = own.shape
    narrow, group = lax.axis_index("narrow"), lax.axis_index("groups")
    sums = [own[i] + arrived[i].astype(jnp.float32) + crossed[i].astype(jnp.float32) for i in range(3)]
    start = pl.multiple_of((narrow * groups + group) * width, width)
    product, d_gate, d_up = local_grads(*sums, scale[:, pl.ds(start, width)])
    message[0:tokens, :] = d_gate
    message[tokens : 2 * tokens, :] = d_up
    near_gate[0:tokens, :] = d_gate
    near_up[...] = d_up
    half = tokens // groups
    for side, (source, target) in enumerate(((relayed, grads), (other_relayed, other_grads))):
        marks = source[source.shape[0] - 1].astype(jnp.float32)
        seq = jnp.concatenate(
            [
                jnp.concatenate([marks[:, k * 128 : (k + 1) * 128]] * (width // 128), axis=1)
                for k in range(half // 8)
            ],
            axis=0,
        )
        part = product[side * half : (side + 1) * half]
        for e in range(SEQS):
            total = jnp.sum(jnp.where(seq == float(e), part, 0.0), axis=0, keepdims=True)
            target[e : e + 1, :] = total
            stage[side * SEQS + e : side * SEQS + e + 1, :] = total
    every = stage[...]
    squares = jnp.broadcast_to(jnp.sum(every * every, axis=1, keepdims=True), every.shape)
    tail = jnp.concatenate(split_high(squares), axis=0).astype(jnp.bfloat16)
    message[2 * tokens :, :] = tail
    near_gate[tokens:, :] = tail


TILE = 512


def backward_part(grads, gate, up, start):
    d_gate, d_up = grads
    gate_term = contract_rows(gate[start : start + TILE, :], d_gate)
    return gate_term + contract_rows(up[start : start + TILE, :], d_up)


def halves(message):
    tokens = (message.shape[0] - 16) // 2
    return message[0:tokens, :], message[tokens : 2 * tokens, :]


def backward_first_kernel(message, gate, up, total):
    for start in range(0, total.shape[0], TILE):
        total[start : start + TILE, :] = backward_part(halves(message), gate, up, start)


def backward_near_kernel(d_gate, d_up, gate, up, before, total):
    tokens = d_up.shape[0]
    for start in range(0, total.shape[0], TILE):
        part = backward_part((d_gate[0:tokens, :], d_up[...]), gate, up, start)
        total[start : start + TILE, :] = before[start : start + TILE, :] + part


def backward_next_kernel(message, gate, up, before, total):
    for start in range(0, total.shape[0], TILE):
        part = backward_part(halves(message), gate, up, start)
        total[start : start + TILE, :] = before[start : start + TILE, :] + part


def split_high(values):
    high = values.astype(jnp.bfloat16).astype(jnp.float32)
    return high, values - high


def backward_last_kernel(share, message, gate, up, before, *refs):
    others, (own, own_squares), sends, (total, stage) = refs[:3], refs[3:5], refs[5:-2], refs[-2:]
    tokens, features = total.shape
    side = features // 2
    for start in range(0, features, TILE):
        part = before[start : start + TILE, :] + backward_part(halves(message), gate, up, start)
        total[:, start : start + TILE] = part.T
    squares = sum(ref[ref.shape[0] - 16 :, 0:128].astype(jnp.float32) for ref in (message,) + others)
    squares = squares[0:8] + squares[8:16]
    own_squares[...] = squares
    tails = split_high(squares)
    wide = len(sends) + 1
    for i, target in enumerate((own,) + tuple(sends)):
        rows = own if i == 0 else stage
        for group in range(2):
            at = (group * wide + i) * share
            for j in range(2):
                to = (2 * group + j) * share
                rows[to : to + share, :] = total[at : at + share, j * side : (j + 1) * side]
        if i > 0:
            for k in range(target.shape[0]):
                target[k, :, 0:side] = stage[8 * k : 8 * k + 8, :].astype(jnp.bfloat16)
                tail = tails[k] if k < 2 else jnp.zeros_like(squares)
                target[k, :, side:] = tail.astype(jnp.bfloat16)


def combine_kernel(share, own, own_squares, other_grads, *refs):
    arrived, (kept_rows, kept_squares, send, total, stage) = refs[:-5], refs[-5:]
    slabs, side = arrived[0].shape[0], own.shape[1]
    squares = own_squares[...]
    for k in range(slabs):
        rows = own[8 * k : 8 * k + 8, :]
        for ref in arrived:
            values = ref[k].astype(jnp.float32)
            rows = rows + values[:, 0:side]
            if k < 2:
                squares = squares + values[:, side:]
        total[8 * k : 8 * k + 8, :] = rows
    kept_squares[...] = squares
    count = 2 * share
    kept_rows[0:count, :] = total[0:count, :]
    stage[...] = jnp.zeros_like(stage)
    stage[0:count, :] = total[count : 2 * count, :]
    width = other_grads.shape[1]
    for i, rows in enumerate(split_high(other_grads[...])):
        stage[16 + i * SEQS : 16 + (i + 1) * SEQS, 0:width] = rows
    for i, rows in enumerate(split_high(squares)):
        stage[16:24, width + i * 128 : width + (i + 1) * 128] = rows
    for k in range(3):
        send[k] = stage[8 * k : 8 * k + 8, :].astype(jnp.bfloat16)


def last_kernel(share, own, own_squares, arrived, grads, input_grad, example_grads, norms, stage):
    side, width = own.shape[1], grads.shape[1]
    group = lax.axis_index("groups")
    for k in range(2):
        stage[8 * k : 8 * k + 8, :] = own[8 * k : 8 * k + 8, :] + arrived[k].astype(jnp.float32)
    for j in range(2):
        rows = stage[j * share : (j + 1) * share, :]
        input_grad[:, j * side : (j + 1) * side] = rows.astype(jnp.bfloat16)
    tail = arrived[2].astype(jnp.float32)
    other = tail[0:SEQS, 0:width] + tail[SEQS : 2 * SEQS, 0:width]
    example_grads[:, pl.ds(pl.multiple_of(group * width, width), width)] = grads[...]
    example_grads[:, pl.ds(pl.multiple_of((1 - group) * width, width), width)] = other
    squares = tail[:, width : width + 128] + tail[:, width + 128 : width + 256]
    roots = jnp.sqrt(own_squares[0:SEQS, :] + squares[SEQS : 2 * SEQS])
    for e in range(SEQS):
        norms[e] = jnp.max(roots[e : e + 1])


def shared(inputs, cotangent, gate_weight, up_weight, down_weight, ia3_scale, seq_ids):
    groups, wide, strips = lax.axis_size("groups"), lax.axis_size("wide"), lax.axis_size("narrow")
    share, features = inputs.shape
    width = gate_weight.shape[1] // (strips * groups)
    half = share * wide
    tokens = half * groups
    f32, bf16 = jnp.float32, jnp.bfloat16
    slabs = 4 * share // 8
    weights = tuple(
        pltpu.with_memory_space_constraint(weight, pltpu.HBM)
        for weight in (gate_weight, up_weight, down_weight)
    )
    weight_shapes = [
        pltpu.VMEM((features, width), bf16),
        pltpu.VMEM((features, width), bf16),
        pltpu.VMEM((width, features), bf16),
    ]
    kept = {}

    def load(name, pieces, after=()):
        args = weights + tuple(after)
        arrays = call(
            functools.partial(load_kernel, pieces, groups),
            name,
            [weight_shapes[kind] for kind, _ in pieces],
            args,
            {i: pltpu.HBM if i < 3 else pl.ANY for i in range(len(args))},
            [pltpu.SemaphoreType.DMA((len(pieces), CHUNKS))],
        )
        kept.update(zip(pieces, arrays))

    def call_loading(body, name, pieces, outs, args, scratch=()):
        made = call(
            loading(body, pieces, groups, (len(outs), len(outs) + len(scratch))),
            name,
            [weight_shapes[kind] for kind, _ in pieces] + outs,
            list(weights) + args,
            {i: pltpu.HBM for i in range(3)},
            list(scratch) + [pltpu.SemaphoreType.DMA((len(pieces), CHUNKS))],
        )
        kept.update(zip(pieces, made))
        return made[len(pieces) :]

    def hold(strip, kinds=WHOLE_STRIP):
        return [held(kept[kind, strip]) for kind in kinds]

    packed = call(
        pack_kernel,
        "pack",
        pltpu.VMEM((slabs, 8, features // 2), bf16),
        [pltpu.with_memory_space_constraint(array, pltpu.HBM) for array in (inputs, cotangent)],
        scratch=[pltpu.VMEM((4 * share, features // 2), f32)],
    )
    arrived = [exchange(packed, "wide", s) for s in range(1, wide)]
    load("load_a", [(kind, 3) for kind in WHOLE_STRIP])
    relayed = call(
        functools.partial(relay_kernel, share),
        "relay",
        pltpu.VMEM((wide * slabs + 1, 8, features // 2), bf16),
        [packed] + arrived + [seq_ids] + hold(3, [GATE]),
        {wide: pltpu.SMEM},
    )
    other_relayed = exchange(relayed, "groups", 1)
    load("load_b", [(kind, 2) for kind in WHOLE_STRIP] + [(GATE, 1)], [relayed])

    part = pltpu.VMEM((3, tokens, width), f32)
    near_shape = pltpu.VMEM((3, tokens, width), bf16)
    tokens_all, cotans_all, diagonal = call_loading(
        functools.partial(first_kernel, share),
        "forward_3",
        [(UP, 1)],
        [pltpu.VMEM((tokens, features), bf16)] * 2 + [part],
        [relayed, other_relayed] + hold(3) + hold(2, [GATE]),
        [pltpu.VMEM((tokens, features), f32)] * 2,
    )
    panel = [tokens_all, cotans_all]
    diagonal = exchange(diagonal, "narrow", 1)
    (second,) = call_loading(forward_kernel, "forward_2", [(DOWN, 1)], [part], panel + hold(2))
    crossing = call(join_kernel, "join", near_shape, [held(second), diagonal])
    crossed = exchange(crossing, "narrow", 2)
    (near,) = call_loading(
        forward_kernel, "forward_1", [(UP, 0), (DOWN, 0)], [near_shape], panel + hold(1) + [held(crossing)]
    )
    near = exchange(near, "narrow", 1)
    own_part, kept[GATE, 0] = call(
        functools.partial(own_strip_kernel, groups),
        "forward_0",
        [part, weight_shapes[GATE]],
        list(weights) + panel + hold(0, [UP, DOWN]),
        {i: pltpu.HBM for i in range(3)},
        [pltpu.SemaphoreType.DMA((1, CHUNKS))],
    )

    resident = [array for s in range(strips) for array in hold(s, [GATE, UP])]
    message, near_gate, near_up, grads, other_grads = call(
        functools.partial(middle_kernel, groups),
        "middle",
        [
            pltpu.VMEM((2 * tokens + 16, width), bf16),
            pltpu.VMEM((tokens + 16, width), bf16),
            pltpu.VMEM((tokens, width), bf16),
            pltpu.VMEM((SEQS, width), f32),
            pltpu.VMEM((SEQS, width), f32),
        ],
        [own_part, near, crossed, ia3_scale[None, :], relayed, other_relayed] + resident,
        scratch=[pltpu.VMEM((groups * SEQS, width), f32)],
    )

    total = pltpu.VMEM((features, tokens), f32)
    near_gate, near_up = exchange(near_gate, "narrow", 1), exchange(near_up, "narrow", 1)
    message_2 = exchange(message, "narrow", 2)
    sums = call(backward_first_kernel, "backward_0", total, [message] + hold(0, [GATE, UP]))
    sums = call(backward_near_kernel, "backward_1", total, [near_gate, near_up] + hold(1, [GATE, UP]) + [sums])
    message_2, sums = lax.optimization_barrier((message_2, sums))
    message_3 = exchange(message_2, "narrow", 1)
    sums = call(backward_next_kernel, "backward_2", total, [message_2] + hold(2, [GATE, UP]) + [sums])
    side = features // 2
    block = pltpu.VMEM((slabs, 8, side + 128), bf16)
    own, own_squares, *sends = call(
        functools.partial(backward_last_kernel, share),
        "backward_3",
        [pltpu.VMEM((4 * share, side), f32), pltpu.VMEM((8, 128), f32)] + [block] * (wide - 1),
        [message_3] + hold(3, [GATE, UP]) + [sums, message, near_gate, message_2],
        scratch=[pltpu.VMEM((tokens, features), f32), pltpu.VMEM((4 * share, side), f32)],
    )
    arrived = [exchange(sends[s - 1], "wide", s) for s in reversed(range(1, wide))]
    own, own_squares, send = call(
        functools.partial(combine_kernel, share),
        "combine",
        [pltpu.VMEM((16, side), f32), pltpu.VMEM((8, 128), f32), pltpu.VMEM((3, 8, side), bf16)],
        [own, own_squares, other_grads] + arrived,
        scratch=[pltpu.VMEM((4 * share, side), f32), pltpu.VMEM((24, side), f32)],
    )
    input_grad, example_grads, norms = call(
        functools.partial(last_kernel, share),
        "last",
        [
            jax.ShapeDtypeStruct((share, features), bf16),
            jax.ShapeDtypeStruct((SEQS, groups * width), f32),
            jax.ShapeDtypeStruct((SEQS,), f32),
        ],
        [own, own_squares, exchange(send, "groups", 1), grads],
        scratch=[pltpu.VMEM((16, side), f32)],
        out_spaces={2: pltpu.SMEM},
    )
    return (example_grads, norms, input_grad)


def power_of_two(number):
    return number & (number - 1) == 0


def local(inputs, cotangent, gate_weight, up_weight, down_weight, ia3_scale, seq_ids):
    groups, wide, narrow = lax.axis_size("groups"), lax.axis_size("wide"), lax.axis_size("narrow")
    share, (features, hidden) = inputs.shape[0], gate_weight.shape
    width = hidden // (narrow * groups)
    fits = (
        groups == 2
        and narrow == 4
        and power_of_two(wide)
        and hidden % (narrow * groups * 256) == 0
        and features >= 2048
        and width <= features // 2 - 256
        and features % (2 * TILE) == 0
        and share in (4, 6)
        and (share * wide) % 8 == 0
        and share * wide <= 64
        and 3 * features * hidden // groups * 2 <= 40 << 20
    )
    plan = shared if fits else whole_block
    return plan(inputs, cotangent, gate_weight, up_weight, down_weight, ia3_scale, seq_ids)


def solution(mesh):
    return jax.shard_map(
        local,
        mesh=mesh,
        in_specs=(
            P(("groups", "wide"), "narrow"),
            P(("groups", "wide"), "narrow"),
            P("narrow", "wide"),
            P("narrow", "wide"),
            P("wide", "narrow"),
            P("wide"),
            P("groups"),
        ),
        out_specs=(P("groups", ("wide", "narrow")), P("groups"), P(("groups", "wide"), "narrow")),
        check_vma=False,
    )
```

```python
import functools
import math

import jax
import jax.numpy as jnp
from jax import lax
from jax.experimental import pallas as pl
from jax.experimental.pallas import tpu as pltpu
from jax.sharding import PartitionSpec as P

SEQS = 4
KERNEL_VMEM = 6 << 20


def contract_rows(left, right):
    return lax.dot_general(
        left, right, (((1,), (1,)), ((), ())), preferred_element_type=jnp.float32
    )


def local_grads(gate_pre, up_pre, mid_grad, scale_part):
    sigmoid_gate = jax.nn.sigmoid(gate_pre)
    activation = gate_pre * sigmoid_gate
    hidden = activation * up_pre
    scaled = scale_part * mid_grad
    d_up = (scaled * activation).astype(jnp.bfloat16)
    d_gate = (scaled * up_pre * sigmoid_gate * (1.0 + gate_pre * (1.0 - sigmoid_gate))).astype(
        jnp.bfloat16
    )
    return (hidden * mid_grad, d_gate, d_up)


def whole_block(inputs, cotangent, gate_weight, up_weight, down_weight, ia3_scale, seq_ids):
    panel_inputs = lax.all_gather(inputs, "wide", axis=0, tiled=True)
    panel_cotangent = lax.all_gather(cotangent, "wide", axis=0, tiled=True)
    gate_part = jnp.dot(panel_inputs, gate_weight, preferred_element_type=jnp.float32)
    up_part = jnp.dot(panel_inputs, up_weight, preferred_element_type=jnp.float32)
    mid_part = contract_rows(panel_cotangent, down_weight)
    quarter = gate_weight.shape[1] // lax.axis_size("narrow")
    position = lax.axis_index("narrow")
    onehot_full = (seq_ids[None, :] == jnp.arange(SEQS, dtype=jnp.int32)[:, None]).astype(
        jnp.float32
    )
    gate_pre, up_pre, mid_grad = (
        lax.psum_scatter(gate_part, "narrow", scatter_dimension=1, tiled=True),
        lax.psum_scatter(up_part, "narrow", scatter_dimension=1, tiled=True),
        lax.psum_scatter(mid_part, "narrow", scatter_dimension=1, tiled=True),
    )
    scale_part = lax.dynamic_slice_in_dim(ia3_scale, position * quarter, quarter, 0)
    product, d_gate, d_up = local_grads(gate_pre, up_pre, mid_grad, scale_part[None, :])
    example_grads = jnp.dot(onehot_full, product, precision=lax.Precision.HIGHEST)
    whole_gate, whole_up = (
        lax.all_gather(d_gate, "narrow", axis=1, tiled=True),
        lax.all_gather(d_up, "narrow", axis=1, tiled=True),
    )
    squares = lax.psum(jnp.sum(example_grads * example_grads, axis=1), ("wide", "narrow"))
    grad_norms = jnp.sqrt(squares)
    input_grad = lax.psum_scatter(
        contract_rows(whole_gate, gate_weight) + contract_rows(whole_up, up_weight),
        "wide",
        scatter_dimension=0,
        tiled=True,
    ).astype(jnp.bfloat16)
    return (example_grads, grad_norms, input_grad)


def exchange(array, axis, step):
    axes = axis if isinstance(axis, tuple) else (axis,)
    size = math.prod(lax.axis_size(name) for name in axes)
    return lax.ppermute(array, axes, [(i, i ^ step) for i in range(size)])


def held(array):
    return pltpu.with_memory_space_constraint(array, pltpu.VMEM)


def call(body, name, outs, args, spaces=None, scratch=(), out_spaces=None):
    spaces, out_spaces = spaces or {}, out_spaces or {}
    many = isinstance(outs, list)
    out_specs = [
        pl.BlockSpec(memory_space=out_spaces.get(i, pltpu.VMEM)) for i in range(len(outs) if many else 1)
    ]
    return pl.pallas_call(
        body,
        out_shape=outs,
        in_specs=[pl.BlockSpec(memory_space=spaces.get(i, pltpu.VMEM)) for i in range(len(args))],
        out_specs=out_specs if many else out_specs[0],
        scratch_shapes=list(scratch),
        compiler_params=pltpu.CompilerParams(vmem_limit_bytes=KERNEL_VMEM),
        cost_estimate=pl.CostEstimate(flops=1000, bytes_accessed=1000, transcendentals=0),
        name=name,
    )(*args)


def pack_kernel(inputs, cotangent, out, stage):
    share, features = inputs.shape
    half = features // 2
    for i, ref in enumerate((inputs, cotangent)):
        rows = ref[...].astype(jnp.float32)
        for j in range(2):
            stage[(2 * i + j) * share : (2 * i + j + 1) * share, :] = rows[:, j * half : (j + 1) * half]
    for k in range(out.shape[0]):
        out[k] = stage[8 * k : 8 * k + 8, :].astype(jnp.bfloat16)


def keys_kernel(share, ids, marks):
    position = lax.axis_index("wide")
    row = lax.broadcasted_iota(jnp.int32, (8, 128), 0)
    keys = []
    for k in range(WIDE * share // 8):
        key = jnp.zeros((8, 128), jnp.int32)
        for r in range(8):
            block, j = divmod(8 * k + r, share)
            key = jnp.where(row == r, ids[(position ^ block) * share + j], key)
        keys.append(key.astype(jnp.float32))
    keys.append(jnp.zeros((8, marks.shape[1] - 128 * len(keys)), jnp.float32))
    marks[...] = jnp.concatenate(keys, axis=1).astype(jnp.bfloat16)


def relay_kernel(own, far, marks, pair, marked):
    slabs = own.shape[0]
    for target in (pair, marked):
        target[0:slabs] = own[...]
        target[slabs : 2 * slabs] = far[...]
    marked[2 * slabs] = marks[...]


WIDE, NEXT, FAR = 4, 1, 3
GATE, UP, DOWN = range(3)
WHOLE_STRIP = (GATE, UP, DOWN)
CHUNKS = 4


def start_loads(pieces, groups, sources, targets, sem):
    copies = []
    for i, (kind, strip) in enumerate(pieces):
        target = targets[i]
        width = target.shape[0 if kind == DOWN else 1]
        owner = lax.axis_index("narrow") ^ strip
        start = pl.multiple_of((owner * groups + lax.axis_index("groups")) * width, width)
        source = sources[kind]
        source = source.at[pl.ds(start, width), :] if kind == DOWN else source.at[:, pl.ds(start, width)]
        size = target.shape[0] // CHUNKS
        for c in range(CHUNKS):
            span = slice(c * size, (c + 1) * size)
            copies.append(pltpu.make_async_copy(source.at[span, :], target.at[span, :], sem.at[i, c]))
    for copy in copies:
        copy.start()
    return copies


def load_kernel(pieces, groups, *refs):
    count = len(pieces)
    for copy in start_loads(pieces, groups, refs[:3], refs[-1 - count : -1], refs[-1]):
        copy.wait()


def loading(body, pieces, groups, outs):
    count = len(pieces)

    def kernel(*refs):
        sources, rest = refs[:3], refs[3:]
        at = len(rest) - outs[1] - 1 - count
        targets, sem = rest[at : at + count], rest[at + count + outs[1]]
        copies = start_loads(pieces, groups, sources, targets, sem)
        body(*rest[:at], *rest[at + count : at + count + outs[1]])
        for copy in copies:
            copy.wait()

    return kernel


def strip_parts(tokens, cotans, gate, up, down, put):
    tile = 256

    @pl.loop(0, gate.shape[1] // tile)
    def _(i):
        span = pl.ds(pl.multiple_of(i * tile, tile), tile)
        put(GATE, span, jnp.dot(tokens[...], gate[:, span], preferred_element_type=jnp.float32))
        put(UP, span, jnp.dot(tokens[...], up[:, span], preferred_element_type=jnp.float32))
        put(DOWN, span, contract_rows(cotans[...], down[span, :]))


def forward_kernel(tokens, cotans, gate, up, down, *refs):
    out = refs[-1]

    def put(kind, span, part):
        out[kind, :, span] = part.astype(out.dtype)

    strip_parts(tokens, cotans, gate, up, down, put)


def join_kernel(own, arrived, out):
    out[...] = (own[...] + arrived[...]).astype(out.dtype)


def first_kernel(share, marked, beside, other, diagonal, gate, up, down, *refs):
    tokens, cotans, part, rows, cots = refs[-5:]
    slabs, half = 4 * share // 8, rows.shape[1] // 2
    for source, places in (
        (marked, (0, FAR)),
        (beside, (NEXT, FAR ^ NEXT)),
        (other, (WIDE, WIDE + FAR)),
        (diagonal, (WIDE + NEXT, WIDE + (FAR ^ NEXT))),
    ):
        for i, place in enumerate(places):
            packed = source[i * slabs : (i + 1) * slabs].astype(jnp.float32).reshape(4 * share, half)
            for j, target in enumerate((rows, rows, cots, cots)):
                span = slice((j % 2) * half, (j % 2 + 1) * half)
                target[place * share : (place + 1) * share, span] = packed[j * share : (j + 1) * share]
    tokens[...] = rows[...].astype(jnp.bfloat16)
    cotans[...] = cots[...].astype(jnp.bfloat16)
    forward_kernel(tokens, cotans, gate, up, down, part)


def own_strip_kernel(groups, *refs):
    sources, (tokens, cotans, up, down) = refs[:3], refs[3:7]
    out, gate, sem = refs[-3:]
    copies = start_loads([(GATE, 0)], groups, sources, [gate], sem)
    tile = 256

    @pl.loop(0, up.shape[1] // tile)
    def _(i):
        span = pl.ds(pl.multiple_of(i * tile, tile), tile)
        out[UP, :, span] = jnp.dot(tokens[...], up[:, span], preferred_element_type=jnp.float32)
        out[DOWN, :, span] = contract_rows(cotans[...], down[span, :])

    for copy in copies:
        copy.wait()
    out[GATE] = jnp.dot(tokens[...], gate[...], preferred_element_type=jnp.float32)


def middle_kernel(groups, *refs):
    own, arrived, crossed, scale, relayed, other_relayed = refs[:6]
    message, near_gate, near_up, grads, other_grads, stage = refs[-6:]
    _, tokens, width = own.shape
    narrow, group = lax.axis_index("narrow"), lax.axis_index("groups")
    sums = [own[i] + arrived[i].astype(jnp.float32) + crossed[i].astype(jnp.float32) for i in range(3)]
    start = pl.multiple_of((narrow * groups + group) * width, width)
    product, d_gate, d_up = local_grads(*sums, scale[:, pl.ds(start, width)])
    message[0:tokens, :] = d_gate
    message[tokens : 2 * tokens, :] = d_up
    near_gate[0:tokens, :] = d_gate
    near_up[...] = d_up
    half = tokens // groups
    for side, (source, target) in enumerate(((relayed, grads), (other_relayed, other_grads))):
        marks = source[source.shape[0] - 1].astype(jnp.float32)
        seq = jnp.concatenate(
            [
                jnp.concatenate([marks[:, k * 128 : (k + 1) * 128]] * (width // 128), axis=1)
                for k in range(half // 8)
            ],
            axis=0,
        )
        part = product[side * half : (side + 1) * half]
        for e in range(SEQS):
            total = jnp.sum(jnp.where(seq == float(e), part, 0.0), axis=0, keepdims=True)
            target[e : e + 1, :] = total
            stage[side * SEQS + e : side * SEQS + e + 1, :] = total
    every = stage[...]
    squares = jnp.broadcast_to(jnp.sum(every * every, axis=1, keepdims=True), every.shape)
    tail = jnp.concatenate(split_high(squares), axis=0).astype(jnp.bfloat16)
    message[2 * tokens :, :] = tail
    near_gate[tokens:, :] = tail


TILE = 512


def backward_part(grads, gate, up, start):
    d_gate, d_up = grads
    gate_term = contract_rows(gate[start : start + TILE, :], d_gate)
    return gate_term + contract_rows(up[start : start + TILE, :], d_up)


def halves(message):
    tokens = (message.shape[0] - 16) // 2
    return message[0:tokens, :], message[tokens : 2 * tokens, :]


def backward_first_kernel(message, gate, up, total):
    for start in range(0, total.shape[0], TILE):
        total[start : start + TILE, :] = backward_part(halves(message), gate, up, start)


def backward_near_kernel(d_gate, d_up, gate, up, before, total):
    tokens = d_up.shape[0]
    for start in range(0, total.shape[0], TILE):
        part = backward_part((d_gate[0:tokens, :], d_up[...]), gate, up, start)
        total[start : start + TILE, :] = before[start : start + TILE, :] + part


def backward_next_kernel(message, gate, up, before, total):
    for start in range(0, total.shape[0], TILE):
        part = backward_part(halves(message), gate, up, start)
        total[start : start + TILE, :] = before[start : start + TILE, :] + part


def split_high(values):
    high = values.astype(jnp.bfloat16).astype(jnp.float32)
    return high, values - high


def backward_last_kernel(share, message, gate, up, before, *refs):
    others, other_grads, (own, own_squares), sends, (total, stage) = refs[:3], refs[3], refs[4:6], refs[6:9], refs[9:]
    tokens, features = total.shape
    side = features // 2
    for start in range(0, features, TILE):
        part = before[start : start + TILE, :] + backward_part(halves(message), gate, up, start)
        total[:, start : start + TILE] = part.T
    squares = sum(ref[ref.shape[0] - 16 :, 0:128].astype(jnp.float32) for ref in (message,) + others)
    squares = squares[0:8] + squares[8:16]
    own_squares[...] = squares
    tails = split_high(squares)
    slabs = 4 * share // 8
    for target, group, nearby in zip((own,) + tuple(sends), (0, 0, 1, 1), (0, NEXT, 0, NEXT)):
        rows = own if target is own else stage
        for i, place in enumerate((nearby, nearby ^ FAR)):
            at = (group * WIDE + place) * share
            for j in range(2):
                to = (2 * i + j) * share
                rows[to : to + share, :] = total[at : at + share, j * side : (j + 1) * side]
        if target is not own:
            for k in range(slabs):
                target[k, :, 0:side] = stage[8 * k : 8 * k + 8, :].astype(jnp.bfloat16)
                if target.shape[2] > side:
                    tail = tails[k] if k < 2 else jnp.zeros_like(squares)
                    target[k, :, side:] = tail.astype(jnp.bfloat16)
    width = other_grads.shape[1]
    stage[0:8, :] = jnp.zeros((8, side), jnp.float32)
    for i, rows in enumerate(split_high(other_grads[...])):
        stage[i * SEQS : (i + 1) * SEQS, 0:width] = rows
    for i, rows in enumerate(tails):
        stage[0:8, width + i * 128 : width + (i + 1) * 128] = rows
    sends[1][slabs] = stage[0:8, :].astype(jnp.bfloat16)


def combine_kernel(share, own, own_squares, beside, across, diagonal, *refs):
    kept_rows, other_grads, send, total, stage = refs
    slabs, side = beside.shape[0], own.shape[1]
    width = other_grads.shape[1]
    for k in range(slabs):
        rows = own[8 * k : 8 * k + 8, :] + across[k].astype(jnp.float32)
        for ref in (beside, diagonal):
            rows = rows + ref[k, :, 0:side].astype(jnp.float32)
        total[8 * k : 8 * k + 8, :] = rows
    tail = across[slabs].astype(jnp.float32)
    other_grads[...] = tail[0:SEQS, 0:width] + tail[SEQS : 2 * SEQS, 0:width]
    same, turned = own_squares[...], tail[:, width : width + 128] + tail[:, width + 128 : width + 256]
    for k in range(2):
        same = same + beside[k, :, side:].astype(jnp.float32)
        turned = turned + diagonal[k, :, side:].astype(jnp.float32)
    squares = same[0:SEQS] + turned[SEQS : 2 * SEQS]
    count = 2 * share
    kept_rows[...] = jnp.zeros_like(kept_rows)
    stage[...] = jnp.zeros_like(stage)
    kept_rows[0:count, :] = total[0:count, :]
    stage[0:count, :] = total[count : 2 * count, :]
    high, low = split_high(squares)
    for e in range(SEQS):
        span = slice(e * 128, (e + 1) * 128)
        for ref in (kept_rows, stage):
            ref[count : count + 1, span] = high[e : e + 1]
            ref[count + 1 : count + 2, span] = low[e : e + 1]
    for k in range(2):
        send[k] = stage[8 * k : 8 * k + 8, :].astype(jnp.bfloat16)


def last_kernel(share, own, arrived, grads, other_grads, input_grad, example_grads, norms, stage):
    side, width = own.shape[1], grads.shape[1]
    group = lax.axis_index("groups")
    for k in range(2):
        stage[8 * k : 8 * k + 8, :] = own[8 * k : 8 * k + 8, :] + arrived[k].astype(jnp.float32)
    for j in range(2):
        rows = stage[j * share : (j + 1) * share, :]
        input_grad[:, j * side : (j + 1) * side] = rows.astype(jnp.bfloat16)
    example_grads[:, pl.ds(pl.multiple_of(group * width, width), width)] = grads[...]
    example_grads[:, pl.ds(pl.multiple_of((1 - group) * width, width), width)] = other_grads[...]
    count = 2 * share
    squares = stage[count : count + 1, 0 : SEQS * 128] + stage[count + 1 : count + 2, 0 : SEQS * 128]
    roots = jnp.sqrt(squares)
    for e in range(SEQS):
        norms[e] = jnp.max(roots[:, e * 128 : (e + 1) * 128])


def shared(inputs, cotangent, gate_weight, up_weight, down_weight, ia3_scale, seq_ids):
    groups, wide, strips = lax.axis_size("groups"), lax.axis_size("wide"), lax.axis_size("narrow")
    share, features = inputs.shape
    width = gate_weight.shape[1] // (strips * groups)
    half = share * wide
    tokens = half * groups
    f32, bf16 = jnp.float32, jnp.bfloat16
    slabs, side = 4 * share // 8, features // 2
    weights = tuple(
        pltpu.with_memory_space_constraint(weight, pltpu.HBM)
        for weight in (gate_weight, up_weight, down_weight)
    )
    weight_shapes = [
        pltpu.VMEM((features, width), bf16),
        pltpu.VMEM((features, width), bf16),
        pltpu.VMEM((width, features), bf16),
    ]
    kept = {}

    def load(name, pieces, after=()):
        args = weights + tuple(after)
        arrays = call(
            functools.partial(load_kernel, pieces, groups),
            name,
            [weight_shapes[kind] for kind, _ in pieces],
            args,
            {i: pltpu.HBM if i < 3 else pl.ANY for i in range(len(args))},
            [pltpu.SemaphoreType.DMA((len(pieces), CHUNKS))],
        )
        kept.update(zip(pieces, arrays))

    def call_loading(body, name, pieces, outs, args, scratch=(), spaces=None):
        made = call(
            loading(body, pieces, groups, (len(outs), len(outs) + len(scratch))),
            name,
            [weight_shapes[kind] for kind, _ in pieces] + outs,
            list(weights) + args,
            {**{i: pltpu.HBM for i in range(3)}, **(spaces or {})},
            list(scratch) + [pltpu.SemaphoreType.DMA((len(pieces), CHUNKS))],
        )
        kept.update(zip(pieces, made))
        return made[len(pieces) :]

    def hold(strip, kinds=WHOLE_STRIP):
        return [held(kept[kind, strip]) for kind in kinds]

    packed = call(
        pack_kernel,
        "pack",
        pltpu.VMEM((slabs, 8, features // 2), bf16),
        [pltpu.with_memory_space_constraint(array, pltpu.HBM) for array in (inputs, cotangent)],
        scratch=[pltpu.VMEM((4 * share, features // 2), f32)],
    )
    far = exchange(packed, "wide", FAR)
    (marks,) = call_loading(
        functools.partial(keys_kernel, share),
        "load_a",
        [(kind, 3) for kind in WHOLE_STRIP],
        [pltpu.VMEM((8, side), bf16)],
        [pltpu.with_memory_space_constraint(seq_ids, pltpu.HBM)],
        spaces={3: pltpu.SMEM},
    )
    pair, marked = call(
        relay_kernel,
        "relay",
        [pltpu.VMEM((2 * slabs, 8, side), bf16), pltpu.VMEM((2 * slabs + 1, 8, side), bf16)],
        [packed, far, marks],
    )
    diagonal = exchange(pair, ("groups", "wide"), WIDE + NEXT)
    other_marked = exchange(marked, "groups", 1)
    beside = exchange(pair, "wide", NEXT)
    load("load_b", [(kind, 2) for kind in WHOLE_STRIP], [pair])

    part = pltpu.VMEM((3, tokens, width), f32)
    near_shape = pltpu.VMEM((3, tokens, width), bf16)
    tokens_all, cotans_all, diagonal = call_loading(
        functools.partial(first_kernel, share),
        "forward_3",
        [(GATE, 1), (DOWN, 1)],
        [pltpu.VMEM((tokens, features), bf16)] * 2 + [part],
        [marked, beside, other_marked, diagonal] + hold(3) + hold(2, [GATE]),
        [pltpu.VMEM((tokens, features), f32)] * 2,
    )
    panel = [tokens_all, cotans_all]
    diagonal = exchange(diagonal, "narrow", 1)
    (second,) = call_loading(forward_kernel, "forward_2", [(UP, 1)], [part], panel + hold(2))
    crossing = call(join_kernel, "join", near_shape, [held(second), diagonal])
    crossed = exchange(crossing, "narrow", 2)
    (near,) = call_loading(
        forward_kernel, "forward_1", [(UP, 0), (DOWN, 0)], [near_shape], panel + hold(1) + [held(crossing)]
    )
    near = exchange(near, "narrow", 1)
    own_part, kept[GATE, 0] = call(
        functools.partial(own_strip_kernel, groups),
        "forward_0",
        [part, weight_shapes[GATE]],
        list(weights) + panel + hold(0, [UP, DOWN]),
        {i: pltpu.HBM for i in range(3)},
        [pltpu.SemaphoreType.DMA((1, CHUNKS))],
    )

    resident = [array for s in range(strips) for array in hold(s, [GATE, UP])]
    message, near_gate, near_up, grads, other_grads = call(
        functools.partial(middle_kernel, groups),
        "middle",
        [
            pltpu.VMEM((2 * tokens + 16, width), bf16),
            pltpu.VMEM((tokens + 16, width), bf16),
            pltpu.VMEM((tokens, width), bf16),
            pltpu.VMEM((SEQS, width), f32),
            pltpu.VMEM((SEQS, width), f32),
        ],
        [own_part, near, crossed, ia3_scale[None, :], marked, other_marked] + resident,
        scratch=[pltpu.VMEM((groups * SEQS, width), f32)],
    )

    total = pltpu.VMEM((features, tokens), f32)
    near_gate, near_up = exchange(near_gate, "narrow", 1), exchange(near_up, "narrow", 1)
    message_2 = exchange(message, "narrow", 2)
    sums = call(backward_first_kernel, "backward_0", total, [message] + hold(0, [GATE, UP]))
    sums = call(backward_near_kernel, "backward_1", total, [near_gate, near_up] + hold(1, [GATE, UP]) + [sums])
    message_2, sums = lax.optimization_barrier((message_2, sums))
    message_3 = exchange(message_2, "narrow", 1)
    sums = call(backward_next_kernel, "backward_2", total, [message_2] + hold(2, [GATE, UP]) + [sums])
    block = pltpu.VMEM((slabs, 8, side + 128), bf16)
    own, own_squares, *sends = call(
        functools.partial(backward_last_kernel, share),
        "backward_3",
        [
            pltpu.VMEM((4 * share, side), f32),
            pltpu.VMEM((8, 128), f32),
            block,
            pltpu.VMEM((slabs + 1, 8, side), bf16),
            block,
        ],
        [message_3] + hold(3, [GATE, UP]) + [sums, message, near_gate, message_2, other_grads],
        scratch=[pltpu.VMEM((tokens, features), f32), pltpu.VMEM((4 * share, side), f32)],
    )
    diagonal = exchange(sends[2], ("groups", "wide"), WIDE + NEXT)
    across = exchange(sends[1], "groups", 1)
    beside = exchange(sends[0], "wide", NEXT)
    own, other_grads, send = call(
        functools.partial(combine_kernel, share),
        "combine",
        [pltpu.VMEM((16, side), f32), pltpu.VMEM((SEQS, width), f32), pltpu.VMEM((2, 8, side), bf16)],
        [own, own_squares, beside, across, diagonal],
        scratch=[pltpu.VMEM((4 * share, side), f32), pltpu.VMEM((16, side), f32)],
    )
    input_grad, example_grads, norms = call(
        functools.partial(last_kernel, share),
        "last",
        [
            jax.ShapeDtypeStruct((share, features), bf16),
            jax.ShapeDtypeStruct((SEQS, groups * width), f32),
            jax.ShapeDtypeStruct((SEQS,), f32),
        ],
        [own, exchange(send, "wide", FAR), grads, other_grads],
        scratch=[pltpu.VMEM((16, side), f32)],
        out_spaces={2: pltpu.SMEM},
    )
    return (example_grads, norms, input_grad)


def local(inputs, cotangent, gate_weight, up_weight, down_weight, ia3_scale, seq_ids):
    groups, wide, narrow = lax.axis_size("groups"), lax.axis_size("wide"), lax.axis_size("narrow")
    share, (features, hidden) = inputs.shape[0], gate_weight.shape
    width = hidden // (narrow * groups)
    fits = (
        groups == 2
        and narrow == 4
        and wide == WIDE
        and hidden % (narrow * groups * 256) == 0
        and features >= 2048
        and width <= features // 2 - 256
        and features % (2 * TILE) == 0
        and share in (4, 6)
        and (share * wide) % 8 == 0
        and share * wide <= 64
        and 3 * features * hidden // groups * 2 <= 40 << 20
    )
    plan = shared if fits else whole_block
    return plan(inputs, cotangent, gate_weight, up_weight, down_weight, ia3_scale, seq_ids)


def solution(mesh):
    return jax.shard_map(
        local,
        mesh=mesh,
        in_specs=(
            P(("groups", "wide"), "narrow"),
            P(("groups", "wide"), "narrow"),
            P("narrow", "wide"),
            P("narrow", "wide"),
            P("wide", "narrow"),
            P("wide"),
            P("groups"),
        ),
        out_specs=(P("groups", ("wide", "narrow")), P("groups"), P(("groups", "wide"), "narrow")),
        check_vma=False,
    )
```

```python
import functools
import math

import jax
import jax.numpy as jnp
from jax import lax
from jax.experimental import pallas as pl
from jax.experimental.pallas import tpu as pltpu
from jax.sharding import PartitionSpec as P

SEQS = 4
KERNEL_VMEM = 6 << 20


def contract_rows(left, right):
    return lax.dot_general(
        left, right, (((1,), (1,)), ((), ())), preferred_element_type=jnp.float32
    )


def local_grads(gate_pre, up_pre, mid_grad, scale_part):
    sigmoid_gate = jax.nn.sigmoid(gate_pre)
    activation = gate_pre * sigmoid_gate
    hidden = activation * up_pre
    scaled = scale_part * mid_grad
    d_up = (scaled * activation).astype(jnp.bfloat16)
    d_gate = (scaled * up_pre * sigmoid_gate * (1.0 + gate_pre * (1.0 - sigmoid_gate))).astype(
        jnp.bfloat16
    )
    return (hidden * mid_grad, d_gate, d_up)


def whole_block(inputs, cotangent, gate_weight, up_weight, down_weight, ia3_scale, seq_ids):
    panel_inputs = lax.all_gather(inputs, "wide", axis=0, tiled=True)
    panel_cotangent = lax.all_gather(cotangent, "wide", axis=0, tiled=True)
    gate_part = jnp.dot(panel_inputs, gate_weight, preferred_element_type=jnp.float32)
    up_part = jnp.dot(panel_inputs, up_weight, preferred_element_type=jnp.float32)
    mid_part = contract_rows(panel_cotangent, down_weight)
    quarter = gate_weight.shape[1] // lax.axis_size("narrow")
    position = lax.axis_index("narrow")
    onehot_full = (seq_ids[None, :] == jnp.arange(SEQS, dtype=jnp.int32)[:, None]).astype(
        jnp.float32
    )
    gate_pre, up_pre, mid_grad = (
        lax.psum_scatter(gate_part, "narrow", scatter_dimension=1, tiled=True),
        lax.psum_scatter(up_part, "narrow", scatter_dimension=1, tiled=True),
        lax.psum_scatter(mid_part, "narrow", scatter_dimension=1, tiled=True),
    )
    scale_part = lax.dynamic_slice_in_dim(ia3_scale, position * quarter, quarter, 0)
    product, d_gate, d_up = local_grads(gate_pre, up_pre, mid_grad, scale_part[None, :])
    example_grads = jnp.dot(onehot_full, product, precision=lax.Precision.HIGHEST)
    whole_gate, whole_up = (
        lax.all_gather(d_gate, "narrow", axis=1, tiled=True),
        lax.all_gather(d_up, "narrow", axis=1, tiled=True),
    )
    squares = lax.psum(jnp.sum(example_grads * example_grads, axis=1), ("wide", "narrow"))
    grad_norms = jnp.sqrt(squares)
    input_grad = lax.psum_scatter(
        contract_rows(whole_gate, gate_weight) + contract_rows(whole_up, up_weight),
        "wide",
        scatter_dimension=0,
        tiled=True,
    ).astype(jnp.bfloat16)
    return (example_grads, grad_norms, input_grad)


def exchange(array, axis, step):
    axes = axis if isinstance(axis, tuple) else (axis,)
    size = math.prod(lax.axis_size(name) for name in axes)
    return lax.ppermute(array, axes, [(i, i ^ step) for i in range(size)])


def held(array):
    return pltpu.with_memory_space_constraint(array, pltpu.VMEM)


def call(body, name, outs, args, spaces=None, scratch=(), out_spaces=None):
    spaces, out_spaces = spaces or {}, out_spaces or {}
    many = isinstance(outs, list)
    out_specs = [
        pl.BlockSpec(memory_space=out_spaces.get(i, pltpu.VMEM)) for i in range(len(outs) if many else 1)
    ]
    return pl.pallas_call(
        body,
        out_shape=outs,
        in_specs=[pl.BlockSpec(memory_space=spaces.get(i, pltpu.VMEM)) for i in range(len(args))],
        out_specs=out_specs if many else out_specs[0],
        scratch_shapes=list(scratch),
        compiler_params=pltpu.CompilerParams(vmem_limit_bytes=KERNEL_VMEM),
        cost_estimate=pl.CostEstimate(flops=1000, bytes_accessed=1000, transcendentals=0),
        name=name,
    )(*args)


def pack_kernel(inputs, cotangent, out, stage):
    share, features = inputs.shape
    half = features // 2
    for i, ref in enumerate((inputs, cotangent)):
        rows = ref[...].astype(jnp.float32)
        for j in range(2):
            stage[(2 * i + j) * share : (2 * i + j + 1) * share, :] = rows[:, j * half : (j + 1) * half]
    for k in range(out.shape[0]):
        out[k] = stage[8 * k : 8 * k + 8, :].astype(jnp.bfloat16)


def keys_kernel(share, ids, marks):
    position = lax.axis_index("wide")
    row = lax.broadcasted_iota(jnp.int32, (8, 128), 0)
    keys = []
    for k in range(WIDE * share // 8):
        key = jnp.zeros((8, 128), jnp.int32)
        for r in range(8):
            block, j = divmod(8 * k + r, share)
            key = jnp.where(row == r, ids[(position ^ block) * share + j], key)
        keys.append(key.astype(jnp.float32))
    keys.append(jnp.zeros((8, marks.shape[1] - 128 * len(keys)), jnp.float32))
    marks[...] = jnp.concatenate(keys, axis=1).astype(jnp.bfloat16)


def relay_kernel(own, far, marks, pair, marked):
    slabs = own.shape[0]
    for target in (pair, marked):
        target[0:slabs] = own[...]
        target[slabs : 2 * slabs] = far[...]
    marked[2 * slabs] = marks[...]


WIDE, NEXT, FAR = 4, 1, 3
GATE, UP, DOWN = range(3)
WHOLE_STRIP = (GATE, UP, DOWN)
CHUNKS = 4


def start_loads(pieces, groups, sources, targets, sem):
    copies = []
    for i, (kind, strip) in enumerate(pieces):
        target = targets[i]
        width = target.shape[0 if kind == DOWN else 1]
        owner = lax.axis_index("narrow") ^ strip
        start = pl.multiple_of((owner * groups + lax.axis_index("groups")) * width, width)
        source = sources[kind]
        source = source.at[pl.ds(start, width), :] if kind == DOWN else source.at[:, pl.ds(start, width)]
        size = target.shape[0] // CHUNKS
        for c in range(CHUNKS):
            span = slice(c * size, (c + 1) * size)
            copies.append(pltpu.make_async_copy(source.at[span, :], target.at[span, :], sem.at[i, c]))
    for copy in copies:
        copy.start()
    return copies


def load_kernel(pieces, groups, *refs):
    count = len(pieces)
    for copy in start_loads(pieces, groups, refs[:3], refs[-1 - count : -1], refs[-1]):
        copy.wait()


def loading(body, pieces, groups, outs):
    count = len(pieces)

    def kernel(*refs):
        sources, rest = refs[:3], refs[3:]
        at = len(rest) - outs[1] - 1 - count
        targets, sem = rest[at : at + count], rest[at + count + outs[1]]
        copies = start_loads(pieces, groups, sources, targets, sem)

        @pl.when(lax.axis_index("narrow") >= 0)
        def _():
            body(*rest[:at], *rest[at + count : at + count + outs[1]])

        for copy in copies:
            copy.wait()

    return kernel


def strip_parts(tokens, cotans, gate, up, down, put):
    tile = 256

    @pl.loop(0, gate.shape[1] // tile)
    def _(i):
        span = pl.ds(pl.multiple_of(i * tile, tile), tile)
        put(GATE, span, jnp.dot(tokens[...], gate[:, span], preferred_element_type=jnp.float32))
        put(UP, span, jnp.dot(tokens[...], up[:, span], preferred_element_type=jnp.float32))
        put(DOWN, span, contract_rows(cotans[...], down[span, :]))


def forward_kernel(tokens, cotans, gate, up, down, *refs):
    out = refs[-1]

    def put(kind, span, part):
        out[kind, :, span] = part.astype(out.dtype)

    strip_parts(tokens, cotans, gate, up, down, put)


def join_kernel(own, arrived, out):
    out[...] = (own[...] + arrived[...]).astype(out.dtype)


def first_kernel(share, marked, beside, other, diagonal, gate, up, down, *refs):
    tokens, cotans, part, rows, cots = refs[-5:]
    slabs, half = 4 * share // 8, rows.shape[1] // 2
    for source, places in (
        (marked, (0, FAR)),
        (beside, (NEXT, FAR ^ NEXT)),
        (other, (WIDE, WIDE + FAR)),
        (diagonal, (WIDE + NEXT, WIDE + (FAR ^ NEXT))),
    ):
        for i, place in enumerate(places):
            packed = source[i * slabs : (i + 1) * slabs].astype(jnp.float32).reshape(4 * share, half)
            for j, target in enumerate((rows, rows, cots, cots)):
                span = slice((j % 2) * half, (j % 2 + 1) * half)
                target[place * share : (place + 1) * share, span] = packed[j * share : (j + 1) * share]
    tokens[...] = rows[...].astype(jnp.bfloat16)
    cotans[...] = cots[...].astype(jnp.bfloat16)
    forward_kernel(tokens, cotans, gate, up, down, part)


def own_strip_kernel(groups, *refs):
    sources, (tokens, cotans, up, down) = refs[:3], refs[3:7]
    out, gate, sem = refs[-3:]
    copies = start_loads([(GATE, 0)], groups, sources, [gate], sem)
    tile = 256

    @pl.loop(0, up.shape[1] // tile)
    def _(i):
        span = pl.ds(pl.multiple_of(i * tile, tile), tile)
        out[UP, :, span] = jnp.dot(tokens[...], up[:, span], preferred_element_type=jnp.float32)
        out[DOWN, :, span] = contract_rows(cotans[...], down[span, :])

    for copy in copies:
        copy.wait()
    out[GATE] = jnp.dot(tokens[...], gate[...], preferred_element_type=jnp.float32)


def middle_kernel(groups, *refs):
    own, arrived, crossed, scale, relayed, other_relayed = refs[:6]
    message, near_gate, near_up, grads, other_grads, stage = refs[-6:]
    _, tokens, width = own.shape
    narrow, group = lax.axis_index("narrow"), lax.axis_index("groups")
    sums = [own[i] + arrived[i].astype(jnp.float32) + crossed[i].astype(jnp.float32) for i in range(3)]
    start = pl.multiple_of((narrow * groups + group) * width, width)
    product, d_gate, d_up = local_grads(*sums, scale[:, pl.ds(start, width)])
    message[0:tokens, :] = d_gate
    message[tokens : 2 * tokens, :] = d_up
    near_gate[0:tokens, :] = d_gate
    near_up[...] = d_up
    half = tokens // groups
    for side, (source, target) in enumerate(((relayed, grads), (other_relayed, other_grads))):
        marks = source[source.shape[0] - 1].astype(jnp.float32)
        seq = jnp.concatenate(
            [
                jnp.concatenate([marks[:, k * 128 : (k + 1) * 128]] * (width // 128), axis=1)
                for k in range(half // 8)
            ],
            axis=0,
        )
        part = product[side * half : (side + 1) * half]
        for e in range(SEQS):
            total = jnp.sum(jnp.where(seq == float(e), part, 0.0), axis=0, keepdims=True)
            target[e : e + 1, :] = total
            stage[side * SEQS + e : side * SEQS + e + 1, :] = total
    every = stage[...]
    squares = jnp.broadcast_to(jnp.sum(every * every, axis=1, keepdims=True), every.shape)
    tail = jnp.concatenate(split_high(squares), axis=0).astype(jnp.bfloat16)
    message[2 * tokens :, :] = tail
    near_gate[tokens:, :] = tail


TILE = 512


def backward_part(grads, gate, up, start):
    d_gate, d_up = grads
    gate_term = contract_rows(gate[start : start + TILE, :], d_gate)
    return gate_term + contract_rows(up[start : start + TILE, :], d_up)


def halves(message):
    tokens = (message.shape[0] - 16) // 2
    return message[0:tokens, :], message[tokens : 2 * tokens, :]


def backward_first_kernel(message, gate, up, total):
    for start in range(0, total.shape[0], TILE):
        total[start : start + TILE, :] = backward_part(halves(message), gate, up, start)


def backward_near_kernel(d_gate, d_up, gate, up, before, total):
    tokens = d_up.shape[0]
    for start in range(0, total.shape[0], TILE):
        part = backward_part((d_gate[0:tokens, :], d_up[...]), gate, up, start)
        total[start : start + TILE, :] = before[start : start + TILE, :] + part


def backward_next_kernel(message, gate, up, before, total):
    for start in range(0, total.shape[0], TILE):
        part = backward_part(halves(message), gate, up, start)
        total[start : start + TILE, :] = before[start : start + TILE, :] + part


def split_high(values):
    high = values.astype(jnp.bfloat16).astype(jnp.float32)
    return high, values - high


def backward_last_kernel(share, message, gate, up, before, *refs):
    others, other_grads, (own, own_squares), sends, (total, stage) = refs[:3], refs[3], refs[4:6], refs[6:9], refs[9:]
    tokens, features = total.shape
    side = features // 2
    for start in range(0, features, TILE):
        part = before[start : start + TILE, :] + backward_part(halves(message), gate, up, start)
        total[:, start : start + TILE] = part.T
    squares = sum(ref[ref.shape[0] - 16 :, 0:128].astype(jnp.float32) for ref in (message,) + others)
    squares = squares[0:8] + squares[8:16]
    own_squares[...] = squares
    tails = split_high(squares)
    slabs = 4 * share // 8
    for target, group, nearby in zip((own,) + tuple(sends), (0, 0, 1, 1), (0, NEXT, 0, NEXT)):
        rows = own if target is own else stage
        for i, place in enumerate((nearby, nearby ^ FAR)):
            at = (group * WIDE + place) * share
            for j in range(2):
                to = (2 * i + j) * share
                rows[to : to + share, :] = total[at : at + share, j * side : (j + 1) * side]
        if target is not own:
            for k in range(slabs):
                target[k, :, 0:side] = stage[8 * k : 8 * k + 8, :].astype(jnp.bfloat16)
                if target.shape[2] > side:
                    tail = tails[k] if k < 2 else jnp.zeros_like(squares)
                    target[k, :, side:] = tail.astype(jnp.bfloat16)
    width = other_grads.shape[1]
    stage[0:8, :] = jnp.zeros((8, side), jnp.float32)
    for i, rows in enumerate(split_high(other_grads[...])):
        stage[i * SEQS : (i + 1) * SEQS, 0:width] = rows
    for i, rows in enumerate(tails):
        stage[0:8, width + i * 128 : width + (i + 1) * 128] = rows
    sends[1][slabs] = stage[0:8, :].astype(jnp.bfloat16)


def combine_kernel(share, own, own_squares, diagonal, across, beside, *refs):
    kept_rows, other_grads, send, total, stage = refs
    slabs, side = beside.shape[0], own.shape[1]
    width = other_grads.shape[1]
    for k in range(slabs):
        rows = own[8 * k : 8 * k + 8, :] + across[k].astype(jnp.float32)
        for ref in (beside, diagonal):
            rows = rows + ref[k, :, 0:side].astype(jnp.float32)
        total[8 * k : 8 * k + 8, :] = rows
    tail = across[slabs].astype(jnp.float32)
    other_grads[...] = tail[0:SEQS, 0:width] + tail[SEQS : 2 * SEQS, 0:width]
    same, turned = own_squares[...], tail[:, width : width + 128] + tail[:, width + 128 : width + 256]
    for k in range(2):
        same = same + beside[k, :, side:].astype(jnp.float32)
        turned = turned + diagonal[k, :, side:].astype(jnp.float32)
    squares = same[0:SEQS] + turned[SEQS : 2 * SEQS]
    count = 2 * share
    kept_rows[...] = jnp.zeros_like(kept_rows)
    stage[...] = jnp.zeros_like(stage)
    kept_rows[0:count, :] = total[0:count, :]
    stage[0:count, :] = total[count : 2 * count, :]
    high, low = split_high(squares)
    for e in range(SEQS):
        span = slice(e * 128, (e + 1) * 128)
        for ref in (kept_rows, stage):
            ref[count : count + 1, span] = high[e : e + 1]
            ref[count + 1 : count + 2, span] = low[e : e + 1]
    for k in range(2):
        send[k] = stage[8 * k : 8 * k + 8, :].astype(jnp.bfloat16)


def last_kernel(share, own, arrived, grads, other_grads, input_grad, example_grads, norms, stage):
    side, width = own.shape[1], grads.shape[1]
    group = lax.axis_index("groups")
    for k in range(2):
        stage[8 * k : 8 * k + 8, :] = own[8 * k : 8 * k + 8, :] + arrived[k].astype(jnp.float32)
    for j in range(2):
        rows = stage[j * share : (j + 1) * share, :]
        input_grad[:, j * side : (j + 1) * side] = rows.astype(jnp.bfloat16)
    example_grads[:, pl.ds(pl.multiple_of(group * width, width), width)] = grads[...]
    example_grads[:, pl.ds(pl.multiple_of((1 - group) * width, width), width)] = other_grads[...]
    count = 2 * share
    squares = stage[count : count + 1, 0 : SEQS * 128] + stage[count + 1 : count + 2, 0 : SEQS * 128]
    roots = jnp.sqrt(squares)
    for e in range(SEQS):
        norms[e] = jnp.max(roots[:, e * 128 : (e + 1) * 128])


def shared(inputs, cotangent, gate_weight, up_weight, down_weight, ia3_scale, seq_ids):
    groups, wide, strips = lax.axis_size("groups"), lax.axis_size("wide"), lax.axis_size("narrow")
    share, features = inputs.shape
    width = gate_weight.shape[1] // (strips * groups)
    half = share * wide
    tokens = half * groups
    f32, bf16 = jnp.float32, jnp.bfloat16
    slabs, side = 4 * share // 8, features // 2
    weights = tuple(
        pltpu.with_memory_space_constraint(weight, pltpu.HBM)
        for weight in (gate_weight, up_weight, down_weight)
    )
    weight_shapes = [
        pltpu.VMEM((features, width), bf16),
        pltpu.VMEM((features, width), bf16),
        pltpu.VMEM((width, features), bf16),
    ]
    kept = {}

    def load(name, pieces, after=()):
        args = weights + tuple(after)
        arrays = call(
            functools.partial(load_kernel, pieces, groups),
            name,
            [weight_shapes[kind] for kind, _ in pieces],
            args,
            {i: pltpu.HBM if i < 3 else pl.ANY for i in range(len(args))},
            [pltpu.SemaphoreType.DMA((len(pieces), CHUNKS))],
        )
        kept.update(zip(pieces, arrays))

    def call_loading(body, name, pieces, outs, args, scratch=(), spaces=None):
        made = call(
            loading(body, pieces, groups, (len(outs), len(outs) + len(scratch))),
            name,
            [weight_shapes[kind] for kind, _ in pieces] + outs,
            list(weights) + args,
            {**{i: pltpu.HBM for i in range(3)}, **(spaces or {})},
            list(scratch) + [pltpu.SemaphoreType.DMA((len(pieces), CHUNKS))],
        )
        kept.update(zip(pieces, made))
        return made[len(pieces) :]

    def hold(strip, kinds=WHOLE_STRIP):
        return [held(kept[kind, strip]) for kind in kinds]

    packed = call(
        pack_kernel,
        "pack",
        pltpu.VMEM((slabs, 8, features // 2), bf16),
        [pltpu.with_memory_space_constraint(array, pltpu.HBM) for array in (inputs, cotangent)],
        scratch=[pltpu.VMEM((4 * share, features // 2), f32)],
    )
    far = exchange(packed, "wide", FAR)
    (marks,) = call_loading(
        functools.partial(keys_kernel, share),
        "load_a",
        [(kind, 3) for kind in WHOLE_STRIP],
        [pltpu.VMEM((8, side), bf16)],
        [pltpu.with_memory_space_constraint(seq_ids, pltpu.HBM)],
        spaces={3: pltpu.SMEM},
    )
    pair, marked = call(
        relay_kernel,
        "relay",
        [pltpu.VMEM((2 * slabs, 8, side), bf16), pltpu.VMEM((2 * slabs + 1, 8, side), bf16)],
        [packed, far, marks],
    )
    diagonal = exchange(pair, ("groups", "wide"), WIDE + NEXT)
    other_marked = exchange(marked, "groups", 1)
    beside = exchange(pair, "wide", NEXT)
    load("load_b", [(kind, 2) for kind in WHOLE_STRIP], [pair])

    part = pltpu.VMEM((3, tokens, width), f32)
    near_shape = pltpu.VMEM((3, tokens, width), bf16)
    tokens_all, cotans_all, diagonal = call_loading(
        functools.partial(first_kernel, share),
        "forward_3",
        [(GATE, 1), (DOWN, 1)],
        [pltpu.VMEM((tokens, features), bf16)] * 2 + [part],
        [marked, beside, other_marked, diagonal] + hold(3) + hold(2, [GATE]),
        [pltpu.VMEM((tokens, features), f32)] * 2,
    )
    panel = [tokens_all, cotans_all]
    diagonal = exchange(diagonal, "narrow", 1)
    (second,) = call_loading(forward_kernel, "forward_2", [(UP, 1)], [part], panel + hold(2))
    crossing = call(join_kernel, "join", near_shape, [held(second), diagonal])
    crossed = exchange(crossing, "narrow", 2)
    (near,) = call_loading(
        forward_kernel, "forward_1", [(UP, 0), (DOWN, 0)], [near_shape], panel + hold(1) + [held(crossing)]
    )
    near = exchange(near, "narrow", 1)
    own_part, kept[GATE, 0] = call(
        functools.partial(own_strip_kernel, groups),
        "forward_0",
        [part, weight_shapes[GATE]],
        list(weights) + panel + hold(0, [UP, DOWN]),
        {i: pltpu.HBM for i in range(3)},
        [pltpu.SemaphoreType.DMA((1, CHUNKS))],
    )

    resident = [array for s in range(strips) for array in hold(s, [GATE, UP])]
    message, near_gate, near_up, grads, other_grads = call(
        functools.partial(middle_kernel, groups),
        "middle",
        [
            pltpu.VMEM((2 * tokens + 16, width), bf16),
            pltpu.VMEM((tokens + 16, width), bf16),
            pltpu.VMEM((tokens, width), bf16),
            pltpu.VMEM((SEQS, width), f32),
            pltpu.VMEM((SEQS, width), f32),
        ],
        [own_part, near, crossed, ia3_scale[None, :], marked, other_marked] + resident,
        scratch=[pltpu.VMEM((groups * SEQS, width), f32)],
    )

    total = pltpu.VMEM((features, tokens), f32)
    near_gate, near_up = exchange(near_gate, "narrow", 1), exchange(near_up, "narrow", 1)
    message_2 = exchange(message, "narrow", 2)
    sums = call(backward_first_kernel, "backward_0", total, [message] + hold(0, [GATE, UP]))
    sums = call(backward_near_kernel, "backward_1", total, [near_gate, near_up] + hold(1, [GATE, UP]) + [sums])
    message_2, sums = lax.optimization_barrier((message_2, sums))
    message_3 = exchange(message_2, "narrow", 1)
    sums = call(backward_next_kernel, "backward_2", total, [message_2] + hold(2, [GATE, UP]) + [sums])
    block = pltpu.VMEM((slabs, 8, side + 128), bf16)
    own, own_squares, *sends = call(
        functools.partial(backward_last_kernel, share),
        "backward_3",
        [
            pltpu.VMEM((4 * share, side), f32),
            pltpu.VMEM((8, 128), f32),
            block,
            pltpu.VMEM((slabs + 1, 8, side), bf16),
            block,
        ],
        [message_3] + hold(3, [GATE, UP]) + [sums, message, near_gate, message_2, other_grads],
        scratch=[pltpu.VMEM((tokens, features), f32), pltpu.VMEM((4 * share, side), f32)],
    )
    across = exchange(sends[1], "groups", 1)
    beside = exchange(sends[0], "wide", NEXT)
    diagonal = exchange(sends[2], ("groups", "wide"), WIDE + NEXT)
    own, other_grads, send = call(
        functools.partial(combine_kernel, share),
        "combine",
        [pltpu.VMEM((16, side), f32), pltpu.VMEM((SEQS, width), f32), pltpu.VMEM((2, 8, side), bf16)],
        [own, own_squares, diagonal, across, beside],
        scratch=[pltpu.VMEM((4 * share, side), f32), pltpu.VMEM((16, side), f32)],
    )
    input_grad, example_grads, norms = call(
        functools.partial(last_kernel, share),
        "last",
        [
            jax.ShapeDtypeStruct((share, features), bf16),
            jax.ShapeDtypeStruct((SEQS, groups * width), f32),
            jax.ShapeDtypeStruct((SEQS,), f32),
        ],
        [own, exchange(send, "wide", FAR), grads, other_grads],
        scratch=[pltpu.VMEM((16, side), f32)],
        out_spaces={2: pltpu.SMEM},
    )
    return (example_grads, norms, input_grad)


def local(inputs, cotangent, gate_weight, up_weight, down_weight, ia3_scale, seq_ids):
    groups, wide, narrow = lax.axis_size("groups"), lax.axis_size("wide"), lax.axis_size("narrow")
    share, (features, hidden) = inputs.shape[0], gate_weight.shape
    width = hidden // (narrow * groups)
    fits = (
        groups == 2
        and narrow == 4
        and wide == WIDE
        and hidden % (narrow * groups * 256) == 0
        and features >= 2048
        and width <= features // 2 - 256
        and features % (2 * TILE) == 0
        and share in (4, 6)
        and (share * wide) % 8 == 0
        and share * wide <= 64
        and 3 * features * hidden // groups * 2 <= 40 << 20
    )
    plan = shared if fits else whole_block
    return plan(inputs, cotangent, gate_weight, up_weight, down_weight, ia3_scale, seq_ids)


def solution(mesh):
    return jax.shard_map(
        local,
        mesh=mesh,
        in_specs=(
            P(("groups", "wide"), "narrow"),
            P(("groups", "wide"), "narrow"),
            P("narrow", "wide"),
            P("narrow", "wide"),
            P("wide", "narrow"),
            P("wide"),
            P("groups"),
        ),
        out_specs=(P("groups", ("wide", "narrow")), P("groups"), P(("groups", "wide"), "narrow")),
        check_vma=False,
    )
```

```python
import functools
import math

import jax
import jax.numpy as jnp
from jax import lax
from jax.experimental import pallas as pl
from jax.experimental.pallas import tpu as pltpu
from jax.sharding import PartitionSpec as P

SEQS = 4
KERNEL_VMEM = 6 << 20


def contract_rows(left, right):
    return lax.dot_general(
        left, right, (((1,), (1,)), ((), ())), preferred_element_type=jnp.float32
    )


def local_grads(gate_pre, up_pre, mid_grad, scale_part):
    sigmoid_gate = jax.nn.sigmoid(gate_pre)
    activation = gate_pre * sigmoid_gate
    hidden = activation * up_pre
    scaled = scale_part * mid_grad
    d_up = (scaled * activation).astype(jnp.bfloat16)
    d_gate = (scaled * up_pre * sigmoid_gate * (1.0 + gate_pre * (1.0 - sigmoid_gate))).astype(
        jnp.bfloat16
    )
    return (hidden * mid_grad, d_gate, d_up)


def whole_block(inputs, cotangent, gate_weight, up_weight, down_weight, ia3_scale, seq_ids):
    panel_inputs = lax.all_gather(inputs, "wide", axis=0, tiled=True)
    panel_cotangent = lax.all_gather(cotangent, "wide", axis=0, tiled=True)
    gate_part = jnp.dot(panel_inputs, gate_weight, preferred_element_type=jnp.float32)
    up_part = jnp.dot(panel_inputs, up_weight, preferred_element_type=jnp.float32)
    mid_part = contract_rows(panel_cotangent, down_weight)
    quarter = gate_weight.shape[1] // lax.axis_size("narrow")
    position = lax.axis_index("narrow")
    onehot_full = (seq_ids[None, :] == jnp.arange(SEQS, dtype=jnp.int32)[:, None]).astype(
        jnp.float32
    )
    gate_pre, up_pre, mid_grad = (
        lax.psum_scatter(gate_part, "narrow", scatter_dimension=1, tiled=True),
        lax.psum_scatter(up_part, "narrow", scatter_dimension=1, tiled=True),
        lax.psum_scatter(mid_part, "narrow", scatter_dimension=1, tiled=True),
    )
    scale_part = lax.dynamic_slice_in_dim(ia3_scale, position * quarter, quarter, 0)
    product, d_gate, d_up = local_grads(gate_pre, up_pre, mid_grad, scale_part[None, :])
    example_grads = jnp.dot(onehot_full, product, precision=lax.Precision.HIGHEST)
    whole_gate, whole_up = (
        lax.all_gather(d_gate, "narrow", axis=1, tiled=True),
        lax.all_gather(d_up, "narrow", axis=1, tiled=True),
    )
    squares = lax.psum(jnp.sum(example_grads * example_grads, axis=1), ("wide", "narrow"))
    grad_norms = jnp.sqrt(squares)
    input_grad = lax.psum_scatter(
        contract_rows(whole_gate, gate_weight) + contract_rows(whole_up, up_weight),
        "wide",
        scatter_dimension=0,
        tiled=True,
    ).astype(jnp.bfloat16)
    return (example_grads, grad_norms, input_grad)


def exchange(array, axis, step):
    axes = axis if isinstance(axis, tuple) else (axis,)
    size = math.prod(lax.axis_size(name) for name in axes)
    return lax.ppermute(array, axes, [(i, i ^ step) for i in range(size)])


def held(array):
    return pltpu.with_memory_space_constraint(array, pltpu.VMEM)


def call(body, name, outs, args, spaces=None, scratch=(), out_spaces=None):
    spaces, out_spaces = spaces or {}, out_spaces or {}
    many = isinstance(outs, list)
    out_specs = [
        pl.BlockSpec(memory_space=out_spaces.get(i, pltpu.VMEM)) for i in range(len(outs) if many else 1)
    ]
    return pl.pallas_call(
        body,
        out_shape=outs,
        in_specs=[pl.BlockSpec(memory_space=spaces.get(i, pltpu.VMEM)) for i in range(len(args))],
        out_specs=out_specs if many else out_specs[0],
        scratch_shapes=list(scratch),
        compiler_params=pltpu.CompilerParams(vmem_limit_bytes=KERNEL_VMEM),
        cost_estimate=pl.CostEstimate(flops=1000, bytes_accessed=1000, transcendentals=0),
        name=name,
    )(*args)


def pack_kernel(inputs, cotangent, out, stage):
    share, features = inputs.shape
    half = features // 2
    for i, ref in enumerate((inputs, cotangent)):
        rows = ref[...].astype(jnp.float32)
        for j in range(2):
            stage[(2 * i + j) * share : (2 * i + j + 1) * share, :] = rows[:, j * half : (j + 1) * half]
    for k in range(out.shape[0]):
        out[k] = stage[8 * k : 8 * k + 8, :].astype(jnp.bfloat16)


def fetch_ids(ids_in, marks, ids, sem):
    return pltpu.make_async_copy(ids_in, ids, sem.at[0])


def keys_kernel(share, ids_in, marks, ids, sem):
    fetch_ids(ids_in, marks, ids, sem).wait()
    position, count = lax.axis_index("wide"), ids.shape[1]
    shape = (8, count)
    token, row = (lax.broadcasted_iota(jnp.int32, shape, axis) for axis in (1, 0))
    keys = []
    for base in range(0, WIDE * share, 8):
        at = row + base
        block = sum((at >= share * i).astype(jnp.int32) for i in range(1, WIDE))
        own = token == (position ^ block) * share + (at - block * share)
        key = jnp.sum(jnp.where(own, ids[...].astype(jnp.float32), 0.0), axis=1, keepdims=True)
        keys.append(jnp.broadcast_to(key, (8, 128)))
    keys.append(jnp.zeros((8, marks.shape[1] - 128 * len(keys)), jnp.float32))
    marks[...] = jnp.concatenate(keys, axis=1).astype(jnp.bfloat16)


def relay_kernel(own, far, marks, pair, marked):
    slabs = own.shape[0]
    for target in (pair, marked):
        target[0:slabs] = own[...]
        target[slabs : 2 * slabs] = far[...]
    marked[2 * slabs] = marks[...]


WIDE, NEXT, FAR = 4, 1, 3
GATE, UP, DOWN = range(3)
WHOLE_STRIP = (GATE, UP, DOWN)
CHUNKS = 4


def start_loads(pieces, groups, sources, targets, sem):
    copies = []
    for i, (kind, strip) in enumerate(pieces):
        target = targets[i]
        width = target.shape[0 if kind == DOWN else 1]
        owner = lax.axis_index("narrow") ^ strip
        start = pl.multiple_of((owner * groups + lax.axis_index("groups")) * width, width)
        source = sources[kind]
        source = source.at[pl.ds(start, width), :] if kind == DOWN else source.at[:, pl.ds(start, width)]
        size = target.shape[0] // CHUNKS
        for c in range(CHUNKS):
            span = slice(c * size, (c + 1) * size)
            copies.append(pltpu.make_async_copy(source.at[span, :], target.at[span, :], sem.at[i, c]))
    for copy in copies:
        copy.start()
    return copies


def load_kernel(pieces, groups, *refs):
    count = len(pieces)
    for copy in start_loads(pieces, groups, refs[:3], refs[-1 - count : -1], refs[-1]):
        copy.wait()


def loading(body, pieces, groups, outs, own_copy=None):
    count = len(pieces)

    def kernel(*refs):
        sources, rest = refs[:3], refs[3:]
        at = len(rest) - outs[1] - 1 - count
        targets, sem = rest[at : at + count], rest[at + count + outs[1]]
        own = rest[:at] + rest[at + count : at + count + outs[1]]
        if own_copy is not None:
            own_copy(*own).start()
        copies = start_loads(pieces, groups, sources, targets, sem)

        @pl.when(lax.axis_index("narrow") >= 0)
        def _():
            body(*own)

        for copy in copies:
            copy.wait()

    return kernel


def strip_parts(tokens, cotans, gate, up, down, put):
    tile = 256

    @pl.loop(0, gate.shape[1] // tile)
    def _(i):
        span = pl.ds(pl.multiple_of(i * tile, tile), tile)
        put(GATE, span, jnp.dot(tokens[...], gate[:, span], preferred_element_type=jnp.float32))
        put(UP, span, jnp.dot(tokens[...], up[:, span], preferred_element_type=jnp.float32))
        put(DOWN, span, contract_rows(cotans[...], down[span, :]))


def forward_kernel(tokens, cotans, gate, up, down, *refs):
    out = refs[-1]

    def put(kind, span, part):
        out[kind, :, span] = part.astype(out.dtype)

    strip_parts(tokens, cotans, gate, up, down, put)


def join_kernel(own, arrived, out):
    out[...] = (own[...] + arrived[...]).astype(out.dtype)


def first_kernel(share, marked, beside, other, diagonal, gate, up, down, *refs):
    tokens, cotans, part, rows, cots = refs[-5:]
    slabs, half = 4 * share // 8, rows.shape[1] // 2
    for source, places in (
        (marked, (0, FAR)),
        (beside, (NEXT, FAR ^ NEXT)),
        (other, (WIDE, WIDE + FAR)),
        (diagonal, (WIDE + NEXT, WIDE + (FAR ^ NEXT))),
    ):
        for i, place in enumerate(places):
            packed = source[i * slabs : (i + 1) * slabs].astype(jnp.float32).reshape(4 * share, half)
            for j, target in enumerate((rows, rows, cots, cots)):
                span = slice((j % 2) * half, (j % 2 + 1) * half)
                target[place * share : (place + 1) * share, span] = packed[j * share : (j + 1) * share]
    tokens[...] = rows[...].astype(jnp.bfloat16)
    cotans[...] = cots[...].astype(jnp.bfloat16)
    forward_kernel(tokens, cotans, gate, up, down, part)


def own_strip_kernel(groups, *refs):
    sources, (tokens, cotans, up, down) = refs[:3], refs[3:7]
    out, gate, sem = refs[-3:]
    copies = start_loads([(GATE, 0)], groups, sources, [gate], sem)
    tile = 256

    @pl.loop(0, up.shape[1] // tile)
    def _(i):
        span = pl.ds(pl.multiple_of(i * tile, tile), tile)
        out[UP, :, span] = jnp.dot(tokens[...], up[:, span], preferred_element_type=jnp.float32)
        out[DOWN, :, span] = contract_rows(cotans[...], down[span, :])

    for copy in copies:
        copy.wait()
    out[GATE] = jnp.dot(tokens[...], gate[...], preferred_element_type=jnp.float32)


def middle_kernel(groups, *refs):
    own, arrived, crossed, scale, relayed, other_relayed = refs[:6]
    message, near_gate, near_up, grads, other_grads, stage = refs[-6:]
    _, tokens, width = own.shape
    narrow, group = lax.axis_index("narrow"), lax.axis_index("groups")
    sums = [own[i] + arrived[i].astype(jnp.float32) + crossed[i].astype(jnp.float32) for i in range(3)]
    start = pl.multiple_of((narrow * groups + group) * width, width)
    product, d_gate, d_up = local_grads(*sums, scale[:, pl.ds(start, width)])
    message[0:tokens, :] = d_gate
    message[tokens : 2 * tokens, :] = d_up
    near_gate[0:tokens, :] = d_gate
    near_up[...] = d_up
    half = tokens // groups
    for side, (source, target) in enumerate(((relayed, grads), (other_relayed, other_grads))):
        marks = source[source.shape[0] - 1].astype(jnp.float32)
        seq = jnp.concatenate(
            [
                jnp.concatenate([marks[:, k * 128 : (k + 1) * 128]] * (width // 128), axis=1)
                for k in range(half // 8)
            ],
            axis=0,
        )
        part = product[side * half : (side + 1) * half]
        for e in range(SEQS):
            total = jnp.sum(jnp.where(seq == float(e), part, 0.0), axis=0, keepdims=True)
            target[e : e + 1, :] = total
            stage[side * SEQS + e : side * SEQS + e + 1, :] = total
    every = stage[...]
    squares = jnp.broadcast_to(jnp.sum(every * every, axis=1, keepdims=True), every.shape)
    tail = jnp.concatenate(split_high(squares), axis=0).astype(jnp.bfloat16)
    message[2 * tokens :, :] = tail
    near_gate[tokens:, :] = tail


TILE = 512


def backward_part(grads, gate, up, start):
    d_gate, d_up = grads
    gate_term = contract_rows(gate[start : start + TILE, :], d_gate)
    return gate_term + contract_rows(up[start : start + TILE, :], d_up)


def halves(message):
    tokens = (message.shape[0] - 16) // 2
    return message[0:tokens, :], message[tokens : 2 * tokens, :]


def backward_first_kernel(message, gate, up, total):
    for start in range(0, total.shape[0], TILE):
        total[start : start + TILE, :] = backward_part(halves(message), gate, up, start)


def backward_near_kernel(d_gate, d_up, gate, up, before, total):
    tokens = d_up.shape[0]
    for start in range(0, total.shape[0], TILE):
        part = backward_part((d_gate[0:tokens, :], d_up[...]), gate, up, start)
        total[start : start + TILE, :] = before[start : start + TILE, :] + part


def backward_next_kernel(message, gate, up, before, total):
    for start in range(0, total.shape[0], TILE):
        part = backward_part(halves(message), gate, up, start)
        total[start : start + TILE, :] = before[start : start + TILE, :] + part


def split_high(values):
    high = values.astype(jnp.bfloat16).astype(jnp.float32)
    return high, values - high


def backward_last_kernel(share, message, gate, up, before, *refs):
    others, (own, own_squares), sends, (total, stage) = refs[:3], refs[3:5], refs[5:-2], refs[-2:]
    tokens, features = total.shape
    side = features // 2
    for start in range(0, features, TILE):
        part = before[start : start + TILE, :] + backward_part(halves(message), gate, up, start)
        total[:, start : start + TILE] = part.T
    squares = sum(ref[ref.shape[0] - 16 :, 0:128].astype(jnp.float32) for ref in (message,) + others)
    squares = squares[0:8] + squares[8:16]
    own_squares[...] = squares
    tails = split_high(squares)
    wide = len(sends) + 1
    for i, target in enumerate((own,) + tuple(sends)):
        rows = own if i == 0 else stage
        for group in range(2):
            at = (group * wide + i) * share
            for j in range(2):
                to = (2 * group + j) * share
                rows[to : to + share, :] = total[at : at + share, j * side : (j + 1) * side]
        if i > 0:
            for k in range(target.shape[0]):
                target[k, :, 0:side] = stage[8 * k : 8 * k + 8, :].astype(jnp.bfloat16)
                tail = tails[k] if k < 2 else jnp.zeros_like(squares)
                target[k, :, side:] = tail.astype(jnp.bfloat16)


def combine_kernel(share, own, own_squares, other_grads, *refs):
    arrived, (kept_rows, kept_squares, send, total, stage) = refs[:-5], refs[-5:]
    slabs, side = arrived[0].shape[0], own.shape[1]
    squares = own_squares[...]
    for k in range(slabs):
        rows = own[8 * k : 8 * k + 8, :]
        for ref in arrived:
            values = ref[k].astype(jnp.float32)
            rows = rows + values[:, 0:side]
            if k < 2:
                squares = squares + values[:, side:]
        total[8 * k : 8 * k + 8, :] = rows
    kept_squares[...] = squares
    count = 2 * share
    kept_rows[0:count, :] = total[0:count, :]
    stage[...] = jnp.zeros_like(stage)
    stage[0:count, :] = total[count : 2 * count, :]
    width = other_grads.shape[1]
    for i, rows in enumerate(split_high(other_grads[...])):
        stage[16 + i * SEQS : 16 + (i + 1) * SEQS, 0:width] = rows
    for i, rows in enumerate(split_high(squares)):
        stage[16:24, width + i * 128 : width + (i + 1) * 128] = rows
    for k in range(3):
        send[k] = stage[8 * k : 8 * k + 8, :].astype(jnp.bfloat16)


def last_kernel(share, own, own_squares, arrived, grads, input_grad, example_grads, norms, stage):
    side, width = own.shape[1], grads.shape[1]
    group = lax.axis_index("groups")
    for k in range(2):
        stage[8 * k : 8 * k + 8, :] = own[8 * k : 8 * k + 8, :] + arrived[k].astype(jnp.float32)
    for j in range(2):
        rows = stage[j * share : (j + 1) * share, :]
        input_grad[:, j * side : (j + 1) * side] = rows.astype(jnp.bfloat16)
    tail = arrived[2].astype(jnp.float32)
    other = tail[0:SEQS, 0:width] + tail[SEQS : 2 * SEQS, 0:width]
    example_grads[:, pl.ds(pl.multiple_of(group * width, width), width)] = grads[...]
    example_grads[:, pl.ds(pl.multiple_of((1 - group) * width, width), width)] = other
    squares = tail[:, width : width + 128] + tail[:, width + 128 : width + 256]
    roots = jnp.sqrt(own_squares[0:SEQS, :] + squares[SEQS : 2 * SEQS])
    for e in range(SEQS):
        norms[e] = jnp.max(roots[e : e + 1])


def shared(inputs, cotangent, gate_weight, up_weight, down_weight, ia3_scale, seq_ids):
    groups, wide, strips = lax.axis_size("groups"), lax.axis_size("wide"), lax.axis_size("narrow")
    share, features = inputs.shape
    width = gate_weight.shape[1] // (strips * groups)
    half = share * wide
    tokens = half * groups
    f32, bf16 = jnp.float32, jnp.bfloat16
    slabs, side = 4 * share // 8, features // 2
    weights = tuple(
        pltpu.with_memory_space_constraint(weight, pltpu.HBM)
        for weight in (gate_weight, up_weight, down_weight)
    )
    weight_shapes = [
        pltpu.VMEM((features, width), bf16),
        pltpu.VMEM((features, width), bf16),
        pltpu.VMEM((width, features), bf16),
    ]
    kept = {}

    def load(name, pieces, after=()):
        args = weights + tuple(after)
        arrays = call(
            functools.partial(load_kernel, pieces, groups),
            name,
            [weight_shapes[kind] for kind, _ in pieces],
            args,
            {i: pltpu.HBM if i < 3 else pl.ANY for i in range(len(args))},
            [pltpu.SemaphoreType.DMA((len(pieces), CHUNKS))],
        )
        kept.update(zip(pieces, arrays))

    def call_loading(body, name, pieces, outs, args, scratch=(), spaces=None, own_copy=None):
        made = call(
            loading(body, pieces, groups, (len(outs), len(outs) + len(scratch)), own_copy),
            name,
            [weight_shapes[kind] for kind, _ in pieces] + outs,
            list(weights) + args,
            {**{i: pltpu.HBM for i in range(3)}, **(spaces or {})},
            list(scratch) + [pltpu.SemaphoreType.DMA((len(pieces), CHUNKS))],
        )
        kept.update(zip(pieces, made))
        return made[len(pieces) :]

    def hold(strip, kinds=WHOLE_STRIP):
        return [held(kept[kind, strip]) for kind in kinds]

    packed = call(
        pack_kernel,
        "pack",
        pltpu.VMEM((slabs, 8, features // 2), bf16),
        [pltpu.with_memory_space_constraint(array, pltpu.HBM) for array in (inputs, cotangent)],
        scratch=[pltpu.VMEM((4 * share, features // 2), f32)],
    )
    far = exchange(packed, "wide", FAR)
    (marks,) = call_loading(
        functools.partial(keys_kernel, share),
        "load_a",
        [(kind, 3) for kind in WHOLE_STRIP],
        [pltpu.VMEM((8, side), bf16)],
        [pltpu.with_memory_space_constraint(seq_ids[None, :], pltpu.HBM)],
        [pltpu.VMEM((1, half), jnp.int32), pltpu.SemaphoreType.DMA((1,))],
        {3: pltpu.HBM},
        fetch_ids,
    )
    pair, marked = call(
        relay_kernel,
        "relay",
        [pltpu.VMEM((2 * slabs, 8, side), bf16), pltpu.VMEM((2 * slabs + 1, 8, side), bf16)],
        [packed, far, marks],
    )
    diagonal = exchange(pair, ("groups", "wide"), WIDE + NEXT)
    other_marked = exchange(marked, "groups", 1)
    beside = exchange(pair, "wide", NEXT)
    load("load_b", [(kind, 2) for kind in WHOLE_STRIP], [pair])

    part = pltpu.VMEM((3, tokens, width), f32)
    near_shape = pltpu.VMEM((3, tokens, width), bf16)
    tokens_all, cotans_all, diagonal = call_loading(
        functools.partial(first_kernel, share),
        "forward_3",
        [(GATE, 1), (DOWN, 1)],
        [pltpu.VMEM((tokens, features), bf16)] * 2 + [part],
        [marked, beside, other_marked, diagonal] + hold(3) + hold(2, [GATE]),
        [pltpu.VMEM((tokens, features), f32)] * 2,
    )
    panel = [tokens_all, cotans_all]
    diagonal = exchange(diagonal, "narrow", 1)
    (second,) = call_loading(forward_kernel, "forward_2", [(UP, 1)], [part], panel + hold(2))
    crossing = call(join_kernel, "join", near_shape, [held(second), diagonal])
    crossed = exchange(crossing, "narrow", 2)
    (near,) = call_loading(
        forward_kernel, "forward_1", [(UP, 0), (DOWN, 0)], [near_shape], panel + hold(1) + [held(crossing)]
    )
    near = exchange(near, "narrow", 1)
    own_part, kept[GATE, 0] = call(
        functools.partial(own_strip_kernel, groups),
        "forward_0",
        [part, weight_shapes[GATE]],
        list(weights) + panel + hold(0, [UP, DOWN]),
        {i: pltpu.HBM for i in range(3)},
        [pltpu.SemaphoreType.DMA((1, CHUNKS))],
    )

    resident = [array for s in range(strips) for array in hold(s, [GATE, UP])]
    message, near_gate, near_up, grads, other_grads = call(
        functools.partial(middle_kernel, groups),
        "middle",
        [
            pltpu.VMEM((2 * tokens + 16, width), bf16),
            pltpu.VMEM((tokens + 16, width), bf16),
            pltpu.VMEM((tokens, width), bf16),
            pltpu.VMEM((SEQS, width), f32),
            pltpu.VMEM((SEQS, width), f32),
        ],
        [own_part, near, crossed, ia3_scale[None, :], marked, other_marked] + resident,
        scratch=[pltpu.VMEM((groups * SEQS, width), f32)],
    )

    total = pltpu.VMEM((features, tokens), f32)
    near_gate, near_up = exchange(near_gate, "narrow", 1), exchange(near_up, "narrow", 1)
    message_2 = exchange(message, "narrow", 2)
    sums = call(backward_first_kernel, "backward_0", total, [message] + hold(0, [GATE, UP]))
    sums = call(backward_near_kernel, "backward_1", total, [near_gate, near_up] + hold(1, [GATE, UP]) + [sums])
    message_2, sums = lax.optimization_barrier((message_2, sums))
    message_3 = exchange(message_2, "narrow", 1)
    sums = call(backward_next_kernel, "backward_2", total, [message_2] + hold(2, [GATE, UP]) + [sums])
    block = pltpu.VMEM((slabs, 8, side + 128), bf16)
    own, own_squares, *sends = call(
        functools.partial(backward_last_kernel, share),
        "backward_3",
        [pltpu.VMEM((4 * share, side), f32), pltpu.VMEM((8, 128), f32)] + [block] * (wide - 1),
        [message_3] + hold(3, [GATE, UP]) + [sums, message, near_gate, message_2],
        scratch=[pltpu.VMEM((tokens, features), f32), pltpu.VMEM((4 * share, side), f32)],
    )
    arrived = [exchange(sends[s - 1], "wide", s) for s in reversed(range(1, wide))]
    own, own_squares, send = call(
        functools.partial(combine_kernel, share),
        "combine",
        [pltpu.VMEM((16, side), f32), pltpu.VMEM((8, 128), f32), pltpu.VMEM((3, 8, side), bf16)],
        [own, own_squares, other_grads] + arrived,
        scratch=[pltpu.VMEM((4 * share, side), f32), pltpu.VMEM((24, side), f32)],
    )
    input_grad, example_grads, norms = call(
        functools.partial(last_kernel, share),
        "last",
        [
            jax.ShapeDtypeStruct((share, features), bf16),
            jax.ShapeDtypeStruct((SEQS, groups * width), f32),
            jax.ShapeDtypeStruct((SEQS,), f32),
        ],
        [own, own_squares, exchange(send, "groups", 1), grads],
        scratch=[pltpu.VMEM((16, side), f32)],
        out_spaces={2: pltpu.SMEM},
    )
    return (example_grads, norms, input_grad)


def local(inputs, cotangent, gate_weight, up_weight, down_weight, ia3_scale, seq_ids):
    groups, wide, narrow = lax.axis_size("groups"), lax.axis_size("wide"), lax.axis_size("narrow")
    share, (features, hidden) = inputs.shape[0], gate_weight.shape
    width = hidden // (narrow * groups)
    fits = (
        groups == 2
        and narrow == 4
        and wide == WIDE
        and hidden % (narrow * groups * 256) == 0
        and features >= 2048
        and width <= features // 2 - 256
        and features % (2 * TILE) == 0
        and share in (4, 6)
        and (share * wide) % 8 == 0
        and share * wide <= 64
        and 3 * features * hidden // groups * 2 <= 40 << 20
    )
    plan = shared if fits else whole_block
    return plan(inputs, cotangent, gate_weight, up_weight, down_weight, ia3_scale, seq_ids)


def solution(mesh):
    return jax.shard_map(
        local,
        mesh=mesh,
        in_specs=(
            P(("groups", "wide"), "narrow"),
            P(("groups", "wide"), "narrow"),
            P("narrow", "wide"),
            P("narrow", "wide"),
            P("wide", "narrow"),
            P("wide"),
            P("groups"),
        ),
        out_specs=(P("groups", ("wide", "narrow")), P("groups"), P(("groups", "wide"), "narrow")),
        check_vma=False,
    )
```

```python
import functools
import math

import jax
import jax.numpy as jnp
from jax import lax
from jax.experimental import pallas as pl
from jax.experimental.pallas import tpu as pltpu
from jax.sharding import PartitionSpec as P

SEQS = 4
KERNEL_VMEM = 6 << 20


def contract_rows(left, right):
    return lax.dot_general(
        left, right, (((1,), (1,)), ((), ())), preferred_element_type=jnp.float32
    )


def local_grads(gate_pre, up_pre, mid_grad, scale_part):
    sigmoid_gate = jax.nn.sigmoid(gate_pre)
    activation = gate_pre * sigmoid_gate
    hidden = activation * up_pre
    scaled = scale_part * mid_grad
    d_up = (scaled * activation).astype(jnp.bfloat16)
    d_gate = (scaled * up_pre * sigmoid_gate * (1.0 + gate_pre * (1.0 - sigmoid_gate))).astype(
        jnp.bfloat16
    )
    return (hidden * mid_grad, d_gate, d_up)


def whole_block(inputs, cotangent, gate_weight, up_weight, down_weight, ia3_scale, seq_ids):
    panel_inputs = lax.all_gather(inputs, "wide", axis=0, tiled=True)
    panel_cotangent = lax.all_gather(cotangent, "wide", axis=0, tiled=True)
    gate_part = jnp.dot(panel_inputs, gate_weight, preferred_element_type=jnp.float32)
    up_part = jnp.dot(panel_inputs, up_weight, preferred_element_type=jnp.float32)
    mid_part = contract_rows(panel_cotangent, down_weight)
    quarter = gate_weight.shape[1] // lax.axis_size("narrow")
    position = lax.axis_index("narrow")
    onehot_full = (seq_ids[None, :] == jnp.arange(SEQS, dtype=jnp.int32)[:, None]).astype(
        jnp.float32
    )
    gate_pre, up_pre, mid_grad = (
        lax.psum_scatter(gate_part, "narrow", scatter_dimension=1, tiled=True),
        lax.psum_scatter(up_part, "narrow", scatter_dimension=1, tiled=True),
        lax.psum_scatter(mid_part, "narrow", scatter_dimension=1, tiled=True),
    )
    scale_part = lax.dynamic_slice_in_dim(ia3_scale, position * quarter, quarter, 0)
    product, d_gate, d_up = local_grads(gate_pre, up_pre, mid_grad, scale_part[None, :])
    example_grads = jnp.dot(onehot_full, product, precision=lax.Precision.HIGHEST)
    whole_gate, whole_up = (
        lax.all_gather(d_gate, "narrow", axis=1, tiled=True),
        lax.all_gather(d_up, "narrow", axis=1, tiled=True),
    )
    squares = lax.psum(jnp.sum(example_grads * example_grads, axis=1), ("wide", "narrow"))
    grad_norms = jnp.sqrt(squares)
    input_grad = lax.psum_scatter(
        contract_rows(whole_gate, gate_weight) + contract_rows(whole_up, up_weight),
        "wide",
        scatter_dimension=0,
        tiled=True,
    ).astype(jnp.bfloat16)
    return (example_grads, grad_norms, input_grad)


def exchange(array, axis, step):
    axes = axis if isinstance(axis, tuple) else (axis,)
    size = math.prod(lax.axis_size(name) for name in axes)
    return lax.ppermute(array, axes, [(i, i ^ step) for i in range(size)])


def held(array):
    return pltpu.with_memory_space_constraint(array, pltpu.VMEM)


def call(body, name, outs, args, spaces=None, scratch=(), out_spaces=None):
    spaces, out_spaces = spaces or {}, out_spaces or {}
    many = isinstance(outs, list)
    out_specs = [
        pl.BlockSpec(memory_space=out_spaces.get(i, pltpu.VMEM)) for i in range(len(outs) if many else 1)
    ]
    return pl.pallas_call(
        body,
        out_shape=outs,
        in_specs=[pl.BlockSpec(memory_space=spaces.get(i, pltpu.VMEM)) for i in range(len(args))],
        out_specs=out_specs if many else out_specs[0],
        scratch_shapes=list(scratch),
        compiler_params=pltpu.CompilerParams(vmem_limit_bytes=KERNEL_VMEM),
        cost_estimate=pl.CostEstimate(flops=1000, bytes_accessed=1000, transcendentals=0),
        name=name,
    )(*args)


def pack_kernel(inputs, cotangent, out, stage):
    share, features = inputs.shape
    half = features // 2
    for i, ref in enumerate((inputs, cotangent)):
        rows = ref[...].astype(jnp.float32)
        for j in range(2):
            stage[(2 * i + j) * share : (2 * i + j + 1) * share, :] = rows[:, j * half : (j + 1) * half]
    for k in range(out.shape[0]):
        out[k] = stage[8 * k : 8 * k + 8, :].astype(jnp.bfloat16)


def fetch_ids(ids_in, marks, ids, sem):
    return pltpu.make_async_copy(ids_in, ids, sem.at[0])


def keys_kernel(share, ids_in, marks, ids, sem):
    fetch_ids(ids_in, marks, ids, sem).wait()
    position, count = lax.axis_index("wide"), ids.shape[1]
    shape = (8, count)
    token, row = (lax.broadcasted_iota(jnp.int32, shape, axis) for axis in (1, 0))
    keys = []
    for base in range(0, WIDE * share, 8):
        at = row + base
        block = sum((at >= share * i).astype(jnp.int32) for i in range(1, WIDE))
        own = token == (position ^ block) * share + (at - block * share)
        key = jnp.sum(jnp.where(own, ids[...].astype(jnp.float32), 0.0), axis=1, keepdims=True)
        keys.append(jnp.broadcast_to(key, (8, 128)))
    keys.append(jnp.zeros((8, marks.shape[1] - 128 * len(keys)), jnp.float32))
    marks[...] = jnp.concatenate(keys, axis=1).astype(jnp.bfloat16)


def relay_kernel(own, far, marks, pair, marked):
    slabs = own.shape[0]
    for target in (pair, marked):
        target[0:slabs] = own[...]
        target[slabs : 2 * slabs] = far[...]
    marked[2 * slabs] = marks[...]


WIDE, NEXT, FAR = 4, 1, 2
GATE, UP, DOWN = range(3)
WHOLE_STRIP = (GATE, UP, DOWN)
CHUNKS = 4


def start_loads(pieces, groups, sources, targets, sem):
    copies = []
    for i, (kind, strip) in enumerate(pieces):
        target = targets[i]
        width = target.shape[0 if kind == DOWN else 1]
        owner = lax.axis_index("narrow") ^ strip
        start = pl.multiple_of((owner * groups + lax.axis_index("groups")) * width, width)
        source = sources[kind]
        source = source.at[pl.ds(start, width), :] if kind == DOWN else source.at[:, pl.ds(start, width)]
        size = target.shape[0] // CHUNKS
        for c in range(CHUNKS):
            span = slice(c * size, (c + 1) * size)
            copies.append(pltpu.make_async_copy(source.at[span, :], target.at[span, :], sem.at[i, c]))
    for copy in copies:
        copy.start()
    return copies


def load_kernel(pieces, groups, *refs):
    count = len(pieces)
    for copy in start_loads(pieces, groups, refs[:3], refs[-1 - count : -1], refs[-1]):
        copy.wait()


def loading(body, pieces, groups, outs, own_copy=None):
    count = len(pieces)

    def kernel(*refs):
        sources, rest = refs[:3], refs[3:]
        at = len(rest) - outs[1] - 1 - count
        targets, sem = rest[at : at + count], rest[at + count + outs[1]]
        own = rest[:at] + rest[at + count : at + count + outs[1]]
        if own_copy is not None:
            own_copy(*own).start()
        copies = start_loads(pieces, groups, sources, targets, sem)

        @pl.when(lax.axis_index("narrow") >= 0)
        def _():
            body(*own)

        for copy in copies:
            copy.wait()

    return kernel


def strip_parts(tokens, cotans, gate, up, down, put):
    tile = 256
    for start in range(0, gate.shape[1], tile):
        span = slice(start, start + tile)
        put(GATE, span, jnp.dot(tokens[...], gate[:, span], preferred_element_type=jnp.float32))
        put(UP, span, jnp.dot(tokens[...], up[:, span], preferred_element_type=jnp.float32))
        put(DOWN, span, contract_rows(cotans[...], down[span, :]))


def forward_kernel(tokens, cotans, gate, up, down, *refs):
    out = refs[-1]

    def put(kind, span, part):
        out[kind, :, span] = part.astype(out.dtype)

    strip_parts(tokens, cotans, gate, up, down, put)


def join_kernel(own, arrived, out):
    out[...] = (own[...] + arrived[...]).astype(out.dtype)


def first_kernel(share, marked, beside, other, diagonal, gate, up, down, *refs):
    tokens, cotans, part, rows, cots = refs[-5:]
    slabs, half = 4 * share // 8, rows.shape[1] // 2
    for source, places in (
        (marked, (0, FAR)),
        (beside, (NEXT, FAR ^ NEXT)),
        (other, (WIDE, WIDE + FAR)),
        (diagonal, (WIDE + NEXT, WIDE + (FAR ^ NEXT))),
    ):
        for i, place in enumerate(places):
            packed = source[i * slabs : (i + 1) * slabs].astype(jnp.float32).reshape(4 * share, half)
            for j, target in enumerate((rows, rows, cots, cots)):
                span = slice((j % 2) * half, (j % 2 + 1) * half)
                target[place * share : (place + 1) * share, span] = packed[j * share : (j + 1) * share]
    tokens[...] = rows[...].astype(jnp.bfloat16)
    cotans[...] = cots[...].astype(jnp.bfloat16)
    forward_kernel(tokens, cotans, gate, up, down, part)


def own_strip_kernel(groups, *refs):
    sources, (tokens, cotans, up, down) = refs[:3], refs[3:7]
    out, gate, sem = refs[-3:]
    copies = start_loads([(GATE, 0)], groups, sources, [gate], sem)

    @pl.when(lax.axis_index("narrow") >= 0)
    def _():
        out[UP] = jnp.dot(tokens[...], up[...], preferred_element_type=jnp.float32)
        out[DOWN] = contract_rows(cotans[...], down[...])

    for copy in copies:
        copy.wait()
    out[GATE] = jnp.dot(tokens[...], gate[...], preferred_element_type=jnp.float32)


def middle_kernel(groups, *refs):
    own, arrived, crossed, scale, relayed, other_relayed = refs[:6]
    message, near_gate, near_up, grads, other_grads, stage = refs[-6:]
    _, tokens, width = own.shape
    narrow, group = lax.axis_index("narrow"), lax.axis_index("groups")
    sums = [own[i] + arrived[i].astype(jnp.float32) + crossed[i].astype(jnp.float32) for i in range(3)]
    start = pl.multiple_of((narrow * groups + group) * width, width)
    product, d_gate, d_up = local_grads(*sums, scale[:, pl.ds(start, width)])
    message[0:tokens, :] = d_gate
    message[tokens : 2 * tokens, :] = d_up
    near_gate[0:tokens, :] = d_gate
    near_up[...] = d_up
    half = tokens // groups
    for side, (source, target) in enumerate(((relayed, grads), (other_relayed, other_grads))):
        marks = source[source.shape[0] - 1].astype(jnp.float32)
        seq = jnp.concatenate(
            [
                jnp.concatenate([marks[:, k * 128 : (k + 1) * 128]] * (width // 128), axis=1)
                for k in range(half // 8)
            ],
            axis=0,
        )
        part = product[side * half : (side + 1) * half]
        for e in range(SEQS):
            total = jnp.sum(jnp.where(seq == float(e), part, 0.0), axis=0, keepdims=True)
            target[e : e + 1, :] = total
            stage[side * SEQS + e : side * SEQS + e + 1, :] = total
    every = stage[...]
    squares = jnp.broadcast_to(jnp.sum(every * every, axis=1, keepdims=True), every.shape)
    tail = jnp.concatenate(split_high(squares), axis=0).astype(jnp.bfloat16)
    message[2 * tokens :, :] = tail
    near_gate[tokens:, :] = tail


TILE = 512


def backward_part(grads, gate, up, start):
    d_gate, d_up = grads
    gate_term = contract_rows(gate[start : start + TILE, :], d_gate)
    return gate_term + contract_rows(up[start : start + TILE, :], d_up)


def halves(message):
    tokens = (message.shape[0] - 16) // 2
    return message[0:tokens, :], message[tokens : 2 * tokens, :]


def backward_first_kernel(message, gate, up, total):
    for start in range(0, total.shape[0], TILE):
        total[start : start + TILE, :] = backward_part(halves(message), gate, up, start)


def backward_near_kernel(d_gate, d_up, gate, up, before, total):
    tokens = d_up.shape[0]
    for start in range(0, total.shape[0], TILE):
        part = backward_part((d_gate[0:tokens, :], d_up[...]), gate, up, start)
        total[start : start + TILE, :] = before[start : start + TILE, :] + part


def backward_next_kernel(message, gate, up, before, total):
    for start in range(0, total.shape[0], TILE):
        part = backward_part(halves(message), gate, up, start)
        total[start : start + TILE, :] = before[start : start + TILE, :] + part


def split_high(values):
    high = values.astype(jnp.bfloat16).astype(jnp.float32)
    return high, values - high


def backward_last_kernel(share, message, gate, up, before, *refs):
    others, (own, own_squares), sends, (total, stage) = refs[:3], refs[3:5], refs[5:-2], refs[-2:]
    tokens, features = total.shape
    side = features // 2
    for start in range(0, features, TILE):
        part = before[start : start + TILE, :] + backward_part(halves(message), gate, up, start)
        total[:, start : start + TILE] = part.T
    squares = sum(ref[ref.shape[0] - 16 :, 0:128].astype(jnp.float32) for ref in (message,) + others)
    squares = squares[0:8] + squares[8:16]
    own_squares[...] = squares
    tails = split_high(squares)
    wide = len(sends) + 1
    for i, target in enumerate((own,) + tuple(sends)):
        rows = own if i == 0 else stage
        for group in range(2):
            at = (group * wide + i) * share
            for j in range(2):
                to = (2 * group + j) * share
                rows[to : to + share, :] = total[at : at + share, j * side : (j + 1) * side]
        if i > 0:
            for k in range(target.shape[0]):
                target[k, :, 0:side] = stage[8 * k : 8 * k + 8, :].astype(jnp.bfloat16)
                tail = tails[k] if k < 2 else jnp.zeros_like(squares)
                target[k, :, side:] = tail.astype(jnp.bfloat16)


def combine_kernel(share, own, own_squares, *refs):
    arrived, (kept_rows, send, total, stage) = refs[:-4], refs[-4:]
    slabs, side = arrived[0].shape[0], own.shape[1]
    squares = own_squares[...]
    for k in range(slabs):
        rows = own[8 * k : 8 * k + 8, :]
        for ref in arrived:
            values = ref[k].astype(jnp.float32)
            rows = rows + values[:, 0:side]
            if k < 2:
                squares = squares + values[:, side:]
        total[8 * k : 8 * k + 8, :] = rows
    count = 2 * share
    tails = split_high(squares)
    for group, target in enumerate((kept_rows, stage)):
        target[...] = jnp.zeros_like(target)
        target[0:count, :] = total[group * count : (group + 1) * count, :]
        for i, rows in enumerate(tails):
            for e in range(SEQS):
                row = rows[group * SEQS + e : group * SEQS + e + 1]
                target[count + i : count + i + 1, e * 128 : (e + 1) * 128] = row
    for k in range(2):
        send[k] = stage[8 * k : 8 * k + 8, :].astype(jnp.bfloat16)


def last_kernel(share, own, arrived, grads, other_grads, input_grad, example_grads, norms, stage):
    side, width = own.shape[1], grads.shape[1]
    group = lax.axis_index("groups")
    for k in range(2):
        stage[8 * k : 8 * k + 8, :] = own[8 * k : 8 * k + 8, :] + arrived[k].astype(jnp.float32)
    for j in range(2):
        rows = stage[j * share : (j + 1) * share, :]
        input_grad[:, j * side : (j + 1) * side] = rows.astype(jnp.bfloat16)
    example_grads[:, pl.ds(pl.multiple_of(group * width, width), width)] = grads[...]
    example_grads[:, pl.ds(pl.multiple_of((1 - group) * width, width), width)] = other_grads[...]
    count = 2 * share
    roots = jnp.sqrt(stage[count : count + 1, 0 : SEQS * 128] + stage[count + 1 : count + 2, 0 : SEQS * 128])
    for e in range(SEQS):
        norms[e] = jnp.max(roots[:, e * 128 : (e + 1) * 128])


def shared(inputs, cotangent, gate_weight, up_weight, down_weight, ia3_scale, seq_ids):
    groups, wide, strips = lax.axis_size("groups"), lax.axis_size("wide"), lax.axis_size("narrow")
    share, features = inputs.shape
    width = gate_weight.shape[1] // (strips * groups)
    half = share * wide
    tokens = half * groups
    f32, bf16 = jnp.float32, jnp.bfloat16
    slabs, side = 4 * share // 8, features // 2
    weights = tuple(
        pltpu.with_memory_space_constraint(weight, pltpu.HBM)
        for weight in (gate_weight, up_weight, down_weight)
    )
    weight_shapes = [
        pltpu.VMEM((features, width), bf16),
        pltpu.VMEM((features, width), bf16),
        pltpu.VMEM((width, features), bf16),
    ]
    kept = {}

    def load(name, pieces, after=()):
        args = weights + tuple(after)
        arrays = call(
            functools.partial(load_kernel, pieces, groups),
            name,
            [weight_shapes[kind] for kind, _ in pieces],
            args,
            {i: pltpu.HBM if i < 3 else pl.ANY for i in range(len(args))},
            [pltpu.SemaphoreType.DMA((len(pieces), CHUNKS))],
        )
        kept.update(zip(pieces, arrays))

    def call_loading(body, name, pieces, outs, args, scratch=(), spaces=None, own_copy=None):
        made = call(
            loading(body, pieces, groups, (len(outs), len(outs) + len(scratch)), own_copy),
            name,
            [weight_shapes[kind] for kind, _ in pieces] + outs,
            list(weights) + args,
            {**{i: pltpu.HBM for i in range(3)}, **(spaces or {})},
            list(scratch) + [pltpu.SemaphoreType.DMA((len(pieces), CHUNKS))],
        )
        kept.update(zip(pieces, made))
        return made[len(pieces) :]

    def hold(strip, kinds=WHOLE_STRIP):
        return [held(kept[kind, strip]) for kind in kinds]

    packed = call(
        pack_kernel,
        "pack",
        pltpu.VMEM((slabs, 8, features // 2), bf16),
        [pltpu.with_memory_space_constraint(array, pltpu.HBM) for array in (inputs, cotangent)],
        scratch=[pltpu.VMEM((4 * share, features // 2), f32)],
    )
    far = exchange(packed, "wide", FAR)
    (marks,) = call_loading(
        functools.partial(keys_kernel, share),
        "load_a",
        [(kind, 3) for kind in WHOLE_STRIP],
        [pltpu.VMEM((8, side), bf16)],
        [pltpu.with_memory_space_constraint(seq_ids[None, :], pltpu.HBM)],
        [pltpu.VMEM((1, half), jnp.int32), pltpu.SemaphoreType.DMA((1,))],
        {3: pltpu.HBM},
        fetch_ids,
    )
    pair, marked = call(
        relay_kernel,
        "relay",
        [pltpu.VMEM((2 * slabs, 8, side), bf16), pltpu.VMEM((2 * slabs + 1, 8, side), bf16)],
        [packed, far, marks],
    )
    diagonal = exchange(pair, ("groups", "wide"), WIDE + NEXT)
    other_marked = exchange(marked, "groups", 1)
    beside = exchange(pair, "wide", NEXT)
    load("load_b", [(kind, 2) for kind in WHOLE_STRIP], [pair])

    part = pltpu.VMEM((3, tokens, width), f32)
    near_shape = pltpu.VMEM((3, tokens, width), bf16)
    tokens_all, cotans_all, diagonal = call_loading(
        functools.partial(first_kernel, share),
        "forward_3",
        [(GATE, 1), (DOWN, 1)],
        [pltpu.VMEM((tokens, features), bf16)] * 2 + [part],
        [marked, beside, other_marked, diagonal] + hold(3) + hold(2, [GATE]),
        [pltpu.VMEM((tokens, features), f32)] * 2,
    )
    panel = [tokens_all, cotans_all]
    diagonal = exchange(diagonal, "narrow", 1)
    (second,) = call_loading(forward_kernel, "forward_2", [(UP, 1)], [part], panel + hold(2))
    crossing = call(join_kernel, "join", near_shape, [held(second), diagonal])
    crossed = exchange(crossing, "narrow", 2)
    (near,) = call_loading(
        forward_kernel, "forward_1", [(UP, 0), (DOWN, 0)], [near_shape], panel + hold(1) + [held(crossing)]
    )
    near = exchange(near, "narrow", 1)
    own_part, kept[GATE, 0] = call(
        functools.partial(own_strip_kernel, groups),
        "forward_0",
        [part, weight_shapes[GATE]],
        list(weights) + panel + hold(0, [UP, DOWN]),
        {i: pltpu.HBM for i in range(3)},
        [pltpu.SemaphoreType.DMA((1, CHUNKS))],
    )

    resident = [array for s in range(strips) for array in hold(s, [GATE, UP])]
    message, near_gate, near_up, grads, other_grads = call(
        functools.partial(middle_kernel, groups),
        "middle",
        [
            pltpu.VMEM((2 * tokens + 16, width), bf16),
            pltpu.VMEM((tokens + 16, width), bf16),
            pltpu.VMEM((tokens, width), bf16),
            pltpu.VMEM((SEQS, width), f32),
            pltpu.VMEM((SEQS, width), f32),
        ],
        [own_part, near, crossed, ia3_scale[None, :], marked, other_marked] + resident,
        scratch=[pltpu.VMEM((groups * SEQS, width), f32)],
    )

    total = pltpu.VMEM((features, tokens), f32)
    near_gate, near_up = exchange(near_gate, "narrow", 1), exchange(near_up, "narrow", 1)
    message_2 = exchange(message, "narrow", 2)
    sums = call(backward_first_kernel, "backward_0", total, [message] + hold(0, [GATE, UP]))
    sums = call(backward_near_kernel, "backward_1", total, [near_gate, near_up] + hold(1, [GATE, UP]) + [sums])
    message_2, sums = lax.optimization_barrier((message_2, sums))
    message_3 = exchange(message_2, "narrow", 1)
    sums = call(backward_next_kernel, "backward_2", total, [message_2] + hold(2, [GATE, UP]) + [sums])
    block = pltpu.VMEM((slabs, 8, side + 128), bf16)
    own, own_squares, *sends = call(
        functools.partial(backward_last_kernel, share),
        "backward_3",
        [pltpu.VMEM((4 * share, side), f32), pltpu.VMEM((8, 128), f32)] + [block] * (wide - 1),
        [message_3] + hold(3, [GATE, UP]) + [sums, message, near_gate, message_2],
        scratch=[pltpu.VMEM((tokens, features), f32), pltpu.VMEM((4 * share, side), f32)],
    )
    arrived = [exchange(sends[s - 1], "wide", s) for s in reversed(range(1, wide))]
    other_grads, own_squares = lax.optimization_barrier((other_grads, own_squares))
    own, send = call(
        functools.partial(combine_kernel, share),
        "combine",
        [pltpu.VMEM((16, side), f32), pltpu.VMEM((2, 8, side), bf16)],
        [own, own_squares] + arrived,
        scratch=[pltpu.VMEM((4 * share, side), f32), pltpu.VMEM((16, side), f32)],
    )
    input_grad, example_grads, norms = call(
        functools.partial(last_kernel, share),
        "last",
        [
            jax.ShapeDtypeStruct((share, features), bf16),
            jax.ShapeDtypeStruct((SEQS, groups * width), f32),
            jax.ShapeDtypeStruct((SEQS,), f32),
        ],
        [own, exchange(send, "groups", 1), grads, exchange(other_grads, "groups", 1)],
        scratch=[pltpu.VMEM((16, side), f32)],
        out_spaces={2: pltpu.SMEM},
    )
    return (example_grads, norms, input_grad)


def local(inputs, cotangent, gate_weight, up_weight, down_weight, ia3_scale, seq_ids):
    groups, wide, narrow = lax.axis_size("groups"), lax.axis_size("wide"), lax.axis_size("narrow")
    share, (features, hidden) = inputs.shape[0], gate_weight.shape
    width = hidden // (narrow * groups)
    fits = (
        groups == 2
        and narrow == 4
        and wide == WIDE
        and hidden % (narrow * groups * 256) == 0
        and features >= 2048
        and width <= features // 2 - 256
        and features % (2 * TILE) == 0
        and share in (4, 6)
        and (share * wide) % 8 == 0
        and share * wide <= 64
        and 3 * features * hidden // groups * 2 <= 40 << 20
    )
    plan = shared if fits else whole_block
    return plan(inputs, cotangent, gate_weight, up_weight, down_weight, ia3_scale, seq_ids)


def solution(mesh):
    return jax.shard_map(
        local,
        mesh=mesh,
        in_specs=(
            P(("groups", "wide"), "narrow"),
            P(("groups", "wide"), "narrow"),
            P("narrow", "wide"),
            P("narrow", "wide"),
            P("wide", "narrow"),
            P("wide"),
            P("groups"),
        ),
        out_specs=(P("groups", ("wide", "narrow")), P("groups"), P(("groups", "wide"), "narrow")),
        check_vma=False,
    )
```

```python
import functools
import math

import jax
import jax.numpy as jnp
from jax import lax
from jax.experimental import pallas as pl
from jax.experimental.pallas import tpu as pltpu
from jax.sharding import PartitionSpec as P

SEQS = 4
KERNEL_VMEM = 6 << 20


def contract_rows(left, right):
    return lax.dot_general(
        left, right, (((1,), (1,)), ((), ())), preferred_element_type=jnp.float32
    )


def local_grads(gate_pre, up_pre, mid_grad, scale_part):
    sigmoid_gate = jax.nn.sigmoid(gate_pre)
    activation = gate_pre * sigmoid_gate
    hidden = activation * up_pre
    scaled = scale_part * mid_grad
    d_up = (scaled * activation).astype(jnp.bfloat16)
    d_gate = (scaled * up_pre * sigmoid_gate * (1.0 + gate_pre * (1.0 - sigmoid_gate))).astype(
        jnp.bfloat16
    )
    return (hidden * mid_grad, d_gate, d_up)


def whole_block(inputs, cotangent, gate_weight, up_weight, down_weight, ia3_scale, seq_ids):
    panel_inputs = lax.all_gather(inputs, "wide", axis=0, tiled=True)
    panel_cotangent = lax.all_gather(cotangent, "wide", axis=0, tiled=True)
    gate_part = jnp.dot(panel_inputs, gate_weight, preferred_element_type=jnp.float32)
    up_part = jnp.dot(panel_inputs, up_weight, preferred_element_type=jnp.float32)
    mid_part = contract_rows(panel_cotangent, down_weight)
    quarter = gate_weight.shape[1] // lax.axis_size("narrow")
    position = lax.axis_index("narrow")
    onehot_full = (seq_ids[None, :] == jnp.arange(SEQS, dtype=jnp.int32)[:, None]).astype(
        jnp.float32
    )
    gate_pre, up_pre, mid_grad = (
        lax.psum_scatter(gate_part, "narrow", scatter_dimension=1, tiled=True),
        lax.psum_scatter(up_part, "narrow", scatter_dimension=1, tiled=True),
        lax.psum_scatter(mid_part, "narrow", scatter_dimension=1, tiled=True),
    )
    scale_part = lax.dynamic_slice_in_dim(ia3_scale, position * quarter, quarter, 0)
    product, d_gate, d_up = local_grads(gate_pre, up_pre, mid_grad, scale_part[None, :])
    example_grads = jnp.dot(onehot_full, product, precision=lax.Precision.HIGHEST)
    whole_gate, whole_up = (
        lax.all_gather(d_gate, "narrow", axis=1, tiled=True),
        lax.all_gather(d_up, "narrow", axis=1, tiled=True),
    )
    squares = lax.psum(jnp.sum(example_grads * example_grads, axis=1), ("wide", "narrow"))
    grad_norms = jnp.sqrt(squares)
    input_grad = lax.psum_scatter(
        contract_rows(whole_gate, gate_weight) + contract_rows(whole_up, up_weight),
        "wide",
        scatter_dimension=0,
        tiled=True,
    ).astype(jnp.bfloat16)
    return (example_grads, grad_norms, input_grad)


def exchange(array, axis, step):
    axes = axis if isinstance(axis, tuple) else (axis,)
    size = math.prod(lax.axis_size(name) for name in axes)
    return lax.ppermute(array, axes, [(i, i ^ step) for i in range(size)])


def held(array):
    return pltpu.with_memory_space_constraint(array, pltpu.VMEM)


def call(body, name, outs, args, spaces=None, scratch=(), out_spaces=None):
    spaces, out_spaces = spaces or {}, out_spaces or {}
    many = isinstance(outs, list)
    out_specs = [
        pl.BlockSpec(memory_space=out_spaces.get(i, pltpu.VMEM)) for i in range(len(outs) if many else 1)
    ]
    return pl.pallas_call(
        body,
        out_shape=outs,
        in_specs=[pl.BlockSpec(memory_space=spaces.get(i, pltpu.VMEM)) for i in range(len(args))],
        out_specs=out_specs if many else out_specs[0],
        scratch_shapes=list(scratch),
        compiler_params=pltpu.CompilerParams(vmem_limit_bytes=KERNEL_VMEM),
        cost_estimate=pl.CostEstimate(flops=1000, bytes_accessed=1000, transcendentals=0),
        name=name,
    )(*args)


def pack_kernel(inputs, cotangent, out, stage):
    share, features = inputs.shape
    half = features // 2
    for i, ref in enumerate((inputs, cotangent)):
        rows = ref[...].astype(jnp.float32)
        for j in range(2):
            stage[(2 * i + j) * share : (2 * i + j + 1) * share, :] = rows[:, j * half : (j + 1) * half]
    for k in range(out.shape[0]):
        out[k] = stage[8 * k : 8 * k + 8, :].astype(jnp.bfloat16)


def fetch_ids(ids_in, marks, ids, sem):
    return pltpu.make_async_copy(ids_in, ids, sem.at[0])


def keys_kernel(share, ids_in, marks, ids, sem):
    fetch_ids(ids_in, marks, ids, sem).wait()
    position, count = lax.axis_index("wide"), ids.shape[1]
    shape = (8, count)
    token, row = (lax.broadcasted_iota(jnp.int32, shape, axis) for axis in (1, 0))
    keys = []
    for base in range(0, WIDE * share, 8):
        at = row + base
        block = sum((at >= share * i).astype(jnp.int32) for i in range(1, WIDE))
        own = token == (position ^ block) * share + (at - block * share)
        key = jnp.sum(jnp.where(own, ids[...].astype(jnp.float32), 0.0), axis=1, keepdims=True)
        keys.append(jnp.broadcast_to(key, (8, 128)))
    keys.append(jnp.zeros((8, marks.shape[1] - 128 * len(keys)), jnp.float32))
    marks[...] = jnp.concatenate(keys, axis=1).astype(jnp.bfloat16)


def relay_kernel(own, far, marks, pair, marked):
    slabs = own.shape[0]
    for target in (pair, marked):
        target[0:slabs] = own[...]
        target[slabs : 2 * slabs] = far[...]
    marked[2 * slabs] = marks[...]


WIDE, NEXT, FAR = 4, 1, 2
GATE, UP, DOWN = range(3)
WHOLE_STRIP = (GATE, UP, DOWN)
CHUNKS = 4


def start_loads(pieces, groups, sources, targets, sem):
    copies = []
    for i, (kind, strip) in enumerate(pieces):
        target = targets[i]
        width = target.shape[0 if kind == DOWN else 1]
        owner = lax.axis_index("narrow") ^ strip
        start = pl.multiple_of((owner * groups + lax.axis_index("groups")) * width, width)
        source = sources[kind]
        source = source.at[pl.ds(start, width), :] if kind == DOWN else source.at[:, pl.ds(start, width)]
        size = target.shape[0] // CHUNKS
        for c in range(CHUNKS):
            span = slice(c * size, (c + 1) * size)
            copies.append(pltpu.make_async_copy(source.at[span, :], target.at[span, :], sem.at[i, c]))
    for copy in copies:
        copy.start()
    return copies


def load_kernel(pieces, groups, *refs):
    count = len(pieces)
    for copy in start_loads(pieces, groups, refs[:3], refs[-1 - count : -1], refs[-1]):
        copy.wait()


def loading(body, pieces, groups, outs, own_copy=None):
    count = len(pieces)

    def kernel(*refs):
        sources, rest = refs[:3], refs[3:]
        at = len(rest) - outs[1] - 1 - count
        targets, sem = rest[at : at + count], rest[at + count + outs[1]]
        own = rest[:at] + rest[at + count : at + count + outs[1]]
        if own_copy is not None:
            own_copy(*own).start()
        copies = start_loads(pieces, groups, sources, targets, sem)

        @pl.when(lax.axis_index("narrow") >= 0)
        def _():
            body(*own)

        for copy in copies:
            copy.wait()

    return kernel


def strip_parts(tokens, cotans, gate, up, down, put):
    tile = 256
    for start in range(0, gate.shape[1], tile):
        span = slice(start, start + tile)
        put(GATE, span, jnp.dot(tokens[...], gate[:, span], preferred_element_type=jnp.float32))
        put(UP, span, jnp.dot(tokens[...], up[:, span], preferred_element_type=jnp.float32))
        put(DOWN, span, contract_rows(cotans[...], down[span, :]))


def forward_kernel(tokens, cotans, gate, up, down, *refs):
    out = refs[-1]

    def put(kind, span, part):
        out[kind, :, span] = part.astype(out.dtype)

    strip_parts(tokens, cotans, gate, up, down, put)


def join_kernel(own, arrived, out):
    out[...] = (own[...] + arrived[...]).astype(out.dtype)


def first_kernel(share, marked, beside, other, diagonal, gate, up, down, *refs):
    tokens, cotans, part, rows, cots = refs[-5:]
    slabs, half = 4 * share // 8, rows.shape[1] // 2
    for source, places in (
        (marked, (0, FAR)),
        (beside, (NEXT, FAR ^ NEXT)),
        (other, (WIDE, WIDE + FAR)),
        (diagonal, (WIDE + NEXT, WIDE + (FAR ^ NEXT))),
    ):
        for i, place in enumerate(places):
            packed = source[i * slabs : (i + 1) * slabs].astype(jnp.float32).reshape(4 * share, half)
            for j, target in enumerate((rows, rows, cots, cots)):
                span = slice((j % 2) * half, (j % 2 + 1) * half)
                target[place * share : (place + 1) * share, span] = packed[j * share : (j + 1) * share]
    tokens[...] = rows[...].astype(jnp.bfloat16)
    cotans[...] = cots[...].astype(jnp.bfloat16)
    forward_kernel(tokens, cotans, gate, up, down, part)


def own_strip_kernel(groups, *refs):
    sources, (tokens, cotans, up, down) = refs[:3], refs[3:7]
    out, gate, sem = refs[-3:]
    copies = start_loads([(GATE, 0)], groups, sources, [gate], sem)

    @pl.when(lax.axis_index("narrow") >= 0)
    def _():
        out[UP] = jnp.dot(tokens[...], up[...], preferred_element_type=jnp.float32)
        out[DOWN] = contract_rows(cotans[...], down[...])

    for copy in copies:
        copy.wait()
    out[GATE] = jnp.dot(tokens[...], gate[...], preferred_element_type=jnp.float32)


def middle_kernel(groups, *refs):
    own, arrived, crossed, scale, relayed, other_relayed = refs[:6]
    message, near_gate, near_up, grads, other_grads, stage = refs[-6:]
    _, tokens, width = own.shape
    narrow, group = lax.axis_index("narrow"), lax.axis_index("groups")
    sums = [own[i] + arrived[i].astype(jnp.float32) + crossed[i].astype(jnp.float32) for i in range(3)]
    start = pl.multiple_of((narrow * groups + group) * width, width)
    product, d_gate, d_up = local_grads(*sums, scale[:, pl.ds(start, width)])
    message[0:tokens, :] = d_gate
    message[tokens : 2 * tokens, :] = d_up
    near_gate[0:tokens, :] = d_gate
    near_up[...] = d_up
    half = tokens // groups
    for side, (source, target) in enumerate(((relayed, grads), (other_relayed, other_grads))):
        marks = source[source.shape[0] - 1].astype(jnp.float32)
        seq = jnp.concatenate(
            [
                jnp.concatenate([marks[:, k * 128 : (k + 1) * 128]] * (width // 128), axis=1)
                for k in range(half // 8)
            ],
            axis=0,
        )
        part = product[side * half : (side + 1) * half]
        for e in range(SEQS):
            total = jnp.sum(jnp.where(seq == float(e), part, 0.0), axis=0, keepdims=True)
            target[e : e + 1, :] = total
            stage[side * SEQS + e : side * SEQS + e + 1, :] = total
    every = stage[...]
    squares = jnp.broadcast_to(jnp.sum(every * every, axis=1, keepdims=True), every.shape)
    tail = jnp.concatenate(split_high(squares), axis=0).astype(jnp.bfloat16)
    message[2 * tokens :, :] = tail
    near_gate[tokens:, :] = tail


TILE = 512


def backward_part(grads, gate, up, start):
    d_gate, d_up = grads
    gate_term = contract_rows(gate[start : start + TILE, :], d_gate)
    return gate_term + contract_rows(up[start : start + TILE, :], d_up)


def halves(message):
    tokens = (message.shape[0] - 16) // 2
    return message[0:tokens, :], message[tokens : 2 * tokens, :]


def backward_first_kernel(message, gate, up, total):
    for start in range(0, total.shape[0], TILE):
        total[start : start + TILE, :] = backward_part(halves(message), gate, up, start)


def backward_near_kernel(d_gate, d_up, gate, up, before, total):
    tokens = d_up.shape[0]
    for start in range(0, total.shape[0], TILE):
        part = backward_part((d_gate[0:tokens, :], d_up[...]), gate, up, start)
        total[start : start + TILE, :] = before[start : start + TILE, :] + part


def backward_next_kernel(message, gate, up, before, total):
    for start in range(0, total.shape[0], TILE):
        part = backward_part(halves(message), gate, up, start)
        total[start : start + TILE, :] = before[start : start + TILE, :] + part


def split_high(values):
    high = values.astype(jnp.bfloat16).astype(jnp.float32)
    return high, values - high


def backward_last_kernel(share, message, gate, up, before, *refs):
    others, (own, own_squares), sends, (total, stage) = refs[:3], refs[3:5], refs[5:-2], refs[-2:]
    tokens, features = total.shape
    side = features // 2
    for start in range(0, features, TILE):
        part = before[start : start + TILE, :] + backward_part(halves(message), gate, up, start)
        total[:, start : start + TILE] = part.T
    squares = sum(ref[ref.shape[0] - 16 :, 0:128].astype(jnp.float32) for ref in (message,) + others)
    squares = squares[0:8] + squares[8:16]
    own_squares[...] = squares
    tails = split_high(squares)
    wide = len(sends) + 1
    for i, target in enumerate((own,) + tuple(sends)):
        rows = own if i == 0 else stage
        for group in range(2):
            at = (group * wide + i) * share
            for j in range(2):
                to = (2 * group + j) * share
                rows[to : to + share, :] = total[at : at + share, j * side : (j + 1) * side]
        if i > 0:
            for k in range(target.shape[0]):
                target[k, :, 0:side] = stage[8 * k : 8 * k + 8, :].astype(jnp.bfloat16)
                tail = tails[k] if k < 2 else jnp.zeros_like(squares)
                target[k, :, side:] = tail.astype(jnp.bfloat16)


def combine_kernel(share, own, own_squares, other_grads, *refs):
    arrived, (kept_rows, kept_squares, send, total, stage) = refs[:-5], refs[-5:]
    slabs, side = arrived[0].shape[0], own.shape[1]
    squares = own_squares[...]
    for k in range(slabs):
        rows = own[8 * k : 8 * k + 8, :]
        for ref in arrived:
            values = ref[k].astype(jnp.float32)
            rows = rows + values[:, 0:side]
            if k < 2:
                squares = squares + values[:, side:]
        total[8 * k : 8 * k + 8, :] = rows
    kept_squares[...] = squares
    count = 2 * share
    kept_rows[0:count, :] = total[0:count, :]
    stage[...] = jnp.zeros_like(stage)
    stage[0:count, :] = total[count : 2 * count, :]
    width = other_grads.shape[1]
    for i, rows in enumerate(split_high(other_grads[...])):
        stage[16 + i * SEQS : 16 + (i + 1) * SEQS, 0:width] = rows
    for i, rows in enumerate(split_high(squares)):
        stage[16:24, width + i * 128 : width + (i + 1) * 128] = rows
    for k in range(3):
        send[k] = stage[8 * k : 8 * k + 8, :].astype(jnp.bfloat16)


def last_kernel(share, own, own_squares, arrived, grads, input_grad, example_grads, norms, stage):
    side, width = own.shape[1], grads.shape[1]
    group = lax.axis_index("groups")
    for k in range(2):
        stage[8 * k : 8 * k + 8, :] = own[8 * k : 8 * k + 8, :] + arrived[k].astype(jnp.float32)
    for j in range(2):
        rows = stage[j * share : (j + 1) * share, :]
        input_grad[:, j * side : (j + 1) * side] = rows.astype(jnp.bfloat16)
    tail = arrived[2].astype(jnp.float32)
    other = tail[0:SEQS, 0:width] + tail[SEQS : 2 * SEQS, 0:width]
    example_grads[:, pl.ds(pl.multiple_of(group * width, width), width)] = grads[...]
    example_grads[:, pl.ds(pl.multiple_of((1 - group) * width, width), width)] = other
    squares = tail[:, width : width + 128] + tail[:, width + 128 : width + 256]
    roots = jnp.sqrt(own_squares[0:SEQS, :] + squares[SEQS : 2 * SEQS])
    for e in range(SEQS):
        norms[e] = jnp.max(roots[e : e + 1])


def shared(inputs, cotangent, gate_weight, up_weight, down_weight, ia3_scale, seq_ids):
    groups, wide, strips = lax.axis_size("groups"), lax.axis_size("wide"), lax.axis_size("narrow")
    share, features = inputs.shape
    width = gate_weight.shape[1] // (strips * groups)
    half = share * wide
    tokens = half * groups
    f32, bf16 = jnp.float32, jnp.bfloat16
    slabs, side = 4 * share // 8, features // 2
    weights = tuple(
        pltpu.with_memory_space_constraint(weight, pltpu.HBM)
        for weight in (gate_weight, up_weight, down_weight)
    )
    weight_shapes = [
        pltpu.VMEM((features, width), bf16),
        pltpu.VMEM((features, width), bf16),
        pltpu.VMEM((width, features), bf16),
    ]
    kept = {}

    def load(name, pieces, after=()):
        args = weights + tuple(after)
        arrays = call(
            functools.partial(load_kernel, pieces, groups),
            name,
            [weight_shapes[kind] for kind, _ in pieces],
            args,
            {i: pltpu.HBM if i < 3 else pl.ANY for i in range(len(args))},
            [pltpu.SemaphoreType.DMA((len(pieces), CHUNKS))],
        )
        kept.update(zip(pieces, arrays))

    def call_loading(body, name, pieces, outs, args, scratch=(), spaces=None, own_copy=None):
        made = call(
            loading(body, pieces, groups, (len(outs), len(outs) + len(scratch)), own_copy),
            name,
            [weight_shapes[kind] for kind, _ in pieces] + outs,
            list(weights) + args,
            {**{i: pltpu.HBM for i in range(3)}, **(spaces or {})},
            list(scratch) + [pltpu.SemaphoreType.DMA((len(pieces), CHUNKS))],
        )
        kept.update(zip(pieces, made))
        return made[len(pieces) :]

    def hold(strip, kinds=WHOLE_STRIP):
        return [held(kept[kind, strip]) for kind in kinds]

    packed = call(
        pack_kernel,
        "pack",
        pltpu.VMEM((slabs, 8, features // 2), bf16),
        [pltpu.with_memory_space_constraint(array, pltpu.HBM) for array in (inputs, cotangent)],
        scratch=[pltpu.VMEM((4 * share, features // 2), f32)],
    )
    far = exchange(packed, "wide", FAR)
    (marks,) = call_loading(
        functools.partial(keys_kernel, share),
        "load_a",
        [(kind, 3) for kind in WHOLE_STRIP] + [(GATE, 2)],
        [pltpu.VMEM((8, side), bf16)],
        [pltpu.with_memory_space_constraint(seq_ids[None, :], pltpu.HBM)],
        [pltpu.VMEM((1, half), jnp.int32), pltpu.SemaphoreType.DMA((1,))],
        {3: pltpu.HBM},
        fetch_ids,
    )
    pair, marked = call(
        relay_kernel,
        "relay",
        [pltpu.VMEM((2 * slabs, 8, side), bf16), pltpu.VMEM((2 * slabs + 1, 8, side), bf16)],
        [packed, far, marks],
    )
    diagonal = exchange(pair, ("groups", "wide"), WIDE + NEXT)
    other_marked = exchange(marked, "groups", 1)
    beside = exchange(pair, "wide", NEXT)
    load("load_b", [(UP, 2), (DOWN, 2)], [pair])

    part = pltpu.VMEM((3, tokens, width), f32)
    near_shape = pltpu.VMEM((3, tokens, width), bf16)
    tokens_all, cotans_all, diagonal = call_loading(
        functools.partial(first_kernel, share),
        "forward_3",
        [(GATE, 1), (DOWN, 1)],
        [pltpu.VMEM((tokens, features), bf16)] * 2 + [part],
        [marked, beside, other_marked, diagonal] + hold(3) + hold(2, [UP]),
        [pltpu.VMEM((tokens, features), f32)] * 2,
    )
    panel = [tokens_all, cotans_all]
    diagonal = exchange(diagonal, "narrow", 1)
    (second,) = call_loading(forward_kernel, "forward_2", [(UP, 1)], [part], panel + hold(2))
    crossing = call(join_kernel, "join", near_shape, [held(second), diagonal])
    crossed = exchange(crossing, "narrow", 2)
    (near,) = call_loading(
        forward_kernel, "forward_1", [(UP, 0), (DOWN, 0)], [near_shape], panel + hold(1) + [held(crossing)]
    )
    near = exchange(near, "narrow", 1)
    own_part, kept[GATE, 0] = call(
        functools.partial(own_strip_kernel, groups),
        "forward_0",
        [part, weight_shapes[GATE]],
        list(weights) + panel + hold(0, [UP, DOWN]),
        {i: pltpu.HBM for i in range(3)},
        [pltpu.SemaphoreType.DMA((1, CHUNKS))],
    )

    resident = [array for s in range(strips) for array in hold(s, [GATE, UP])]
    message, near_gate, near_up, grads, other_grads = call(
        functools.partial(middle_kernel, groups),
        "middle",
        [
            pltpu.VMEM((2 * tokens + 16, width), bf16),
            pltpu.VMEM((tokens + 16, width), bf16),
            pltpu.VMEM((tokens, width), bf16),
            pltpu.VMEM((SEQS, width), f32),
            pltpu.VMEM((SEQS, width), f32),
        ],
        [own_part, near, crossed, ia3_scale[None, :], marked, other_marked] + resident,
        scratch=[pltpu.VMEM((groups * SEQS, width), f32)],
    )

    total = pltpu.VMEM((features, tokens), f32)
    near_gate, near_up = exchange(near_gate, "narrow", 1), exchange(near_up, "narrow", 1)
    message_2 = exchange(message, "narrow", 2)
    sums = call(backward_first_kernel, "backward_0", total, [message] + hold(0, [GATE, UP]))
    sums = call(backward_near_kernel, "backward_1", total, [near_gate, near_up] + hold(1, [GATE, UP]) + [sums])
    message_2, sums = lax.optimization_barrier((message_2, sums))
    message_3 = exchange(message_2, "narrow", 1)
    sums = call(backward_next_kernel, "backward_2", total, [message_2] + hold(2, [GATE, UP]) + [sums])
    block = pltpu.VMEM((slabs, 8, side + 128), bf16)
    own, own_squares, *sends = call(
        functools.partial(backward_last_kernel, share),
        "backward_3",
        [pltpu.VMEM((4 * share, side), f32), pltpu.VMEM((8, 128), f32)] + [block] * (wide - 1),
        [message_3] + hold(3, [GATE, UP]) + [sums, message, near_gate, message_2],
        scratch=[pltpu.VMEM((tokens, features), f32), pltpu.VMEM((4 * share, side), f32)],
    )
    arrived = [exchange(sends[s - 1], "wide", s) for s in reversed(range(1, wide))]
    own, own_squares, send = call(
        functools.partial(combine_kernel, share),
        "combine",
        [pltpu.VMEM((16, side), f32), pltpu.VMEM((8, 128), f32), pltpu.VMEM((3, 8, side), bf16)],
        [own, own_squares, other_grads] + arrived,
        scratch=[pltpu.VMEM((4 * share, side), f32), pltpu.VMEM((24, side), f32)],
    )
    input_grad, example_grads, norms = call(
        functools.partial(last_kernel, share),
        "last",
        [
            jax.ShapeDtypeStruct((share, features), bf16),
            jax.ShapeDtypeStruct((SEQS, groups * width), f32),
            jax.ShapeDtypeStruct((SEQS,), f32),
        ],
        [own, own_squares, exchange(send, "groups", 1), grads],
        scratch=[pltpu.VMEM((16, side), f32)],
        out_spaces={2: pltpu.SMEM},
    )
    return (example_grads, norms, input_grad)


def local(inputs, cotangent, gate_weight, up_weight, down_weight, ia3_scale, seq_ids):
    groups, wide, narrow = lax.axis_size("groups"), lax.axis_size("wide"), lax.axis_size("narrow")
    share, (features, hidden) = inputs.shape[0], gate_weight.shape
    width = hidden // (narrow * groups)
    fits = (
        groups == 2
        and narrow == 4
        and wide == WIDE
        and hidden % (narrow * groups * 256) == 0
        and features >= 2048
        and width <= features // 2 - 256
        and features % (2 * TILE) == 0
        and share in (4, 6)
        and (share * wide) % 8 == 0
        and share * wide <= 64
        and 3 * features * hidden // groups * 2 <= 40 << 20
    )
    plan = shared if fits else whole_block
    return plan(inputs, cotangent, gate_weight, up_weight, down_weight, ia3_scale, seq_ids)


def solution(mesh):
    return jax.shard_map(
        local,
        mesh=mesh,
        in_specs=(
            P(("groups", "wide"), "narrow"),
            P(("groups", "wide"), "narrow"),
            P("narrow", "wide"),
            P("narrow", "wide"),
            P("wide", "narrow"),
            P("wide"),
            P("groups"),
        ),
        out_specs=(P("groups", ("wide", "narrow")), P("groups"), P(("groups", "wide"), "narrow")),
        check_vma=False,
    )
```

```python
import functools
import math

import jax
import jax.numpy as jnp
from jax import lax
from jax.experimental import pallas as pl
from jax.experimental.pallas import tpu as pltpu
from jax.sharding import PartitionSpec as P

SEQS = 4
KERNEL_VMEM = 6 << 20


def contract_rows(left, right):
    return lax.dot_general(
        left, right, (((1,), (1,)), ((), ())), preferred_element_type=jnp.float32
    )


def local_grads(gate_pre, up_pre, mid_grad, scale_part):
    sigmoid_gate = jax.nn.sigmoid(gate_pre)
    activation = gate_pre * sigmoid_gate
    hidden = activation * up_pre
    scaled = scale_part * mid_grad
    d_up = (scaled * activation).astype(jnp.bfloat16)
    d_gate = (scaled * up_pre * sigmoid_gate * (1.0 + gate_pre * (1.0 - sigmoid_gate))).astype(
        jnp.bfloat16
    )
    return (hidden * mid_grad, d_gate, d_up)


def whole_block(inputs, cotangent, gate_weight, up_weight, down_weight, ia3_scale, seq_ids):
    panel_inputs = lax.all_gather(inputs, "wide", axis=0, tiled=True)
    panel_cotangent = lax.all_gather(cotangent, "wide", axis=0, tiled=True)
    gate_part = jnp.dot(panel_inputs, gate_weight, preferred_element_type=jnp.float32)
    up_part = jnp.dot(panel_inputs, up_weight, preferred_element_type=jnp.float32)
    mid_part = contract_rows(panel_cotangent, down_weight)
    quarter = gate_weight.shape[1] // lax.axis_size("narrow")
    position = lax.axis_index("narrow")
    onehot_full = (seq_ids[None, :] == jnp.arange(SEQS, dtype=jnp.int32)[:, None]).astype(
        jnp.float32
    )
    gate_pre, up_pre, mid_grad = (
        lax.psum_scatter(gate_part, "narrow", scatter_dimension=1, tiled=True),
        lax.psum_scatter(up_part, "narrow", scatter_dimension=1, tiled=True),
        lax.psum_scatter(mid_part, "narrow", scatter_dimension=1, tiled=True),
    )
    scale_part = lax.dynamic_slice_in_dim(ia3_scale, position * quarter, quarter, 0)
    product, d_gate, d_up = local_grads(gate_pre, up_pre, mid_grad, scale_part[None, :])
    example_grads = jnp.dot(onehot_full, product, precision=lax.Precision.HIGHEST)
    whole_gate, whole_up = (
        lax.all_gather(d_gate, "narrow", axis=1, tiled=True),
        lax.all_gather(d_up, "narrow", axis=1, tiled=True),
    )
    squares = lax.psum(jnp.sum(example_grads * example_grads, axis=1), ("wide", "narrow"))
    grad_norms = jnp.sqrt(squares)
    input_grad = lax.psum_scatter(
        contract_rows(whole_gate, gate_weight) + contract_rows(whole_up, up_weight),
        "wide",
        scatter_dimension=0,
        tiled=True,
    ).astype(jnp.bfloat16)
    return (example_grads, grad_norms, input_grad)


def exchange(array, axis, step):
    axes = axis if isinstance(axis, tuple) else (axis,)
    size = math.prod(lax.axis_size(name) for name in axes)
    return lax.ppermute(array, axes, [(i, i ^ step) for i in range(size)])


def held(array):
    return pltpu.with_memory_space_constraint(array, pltpu.VMEM)


def call(body, name, outs, args, spaces=None, scratch=(), out_spaces=None):
    spaces, out_spaces = spaces or {}, out_spaces or {}
    many = isinstance(outs, list)
    out_specs = [
        pl.BlockSpec(memory_space=out_spaces.get(i, pltpu.VMEM)) for i in range(len(outs) if many else 1)
    ]
    return pl.pallas_call(
        body,
        out_shape=outs,
        in_specs=[pl.BlockSpec(memory_space=spaces.get(i, pltpu.VMEM)) for i in range(len(args))],
        out_specs=out_specs if many else out_specs[0],
        scratch_shapes=list(scratch),
        compiler_params=pltpu.CompilerParams(vmem_limit_bytes=KERNEL_VMEM),
        cost_estimate=pl.CostEstimate(flops=1000, bytes_accessed=1000, transcendentals=0),
        name=name,
    )(*args)


def pack_kernel(inputs, cotangent, out, stage):
    share, features = inputs.shape
    half = features // 2
    for i, ref in enumerate((inputs, cotangent)):
        rows = ref[...].astype(jnp.float32)
        for j in range(2):
            stage[(2 * i + j) * share : (2 * i + j + 1) * share, :] = rows[:, j * half : (j + 1) * half]
    for k in range(out.shape[0]):
        out[k] = stage[8 * k : 8 * k + 8, :].astype(jnp.bfloat16)


def fetch_ids(ids_in, marks, ids, sem):
    return pltpu.make_async_copy(ids_in, ids, sem.at[0])


def keys_kernel(share, ids_in, marks, ids, sem):
    fetch_ids(ids_in, marks, ids, sem).wait()
    position, count = lax.axis_index("wide"), ids.shape[1]
    shape = (8, count)
    token, row = (lax.broadcasted_iota(jnp.int32, shape, axis) for axis in (1, 0))
    keys = []
    for base in range(0, WIDE * share, 8):
        at = row + base
        block = sum((at >= share * i).astype(jnp.int32) for i in range(1, WIDE))
        own = token == (position ^ block) * share + (at - block * share)
        key = jnp.sum(jnp.where(own, ids[...].astype(jnp.float32), 0.0), axis=1, keepdims=True)
        keys.append(jnp.broadcast_to(key, (8, 128)))
    keys.append(jnp.zeros((8, marks.shape[1] - 128 * len(keys)), jnp.float32))
    marks[...] = jnp.concatenate(keys, axis=1).astype(jnp.bfloat16)


def relay_kernel(own, far, marks, pair, marked):
    slabs = own.shape[0]
    for target in (pair, marked):
        target[0:slabs] = own[...]
        target[slabs : 2 * slabs] = far[...]
    marked[2 * slabs] = marks[...]


WIDE, NEXT, FAR = 4, 1, 2
GATE, UP, DOWN = range(3)
WHOLE_STRIP = (GATE, UP, DOWN)
CHUNKS = 4


def start_loads(pieces, groups, sources, targets, sem):
    copies = []
    for i, (kind, strip) in enumerate(pieces):
        target = targets[i]
        width = target.shape[0 if kind == DOWN else 1]
        owner = lax.axis_index("narrow") ^ strip
        start = pl.multiple_of((owner * groups + lax.axis_index("groups")) * width, width)
        source = sources[kind]
        source = source.at[pl.ds(start, width), :] if kind == DOWN else source.at[:, pl.ds(start, width)]
        size = target.shape[0] // CHUNKS
        for c in range(CHUNKS):
            span = slice(c * size, (c + 1) * size)
            copies.append(pltpu.make_async_copy(source.at[span, :], target.at[span, :], sem.at[i, c]))
    for copy in copies:
        copy.start()
    return copies


def load_kernel(pieces, groups, *refs):
    count = len(pieces)
    for copy in start_loads(pieces, groups, refs[:3], refs[-1 - count : -1], refs[-1]):
        copy.wait()


def loading(body, pieces, groups, outs, own_copy=None):
    count = len(pieces)

    def kernel(*refs):
        sources, rest = refs[:3], refs[3:]
        at = len(rest) - outs[1] - 1 - count
        targets, sem = rest[at : at + count], rest[at + count + outs[1]]
        own = rest[:at] + rest[at + count : at + count + outs[1]]
        if own_copy is not None:
            own_copy(*own).start()
        copies = start_loads(pieces, groups, sources, targets, sem)

        @pl.when(lax.axis_index("narrow") >= 0)
        def _():
            body(*own)

        for copy in copies:
            copy.wait()

    return kernel


def strip_parts(tokens, cotans, gate, up, down, put):
    tile = 256
    for start in range(0, gate.shape[1], tile):
        span = slice(start, start + tile)
        put(GATE, span, jnp.dot(tokens[...], gate[:, span], preferred_element_type=jnp.float32))
        put(UP, span, jnp.dot(tokens[...], up[:, span], preferred_element_type=jnp.float32))
        put(DOWN, span, contract_rows(cotans[...], down[span, :]))


def forward_kernel(tokens, cotans, gate, up, down, *refs):
    out = refs[-1]

    def put(kind, span, part):
        out[kind, :, span] = part.astype(out.dtype)

    strip_parts(tokens, cotans, gate, up, down, put)


def join_kernel(own, arrived, out):
    out[...] = (own[...] + arrived[...]).astype(out.dtype)


def first_kernel(share, marked, beside, other, diagonal, gate, up, down, *refs):
    tokens, cotans, part, rows, cots = refs[-5:]
    slabs, half = 4 * share // 8, rows.shape[1] // 2
    for source, places in (
        (marked, (0, FAR)),
        (beside, (NEXT, FAR ^ NEXT)),
        (other, (WIDE, WIDE + FAR)),
        (diagonal, (WIDE + NEXT, WIDE + (FAR ^ NEXT))),
    ):
        for i, place in enumerate(places):
            packed = source[i * slabs : (i + 1) * slabs].astype(jnp.float32).reshape(4 * share, half)
            for j, target in enumerate((rows, rows, cots, cots)):
                span = slice((j % 2) * half, (j % 2 + 1) * half)
                target[place * share : (place + 1) * share, span] = packed[j * share : (j + 1) * share]
    tokens[...] = rows[...].astype(jnp.bfloat16)
    cotans[...] = cots[...].astype(jnp.bfloat16)
    forward_kernel(tokens, cotans, gate, up, down, part)


def own_strip_kernel(groups, *refs):
    sources, (tokens, cotans, up, down) = refs[:3], refs[3:7]
    out, gate, sem = refs[-3:]
    copies = start_loads([(GATE, 0)], groups, sources, [gate], sem)

    @pl.when(lax.axis_index("narrow") >= 0)
    def _():
        out[UP] = jnp.dot(tokens[...], up[...], preferred_element_type=jnp.float32)
        out[DOWN] = contract_rows(cotans[...], down[...])

    for copy in copies:
        copy.wait()
    out[GATE] = jnp.dot(tokens[...], gate[...], preferred_element_type=jnp.float32)


def middle_kernel(groups, *refs):
    own, arrived, crossed, scale, relayed, other_relayed = refs[:6]
    message, near_gate, near_up, grads, other_grads, stage = refs[-6:]
    _, tokens, width = own.shape
    narrow, group = lax.axis_index("narrow"), lax.axis_index("groups")
    sums = [own[i] + arrived[i].astype(jnp.float32) + crossed[i].astype(jnp.float32) for i in range(3)]
    start = pl.multiple_of((narrow * groups + group) * width, width)
    product, d_gate, d_up = local_grads(*sums, scale[:, pl.ds(start, width)])
    message[0:tokens, :] = d_gate
    message[tokens : 2 * tokens, :] = d_up
    near_gate[0:tokens, :] = d_gate
    near_up[...] = d_up
    half = tokens // groups
    for side, (source, target) in enumerate(((relayed, grads), (other_relayed, other_grads))):
        marks = source[source.shape[0] - 1].astype(jnp.float32)
        seq = jnp.concatenate(
            [
                jnp.concatenate([marks[:, k * 128 : (k + 1) * 128]] * (width // 128), axis=1)
                for k in range(half // 8)
            ],
            axis=0,
        )
        part = product[side * half : (side + 1) * half]
        for e in range(SEQS):
            total = jnp.sum(jnp.where(seq == float(e), part, 0.0), axis=0, keepdims=True)
            target[e : e + 1, :] = total
            stage[side * SEQS + e : side * SEQS + e + 1, :] = total
    every = stage[...]
    squares = jnp.broadcast_to(jnp.sum(every * every, axis=1, keepdims=True), every.shape)
    tail = jnp.concatenate(split_high(squares), axis=0).astype(jnp.bfloat16)
    message[2 * tokens :, :] = tail
    near_gate[tokens:, :] = tail


TILE = 512


def backward_part(grads, gate, up, start):
    d_gate, d_up = grads
    gate_term = contract_rows(gate[start : start + TILE, :], d_gate)
    return gate_term + contract_rows(up[start : start + TILE, :], d_up)


def halves(message):
    tokens = (message.shape[0] - 16) // 2
    return message[0:tokens, :], message[tokens : 2 * tokens, :]


def backward_first_kernel(message, gate, up, total):
    for start in range(0, total.shape[0], TILE):
        total[start : start + TILE, :] = backward_part(halves(message), gate, up, start)


def backward_near_kernel(d_gate, d_up, gate, up, before, total):
    tokens = d_up.shape[0]
    for start in range(0, total.shape[0], TILE):
        part = backward_part((d_gate[0:tokens, :], d_up[...]), gate, up, start)
        total[start : start + TILE, :] = before[start : start + TILE, :] + part


def backward_next_kernel(message, gate, up, before, total):
    for start in range(0, total.shape[0], TILE):
        part = backward_part(halves(message), gate, up, start)
        total[start : start + TILE, :] = before[start : start + TILE, :] + part


def split_high(values):
    high = values.astype(jnp.bfloat16).astype(jnp.float32)
    return high, values - high


def backward_last_kernel(share, message, gate, up, before, *refs):
    others, other_grads, (own, own_squares), sends, (total, stage) = refs[:3], refs[3], refs[4:6], refs[6:9], refs[9:]
    tokens, features = total.shape
    side = features // 2
    for start in range(0, features, TILE):
        part = before[start : start + TILE, :] + backward_part(halves(message), gate, up, start)
        total[:, start : start + TILE] = part.T
    squares = sum(ref[ref.shape[0] - 16 :, 0:128].astype(jnp.float32) for ref in (message,) + others)
    squares = squares[0:8] + squares[8:16]
    own_squares[...] = squares
    tails = split_high(squares)
    slabs = 4 * share // 8
    for target, group, nearby in zip((own,) + tuple(sends), (0, 0, 1, 1), (0, NEXT, 0, NEXT)):
        rows = own if target is own else stage
        for i, place in enumerate((nearby, nearby ^ FAR)):
            at = (group * WIDE + place) * share
            for j in range(2):
                to = (2 * i + j) * share
                rows[to : to + share, :] = total[at : at + share, j * side : (j + 1) * side]
        if target is not own:
            for k in range(slabs):
                target[k, :, 0:side] = stage[8 * k : 8 * k + 8, :].astype(jnp.bfloat16)
                if target.shape[2] > side:
                    tail = tails[k] if k < 2 else jnp.zeros_like(squares)
                    target[k, :, side:] = tail.astype(jnp.bfloat16)
    width = other_grads.shape[1]
    stage[0:8, :] = jnp.zeros((8, side), jnp.float32)
    for i, rows in enumerate(split_high(other_grads[...])):
        stage[i * SEQS : (i + 1) * SEQS, 0:width] = rows
    for i, rows in enumerate(tails):
        stage[0:8, width + i * 128 : width + (i + 1) * 128] = rows
    sends[1][slabs] = stage[0:8, :].astype(jnp.bfloat16)


def combine_kernel(share, own, own_squares, diagonal, across, beside, *refs):
    kept_rows, other_grads, send, total, stage = refs
    slabs, side = beside.shape[0], own.shape[1]
    width = other_grads.shape[1]
    for k in range(slabs):
        rows = own[8 * k : 8 * k + 8, :] + across[k].astype(jnp.float32)
        for ref in (beside, diagonal):
            rows = rows + ref[k, :, 0:side].astype(jnp.float32)
        total[8 * k : 8 * k + 8, :] = rows
    tail = across[slabs].astype(jnp.float32)
    other_grads[...] = tail[0:SEQS, 0:width] + tail[SEQS : 2 * SEQS, 0:width]
    same, turned = own_squares[...], tail[:, width : width + 128] + tail[:, width + 128 : width + 256]
    for k in range(2):
        same = same + beside[k, :, side:].astype(jnp.float32)
        turned = turned + diagonal[k, :, side:].astype(jnp.float32)
    squares = same[0:SEQS] + turned[SEQS : 2 * SEQS]
    count = 2 * share
    kept_rows[...] = jnp.zeros_like(kept_rows)
    stage[...] = jnp.zeros_like(stage)
    kept_rows[0:count, :] = total[0:count, :]
    stage[0:count, :] = total[count : 2 * count, :]
    high, low = split_high(squares)
    for e in range(SEQS):
        span = slice(e * 128, (e + 1) * 128)
        for ref in (kept_rows, stage):
            ref[count : count + 1, span] = high[e : e + 1]
            ref[count + 1 : count + 2, span] = low[e : e + 1]
    for k in range(2):
        send[k] = stage[8 * k : 8 * k + 8, :].astype(jnp.bfloat16)


def last_kernel(share, own, arrived, grads, other_grads, input_grad, example_grads, norms, stage):
    side, width = own.shape[1], grads.shape[1]
    group = lax.axis_index("groups")
    for k in range(2):
        stage[8 * k : 8 * k + 8, :] = own[8 * k : 8 * k + 8, :] + arrived[k].astype(jnp.float32)
    for j in range(2):
        rows = stage[j * share : (j + 1) * share, :]
        input_grad[:, j * side : (j + 1) * side] = rows.astype(jnp.bfloat16)
    example_grads[:, pl.ds(pl.multiple_of(group * width, width), width)] = grads[...]
    example_grads[:, pl.ds(pl.multiple_of((1 - group) * width, width), width)] = other_grads[...]
    count = 2 * share
    squares = stage[count : count + 1, 0 : SEQS * 128] + stage[count + 1 : count + 2, 0 : SEQS * 128]
    roots = jnp.sqrt(squares)
    for e in range(SEQS):
        norms[e] = jnp.max(roots[:, e * 128 : (e + 1) * 128])


def shared(inputs, cotangent, gate_weight, up_weight, down_weight, ia3_scale, seq_ids):
    groups, wide, strips = lax.axis_size("groups"), lax.axis_size("wide"), lax.axis_size("narrow")
    share, features = inputs.shape
    width = gate_weight.shape[1] // (strips * groups)
    half = share * wide
    tokens = half * groups
    f32, bf16 = jnp.float32, jnp.bfloat16
    slabs, side = 4 * share // 8, features // 2
    weights = tuple(
        pltpu.with_memory_space_constraint(weight, pltpu.HBM)
        for weight in (gate_weight, up_weight, down_weight)
    )
    weight_shapes = [
        pltpu.VMEM((features, width), bf16),
        pltpu.VMEM((features, width), bf16),
        pltpu.VMEM((width, features), bf16),
    ]
    kept = {}

    def load(name, pieces, after=()):
        args = weights + tuple(after)
        arrays = call(
            functools.partial(load_kernel, pieces, groups),
            name,
            [weight_shapes[kind] for kind, _ in pieces],
            args,
            {i: pltpu.HBM if i < 3 else pl.ANY for i in range(len(args))},
            [pltpu.SemaphoreType.DMA((len(pieces), CHUNKS))],
        )
        kept.update(zip(pieces, arrays))

    def call_loading(body, name, pieces, outs, args, scratch=(), spaces=None, own_copy=None):
        made = call(
            loading(body, pieces, groups, (len(outs), len(outs) + len(scratch)), own_copy),
            name,
            [weight_shapes[kind] for kind, _ in pieces] + outs,
            list(weights) + args,
            {**{i: pltpu.HBM for i in range(3)}, **(spaces or {})},
            list(scratch) + [pltpu.SemaphoreType.DMA((len(pieces), CHUNKS))],
        )
        kept.update(zip(pieces, made))
        return made[len(pieces) :]

    def hold(strip, kinds=WHOLE_STRIP):
        return [held(kept[kind, strip]) for kind in kinds]

    packed = call(
        pack_kernel,
        "pack",
        pltpu.VMEM((slabs, 8, features // 2), bf16),
        [pltpu.with_memory_space_constraint(array, pltpu.HBM) for array in (inputs, cotangent)],
        scratch=[pltpu.VMEM((4 * share, features // 2), f32)],
    )
    far = exchange(packed, "wide", FAR)
    (marks,) = call_loading(
        functools.partial(keys_kernel, share),
        "load_a",
        [(kind, 3) for kind in WHOLE_STRIP],
        [pltpu.VMEM((8, side), bf16)],
        [pltpu.with_memory_space_constraint(seq_ids[None, :], pltpu.HBM)],
        [pltpu.VMEM((1, half), jnp.int32), pltpu.SemaphoreType.DMA((1,))],
        {3: pltpu.HBM},
        fetch_ids,
    )
    pair, marked = call(
        relay_kernel,
        "relay",
        [pltpu.VMEM((2 * slabs, 8, side), bf16), pltpu.VMEM((2 * slabs + 1, 8, side), bf16)],
        [packed, far, marks],
    )
    diagonal = exchange(pair, ("groups", "wide"), WIDE + NEXT)
    other_marked = exchange(marked, "groups", 1)
    beside = exchange(pair, "wide", NEXT)
    load("load_b", [(kind, 2) for kind in WHOLE_STRIP], [pair])

    part = pltpu.VMEM((3, tokens, width), f32)
    near_shape = pltpu.VMEM((3, tokens, width), bf16)
    tokens_all, cotans_all, diagonal = call_loading(
        functools.partial(first_kernel, share),
        "forward_3",
        [(GATE, 1), (DOWN, 1)],
        [pltpu.VMEM((tokens, features), bf16)] * 2 + [part],
        [marked, beside, other_marked, diagonal] + hold(3) + hold(2, [GATE]),
        [pltpu.VMEM((tokens, features), f32)] * 2,
    )
    panel = [tokens_all, cotans_all]
    diagonal = exchange(diagonal, "narrow", 1)
    (second,) = call_loading(forward_kernel, "forward_2", [(UP, 1)], [part], panel + hold(2))
    crossing = call(join_kernel, "join", near_shape, [held(second), diagonal])
    crossed = exchange(crossing, "narrow", 2)
    (near,) = call_loading(
        forward_kernel, "forward_1", [(UP, 0), (DOWN, 0)], [near_shape], panel + hold(1) + [held(crossing)]
    )
    near = exchange(near, "narrow", 1)
    own_part, kept[GATE, 0] = call(
        functools.partial(own_strip_kernel, groups),
        "forward_0",
        [part, weight_shapes[GATE]],
        list(weights) + panel + hold(0, [UP, DOWN]),
        {i: pltpu.HBM for i in range(3)},
        [pltpu.SemaphoreType.DMA((1, CHUNKS))],
    )

    resident = [array for s in range(strips) for array in hold(s, [GATE, UP])]
    message, near_gate, near_up, grads, other_grads = call(
        functools.partial(middle_kernel, groups),
        "middle",
        [
            pltpu.VMEM((2 * tokens + 16, width), bf16),
            pltpu.VMEM((tokens + 16, width), bf16),
            pltpu.VMEM((tokens, width), bf16),
            pltpu.VMEM((SEQS, width), f32),
            pltpu.VMEM((SEQS, width), f32),
        ],
        [own_part, near, crossed, ia3_scale[None, :], marked, other_marked] + resident,
        scratch=[pltpu.VMEM((groups * SEQS, width), f32)],
    )

    total = pltpu.VMEM((features, tokens), f32)
    near_gate, near_up = exchange(near_gate, "narrow", 1), exchange(near_up, "narrow", 1)
    message_2 = exchange(message, "narrow", 2)
    sums = call(backward_first_kernel, "backward_0", total, [message] + hold(0, [GATE, UP]))
    sums = call(backward_near_kernel, "backward_1", total, [near_gate, near_up] + hold(1, [GATE, UP]) + [sums])
    message_2, sums = lax.optimization_barrier((message_2, sums))
    message_3 = exchange(message_2, "narrow", 1)
    sums = call(backward_next_kernel, "backward_2", total, [message_2] + hold(2, [GATE, UP]) + [sums])
    block = pltpu.VMEM((slabs, 8, side + 128), bf16)
    own, own_squares, *sends = call(
        functools.partial(backward_last_kernel, share),
        "backward_3",
        [
            pltpu.VMEM((4 * share, side), f32),
            pltpu.VMEM((8, 128), f32),
            block,
            pltpu.VMEM((slabs + 1, 8, side), bf16),
            block,
        ],
        [message_3] + hold(3, [GATE, UP]) + [sums, message, near_gate, message_2, other_grads],
        scratch=[pltpu.VMEM((tokens, features), f32), pltpu.VMEM((4 * share, side), f32)],
    )
    across = exchange(sends[1], "groups", 1)
    beside = exchange(sends[0], "wide", NEXT)
    diagonal = exchange(sends[2], ("groups", "wide"), WIDE + NEXT)
    own, other_grads, send = call(
        functools.partial(combine_kernel, share),
        "combine",
        [pltpu.VMEM((16, side), f32), pltpu.VMEM((SEQS, width), f32), pltpu.VMEM((2, 8, side), bf16)],
        [own, own_squares, diagonal, across, beside],
        scratch=[pltpu.VMEM((4 * share, side), f32), pltpu.VMEM((16, side), f32)],
    )
    input_grad, example_grads, norms = call(
        functools.partial(last_kernel, share),
        "last",
        [
            jax.ShapeDtypeStruct((share, features), bf16),
            jax.ShapeDtypeStruct((SEQS, groups * width), f32),
            jax.ShapeDtypeStruct((SEQS,), f32),
        ],
        [own, exchange(send, "wide", FAR), grads, other_grads],
        scratch=[pltpu.VMEM((16, side), f32)],
        out_spaces={2: pltpu.SMEM},
    )
    return (example_grads, norms, input_grad)


def local(inputs, cotangent, gate_weight, up_weight, down_weight, ia3_scale, seq_ids):
    groups, wide, narrow = lax.axis_size("groups"), lax.axis_size("wide"), lax.axis_size("narrow")
    share, (features, hidden) = inputs.shape[0], gate_weight.shape
    width = hidden // (narrow * groups)
    fits = (
        groups == 2
        and narrow == 4
        and wide == WIDE
        and hidden % (narrow * groups * 256) == 0
        and features >= 2048
        and width <= features // 2 - 256
        and features % (2 * TILE) == 0
        and share in (4, 6)
        and (share * wide) % 8 == 0
        and share * wide <= 64
        and 3 * features * hidden // groups * 2 <= 40 << 20
    )
    plan = shared if fits else whole_block
    return plan(inputs, cotangent, gate_weight, up_weight, down_weight, ia3_scale, seq_ids)


def solution(mesh):
    return jax.shard_map(
        local,
        mesh=mesh,
        in_specs=(
            P(("groups", "wide"), "narrow"),
            P(("groups", "wide"), "narrow"),
            P("narrow", "wide"),
            P("narrow", "wide"),
            P("wide", "narrow"),
            P("wide"),
            P("groups"),
        ),
        out_specs=(P("groups", ("wide", "narrow")), P("groups"), P(("groups", "wide"), "narrow")),
        check_vma=False,
    )
```

```python
import functools
import math

import jax
import jax.numpy as jnp
from jax import lax
from jax.experimental import pallas as pl
from jax.experimental.pallas import tpu as pltpu
from jax.sharding import PartitionSpec as P

SEQS = 4
KERNEL_VMEM = 6 << 20


def contract_rows(left, right):
    return lax.dot_general(
        left, right, (((1,), (1,)), ((), ())), preferred_element_type=jnp.float32
    )


def local_grads(gate_pre, up_pre, mid_grad, scale_part):
    sigmoid_gate = jax.nn.sigmoid(gate_pre)
    activation = gate_pre * sigmoid_gate
    hidden = activation * up_pre
    scaled = scale_part * mid_grad
    d_up = (scaled * activation).astype(jnp.bfloat16)
    d_gate = (scaled * up_pre * sigmoid_gate * (1.0 + gate_pre * (1.0 - sigmoid_gate))).astype(
        jnp.bfloat16
    )
    return (hidden * mid_grad, d_gate, d_up)


def whole_block(inputs, cotangent, gate_weight, up_weight, down_weight, ia3_scale, seq_ids):
    panel_inputs = lax.all_gather(inputs, "wide", axis=0, tiled=True)
    panel_cotangent = lax.all_gather(cotangent, "wide", axis=0, tiled=True)
    gate_part = jnp.dot(panel_inputs, gate_weight, preferred_element_type=jnp.float32)
    up_part = jnp.dot(panel_inputs, up_weight, preferred_element_type=jnp.float32)
    mid_part = contract_rows(panel_cotangent, down_weight)
    quarter = gate_weight.shape[1] // lax.axis_size("narrow")
    position = lax.axis_index("narrow")
    onehot_full = (seq_ids[None, :] == jnp.arange(SEQS, dtype=jnp.int32)[:, None]).astype(
        jnp.float32
    )
    gate_pre, up_pre, mid_grad = (
        lax.psum_scatter(gate_part, "narrow", scatter_dimension=1, tiled=True),
        lax.psum_scatter(up_part, "narrow", scatter_dimension=1, tiled=True),
        lax.psum_scatter(mid_part, "narrow", scatter_dimension=1, tiled=True),
    )
    scale_part = lax.dynamic_slice_in_dim(ia3_scale, position * quarter, quarter, 0)
    product, d_gate, d_up = local_grads(gate_pre, up_pre, mid_grad, scale_part[None, :])
    example_grads = jnp.dot(onehot_full, product, precision=lax.Precision.HIGHEST)
    whole_gate, whole_up = (
        lax.all_gather(d_gate, "narrow", axis=1, tiled=True),
        lax.all_gather(d_up, "narrow", axis=1, tiled=True),
    )
    squares = lax.psum(jnp.sum(example_grads * example_grads, axis=1), ("wide", "narrow"))
    grad_norms = jnp.sqrt(squares)
    input_grad = lax.psum_scatter(
        contract_rows(whole_gate, gate_weight) + contract_rows(whole_up, up_weight),
        "wide",
        scatter_dimension=0,
        tiled=True,
    ).astype(jnp.bfloat16)
    return (example_grads, grad_norms, input_grad)


def exchange(array, axis, step):
    axes = axis if isinstance(axis, tuple) else (axis,)
    size = math.prod(lax.axis_size(name) for name in axes)
    return lax.ppermute(array, axes, [(i, i ^ step) for i in range(size)])


def exchange_by_core(array, even, odd):
    axes = ("groups", "wide", "narrow")
    narrow = lax.axis_size("narrow")
    size = math.prod(lax.axis_size(name) for name in axes)
    return lax.ppermute(array, axes, [(i, i ^ ((odd if i % 2 else even) * narrow)) for i in range(size)])


def on_odd_core():
    return lax.axis_index("narrow") % 2 == 1


def held(array):
    return pltpu.with_memory_space_constraint(array, pltpu.VMEM)


def call(body, name, outs, args, spaces=None, scratch=(), out_spaces=None):
    spaces, out_spaces = spaces or {}, out_spaces or {}
    many = isinstance(outs, list)
    out_specs = [
        pl.BlockSpec(memory_space=out_spaces.get(i, pltpu.VMEM)) for i in range(len(outs) if many else 1)
    ]
    return pl.pallas_call(
        body,
        out_shape=outs,
        in_specs=[pl.BlockSpec(memory_space=spaces.get(i, pltpu.VMEM)) for i in range(len(args))],
        out_specs=out_specs if many else out_specs[0],
        scratch_shapes=list(scratch),
        compiler_params=pltpu.CompilerParams(vmem_limit_bytes=KERNEL_VMEM),
        cost_estimate=pl.CostEstimate(flops=1000, bytes_accessed=1000, transcendentals=0),
        name=name,
    )(*args)


def pack_kernel(inputs, cotangent, out, stage):
    share, features = inputs.shape
    half = features // 2
    for i, ref in enumerate((inputs, cotangent)):
        rows = ref[...].astype(jnp.float32)
        for j in range(2):
            stage[(2 * i + j) * share : (2 * i + j + 1) * share, :] = rows[:, j * half : (j + 1) * half]
    for k in range(out.shape[0]):
        out[k] = stage[8 * k : 8 * k + 8, :].astype(jnp.bfloat16)


def fetch_ids(ids_in, marks, ids, sem):
    return pltpu.make_async_copy(ids_in, ids, sem.at[0])


def keys_kernel(share, ids_in, marks, ids, sem):
    fetch_ids(ids_in, marks, ids, sem).wait()
    position, count = lax.axis_index("wide"), ids.shape[1]
    shape = (8, count)
    token, row = (lax.broadcasted_iota(jnp.int32, shape, axis) for axis in (1, 0))
    keys = []
    for base in range(0, WIDE * share, 8):
        at = row + base
        block = sum((at >= share * i).astype(jnp.int32) for i in range(1, WIDE))
        own = token == (position ^ block) * share + (at - block * share)
        key = jnp.sum(jnp.where(own, ids[...].astype(jnp.float32), 0.0), axis=1, keepdims=True)
        keys.append(jnp.broadcast_to(key, (8, 128)))
    keys.append(jnp.zeros((8, marks.shape[1] - 128 * len(keys)), jnp.float32))
    marks[...] = jnp.concatenate(keys, axis=1).astype(jnp.bfloat16)


def relay_kernel(own, far, marks, pair, marked):
    slabs = own.shape[0]
    for target in (pair, marked):
        target[0:slabs] = own[...]
        target[slabs : 2 * slabs] = far[...]
    marked[2 * slabs] = marks[...]


WIDE, NEXT, FAR = 4, 1, 2
GATE, UP, DOWN = range(3)
WHOLE_STRIP = (GATE, UP, DOWN)
CHUNKS = 4


def start_loads(pieces, groups, sources, targets, sem):
    copies = []
    for i, (kind, strip) in enumerate(pieces):
        target = targets[i]
        width = target.shape[0 if kind == DOWN else 1]
        owner = lax.axis_index("narrow") ^ strip
        start = pl.multiple_of((owner * groups + lax.axis_index("groups")) * width, width)
        source = sources[kind]
        source = source.at[pl.ds(start, width), :] if kind == DOWN else source.at[:, pl.ds(start, width)]
        size = target.shape[0] // CHUNKS
        for c in range(CHUNKS):
            span = slice(c * size, (c + 1) * size)
            copies.append(pltpu.make_async_copy(source.at[span, :], target.at[span, :], sem.at[i, c]))
    for copy in copies:
        copy.start()
    return copies


def load_kernel(pieces, groups, *refs):
    count = len(pieces)
    for copy in start_loads(pieces, groups, refs[:3], refs[-1 - count : -1], refs[-1]):
        copy.wait()


def loading(body, pieces, groups, outs, own_copy=None):
    count = len(pieces)

    def kernel(*refs):
        sources, rest = refs[:3], refs[3:]
        at = len(rest) - outs[1] - 1 - count
        targets, sem = rest[at : at + count], rest[at + count + outs[1]]
        own = rest[:at] + rest[at + count : at + count + outs[1]]
        if own_copy is not None:
            own_copy(*own).start()
        copies = start_loads(pieces, groups, sources, targets, sem)

        @pl.when(lax.axis_index("narrow") >= 0)
        def _():
            body(*own)

        for copy in copies:
            copy.wait()

    return kernel


def strip_parts(tokens, cotans, gate, up, down, put):
    tile = 256
    for start in range(0, gate.shape[1], tile):
        span = slice(start, start + tile)
        put(GATE, span, jnp.dot(tokens[...], gate[:, span], preferred_element_type=jnp.float32))
        put(UP, span, jnp.dot(tokens[...], up[:, span], preferred_element_type=jnp.float32))
        put(DOWN, span, contract_rows(cotans[...], down[span, :]))


def forward_kernel(tokens, cotans, gate, up, down, *refs):
    out = refs[-1]

    def put(kind, span, part):
        out[kind, :, span] = part.astype(out.dtype)

    strip_parts(tokens, cotans, gate, up, down, put)


def join_kernel(own, arrived, out):
    out[...] = (own[...] + arrived[...]).astype(out.dtype)


def first_kernel(share, marked, one, two, diagonal, gate, up, down, *refs):
    tokens, cotans, part, rows, cots = refs[-5:]
    slabs, half = 4 * share // 8, rows.shape[1] // 2
    odd = on_odd_core()

    def slabs_of(ref, i):
        return ref[i * slabs : (i + 1) * slabs].astype(jnp.float32).reshape(4 * share, half)

    for source, places in (
        (lambda i: slabs_of(marked, i), (0, FAR)),
        (lambda i: jnp.where(odd, slabs_of(one, i), slabs_of(two, i)), (NEXT, FAR ^ NEXT)),
        (lambda i: jnp.where(odd, slabs_of(two, i), slabs_of(one, i)), (WIDE, WIDE + FAR)),
        (lambda i: slabs_of(diagonal, i), (WIDE + NEXT, WIDE + (FAR ^ NEXT))),
    ):
        for i, place in enumerate(places):
            packed = source(i)
            for j, target in enumerate((rows, rows, cots, cots)):
                span = slice((j % 2) * half, (j % 2 + 1) * half)
                target[place * share : (place + 1) * share, span] = packed[j * share : (j + 1) * share]
    tokens[...] = rows[...].astype(jnp.bfloat16)
    cotans[...] = cots[...].astype(jnp.bfloat16)
    forward_kernel(tokens, cotans, gate, up, down, part)


def own_strip_kernel(groups, *refs):
    sources, (tokens, cotans, up, down) = refs[:3], refs[3:7]
    out, gate, sem = refs[-3:]
    copies = start_loads([(GATE, 0)], groups, sources, [gate], sem)

    @pl.when(lax.axis_index("narrow") >= 0)
    def _():
        out[UP] = jnp.dot(tokens[...], up[...], preferred_element_type=jnp.float32)
        out[DOWN] = contract_rows(cotans[...], down[...])

    for copy in copies:
        copy.wait()
    out[GATE] = jnp.dot(tokens[...], gate[...], preferred_element_type=jnp.float32)


def middle_kernel(groups, *refs):
    own, arrived, crossed, scale, marked, one, two = refs[:7]
    message, near_gate, near_up, grads, other_grads, stage = refs[-6:]
    _, tokens, width = own.shape
    narrow, group = lax.axis_index("narrow"), lax.axis_index("groups")
    sums = [own[i] + arrived[i].astype(jnp.float32) + crossed[i].astype(jnp.float32) for i in range(3)]
    start = pl.multiple_of((narrow * groups + group) * width, width)
    product, d_gate, d_up = local_grads(*sums, scale[:, pl.ds(start, width)])
    message[0:tokens, :] = d_gate
    message[tokens : 2 * tokens, :] = d_up
    near_gate[0:tokens, :] = d_gate
    near_up[...] = d_up
    half = tokens // groups
    own_marks, marks_one, marks_two = (ref[ref.shape[0] - 1].astype(jnp.float32) for ref in (marked, one, two))
    other_marks = jnp.where(on_odd_core(), marks_two, marks_one)
    for side, (marks, target) in enumerate(((own_marks, grads), (other_marks, other_grads))):
        seq = jnp.concatenate(
            [
                jnp.concatenate([marks[:, k * 128 : (k + 1) * 128]] * (width // 128), axis=1)
                for k in range(half // 8)
            ],
            axis=0,
        )
        part = product[side * half : (side + 1) * half]
        for e in range(SEQS):
            total = jnp.sum(jnp.where(seq == float(e), part, 0.0), axis=0, keepdims=True)
            target[e : e + 1, :] = total
            stage[side * SEQS + e : side * SEQS + e + 1, :] = total
    every = stage[...]
    squares = jnp.broadcast_to(jnp.sum(every * every, axis=1, keepdims=True), every.shape)
    tail = jnp.concatenate(split_high(squares), axis=0).astype(jnp.bfloat16)
    message[2 * tokens :, :] = tail
    near_gate[tokens:, :] = tail


TILE = 512


def backward_part(grads, gate, up, start):
    d_gate, d_up = grads
    gate_term = contract_rows(gate[start : start + TILE, :], d_gate)
    return gate_term + contract_rows(up[start : start + TILE, :], d_up)


def halves(message):
    tokens = (message.shape[0] - 16) // 2
    return message[0:tokens, :], message[tokens : 2 * tokens, :]


def backward_first_kernel(message, gate, up, total):
    for start in range(0, total.shape[0], TILE):
        total[start : start + TILE, :] = backward_part(halves(message), gate, up, start)


def backward_near_kernel(d_gate, d_up, gate, up, before, total):
    tokens = d_up.shape[0]
    for start in range(0, total.shape[0], TILE):
        part = backward_part((d_gate[0:tokens, :], d_up[...]), gate, up, start)
        total[start : start + TILE, :] = before[start : start + TILE, :] + part


def backward_next_kernel(message, gate, up, before, total):
    for start in range(0, total.shape[0], TILE):
        part = backward_part(halves(message), gate, up, start)
        total[start : start + TILE, :] = before[start : start + TILE, :] + part


def split_high(values):
    high = values.astype(jnp.bfloat16).astype(jnp.float32)
    return high, values - high


def backward_last_kernel(share, message, gate, up, before, *refs):
    others, other_grads, (own, own_squares), sends = refs[:3], refs[3], refs[4:6], refs[6:9]
    total, stage, other_stage = refs[9:]
    tokens, features = total.shape
    side = features // 2
    for start in range(0, features, TILE):
        part = before[start : start + TILE, :] + backward_part(halves(message), gate, up, start)
        total[:, start : start + TILE] = part.T
    squares = sum(ref[ref.shape[0] - 16 :, 0:128].astype(jnp.float32) for ref in (message,) + others)
    squares = squares[0:8] + squares[8:16]
    own_squares[...] = squares
    tails = split_high(squares)
    slabs = 4 * share // 8

    def pack_rows(rows, group, nearby):
        for i, place in enumerate((nearby, nearby ^ FAR)):
            at = (group * WIDE + place) * share
            for j in range(2):
                to = (2 * i + j) * share
                rows[to : to + share, :] = total[at : at + share, j * side : (j + 1) * side]

    one, two, diagonal = sends
    pack_rows(own, 0, 0)
    pack_rows(stage, 1, NEXT)
    for k in range(slabs):
        diagonal[k, :, 0:side] = stage[8 * k : 8 * k + 8, :].astype(jnp.bfloat16)
        tail = tails[k] if k < 2 else jnp.zeros_like(squares)
        diagonal[k, :, side:] = tail.astype(jnp.bfloat16)
    odd = on_odd_core()
    pack_rows(stage, 1, 0)
    pack_rows(other_stage, 0, NEXT)
    for k in range(slabs):
        across, beside = stage[8 * k : 8 * k + 8, :], other_stage[8 * k : 8 * k + 8, :]
        one[k] = jnp.where(odd, beside, across).astype(jnp.bfloat16)
        two[k] = jnp.where(odd, across, beside).astype(jnp.bfloat16)
    width = other_grads.shape[1]
    stage[0:8, :] = jnp.zeros((8, side), jnp.float32)
    for i, rows in enumerate(split_high(other_grads[...])):
        stage[i * SEQS : (i + 1) * SEQS, 0:width] = rows
    for i, rows in enumerate(tails):
        stage[0:8, width + i * 128 : width + (i + 1) * 128] = rows
    for target in (one, two):
        target[slabs] = stage[0:8, :].astype(jnp.bfloat16)


def combine_kernel(share, own, own_squares, diagonal, one, two, *refs):
    kept_rows, other_grads, send, total, stage = refs
    slabs, side = diagonal.shape[0], own.shape[1]
    width = other_grads.shape[1]
    for k in range(slabs):
        rows = own[8 * k : 8 * k + 8, :] + diagonal[k, :, 0:side].astype(jnp.float32)
        total[8 * k : 8 * k + 8, :] = rows + one[k].astype(jnp.float32) + two[k].astype(jnp.float32)
    odd = on_odd_core()
    tail_one, tail_two = one[slabs].astype(jnp.float32), two[slabs].astype(jnp.float32)
    across, beside = jnp.where(odd, tail_two, tail_one), jnp.where(odd, tail_one, tail_two)
    other_grads[...] = across[0:SEQS, 0:width] + across[SEQS : 2 * SEQS, 0:width]
    same, turned = (tail[:, width : width + 128] + tail[:, width + 128 : width + 256] for tail in (beside, across))
    same = same + own_squares[...]
    for k in range(2):
        turned = turned + diagonal[k, :, side:].astype(jnp.float32)
    squares = same[0:SEQS] + turned[SEQS : 2 * SEQS]
    count = 2 * share
    kept_rows[...] = jnp.zeros_like(kept_rows)
    stage[...] = jnp.zeros_like(stage)
    kept_rows[0:count, :] = total[0:count, :]
    stage[0:count, :] = total[count : 2 * count, :]
    high, low = split_high(squares)
    for e in range(SEQS):
        span = slice(e * 128, (e + 1) * 128)
        for ref in (kept_rows, stage):
            ref[count : count + 1, span] = high[e : e + 1]
            ref[count + 1 : count + 2, span] = low[e : e + 1]
    for k in range(2):
        send[k] = stage[8 * k : 8 * k + 8, :].astype(jnp.bfloat16)


def last_kernel(share, own, arrived, grads, other_grads, input_grad, example_grads, norms, stage):
    side, width = own.shape[1], grads.shape[1]
    group = lax.axis_index("groups")
    for k in range(2):
        stage[8 * k : 8 * k + 8, :] = own[8 * k : 8 * k + 8, :] + arrived[k].astype(jnp.float32)
    for j in range(2):
        rows = stage[j * share : (j + 1) * share, :]
        input_grad[:, j * side : (j + 1) * side] = rows.astype(jnp.bfloat16)
    example_grads[:, pl.ds(pl.multiple_of(group * width, width), width)] = grads[...]
    example_grads[:, pl.ds(pl.multiple_of((1 - group) * width, width), width)] = other_grads[...]
    count = 2 * share
    squares = stage[count : count + 1, 0 : SEQS * 128] + stage[count + 1 : count + 2, 0 : SEQS * 128]
    roots = jnp.sqrt(squares)
    for e in range(SEQS):
        norms[e] = jnp.max(roots[:, e * 128 : (e + 1) * 128])


def shared(inputs, cotangent, gate_weight, up_weight, down_weight, ia3_scale, seq_ids):
    groups, wide, strips = lax.axis_size("groups"), lax.axis_size("wide"), lax.axis_size("narrow")
    share, features = inputs.shape
    width = gate_weight.shape[1] // (strips * groups)
    half = share * wide
    tokens = half * groups
    f32, bf16 = jnp.float32, jnp.bfloat16
    slabs, side = 4 * share // 8, features // 2
    weights = tuple(
        pltpu.with_memory_space_constraint(weight, pltpu.HBM)
        for weight in (gate_weight, up_weight, down_weight)
    )
    weight_shapes = [
        pltpu.VMEM((features, width), bf16),
        pltpu.VMEM((features, width), bf16),
        pltpu.VMEM((width, features), bf16),
    ]
    kept = {}

    def load(name, pieces, after=()):
        args = weights + tuple(after)
        arrays = call(
            functools.partial(load_kernel, pieces, groups),
            name,
            [weight_shapes[kind] for kind, _ in pieces],
            args,
            {i: pltpu.HBM if i < 3 else pl.ANY for i in range(len(args))},
            [pltpu.SemaphoreType.DMA((len(pieces), CHUNKS))],
        )
        kept.update(zip(pieces, arrays))

    def call_loading(body, name, pieces, outs, args, scratch=(), spaces=None, own_copy=None):
        made = call(
            loading(body, pieces, groups, (len(outs), len(outs) + len(scratch)), own_copy),
            name,
            [weight_shapes[kind] for kind, _ in pieces] + outs,
            list(weights) + args,
            {**{i: pltpu.HBM for i in range(3)}, **(spaces or {})},
            list(scratch) + [pltpu.SemaphoreType.DMA((len(pieces), CHUNKS))],
        )
        kept.update(zip(pieces, made))
        return made[len(pieces) :]

    def hold(strip, kinds=WHOLE_STRIP):
        return [held(kept[kind, strip]) for kind in kinds]

    packed = call(
        pack_kernel,
        "pack",
        pltpu.VMEM((slabs, 8, features // 2), bf16),
        [pltpu.with_memory_space_constraint(array, pltpu.HBM) for array in (inputs, cotangent)],
        scratch=[pltpu.VMEM((4 * share, features // 2), f32)],
    )
    far = exchange(packed, "wide", FAR)
    (marks,) = call_loading(
        functools.partial(keys_kernel, share),
        "load_a",
        [(kind, 3) for kind in WHOLE_STRIP],
        [pltpu.VMEM((8, side), bf16)],
        [pltpu.with_memory_space_constraint(seq_ids[None, :], pltpu.HBM)],
        [pltpu.VMEM((1, half), jnp.int32), pltpu.SemaphoreType.DMA((1,))],
        {3: pltpu.HBM},
        fetch_ids,
    )
    pair, marked = call(
        relay_kernel,
        "relay",
        [pltpu.VMEM((2 * slabs, 8, side), bf16), pltpu.VMEM((2 * slabs + 1, 8, side), bf16)],
        [packed, far, marks],
    )
    diagonal = exchange(pair, ("groups", "wide"), WIDE + NEXT)
    one = exchange_by_core(marked, WIDE, NEXT)
    two = exchange_by_core(marked, NEXT, WIDE)
    load("load_b", [(kind, 2) for kind in WHOLE_STRIP], [pair])

    part = pltpu.VMEM((3, tokens, width), f32)
    near_shape = pltpu.VMEM((3, tokens, width), bf16)
    tokens_all, cotans_all, diagonal = call_loading(
        functools.partial(first_kernel, share),
        "forward_3",
        [(GATE, 1), (DOWN, 1)],
        [pltpu.VMEM((tokens, features), bf16)] * 2 + [part],
        [marked, one, two, diagonal] + hold(3) + hold(2, [GATE]),
        [pltpu.VMEM((tokens, features), f32)] * 2,
    )
    panel = [tokens_all, cotans_all]
    diagonal = exchange(diagonal, "narrow", 1)
    (second,) = call_loading(forward_kernel, "forward_2", [(UP, 1)], [part], panel + hold(2))
    crossing = call(join_kernel, "join", near_shape, [held(second), diagonal])
    crossed = exchange(crossing, "narrow", 2)
    (near,) = call_loading(
        forward_kernel, "forward_1", [(UP, 0), (DOWN, 0)], [near_shape], panel + hold(1) + [held(crossing)]
    )
    near = exchange(near, "narrow", 1)
    own_part, kept[GATE, 0] = call(
        functools.partial(own_strip_kernel, groups),
        "forward_0",
        [part, weight_shapes[GATE]],
        list(weights) + panel + hold(0, [UP, DOWN]),
        {i: pltpu.HBM for i in range(3)},
        [pltpu.SemaphoreType.DMA((1, CHUNKS))],
    )

    resident = [array for s in range(strips) for array in hold(s, [GATE, UP])]
    message, near_gate, near_up, grads, other_grads = call(
        functools.partial(middle_kernel, groups),
        "middle",
        [
            pltpu.VMEM((2 * tokens + 16, width), bf16),
            pltpu.VMEM((tokens + 16, width), bf16),
            pltpu.VMEM((tokens, width), bf16),
            pltpu.VMEM((SEQS, width), f32),
            pltpu.VMEM((SEQS, width), f32),
        ],
        [own_part, near, crossed, ia3_scale[None, :], marked, one, two] + resident,
        scratch=[pltpu.VMEM((groups * SEQS, width), f32)],
    )

    total = pltpu.VMEM((features, tokens), f32)
    near_gate, near_up = exchange(near_gate, "narrow", 1), exchange(near_up, "narrow", 1)
    message_2 = exchange(message, "narrow", 2)
    sums = call(backward_first_kernel, "backward_0", total, [message] + hold(0, [GATE, UP]))
    sums = call(backward_near_kernel, "backward_1", total, [near_gate, near_up] + hold(1, [GATE, UP]) + [sums])
    message_2, sums = lax.optimization_barrier((message_2, sums))
    message_3 = exchange(message_2, "narrow", 1)
    sums = call(backward_next_kernel, "backward_2", total, [message_2] + hold(2, [GATE, UP]) + [sums])
    own, own_squares, *sends = call(
        functools.partial(backward_last_kernel, share),
        "backward_3",
        [
            pltpu.VMEM((4 * share, side), f32),
            pltpu.VMEM((8, 128), f32),
            pltpu.VMEM((slabs + 1, 8, side), bf16),
            pltpu.VMEM((slabs + 1, 8, side), bf16),
            pltpu.VMEM((slabs, 8, side + 128), bf16),
        ],
        [message_3] + hold(3, [GATE, UP]) + [sums, message, near_gate, message_2, other_grads],
        scratch=[pltpu.VMEM((tokens, features), f32)] + [pltpu.VMEM((4 * share, side), f32)] * 2,
    )
    one = exchange_by_core(sends[0], WIDE, NEXT)
    two = exchange_by_core(sends[1], NEXT, WIDE)
    diagonal = exchange(sends[2], ("groups", "wide"), WIDE + NEXT)
    own, other_grads, send = call(
        functools.partial(combine_kernel, share),
        "combine",
        [pltpu.VMEM((16, side), f32), pltpu.VMEM((SEQS, width), f32), pltpu.VMEM((2, 8, side), bf16)],
        [own, own_squares, diagonal, one, two],
        scratch=[pltpu.VMEM((4 * share, side), f32), pltpu.VMEM((16, side), f32)],
    )
    input_grad, example_grads, norms = call(
        functools.partial(last_kernel, share),
        "last",
        [
            jax.ShapeDtypeStruct((share, features), bf16),
            jax.ShapeDtypeStruct((SEQS, groups * width), f32),
            jax.ShapeDtypeStruct((SEQS,), f32),
        ],
        [own, exchange(send, "wide", FAR), grads, other_grads],
        scratch=[pltpu.VMEM((16, side), f32)],
        out_spaces={2: pltpu.SMEM},
    )
    return (example_grads, norms, input_grad)


def local(inputs, cotangent, gate_weight, up_weight, down_weight, ia3_scale, seq_ids):
    groups, wide, narrow = lax.axis_size("groups"), lax.axis_size("wide"), lax.axis_size("narrow")
    share, (features, hidden) = inputs.shape[0], gate_weight.shape
    width = hidden // (narrow * groups)
    fits = (
        groups == 2
        and narrow == 4
        and wide == WIDE
        and hidden % (narrow * groups * 256) == 0
        and features >= 2048
        and width <= features // 2 - 256
        and features % (2 * TILE) == 0
        and share in (4, 6)
        and (share * wide) % 8 == 0
        and share * wide <= 64
        and 3 * features * hidden // groups * 2 <= 40 << 20
    )
    plan = shared if fits else whole_block
    return plan(inputs, cotangent, gate_weight, up_weight, down_weight, ia3_scale, seq_ids)


def solution(mesh):
    return jax.shard_map(
        local,
        mesh=mesh,
        in_specs=(
            P(("groups", "wide"), "narrow"),
            P(("groups", "wide"), "narrow"),
            P("narrow", "wide"),
            P("narrow", "wide"),
            P("wide", "narrow"),
            P("wide"),
            P("groups"),
        ),
        out_specs=(P("groups", ("wide", "narrow")), P("groups"), P(("groups", "wide"), "narrow")),
        check_vma=False,
    )
```

```python
import functools
import math

import jax
import jax.numpy as jnp
from jax import lax
from jax.experimental import pallas as pl
from jax.experimental.pallas import tpu as pltpu
from jax.sharding import PartitionSpec as P

SEQS = 4
KERNEL_VMEM = 6 << 20


def contract_rows(left, right):
    return lax.dot_general(
        left, right, (((1,), (1,)), ((), ())), preferred_element_type=jnp.float32
    )


def local_grads(gate_pre, up_pre, mid_grad, scale_part):
    sigmoid_gate = jax.nn.sigmoid(gate_pre)
    activation = gate_pre * sigmoid_gate
    hidden = activation * up_pre
    scaled = scale_part * mid_grad
    d_up = (scaled * activation).astype(jnp.bfloat16)
    d_gate = (scaled * up_pre * sigmoid_gate * (1.0 + gate_pre * (1.0 - sigmoid_gate))).astype(
        jnp.bfloat16
    )
    return (hidden * mid_grad, d_gate, d_up)


def whole_block(inputs, cotangent, gate_weight, up_weight, down_weight, ia3_scale, seq_ids):
    panel_inputs = lax.all_gather(inputs, "wide", axis=0, tiled=True)
    panel_cotangent = lax.all_gather(cotangent, "wide", axis=0, tiled=True)
    gate_part = jnp.dot(panel_inputs, gate_weight, preferred_element_type=jnp.float32)
    up_part = jnp.dot(panel_inputs, up_weight, preferred_element_type=jnp.float32)
    mid_part = contract_rows(panel_cotangent, down_weight)
    quarter = gate_weight.shape[1] // lax.axis_size("narrow")
    position = lax.axis_index("narrow")
    onehot_full = (seq_ids[None, :] == jnp.arange(SEQS, dtype=jnp.int32)[:, None]).astype(
        jnp.float32
    )
    gate_pre, up_pre, mid_grad = (
        lax.psum_scatter(gate_part, "narrow", scatter_dimension=1, tiled=True),
        lax.psum_scatter(up_part, "narrow", scatter_dimension=1, tiled=True),
        lax.psum_scatter(mid_part, "narrow", scatter_dimension=1, tiled=True),
    )
    scale_part = lax.dynamic_slice_in_dim(ia3_scale, position * quarter, quarter, 0)
    product, d_gate, d_up = local_grads(gate_pre, up_pre, mid_grad, scale_part[None, :])
    example_grads = jnp.dot(onehot_full, product, precision=lax.Precision.HIGHEST)
    whole_gate, whole_up = (
        lax.all_gather(d_gate, "narrow", axis=1, tiled=True),
        lax.all_gather(d_up, "narrow", axis=1, tiled=True),
    )
    squares = lax.psum(jnp.sum(example_grads * example_grads, axis=1), ("wide", "narrow"))
    grad_norms = jnp.sqrt(squares)
    input_grad = lax.psum_scatter(
        contract_rows(whole_gate, gate_weight) + contract_rows(whole_up, up_weight),
        "wide",
        scatter_dimension=0,
        tiled=True,
    ).astype(jnp.bfloat16)
    return (example_grads, grad_norms, input_grad)


def exchange(array, axis, step):
    axes = axis if isinstance(axis, tuple) else (axis,)
    size = math.prod(lax.axis_size(name) for name in axes)
    return lax.ppermute(array, axes, [(i, i ^ step) for i in range(size)])


def held(array):
    return pltpu.with_memory_space_constraint(array, pltpu.VMEM)


def call(body, name, outs, args, spaces=None, scratch=(), out_spaces=None):
    spaces, out_spaces = spaces or {}, out_spaces or {}
    many = isinstance(outs, list)
    out_specs = [
        pl.BlockSpec(memory_space=out_spaces.get(i, pltpu.VMEM)) for i in range(len(outs) if many else 1)
    ]
    return pl.pallas_call(
        body,
        out_shape=outs,
        in_specs=[pl.BlockSpec(memory_space=spaces.get(i, pltpu.VMEM)) for i in range(len(args))],
        out_specs=out_specs if many else out_specs[0],
        scratch_shapes=list(scratch),
        compiler_params=pltpu.CompilerParams(vmem_limit_bytes=KERNEL_VMEM),
        cost_estimate=pl.CostEstimate(flops=1000, bytes_accessed=1000, transcendentals=0),
        name=name,
    )(*args)


def pack_kernel(inputs, cotangent, out, stage):
    share, features = inputs.shape
    half = features // 2
    for i, ref in enumerate((inputs, cotangent)):
        rows = ref[...].astype(jnp.float32)
        for j in range(2):
            stage[(2 * i + j) * share : (2 * i + j + 1) * share, :] = rows[:, j * half : (j + 1) * half]
    for k in range(out.shape[0]):
        out[k] = stage[8 * k : 8 * k + 8, :].astype(jnp.bfloat16)


def fetch_ids(ids_in, marks, ids, sem):
    return pltpu.make_async_copy(ids_in, ids, sem.at[0])


def keys_kernel(share, ids_in, marks, ids, sem):
    fetch_ids(ids_in, marks, ids, sem).wait()
    position, count = lax.axis_index("wide"), ids.shape[1]
    shape = (8, count)
    token, row = (lax.broadcasted_iota(jnp.int32, shape, axis) for axis in (1, 0))
    keys = []
    for base in range(0, WIDE * share, 8):
        at = row + base
        block = sum((at >= share * i).astype(jnp.int32) for i in range(1, WIDE))
        own = token == (position ^ block) * share + (at - block * share)
        key = jnp.sum(jnp.where(own, ids[...].astype(jnp.float32), 0.0), axis=1, keepdims=True)
        keys.append(jnp.broadcast_to(key, (8, 128)))
    keys.append(jnp.zeros((8, marks.shape[1] - 128 * len(keys)), jnp.float32))
    marks[...] = jnp.concatenate(keys, axis=1).astype(jnp.bfloat16)


def relay_kernel(own, far, marks, pair, marked):
    slabs = own.shape[0]
    for target in (pair, marked):
        target[0:slabs] = own[...]
        target[slabs : 2 * slabs] = far[...]
    marked[2 * slabs] = marks[...]


WIDE, NEXT, FAR = 4, 1, 2
GATE, UP, DOWN = range(3)
WHOLE_STRIP = (GATE, UP, DOWN)
CHUNKS = 4


def start_loads(pieces, groups, sources, targets, sem):
    copies = []
    for i, (kind, strip) in enumerate(pieces):
        target = targets[i]
        width = target.shape[0 if kind == DOWN else 1]
        owner = lax.axis_index("narrow") ^ strip
        start = pl.multiple_of((owner * groups + lax.axis_index("groups")) * width, width)
        source = sources[kind]
        source = source.at[pl.ds(start, width), :] if kind == DOWN else source.at[:, pl.ds(start, width)]
        chunks = CHUNKS if len(pieces) == 1 else 1
        size = target.shape[0] // chunks
        for c in range(chunks):
            span = slice(c * size, (c + 1) * size)
            copies.append(pltpu.make_async_copy(source.at[span, :], target.at[span, :], sem.at[i, c]))
    for copy in copies:
        copy.start()
    return copies


def load_kernel(pieces, groups, *refs):
    count = len(pieces)
    for copy in start_loads(pieces, groups, refs[:3], refs[-1 - count : -1], refs[-1]):
        copy.wait()


def loading(body, pieces, groups, outs, own_copy=None):
    count = len(pieces)

    def kernel(*refs):
        sources, rest = refs[:3], refs[3:]
        at = len(rest) - outs[1] - 1 - count
        targets, sem = rest[at : at + count], rest[at + count + outs[1]]
        own = rest[:at] + rest[at + count : at + count + outs[1]]
        if own_copy is not None:
            own_copy(*own).start()
        copies = start_loads(pieces, groups, sources, targets, sem)

        @pl.when(lax.axis_index("narrow") >= 0)
        def _():
            body(*own)

        for copy in copies:
            copy.wait()

    return kernel


def strip_parts(tokens, cotans, gate, up, down, put):
    tile = 256
    for start in range(0, gate.shape[1], tile):
        span = slice(start, start + tile)
        put(GATE, span, jnp.dot(tokens[...], gate[:, span], preferred_element_type=jnp.float32))
        put(UP, span, jnp.dot(tokens[...], up[:, span], preferred_element_type=jnp.float32))
        put(DOWN, span, contract_rows(cotans[...], down[span, :]))


def forward_kernel(tokens, cotans, gate, up, down, *refs):
    out = refs[-1]

    def put(kind, span, part):
        out[kind, :, span] = part.astype(out.dtype)

    strip_parts(tokens, cotans, gate, up, down, put)


def join_kernel(own, arrived, out):
    out[...] = (own[...] + arrived[...]).astype(out.dtype)


def first_kernel(share, marked, beside, other, diagonal, gate, up, down, *refs):
    tokens, cotans, part, rows, cots = refs[-5:]
    slabs, half = 4 * share // 8, rows.shape[1] // 2
    for source, places in (
        (marked, (0, FAR)),
        (beside, (NEXT, FAR ^ NEXT)),
        (other, (WIDE, WIDE + FAR)),
        (diagonal, (WIDE + NEXT, WIDE + (FAR ^ NEXT))),
    ):
        for i, place in enumerate(places):
            packed = source[i * slabs : (i + 1) * slabs].astype(jnp.float32).reshape(4 * share, half)
            for j, target in enumerate((rows, rows, cots, cots)):
                span = slice((j % 2) * half, (j % 2 + 1) * half)
                target[place * share : (place + 1) * share, span] = packed[j * share : (j + 1) * share]
    tokens[...] = rows[...].astype(jnp.bfloat16)
    cotans[...] = cots[...].astype(jnp.bfloat16)
    forward_kernel(tokens, cotans, gate, up, down, part)


def own_strip_kernel(groups, *refs):
    sources, (tokens, cotans, up, down) = refs[:3], refs[3:7]
    out, gate, sem = refs[-3:]
    copies = start_loads([(GATE, 0)], groups, sources, [gate], sem)

    @pl.when(lax.axis_index("narrow") >= 0)
    def _():
        out[UP] = jnp.dot(tokens[...], up[...], preferred_element_type=jnp.float32)
        out[DOWN] = contract_rows(cotans[...], down[...])

    for copy in copies:
        copy.wait()
    out[GATE] = jnp.dot(tokens[...], gate[...], preferred_element_type=jnp.float32)


def to_tiles(values, tiles, first):
    rows, columns = values.shape
    values = values.astype(jnp.float32)
    for i in range(rows // 8):
        for j in range(columns // 128):
            tile = values[8 * i : 8 * i + 8, 128 * j : 128 * j + 128]
            tiles[first + i * (columns // 128) + j] = tile.astype(tiles.dtype)


def from_tiles(tiles, first, rows, columns):
    across = columns // 128
    parts = [
        jnp.concatenate([tiles[first + i * across + j].astype(jnp.float32) for j in range(across)], axis=1)
        for i in range(rows // 8)
    ]
    return jnp.concatenate(parts, axis=0).astype(tiles.dtype)


def middle_kernel(groups, *refs):
    own, arrived, crossed, scale, relayed, other_relayed = refs[:6]
    message, tiles, near_gate, near_up, grads, other_grads, stage = refs[-7:]
    _, tokens, width = own.shape
    narrow, group = lax.axis_index("narrow"), lax.axis_index("groups")
    sums = [own[i] + arrived[i].astype(jnp.float32) + crossed[i].astype(jnp.float32) for i in range(3)]
    start = pl.multiple_of((narrow * groups + group) * width, width)
    product, d_gate, d_up = local_grads(*sums, scale[:, pl.ds(start, width)])
    message[0:tokens, :] = d_gate
    message[tokens : 2 * tokens, :] = d_up
    near_gate[0:tokens, :] = d_gate
    near_up[...] = d_up
    count = tokens // 8 * (width // 128)
    to_tiles(d_gate, tiles, 0)
    to_tiles(d_up, tiles, count)
    half = tokens // groups
    for side, (source, target) in enumerate(((relayed, grads), (other_relayed, other_grads))):
        marks = source[source.shape[0] - 1].astype(jnp.float32)
        seq = jnp.concatenate(
            [
                jnp.concatenate([marks[:, k * 128 : (k + 1) * 128]] * (width // 128), axis=1)
                for k in range(half // 8)
            ],
            axis=0,
        )
        part = product[side * half : (side + 1) * half]
        for e in range(SEQS):
            total = jnp.sum(jnp.where(seq == float(e), part, 0.0), axis=0, keepdims=True)
            target[e : e + 1, :] = total
            stage[side * SEQS + e : side * SEQS + e + 1, :] = total
    every = stage[...]
    squares = jnp.broadcast_to(jnp.sum(every * every, axis=1, keepdims=True), every.shape)
    tail = jnp.concatenate(split_high(squares), axis=0).astype(jnp.bfloat16)
    message[2 * tokens :, :] = tail
    for i, rows in enumerate(split_high(squares)):
        tiles[2 * count + i] = rows[:, 0:128].astype(jnp.bfloat16)
    near_gate[tokens:, :] = tail


TILE = 512


def backward_part(grads, gate, up, start):
    d_gate, d_up = grads
    gate_term = contract_rows(gate[start : start + TILE, :], d_gate)
    return gate_term + contract_rows(up[start : start + TILE, :], d_up)


def halves(message):
    tokens = (message.shape[0] - 16) // 2
    return message[0:tokens, :], message[tokens : 2 * tokens, :]


def halves_of_tiles(tiles, width):
    count = (tiles.shape[0] - 2) // 2
    rows = count // (width // 128) * 8
    return from_tiles(tiles, 0, rows, width), from_tiles(tiles, count, rows, width)


def squares_of(message):
    if len(message.shape) == 3:
        tiles = message.shape[0]
        return message[tiles - 2].astype(jnp.float32) + message[tiles - 1].astype(jnp.float32)
    rows = message[message.shape[0] - 16 :, 0:128].astype(jnp.float32)
    return rows[0:8] + rows[8:16]


def backward_first_kernel(message, gate, up, total):
    for start in range(0, total.shape[0], TILE):
        total[start : start + TILE, :] = backward_part(halves(message), gate, up, start)


def backward_near_kernel(d_gate, d_up, gate, up, before, total):
    tokens = d_up.shape[0]
    for start in range(0, total.shape[0], TILE):
        part = backward_part((d_gate[0:tokens, :], d_up[...]), gate, up, start)
        total[start : start + TILE, :] = before[start : start + TILE, :] + part


def backward_next_kernel(tiles, gate, up, before, total):
    grads = halves_of_tiles(tiles, gate.shape[1])
    for start in range(0, total.shape[0], TILE):
        part = backward_part(grads, gate, up, start)
        total[start : start + TILE, :] = before[start : start + TILE, :] + part


def split_high(values):
    high = values.astype(jnp.bfloat16).astype(jnp.float32)
    return high, values - high


def backward_last_kernel(share, tiles, gate, up, before, *refs):
    others, other_grads, (own, own_squares), sends, (total, stage) = refs[:3], refs[3], refs[4:6], refs[6:9], refs[9:]
    tokens, features = total.shape
    side = features // 2
    grads = halves_of_tiles(tiles, gate.shape[1])
    for start in range(0, features, TILE):
        part = before[start : start + TILE, :] + backward_part(grads, gate, up, start)
        total[:, start : start + TILE] = part.T
    squares = sum(squares_of(ref) for ref in (tiles,) + others)
    own_squares[...] = squares
    tails = split_high(squares)
    slabs = 4 * share // 8
    for target, group, nearby in zip((own,) + tuple(sends), (0, 0, 1, 1), (0, NEXT, 0, NEXT)):
        rows = own if target is own else stage
        for i, place in enumerate((nearby, nearby ^ FAR)):
            at = (group * WIDE + place) * share
            for j in range(2):
                to = (2 * i + j) * share
                rows[to : to + share, :] = total[at : at + share, j * side : (j + 1) * side]
        if target is not own:
            for k in range(slabs):
                target[k, :, 0:side] = stage[8 * k : 8 * k + 8, :].astype(jnp.bfloat16)
                if target.shape[2] > side:
                    tail = tails[k] if k < 2 else jnp.zeros_like(squares)
                    target[k, :, side:] = tail.astype(jnp.bfloat16)
    width = other_grads.shape[1]
    stage[0:8, :] = jnp.zeros((8, side), jnp.float32)
    for i, rows in enumerate(split_high(other_grads[...])):
        stage[i * SEQS : (i + 1) * SEQS, 0:width] = rows
    for i, rows in enumerate(tails):
        stage[0:8, width + i * 128 : width + (i + 1) * 128] = rows
    sends[1][slabs] = stage[0:8, :].astype(jnp.bfloat16)


def combine_kernel(share, own, own_squares, diagonal, across, beside, *refs):
    kept_rows, other_grads, send, total, stage = refs
    slabs, side = beside.shape[0], own.shape[1]
    width = other_grads.shape[1]
    for k in range(slabs):
        rows = own[8 * k : 8 * k + 8, :] + across[k].astype(jnp.float32)
        for ref in (beside, diagonal):
            rows = rows + ref[k, :, 0:side].astype(jnp.float32)
        total[8 * k : 8 * k + 8, :] = rows
    tail = across[slabs].astype(jnp.float32)
    other_grads[...] = tail[0:SEQS, 0:width] + tail[SEQS : 2 * SEQS, 0:width]
    same, turned = own_squares[...], tail[:, width : width + 128] + tail[:, width + 128 : width + 256]
    for k in range(2):
        same = same + beside[k, :, side:].astype(jnp.float32)
        turned = turned + diagonal[k, :, side:].astype(jnp.float32)
    squares = same[0:SEQS] + turned[SEQS : 2 * SEQS]
    count = 2 * share
    kept_rows[...] = jnp.zeros_like(kept_rows)
    stage[...] = jnp.zeros_like(stage)
    kept_rows[0:count, :] = total[0:count, :]
    stage[0:count, :] = total[count : 2 * count, :]
    high, low = split_high(squares)
    for e in range(SEQS):
        span = slice(e * 128, (e + 1) * 128)
        for ref in (kept_rows, stage):
            ref[count : count + 1, span] = high[e : e + 1]
            ref[count + 1 : count + 2, span] = low[e : e + 1]
    for k in range(2):
        send[k] = stage[8 * k : 8 * k + 8, :].astype(jnp.bfloat16)


def last_kernel(share, own, arrived, grads, other_grads, input_grad, example_grads, norms, stage):
    side, width = own.shape[1], grads.shape[1]
    group = lax.axis_index("groups")
    for k in range(2):
        stage[8 * k : 8 * k + 8, :] = own[8 * k : 8 * k + 8, :] + arrived[k].astype(jnp.float32)
    for j in range(2):
        rows = stage[j * share : (j + 1) * share, :]
        input_grad[:, j * side : (j + 1) * side] = rows.astype(jnp.bfloat16)
    example_grads[:, pl.ds(pl.multiple_of(group * width, width), width)] = grads[...]
    example_grads[:, pl.ds(pl.multiple_of((1 - group) * width, width), width)] = other_grads[...]
    count = 2 * share
    squares = stage[count : count + 1, 0 : SEQS * 128] + stage[count + 1 : count + 2, 0 : SEQS * 128]
    roots = jnp.sqrt(squares)
    for e in range(SEQS):
        norms[e] = jnp.max(roots[:, e * 128 : (e + 1) * 128])


def shared(inputs, cotangent, gate_weight, up_weight, down_weight, ia3_scale, seq_ids):
    groups, wide, strips = lax.axis_size("groups"), lax.axis_size("wide"), lax.axis_size("narrow")
    share, features = inputs.shape
    width = gate_weight.shape[1] // (strips * groups)
    half = share * wide
    tokens = half * groups
    f32, bf16 = jnp.float32, jnp.bfloat16
    slabs, side = 4 * share // 8, features // 2
    weights = tuple(
        pltpu.with_memory_space_constraint(weight, pltpu.HBM)
        for weight in (gate_weight, up_weight, down_weight)
    )
    weight_shapes = [
        pltpu.VMEM((features, width), bf16),
        pltpu.VMEM((features, width), bf16),
        pltpu.VMEM((width, features), bf16),
    ]
    kept = {}

    def load(name, pieces, after=()):
        args = weights + tuple(after)
        arrays = call(
            functools.partial(load_kernel, pieces, groups),
            name,
            [weight_shapes[kind] for kind, _ in pieces],
            args,
            {i: pltpu.HBM if i < 3 else pl.ANY for i in range(len(args))},
            [pltpu.SemaphoreType.DMA((len(pieces), CHUNKS))],
        )
        kept.update(zip(pieces, arrays))

    def call_loading(body, name, pieces, outs, args, scratch=(), spaces=None, own_copy=None):
        made = call(
            loading(body, pieces, groups, (len(outs), len(outs) + len(scratch)), own_copy),
            name,
            [weight_shapes[kind] for kind, _ in pieces] + outs,
            list(weights) + args,
            {**{i: pltpu.HBM for i in range(3)}, **(spaces or {})},
            list(scratch) + [pltpu.SemaphoreType.DMA((len(pieces), CHUNKS))],
        )
        kept.update(zip(pieces, made))
        return made[len(pieces) :]

    def hold(strip, kinds=WHOLE_STRIP):
        return [held(kept[kind, strip]) for kind in kinds]

    packed = call(
        pack_kernel,
        "pack",
        pltpu.VMEM((slabs, 8, features // 2), bf16),
        [pltpu.with_memory_space_constraint(array, pltpu.HBM) for array in (inputs, cotangent)],
        scratch=[pltpu.VMEM((4 * share, features // 2), f32)],
    )
    far = exchange(packed, "wide", FAR)
    (marks,) = call_loading(
        functools.partial(keys_kernel, share),
        "load_a",
        [(kind, 3) for kind in WHOLE_STRIP],
        [pltpu.VMEM((8, side), bf16)],
        [pltpu.with_memory_space_constraint(seq_ids[None, :], pltpu.HBM)],
        [pltpu.VMEM((1, half), jnp.int32), pltpu.SemaphoreType.DMA((1,))],
        {3: pltpu.HBM},
        fetch_ids,
    )
    pair, marked = call(
        relay_kernel,
        "relay",
        [pltpu.VMEM((2 * slabs, 8, side), bf16), pltpu.VMEM((2 * slabs + 1, 8, side), bf16)],
        [packed, far, marks],
    )
    diagonal = exchange(pair, ("groups", "wide"), WIDE + NEXT)
    other_marked = exchange(marked, "groups", 1)
    beside = exchange(pair, "wide", NEXT)
    load("load_b", [(kind, 2) for kind in WHOLE_STRIP], [pair])

    part = pltpu.VMEM((3, tokens, width), f32)
    near_shape = pltpu.VMEM((3, tokens, width), bf16)
    tokens_all, cotans_all, diagonal = call_loading(
        functools.partial(first_kernel, share),
        "forward_3",
        [(GATE, 1), (DOWN, 1)],
        [pltpu.VMEM((tokens, features), bf16)] * 2 + [part],
        [marked, beside, other_marked, diagonal] + hold(3) + hold(2, [GATE]),
        [pltpu.VMEM((tokens, features), f32)] * 2,
    )
    panel = [tokens_all, cotans_all]
    diagonal = exchange(diagonal, "narrow", 1)
    (second,) = call_loading(forward_kernel, "forward_2", [(UP, 1)], [part], panel + hold(2))
    crossing = call(join_kernel, "join", near_shape, [held(second), diagonal])
    crossed = exchange(crossing, "narrow", 2)
    (near,) = call_loading(
        forward_kernel, "forward_1", [(UP, 0), (DOWN, 0)], [near_shape], panel + hold(1) + [held(crossing)]
    )
    near = exchange(near, "narrow", 1)
    own_part, kept[GATE, 0] = call(
        functools.partial(own_strip_kernel, groups),
        "forward_0",
        [part, weight_shapes[GATE]],
        list(weights) + panel + hold(0, [UP, DOWN]),
        {i: pltpu.HBM for i in range(3)},
        [pltpu.SemaphoreType.DMA((1, CHUNKS))],
    )

    resident = [array for s in range(strips) for array in hold(s, [GATE, UP])]
    message, tiles, near_gate, near_up, grads, other_grads = call(
        functools.partial(middle_kernel, groups),
        "middle",
        [
            pltpu.VMEM((2 * tokens + 16, width), bf16),
            pltpu.VMEM((2 * (tokens // 8) * (width // 128) + 2, 8, 128), bf16),
            pltpu.VMEM((tokens + 16, width), bf16),
            pltpu.VMEM((tokens, width), bf16),
            pltpu.VMEM((SEQS, width), f32),
            pltpu.VMEM((SEQS, width), f32),
        ],
        [own_part, near, crossed, ia3_scale[None, :], marked, other_marked] + resident,
        scratch=[pltpu.VMEM((groups * SEQS, width), f32)],
    )

    total = pltpu.VMEM((features, tokens), f32)
    near_gate, near_up = exchange(near_gate, "narrow", 1), exchange(near_up, "narrow", 1)
    message_2 = exchange(tiles, "narrow", 2)
    sums = call(backward_first_kernel, "backward_0", total, [message] + hold(0, [GATE, UP]))
    sums = call(backward_near_kernel, "backward_1", total, [near_gate, near_up] + hold(1, [GATE, UP]) + [sums])
    message_2, sums = lax.optimization_barrier((message_2, sums))
    message_3 = exchange(message_2, "narrow", 1)
    sums = call(backward_next_kernel, "backward_2", total, [message_2] + hold(2, [GATE, UP]) + [sums])
    block = pltpu.VMEM((slabs, 8, side + 128), bf16)
    own, own_squares, *sends = call(
        functools.partial(backward_last_kernel, share),
        "backward_3",
        [
            pltpu.VMEM((4 * share, side), f32),
            pltpu.VMEM((8, 128), f32),
            block,
            pltpu.VMEM((slabs + 1, 8, side), bf16),
            block,
        ],
        [message_3] + hold(3, [GATE, UP]) + [sums, message, near_gate, message_2, other_grads],
        scratch=[pltpu.VMEM((tokens, features), f32), pltpu.VMEM((4 * share, side), f32)],
    )
    across = exchange(sends[1], "groups", 1)
    beside = exchange(sends[0], "wide", NEXT)
    diagonal = exchange(sends[2], ("groups", "wide"), WIDE + NEXT)
    own, other_grads, send = call(
        functools.partial(combine_kernel, share),
        "combine",
        [pltpu.VMEM((16, side), f32), pltpu.VMEM((SEQS, width), f32), pltpu.VMEM((2, 8, side), bf16)],
        [own, own_squares, diagonal, across, beside],
        scratch=[pltpu.VMEM((4 * share, side), f32), pltpu.VMEM((16, side), f32)],
    )
    input_grad, example_grads, norms = call(
        functools.partial(last_kernel, share),
        "last",
        [
            jax.ShapeDtypeStruct((share, features), bf16),
            jax.ShapeDtypeStruct((SEQS, groups * width), f32),
            jax.ShapeDtypeStruct((SEQS,), f32),
        ],
        [own, exchange(send, "wide", FAR), grads, other_grads],
        scratch=[pltpu.VMEM((16, side), f32)],
        out_spaces={2: pltpu.SMEM},
    )
    return (example_grads, norms, input_grad)


def local(inputs, cotangent, gate_weight, up_weight, down_weight, ia3_scale, seq_ids):
    groups, wide, narrow = lax.axis_size("groups"), lax.axis_size("wide"), lax.axis_size("narrow")
    share, (features, hidden) = inputs.shape[0], gate_weight.shape
    width = hidden // (narrow * groups)
    fits = (
        groups == 2
        and narrow == 4
        and wide == WIDE
        and hidden % (narrow * groups * 256) == 0
        and features >= 2048
        and width <= features // 2 - 256
        and features % (2 * TILE) == 0
        and share in (4, 6)
        and (share * wide) % 8 == 0
        and share * wide <= 64
        and 3 * features * hidden // groups * 2 <= 40 << 20
    )
    plan = shared if fits else whole_block
    return plan(inputs, cotangent, gate_weight, up_weight, down_weight, ia3_scale, seq_ids)


def solution(mesh):
    return jax.shard_map(
        local,
        mesh=mesh,
        in_specs=(
            P(("groups", "wide"), "narrow"),
            P(("groups", "wide"), "narrow"),
            P("narrow", "wide"),
            P("narrow", "wide"),
            P("wide", "narrow"),
            P("wide"),
            P("groups"),
        ),
        out_specs=(P("groups", ("wide", "narrow")), P("groups"), P(("groups", "wide"), "narrow")),
        check_vma=False,
    )
```

```python
import functools
import math

import jax
import jax.numpy as jnp
from jax import lax
from jax.experimental import pallas as pl
from jax.experimental.pallas import tpu as pltpu
from jax.sharding import PartitionSpec as P

SEQS = 4
KERNEL_VMEM = 6 << 20


def contract_rows(left, right):
    return lax.dot_general(
        left, right, (((1,), (1,)), ((), ())), preferred_element_type=jnp.float32
    )


def local_grads(gate_pre, up_pre, mid_grad, scale_part):
    sigmoid_gate = jax.nn.sigmoid(gate_pre)
    activation = gate_pre * sigmoid_gate
    hidden = activation * up_pre
    scaled = scale_part * mid_grad
    d_up = (scaled * activation).astype(jnp.bfloat16)
    d_gate = (scaled * up_pre * sigmoid_gate * (1.0 + gate_pre * (1.0 - sigmoid_gate))).astype(
        jnp.bfloat16
    )
    return (hidden * mid_grad, d_gate, d_up)


def whole_block(inputs, cotangent, gate_weight, up_weight, down_weight, ia3_scale, seq_ids):
    panel_inputs = lax.all_gather(inputs, "wide", axis=0, tiled=True)
    panel_cotangent = lax.all_gather(cotangent, "wide", axis=0, tiled=True)
    gate_part = jnp.dot(panel_inputs, gate_weight, preferred_element_type=jnp.float32)
    up_part = jnp.dot(panel_inputs, up_weight, preferred_element_type=jnp.float32)
    mid_part = contract_rows(panel_cotangent, down_weight)
    quarter = gate_weight.shape[1] // lax.axis_size("narrow")
    position = lax.axis_index("narrow")
    onehot_full = (seq_ids[None, :] == jnp.arange(SEQS, dtype=jnp.int32)[:, None]).astype(
        jnp.float32
    )
    gate_pre, up_pre, mid_grad = (
        lax.psum_scatter(gate_part, "narrow", scatter_dimension=1, tiled=True),
        lax.psum_scatter(up_part, "narrow", scatter_dimension=1, tiled=True),
        lax.psum_scatter(mid_part, "narrow", scatter_dimension=1, tiled=True),
    )
    scale_part = lax.dynamic_slice_in_dim(ia3_scale, position * quarter, quarter, 0)
    product, d_gate, d_up = local_grads(gate_pre, up_pre, mid_grad, scale_part[None, :])
    example_grads = jnp.dot(onehot_full, product, precision=lax.Precision.HIGHEST)
    whole_gate, whole_up = (
        lax.all_gather(d_gate, "narrow", axis=1, tiled=True),
        lax.all_gather(d_up, "narrow", axis=1, tiled=True),
    )
    squares = lax.psum(jnp.sum(example_grads * example_grads, axis=1), ("wide", "narrow"))
    grad_norms = jnp.sqrt(squares)
    input_grad = lax.psum_scatter(
        contract_rows(whole_gate, gate_weight) + contract_rows(whole_up, up_weight),
        "wide",
        scatter_dimension=0,
        tiled=True,
    ).astype(jnp.bfloat16)
    return (example_grads, grad_norms, input_grad)


def exchange(array, axis, step):
    axes = axis if isinstance(axis, tuple) else (axis,)
    size = math.prod(lax.axis_size(name) for name in axes)
    return lax.ppermute(array, axes, [(i, i ^ step) for i in range(size)])


def held(array):
    return pltpu.with_memory_space_constraint(array, pltpu.VMEM)


def call(body, name, outs, args, spaces=None, scratch=(), out_spaces=None):
    spaces, out_spaces = spaces or {}, out_spaces or {}
    many = isinstance(outs, list)
    out_specs = [
        pl.BlockSpec(memory_space=out_spaces.get(i, pltpu.VMEM)) for i in range(len(outs) if many else 1)
    ]
    return pl.pallas_call(
        body,
        out_shape=outs,
        in_specs=[pl.BlockSpec(memory_space=spaces.get(i, pltpu.VMEM)) for i in range(len(args))],
        out_specs=out_specs if many else out_specs[0],
        scratch_shapes=list(scratch),
        compiler_params=pltpu.CompilerParams(vmem_limit_bytes=KERNEL_VMEM),
        cost_estimate=pl.CostEstimate(flops=1000, bytes_accessed=1000, transcendentals=0),
        name=name,
    )(*args)


def pack_kernel(inputs, cotangent, out, stage):
    share, features = inputs.shape
    half = features // 2
    for i, ref in enumerate((inputs, cotangent)):
        rows = ref[...].astype(jnp.float32)
        for j in range(2):
            stage[(2 * i + j) * share : (2 * i + j + 1) * share, :] = rows[:, j * half : (j + 1) * half]
    for k in range(out.shape[0]):
        out[k] = stage[8 * k : 8 * k + 8, :].astype(jnp.bfloat16)


def fetch_ids(ids_in, marks, ids, sem):
    return pltpu.make_async_copy(ids_in, ids, sem.at[0])


def keys_kernel(share, ids_in, marks, ids, sem):
    fetch_ids(ids_in, marks, ids, sem).wait()
    position, count = lax.axis_index("wide"), ids.shape[1]
    shape = (8, count)
    token, row = (lax.broadcasted_iota(jnp.int32, shape, axis) for axis in (1, 0))
    keys = []
    for base in range(0, WIDE * share, 8):
        at = row + base
        block = sum((at >= share * i).astype(jnp.int32) for i in range(1, WIDE))
        own = token == (position ^ block) * share + (at - block * share)
        key = jnp.sum(jnp.where(own, ids[...].astype(jnp.float32), 0.0), axis=1, keepdims=True)
        keys.append(jnp.broadcast_to(key, (8, 128)))
    keys.append(jnp.zeros((8, marks.shape[1] - 128 * len(keys)), jnp.float32))
    marks[...] = jnp.concatenate(keys, axis=1).astype(jnp.bfloat16)


def relay_kernel(own, far, marks, pair, marked):
    slabs = own.shape[0]
    for target in (pair, marked):
        target[0:slabs] = own[...]
        target[slabs : 2 * slabs] = far[...]
    marked[2 * slabs] = marks[...]


WIDE, NEXT, FAR = 4, 1, 2
GATE, UP, DOWN = range(3)
WHOLE_STRIP = (GATE, UP, DOWN)
CHUNKS = 8


def start_loads(pieces, groups, sources, targets, sem):
    copies = []
    for i, (kind, strip) in enumerate(pieces):
        target = targets[i]
        width = target.shape[0 if kind == DOWN else 1]
        owner = lax.axis_index("narrow") ^ strip
        start = pl.multiple_of((owner * groups + lax.axis_index("groups")) * width, width)
        source = sources[kind]
        source = source.at[pl.ds(start, width), :] if kind == DOWN else source.at[:, pl.ds(start, width)]
        size = target.shape[0] // CHUNKS
        for c in range(CHUNKS):
            span = slice(c * size, (c + 1) * size)
            copies.append(pltpu.make_async_copy(source.at[span, :], target.at[span, :], sem.at[i, c]))
    for copy in copies:
        copy.start()
    return copies


def load_kernel(pieces, groups, *refs):
    count = len(pieces)
    for copy in start_loads(pieces, groups, refs[:3], refs[-1 - count : -1], refs[-1]):
        copy.wait()


def loading(body, pieces, groups, outs, own_copy=None):
    count = len(pieces)

    def kernel(*refs):
        sources, rest = refs[:3], refs[3:]
        at = len(rest) - outs[1] - 1 - count
        targets, sem = rest[at : at + count], rest[at + count + outs[1]]
        own = rest[:at] + rest[at + count : at + count + outs[1]]
        if own_copy is not None:
            own_copy(*own).start()
        copies = start_loads(pieces, groups, sources, targets, sem)

        @pl.when(lax.axis_index("narrow") >= 0)
        def _():
            body(*own)

        for copy in copies:
            copy.wait()

    return kernel


def strip_parts(tokens, cotans, gate, up, down, put):
    tile = 256
    for start in range(0, gate.shape[1], tile):
        span = slice(start, start + tile)
        put(GATE, span, jnp.dot(tokens[...], gate[:, span], preferred_element_type=jnp.float32))
        put(UP, span, jnp.dot(tokens[...], up[:, span], preferred_element_type=jnp.float32))
        put(DOWN, span, contract_rows(cotans[...], down[span, :]))


def forward_kernel(tokens, cotans, gate, up, down, *refs):
    out = refs[-1]

    def put(kind, span, part):
        out[kind, :, span] = part.astype(out.dtype)

    strip_parts(tokens, cotans, gate, up, down, put)


def join_kernel(own, arrived, out):
    out[...] = (own[...] + arrived[...]).astype(out.dtype)


def first_kernel(share, marked, beside, other, diagonal, gate, up, down, *refs):
    tokens, cotans, part, rows, cots = refs[-5:]
    slabs, half = 4 * share // 8, rows.shape[1] // 2
    for source, places in (
        (marked, (0, FAR)),
        (beside, (NEXT, FAR ^ NEXT)),
        (other, (WIDE, WIDE + FAR)),
        (diagonal, (WIDE + NEXT, WIDE + (FAR ^ NEXT))),
    ):
        for i, place in enumerate(places):
            packed = source[i * slabs : (i + 1) * slabs].astype(jnp.float32).reshape(4 * share, half)
            for j, target in enumerate((rows, rows, cots, cots)):
                span = slice((j % 2) * half, (j % 2 + 1) * half)
                target[place * share : (place + 1) * share, span] = packed[j * share : (j + 1) * share]
    tokens[...] = rows[...].astype(jnp.bfloat16)
    cotans[...] = cots[...].astype(jnp.bfloat16)
    forward_kernel(tokens, cotans, gate, up, down, part)


def own_strip_kernel(groups, *refs):
    sources, (tokens, cotans, up, down) = refs[:3], refs[3:7]
    out, gate, sem = refs[-3:]
    copies = start_loads([(GATE, 0)], groups, sources, [gate], sem)

    @pl.when(lax.axis_index("narrow") >= 0)
    def _():
        out[UP] = jnp.dot(tokens[...], up[...], preferred_element_type=jnp.float32)
        out[DOWN] = contract_rows(cotans[...], down[...])

    for copy in copies:
        copy.wait()
    out[GATE] = jnp.dot(tokens[...], gate[...], preferred_element_type=jnp.float32)


def to_tiles(values, tiles, first):
    rows, columns = values.shape
    values = values.astype(jnp.float32)
    for i in range(rows // 8):
        for j in range(columns // 128):
            tile = values[8 * i : 8 * i + 8, 128 * j : 128 * j + 128]
            tiles[first + i * (columns // 128) + j] = tile.astype(tiles.dtype)


def from_tiles(tiles, first, rows, columns):
    across = columns // 128
    parts = [
        jnp.concatenate([tiles[first + i * across + j].astype(jnp.float32) for j in range(across)], axis=1)
        for i in range(rows // 8)
    ]
    return jnp.concatenate(parts, axis=0).astype(tiles.dtype)


def middle_kernel(groups, *refs):
    own, arrived, crossed, scale, relayed, other_relayed = refs[:6]
    message, tiles, near_gate, near_up, grads, other_grads, stage = refs[-7:]
    _, tokens, width = own.shape
    narrow, group = lax.axis_index("narrow"), lax.axis_index("groups")
    sums = [own[i] + arrived[i].astype(jnp.float32) + crossed[i].astype(jnp.float32) for i in range(3)]
    start = pl.multiple_of((narrow * groups + group) * width, width)
    product, d_gate, d_up = local_grads(*sums, scale[:, pl.ds(start, width)])
    message[0:tokens, :] = d_gate
    message[tokens : 2 * tokens, :] = d_up
    near_gate[0:tokens, :] = d_gate
    near_up[...] = d_up
    count = tokens // 8 * (width // 128)
    to_tiles(d_gate, tiles, 0)
    to_tiles(d_up, tiles, count)
    half = tokens // groups
    for side, (source, target) in enumerate(((relayed, grads), (other_relayed, other_grads))):
        marks = source[source.shape[0] - 1].astype(jnp.float32)
        seq = jnp.concatenate(
            [
                jnp.concatenate([marks[:, k * 128 : (k + 1) * 128]] * (width // 128), axis=1)
                for k in range(half // 8)
            ],
            axis=0,
        )
        part = product[side * half : (side + 1) * half]
        for e in range(SEQS):
            total = jnp.sum(jnp.where(seq == float(e), part, 0.0), axis=0, keepdims=True)
            target[e : e + 1, :] = total
            stage[side * SEQS + e : side * SEQS + e + 1, :] = total
    every = stage[...]
    squares = jnp.broadcast_to(jnp.sum(every * every, axis=1, keepdims=True), every.shape)
    tail = jnp.concatenate(split_high(squares), axis=0).astype(jnp.bfloat16)
    message[2 * tokens :, :] = tail
    for i, rows in enumerate(split_high(squares)):
        tiles[2 * count + i] = rows[:, 0:128].astype(jnp.bfloat16)
    near_gate[tokens:, :] = tail


TILE = 512


def backward_part(grads, gate, up, start):
    d_gate, d_up = grads
    gate_term = contract_rows(gate[start : start + TILE, :], d_gate)
    return gate_term + contract_rows(up[start : start + TILE, :], d_up)


def halves(message):
    tokens = (message.shape[0] - 16) // 2
    return message[0:tokens, :], message[tokens : 2 * tokens, :]


def halves_of_tiles(tiles, width):
    count = (tiles.shape[0] - 2) // 2
    rows = count // (width // 128) * 8
    return from_tiles(tiles, 0, rows, width), from_tiles(tiles, count, rows, width)


def squares_of(message):
    if len(message.shape) == 3:
        tiles = message.shape[0]
        return message[tiles - 2].astype(jnp.float32) + message[tiles - 1].astype(jnp.float32)
    rows = message[message.shape[0] - 16 :, 0:128].astype(jnp.float32)
    return rows[0:8] + rows[8:16]


def backward_first_kernel(message, gate, up, total):
    for start in range(0, total.shape[0], TILE):
        total[start : start + TILE, :] = backward_part(halves(message), gate, up, start)


def backward_near_kernel(d_gate, d_up, gate, up, before, total):
    tokens = d_up.shape[0]
    for start in range(0, total.shape[0], TILE):
        part = backward_part((d_gate[0:tokens, :], d_up[...]), gate, up, start)
        total[start : start + TILE, :] = before[start : start + TILE, :] + part


def backward_next_kernel(tiles, gate, up, before, total):
    grads = halves_of_tiles(tiles, gate.shape[1])
    for start in range(0, total.shape[0], TILE):
        part = backward_part(grads, gate, up, start)
        total[start : start + TILE, :] = before[start : start + TILE, :] + part


def split_high(values):
    high = values.astype(jnp.bfloat16).astype(jnp.float32)
    return high, values - high


def backward_last_kernel(share, tiles, gate, up, before, *refs):
    others, other_grads, (own, own_squares), sends, (total, stage) = refs[:3], refs[3], refs[4:6], refs[6:9], refs[9:]
    tokens, features = total.shape
    side = features // 2
    grads = halves_of_tiles(tiles, gate.shape[1])
    for start in range(0, features, TILE):
        part = before[start : start + TILE, :] + backward_part(grads, gate, up, start)
        total[:, start : start + TILE] = part.T
    squares = sum(squares_of(ref) for ref in (tiles,) + others)
    own_squares[...] = squares
    tails = split_high(squares)
    slabs = 4 * share // 8
    for target, group, nearby in zip((own,) + tuple(sends), (0, 0, 1, 1), (0, NEXT, 0, NEXT)):
        rows = own if target is own else stage
        for i, place in enumerate((nearby, nearby ^ FAR)):
            at = (group * WIDE + place) * share
            for j in range(2):
                to = (2 * i + j) * share
                rows[to : to + share, :] = total[at : at + share, j * side : (j + 1) * side]
        if target is not own:
            for k in range(slabs):
                target[k, :, 0:side] = stage[8 * k : 8 * k + 8, :].astype(jnp.bfloat16)
                if target is sends[0]:
                    tail = tails[k] if k < 2 else jnp.zeros_like(squares)
                    target[k, :, side:] = tail.astype(jnp.bfloat16)
    width = other_grads.shape[1]
    stage[0:8, :] = jnp.zeros((8, side), jnp.float32)
    for i, rows in enumerate(split_high(other_grads[...])):
        stage[i * SEQS : (i + 1) * SEQS, 0:width] = rows
    for i, rows in enumerate(tails):
        stage[0:8, width + i * 128 : width + (i + 1) * 128] = rows
    for target in sends[1:]:
        target[slabs] = stage[0:8, :].astype(jnp.bfloat16)


def combine_kernel(share, own, own_squares, diagonal, across, beside, *refs):
    kept_rows, other_grads, send, total, stage = refs
    slabs, side = beside.shape[0], own.shape[1]
    width = other_grads.shape[1]
    for k in range(slabs):
        rows = own[8 * k : 8 * k + 8, :] + across[k].astype(jnp.float32)
        for ref in (beside, diagonal):
            rows = rows + ref[k, :, 0:side].astype(jnp.float32)
        total[8 * k : 8 * k + 8, :] = rows
    tail = across[slabs].astype(jnp.float32)
    other_grads[...] = tail[0:SEQS, 0:width] + tail[SEQS : 2 * SEQS, 0:width]
    same, turned = own_squares[...], jnp.zeros(own_squares.shape, jnp.float32)
    for k in range(2):
        same = same + beside[k, :, side:].astype(jnp.float32)
        for rows in (tail, diagonal[slabs].astype(jnp.float32)):
            turned = turned + rows[:, width + k * 128 : width + (k + 1) * 128]
    squares = same[0:SEQS] + turned[SEQS : 2 * SEQS]
    count = 2 * share
    kept_rows[...] = jnp.zeros_like(kept_rows)
    stage[...] = jnp.zeros_like(stage)
    kept_rows[0:count, :] = total[0:count, :]
    stage[0:count, :] = total[count : 2 * count, :]
    high, low = split_high(squares)
    for e in range(SEQS):
        span = slice(e * 128, (e + 1) * 128)
        for ref in (kept_rows, stage):
            ref[count : count + 1, span] = high[e : e + 1]
            ref[count + 1 : count + 2, span] = low[e : e + 1]
    for k in range(2):
        send[k] = stage[8 * k : 8 * k + 8, :].astype(jnp.bfloat16)


def last_kernel(share, own, arrived, grads, other_grads, input_grad, example_grads, norms, stage):
    side, width = own.shape[1], grads.shape[1]
    group = lax.axis_index("groups")
    for k in range(2):
        stage[8 * k : 8 * k + 8, :] = own[8 * k : 8 * k + 8, :] + arrived[k].astype(jnp.float32)
    for j in range(2):
        rows = stage[j * share : (j + 1) * share, :]
        input_grad[:, j * side : (j + 1) * side] = rows.astype(jnp.bfloat16)
    example_grads[:, pl.ds(pl.multiple_of(group * width, width), width)] = grads[...]
    example_grads[:, pl.ds(pl.multiple_of((1 - group) * width, width), width)] = other_grads[...]
    count = 2 * share
    squares = stage[count : count + 1, 0 : SEQS * 128] + stage[count + 1 : count + 2, 0 : SEQS * 128]
    roots = jnp.sqrt(squares)
    for e in range(SEQS):
        norms[e] = jnp.max(roots[:, e * 128 : (e + 1) * 128])


def shared(inputs, cotangent, gate_weight, up_weight, down_weight, ia3_scale, seq_ids):
    groups, wide, strips = lax.axis_size("groups"), lax.axis_size("wide"), lax.axis_size("narrow")
    share, features = inputs.shape
    width = gate_weight.shape[1] // (strips * groups)
    half = share * wide
    tokens = half * groups
    f32, bf16 = jnp.float32, jnp.bfloat16
    slabs, side = 4 * share // 8, features // 2
    weights = tuple(
        pltpu.with_memory_space_constraint(weight, pltpu.HBM)
        for weight in (gate_weight, up_weight, down_weight)
    )
    weight_shapes = [
        pltpu.VMEM((features, width), bf16),
        pltpu.VMEM((features, width), bf16),
        pltpu.VMEM((width, features), bf16),
    ]
    kept = {}

    def load(name, pieces, after=()):
        args = weights + tuple(after)
        arrays = call(
            functools.partial(load_kernel, pieces, groups),
            name,
            [weight_shapes[kind] for kind, _ in pieces],
            args,
            {i: pltpu.HBM if i < 3 else pl.ANY for i in range(len(args))},
            [pltpu.SemaphoreType.DMA((len(pieces), CHUNKS))],
        )
        kept.update(zip(pieces, arrays))

    def call_loading(body, name, pieces, outs, args, scratch=(), spaces=None, own_copy=None):
        made = call(
            loading(body, pieces, groups, (len(outs), len(outs) + len(scratch)), own_copy),
            name,
            [weight_shapes[kind] for kind, _ in pieces] + outs,
            list(weights) + args,
            {**{i: pltpu.HBM for i in range(3)}, **(spaces or {})},
            list(scratch) + [pltpu.SemaphoreType.DMA((len(pieces), CHUNKS))],
        )
        kept.update(zip(pieces, made))
        return made[len(pieces) :]

    def hold(strip, kinds=WHOLE_STRIP):
        return [held(kept[kind, strip]) for kind in kinds]

    packed = call(
        pack_kernel,
        "pack",
        pltpu.VMEM((slabs, 8, features // 2), bf16),
        [pltpu.with_memory_space_constraint(array, pltpu.HBM) for array in (inputs, cotangent)],
        scratch=[pltpu.VMEM((4 * share, features // 2), f32)],
    )
    far = exchange(packed, "wide", FAR)
    (marks,) = call_loading(
        functools.partial(keys_kernel, share),
        "load_a",
        [(kind, 3) for kind in WHOLE_STRIP],
        [pltpu.VMEM((8, side), bf16)],
        [pltpu.with_memory_space_constraint(seq_ids[None, :], pltpu.HBM)],
        [pltpu.VMEM((1, half), jnp.int32), pltpu.SemaphoreType.DMA((1,))],
        {3: pltpu.HBM},
        fetch_ids,
    )
    pair, marked = call(
        relay_kernel,
        "relay",
        [pltpu.VMEM((2 * slabs, 8, side), bf16), pltpu.VMEM((2 * slabs + 1, 8, side), bf16)],
        [packed, far, marks],
    )
    diagonal = exchange(marked, ("groups", "wide"), WIDE + NEXT)
    other_marked = exchange(marked, "groups", 1)
    beside = exchange(pair, "wide", NEXT)
    load("load_b", [(kind, 2) for kind in WHOLE_STRIP], [pair])

    part = pltpu.VMEM((3, tokens, width), f32)
    near_shape = pltpu.VMEM((3, tokens, width), bf16)
    tokens_all, cotans_all, diagonal = call_loading(
        functools.partial(first_kernel, share),
        "forward_3",
        [(GATE, 1), (DOWN, 1)],
        [pltpu.VMEM((tokens, features), bf16)] * 2 + [part],
        [marked, beside, other_marked, diagonal] + hold(3) + hold(2, [GATE]),
        [pltpu.VMEM((tokens, features), f32)] * 2,
    )
    panel = [tokens_all, cotans_all]
    diagonal = exchange(diagonal, "narrow", 1)
    (second,) = call_loading(forward_kernel, "forward_2", [(UP, 1)], [part], panel + hold(2))
    crossing = call(join_kernel, "join", near_shape, [held(second), diagonal])
    crossed = exchange(crossing, "narrow", 2)
    (near,) = call_loading(
        forward_kernel, "forward_1", [(UP, 0), (DOWN, 0)], [near_shape], panel + hold(1) + [held(crossing)]
    )
    near = exchange(near, "narrow", 1)
    own_part, kept[GATE, 0] = call(
        functools.partial(own_strip_kernel, groups),
        "forward_0",
        [part, weight_shapes[GATE]],
        list(weights) + panel + hold(0, [UP, DOWN]),
        {i: pltpu.HBM for i in range(3)},
        [pltpu.SemaphoreType.DMA((1, CHUNKS))],
    )

    resident = [array for s in range(strips) for array in hold(s, [GATE, UP])]
    message, tiles, near_gate, near_up, grads, other_grads = call(
        functools.partial(middle_kernel, groups),
        "middle",
        [
            pltpu.VMEM((2 * tokens + 16, width), bf16),
            pltpu.VMEM((2 * (tokens // 8) * (width // 128) + 2, 8, 128), bf16),
            pltpu.VMEM((tokens + 16, width), bf16),
            pltpu.VMEM((tokens, width), bf16),
            pltpu.VMEM((SEQS, width), f32),
            pltpu.VMEM((SEQS, width), f32),
        ],
        [own_part, near, crossed, ia3_scale[None, :], marked, other_marked] + resident,
        scratch=[pltpu.VMEM((groups * SEQS, width), f32)],
    )

    total = pltpu.VMEM((features, tokens), f32)
    near_gate, near_up = exchange(near_gate, "narrow", 1), exchange(near_up, "narrow", 1)
    message_2 = exchange(tiles, "narrow", 2)
    sums = call(backward_first_kernel, "backward_0", total, [message] + hold(0, [GATE, UP]))
    sums = call(backward_near_kernel, "backward_1", total, [near_gate, near_up] + hold(1, [GATE, UP]) + [sums])
    message_2, sums = lax.optimization_barrier((message_2, sums))
    message_3 = exchange(message_2, "narrow", 1)
    sums = call(backward_next_kernel, "backward_2", total, [message_2] + hold(2, [GATE, UP]) + [sums])
    block = pltpu.VMEM((slabs, 8, side + 128), bf16)
    own, own_squares, *sends = call(
        functools.partial(backward_last_kernel, share),
        "backward_3",
        [
            pltpu.VMEM((4 * share, side), f32),
            pltpu.VMEM((8, 128), f32),
            block,
            pltpu.VMEM((slabs + 1, 8, side), bf16),
            pltpu.VMEM((slabs + 1, 8, side), bf16),
        ],
        [message_3] + hold(3, [GATE, UP]) + [sums, message, near_gate, message_2, other_grads],
        scratch=[pltpu.VMEM((tokens, features), f32), pltpu.VMEM((4 * share, side), f32)],
    )
    across = exchange(sends[1], "groups", 1)
    beside = exchange(sends[0], "wide", NEXT)
    diagonal = exchange(sends[2], ("groups", "wide"), WIDE + NEXT)
    own, other_grads, send = call(
        functools.partial(combine_kernel, share),
        "combine",
        [pltpu.VMEM((16, side), f32), pltpu.VMEM((SEQS, width), f32), pltpu.VMEM((2, 8, side), bf16)],
        [own, own_squares, diagonal, across, beside],
        scratch=[pltpu.VMEM((4 * share, side), f32), pltpu.VMEM((16, side), f32)],
    )
    input_grad, example_grads, norms = call(
        functools.partial(last_kernel, share),
        "last",
        [
            jax.ShapeDtypeStruct((share, features), bf16),
            jax.ShapeDtypeStruct((SEQS, groups * width), f32),
            jax.ShapeDtypeStruct((SEQS,), f32),
        ],
        [own, exchange(send, "wide", FAR), grads, other_grads],
        scratch=[pltpu.VMEM((16, side), f32)],
        out_spaces={2: pltpu.SMEM},
    )
    return (example_grads, norms, input_grad)


def local(inputs, cotangent, gate_weight, up_weight, down_weight, ia3_scale, seq_ids):
    groups, wide, narrow = lax.axis_size("groups"), lax.axis_size("wide"), lax.axis_size("narrow")
    share, (features, hidden) = inputs.shape[0], gate_weight.shape
    width = hidden // (narrow * groups)
    fits = (
        groups == 2
        and narrow == 4
        and wide == WIDE
        and hidden % (narrow * groups * 256) == 0
        and features >= 2048
        and width <= features // 2 - 256
        and features % (2 * TILE) == 0
        and share in (4, 6)
        and (share * wide) % 8 == 0
        and share * wide <= 64
        and 3 * features * hidden // groups * 2 <= 40 << 20
    )
    plan = shared if fits else whole_block
    return plan(inputs, cotangent, gate_weight, up_weight, down_weight, ia3_scale, seq_ids)


def solution(mesh):
    return jax.shard_map(
        local,
        mesh=mesh,
        in_specs=(
            P(("groups", "wide"), "narrow"),
            P(("groups", "wide"), "narrow"),
            P("narrow", "wide"),
            P("narrow", "wide"),
            P("wide", "narrow"),
            P("wide"),
            P("groups"),
        ),
        out_specs=(P("groups", ("wide", "narrow")), P("groups"), P(("groups", "wide"), "narrow")),
        check_vma=False,
    )
```

```python
import functools
import math

import jax
import jax.numpy as jnp
from jax import lax
from jax.experimental import pallas as pl
from jax.experimental.pallas import tpu as pltpu
from jax.sharding import PartitionSpec as P

SEQS = 4
KERNEL_VMEM = 6 << 20


def contract_rows(left, right):
    return lax.dot_general(
        left, right, (((1,), (1,)), ((), ())), preferred_element_type=jnp.float32
    )


def local_grads(gate_pre, up_pre, mid_grad, scale_part):
    sigmoid_gate = jax.nn.sigmoid(gate_pre)
    activation = gate_pre * sigmoid_gate
    hidden = activation * up_pre
    scaled = scale_part * mid_grad
    d_up = (scaled * activation).astype(jnp.bfloat16)
    d_gate = (scaled * up_pre * sigmoid_gate * (1.0 + gate_pre * (1.0 - sigmoid_gate))).astype(
        jnp.bfloat16
    )
    return (hidden * mid_grad, d_gate, d_up)


def whole_block(inputs, cotangent, gate_weight, up_weight, down_weight, ia3_scale, seq_ids):
    panel_inputs = lax.all_gather(inputs, "wide", axis=0, tiled=True)
    panel_cotangent = lax.all_gather(cotangent, "wide", axis=0, tiled=True)
    gate_part = jnp.dot(panel_inputs, gate_weight, preferred_element_type=jnp.float32)
    up_part = jnp.dot(panel_inputs, up_weight, preferred_element_type=jnp.float32)
    mid_part = contract_rows(panel_cotangent, down_weight)
    quarter = gate_weight.shape[1] // lax.axis_size("narrow")
    position = lax.axis_index("narrow")
    onehot_full = (seq_ids[None, :] == jnp.arange(SEQS, dtype=jnp.int32)[:, None]).astype(
        jnp.float32
    )
    gate_pre, up_pre, mid_grad = (
        lax.psum_scatter(gate_part, "narrow", scatter_dimension=1, tiled=True),
        lax.psum_scatter(up_part, "narrow", scatter_dimension=1, tiled=True),
        lax.psum_scatter(mid_part, "narrow", scatter_dimension=1, tiled=True),
    )
    scale_part = lax.dynamic_slice_in_dim(ia3_scale, position * quarter, quarter, 0)
    product, d_gate, d_up = local_grads(gate_pre, up_pre, mid_grad, scale_part[None, :])
    example_grads = jnp.dot(onehot_full, product, precision=lax.Precision.HIGHEST)
    whole_gate, whole_up = (
        lax.all_gather(d_gate, "narrow", axis=1, tiled=True),
        lax.all_gather(d_up, "narrow", axis=1, tiled=True),
    )
    squares = lax.psum(jnp.sum(example_grads * example_grads, axis=1), ("wide", "narrow"))
    grad_norms = jnp.sqrt(squares)
    input_grad = lax.psum_scatter(
        contract_rows(whole_gate, gate_weight) + contract_rows(whole_up, up_weight),
        "wide",
        scatter_dimension=0,
        tiled=True,
    ).astype(jnp.bfloat16)
    return (example_grads, grad_norms, input_grad)


def exchange(array, axis, step):
    axes = axis if isinstance(axis, tuple) else (axis,)
    size = math.prod(lax.axis_size(name) for name in axes)
    return lax.ppermute(array, axes, [(i, i ^ step) for i in range(size)])


def held(array):
    return pltpu.with_memory_space_constraint(array, pltpu.VMEM)


def call(body, name, outs, args, spaces=None, scratch=(), out_spaces=None):
    spaces, out_spaces = spaces or {}, out_spaces or {}
    many = isinstance(outs, list)
    out_specs = [
        pl.BlockSpec(memory_space=out_spaces.get(i, pltpu.VMEM)) for i in range(len(outs) if many else 1)
    ]
    return pl.pallas_call(
        body,
        out_shape=outs,
        in_specs=[pl.BlockSpec(memory_space=spaces.get(i, pltpu.VMEM)) for i in range(len(args))],
        out_specs=out_specs if many else out_specs[0],
        scratch_shapes=list(scratch),
        compiler_params=pltpu.CompilerParams(vmem_limit_bytes=KERNEL_VMEM),
        cost_estimate=pl.CostEstimate(flops=1000, bytes_accessed=1000, transcendentals=0),
        name=name,
    )(*args)


def pack_kernel(inputs, cotangent, out, stage):
    share, features = inputs.shape
    half = features // 2
    for i, ref in enumerate((inputs, cotangent)):
        rows = ref[...].astype(jnp.float32)
        for j in range(2):
            stage[(2 * i + j) * share : (2 * i + j + 1) * share, :] = rows[:, j * half : (j + 1) * half]
    for k in range(out.shape[0]):
        out[k] = stage[8 * k : 8 * k + 8, :].astype(jnp.bfloat16)


def fetch_ids(ids_in, marks, ids, sem):
    return pltpu.make_async_copy(ids_in, ids, sem.at[0])


def keys_kernel(share, ids_in, marks, ids, sem):
    fetch_ids(ids_in, marks, ids, sem).wait()
    position, count = lax.axis_index("wide"), ids.shape[1]
    shape = (8, count)
    token, row = (lax.broadcasted_iota(jnp.int32, shape, axis) for axis in (1, 0))
    keys = []
    for base in range(0, WIDE * share, 8):
        at = row + base
        block = sum((at >= share * i).astype(jnp.int32) for i in range(1, WIDE))
        own = token == (position ^ block) * share + (at - block * share)
        key = jnp.sum(jnp.where(own, ids[...].astype(jnp.float32), 0.0), axis=1, keepdims=True)
        keys.append(jnp.broadcast_to(key, (8, 128)))
    keys.append(jnp.zeros((8, marks.shape[1] - 128 * len(keys)), jnp.float32))
    marks[...] = jnp.concatenate(keys, axis=1).astype(jnp.bfloat16)


def relay_kernel(own, far, marks, pair, marked):
    slabs = own.shape[0]
    for target in (pair, marked):
        target[0:slabs] = own[...]
        target[slabs : 2 * slabs] = far[...]
    marked[2 * slabs] = marks[...]


WIDE, NEXT, FAR = 4, 1, 2
GATE, UP, DOWN = range(3)
WHOLE_STRIP = (GATE, UP, DOWN)
CHUNKS = 4


def start_loads(pieces, groups, sources, targets, sem):
    copies = []
    for i, (kind, strip) in enumerate(pieces):
        target = targets[i]
        width = target.shape[0 if kind == DOWN else 1]
        owner = lax.axis_index("narrow") ^ strip
        start = pl.multiple_of((owner * groups + lax.axis_index("groups")) * width, width)
        source = sources[kind]
        source = source.at[pl.ds(start, width), :] if kind == DOWN else source.at[:, pl.ds(start, width)]
        size = target.shape[0] // CHUNKS
        for c in range(CHUNKS):
            span = slice(c * size, (c + 1) * size)
            copies.append(pltpu.make_async_copy(source.at[span, :], target.at[span, :], sem.at[i, c]))
    for copy in copies:
        copy.start()
    return copies


def load_kernel(pieces, groups, *refs):
    count = len(pieces)
    for copy in start_loads(pieces, groups, refs[:3], refs[-1 - count : -1], refs[-1]):
        copy.wait()


def loading(body, pieces, groups, outs, own_copy=None):
    count = len(pieces)

    def kernel(*refs):
        sources, rest = refs[:3], refs[3:]
        at = len(rest) - outs[1] - 1 - count
        targets, sem = rest[at : at + count], rest[at + count + outs[1]]
        own = rest[:at] + rest[at + count : at + count + outs[1]]
        if own_copy is not None:
            own_copy(*own).start()
        copies = start_loads(pieces, groups, sources, targets, sem)

        @pl.when(lax.axis_index("narrow") >= 0)
        def _():
            body(*own)

        for copy in copies:
            copy.wait()

    return kernel


def strip_parts(tokens, cotans, gate, up, down, put):
    tile = 256
    for start in range(0, gate.shape[1], tile):
        span = slice(start, start + tile)
        put(GATE, span, jnp.dot(tokens[...], gate[:, span], preferred_element_type=jnp.float32))
        put(UP, span, jnp.dot(tokens[...], up[:, span], preferred_element_type=jnp.float32))
        put(DOWN, span, contract_rows(cotans[...], down[span, :]))


def forward_kernel(tokens, cotans, gate, up, down, *refs):
    out = refs[-1]

    def put(kind, span, part):
        out[kind, :, span] = part.astype(out.dtype)

    strip_parts(tokens, cotans, gate, up, down, put)


def join_kernel(own, arrived, out):
    out[...] = (own[...] + arrived[...]).astype(out.dtype)


def first_kernel(share, marked, beside, other, diagonal, gate, up, down, *refs):
    tokens, cotans, part, rows, cots = refs[-5:]
    slabs, half = 4 * share // 8, rows.shape[1] // 2
    for source, places in (
        (marked, (0, FAR)),
        (beside, (NEXT, FAR ^ NEXT)),
        (other, (WIDE, WIDE + FAR)),
        (diagonal, (WIDE + NEXT, WIDE + (FAR ^ NEXT))),
    ):
        for i, place in enumerate(places):
            packed = source[i * slabs : (i + 1) * slabs].astype(jnp.float32).reshape(4 * share, half)
            for j, target in enumerate((rows, rows, cots, cots)):
                span = slice((j % 2) * half, (j % 2 + 1) * half)
                target[place * share : (place + 1) * share, span] = packed[j * share : (j + 1) * share]
    tokens[...] = rows[...].astype(jnp.bfloat16)
    cotans[...] = cots[...].astype(jnp.bfloat16)
    forward_kernel(tokens, cotans, gate, up, down, part)


def own_strip_kernel(groups, *refs):
    sources, (tokens, cotans, up, down) = refs[:3], refs[3:7]
    out, gate, sem = refs[-3:]
    copies = start_loads([(GATE, 0)], groups, sources, [gate], sem)

    @pl.when(lax.axis_index("narrow") >= 0)
    def _():
        out[UP] = jnp.dot(tokens[...], up[...], preferred_element_type=jnp.float32)
        out[DOWN] = contract_rows(cotans[...], down[...])

    for copy in copies:
        copy.wait()
    out[GATE] = jnp.dot(tokens[...], gate[...], preferred_element_type=jnp.float32)


def to_tiles(values, tiles, first):
    rows, columns = values.shape
    values = values.astype(jnp.float32)
    for i in range(rows // 8):
        for j in range(columns // 128):
            tile = values[8 * i : 8 * i + 8, 128 * j : 128 * j + 128]
            tiles[first + i * (columns // 128) + j] = tile.astype(tiles.dtype)


def from_tiles(tiles, first, rows, columns):
    across = columns // 128
    parts = [
        jnp.concatenate([tiles[first + i * across + j].astype(jnp.float32) for j in range(across)], axis=1)
        for i in range(rows // 8)
    ]
    return jnp.concatenate(parts, axis=0).astype(tiles.dtype)


def middle_kernel(groups, *refs):
    own, arrived, crossed, scale, relayed, other_relayed = refs[:6]
    message, tiles, near_tiles, grads, other_grads, stage = refs[-6:]
    _, tokens, width = own.shape
    narrow, group = lax.axis_index("narrow"), lax.axis_index("groups")
    sums = [own[i] + arrived[i].astype(jnp.float32) + crossed[i].astype(jnp.float32) for i in range(3)]
    start = pl.multiple_of((narrow * groups + group) * width, width)
    product, d_gate, d_up = local_grads(*sums, scale[:, pl.ds(start, width)])
    message[0:tokens, :] = d_gate
    message[tokens : 2 * tokens, :] = d_up
    count = tokens // 8 * (width // 128)
    for target in (tiles, near_tiles):
        to_tiles(d_gate, target, 0)
        to_tiles(d_up, target, count)
    half = tokens // groups
    for side, (source, target) in enumerate(((relayed, grads), (other_relayed, other_grads))):
        marks = source[source.shape[0] - 1].astype(jnp.float32)
        seq = jnp.concatenate(
            [
                jnp.concatenate([marks[:, k * 128 : (k + 1) * 128]] * (width // 128), axis=1)
                for k in range(half // 8)
            ],
            axis=0,
        )
        part = product[side * half : (side + 1) * half]
        for e in range(SEQS):
            total = jnp.sum(jnp.where(seq == float(e), part, 0.0), axis=0, keepdims=True)
            target[e : e + 1, :] = total
            stage[side * SEQS + e : side * SEQS + e + 1, :] = total
    every = stage[...]
    squares = jnp.broadcast_to(jnp.sum(every * every, axis=1, keepdims=True), every.shape)
    tail = jnp.concatenate(split_high(squares), axis=0).astype(jnp.bfloat16)
    message[2 * tokens :, :] = tail
    for i, rows in enumerate(split_high(squares)):
        for target in (tiles, near_tiles):
            target[2 * count + i] = rows[:, 0:128].astype(jnp.bfloat16)
    tiles[2 * count + 2] = jnp.zeros((8, 128), jnp.bfloat16)


TILE = 512


def backward_part(grads, gate, up, start):
    d_gate, d_up = grads
    gate_term = contract_rows(gate[start : start + TILE, :], d_gate)
    return gate_term + contract_rows(up[start : start + TILE, :], d_up)


def halves(message):
    tokens = (message.shape[0] - 16) // 2
    return message[0:tokens, :], message[tokens : 2 * tokens, :]


def halves_of_tiles(tiles, width):
    count = (tiles.shape[0] - 2) // 2
    rows = count // (width // 128) * 8
    return from_tiles(tiles, 0, rows, width), from_tiles(tiles, count, rows, width)


def squares_of(message):
    if len(message.shape) == 3:
        first = (message.shape[0] - 2) // 2 * 2
        return message[first].astype(jnp.float32) + message[first + 1].astype(jnp.float32)
    rows = message[message.shape[0] - 16 :, 0:128].astype(jnp.float32)
    return rows[0:8] + rows[8:16]


def backward_first_kernel(message, gate, up, total):
    for start in range(0, total.shape[0], TILE):
        total[start : start + TILE, :] = backward_part(halves(message), gate, up, start)


def backward_next_kernel(tiles, gate, up, before, total):
    grads = halves_of_tiles(tiles, gate.shape[1])
    for start in range(0, total.shape[0], TILE):
        part = backward_part(grads, gate, up, start)
        total[start : start + TILE, :] = before[start : start + TILE, :] + part


def split_high(values):
    high = values.astype(jnp.bfloat16).astype(jnp.float32)
    return high, values - high


def backward_last_kernel(share, tiles, gate, up, before, *refs):
    others, other_grads, (own, own_squares), sends, (total, stage) = refs[:3], refs[3], refs[4:6], refs[6:9], refs[9:]
    tokens, features = total.shape
    side = features // 2
    grads = halves_of_tiles(tiles, gate.shape[1])
    for start in range(0, features, TILE):
        part = before[start : start + TILE, :] + backward_part(grads, gate, up, start)
        total[:, start : start + TILE] = part.T
    squares = sum(squares_of(ref) for ref in (tiles,) + others)
    own_squares[...] = squares
    tails = split_high(squares)
    slabs = 4 * share // 8
    for target, group, nearby in zip((own,) + tuple(sends), (0, 0, 1, 1), (0, NEXT, 0, NEXT)):
        rows = own if target is own else stage
        for i, place in enumerate((nearby, nearby ^ FAR)):
            at = (group * WIDE + place) * share
            for j in range(2):
                to = (2 * i + j) * share
                rows[to : to + share, :] = total[at : at + share, j * side : (j + 1) * side]
        if target is not own:
            for k in range(slabs):
                target[k, :, 0:side] = stage[8 * k : 8 * k + 8, :].astype(jnp.bfloat16)
                if target.shape[2] > side:
                    tail = tails[k] if k < 2 else jnp.zeros_like(squares)
                    target[k, :, side:] = tail.astype(jnp.bfloat16)
    width = other_grads.shape[1]
    stage[0:8, :] = jnp.zeros((8, side), jnp.float32)
    for i, rows in enumerate(split_high(other_grads[...])):
        stage[i * SEQS : (i + 1) * SEQS, 0:width] = rows
    for i, rows in enumerate(tails):
        stage[0:8, width + i * 128 : width + (i + 1) * 128] = rows
    sends[1][slabs] = stage[0:8, :].astype(jnp.bfloat16)


def combine_kernel(share, own, own_squares, diagonal, across, beside, *refs):
    kept_rows, other_grads, send, total, stage = refs
    slabs, side = beside.shape[0], own.shape[1]
    width = other_grads.shape[1]
    for k in range(slabs):
        rows = own[8 * k : 8 * k + 8, :] + across[k].astype(jnp.float32)
        for ref in (beside, diagonal):
            rows = rows + ref[k, :, 0:side].astype(jnp.float32)
        total[8 * k : 8 * k + 8, :] = rows
    tail = across[slabs].astype(jnp.float32)
    other_grads[...] = tail[0:SEQS, 0:width] + tail[SEQS : 2 * SEQS, 0:width]
    same, turned = own_squares[...], tail[:, width : width + 128] + tail[:, width + 128 : width + 256]
    for k in range(2):
        same = same + beside[k, :, side:].astype(jnp.float32)
        turned = turned + diagonal[k, :, side:].astype(jnp.float32)
    squares = same[0:SEQS] + turned[SEQS : 2 * SEQS]
    count = 2 * share
    kept_rows[...] = jnp.zeros_like(kept_rows)
    stage[...] = jnp.zeros_like(stage)
    kept_rows[0:count, :] = total[0:count, :]
    stage[0:count, :] = total[count : 2 * count, :]
    high, low = split_high(squares)
    for e in range(SEQS):
        span = slice(e * 128, (e + 1) * 128)
        for ref in (kept_rows, stage):
            ref[count : count + 1, span] = high[e : e + 1]
            ref[count + 1 : count + 2, span] = low[e : e + 1]
    for k in range(2):
        send[k] = stage[8 * k : 8 * k + 8, :].astype(jnp.bfloat16)


def last_kernel(share, own, arrived, grads, other_grads, input_grad, example_grads, norms, stage):
    side, width = own.shape[1], grads.shape[1]
    group = lax.axis_index("groups")
    for k in range(2):
        stage[8 * k : 8 * k + 8, :] = own[8 * k : 8 * k + 8, :] + arrived[k].astype(jnp.float32)
    for j in range(2):
        rows = stage[j * share : (j + 1) * share, :]
        input_grad[:, j * side : (j + 1) * side] = rows.astype(jnp.bfloat16)
    example_grads[:, pl.ds(pl.multiple_of(group * width, width), width)] = grads[...]
    example_grads[:, pl.ds(pl.multiple_of((1 - group) * width, width), width)] = other_grads[...]
    count = 2 * share
    squares = stage[count : count + 1, 0 : SEQS * 128] + stage[count + 1 : count + 2, 0 : SEQS * 128]
    roots = jnp.sqrt(squares)
    for e in range(SEQS):
        norms[e] = jnp.max(roots[:, e * 128 : (e + 1) * 128])


def shared(inputs, cotangent, gate_weight, up_weight, down_weight, ia3_scale, seq_ids):
    groups, wide, strips = lax.axis_size("groups"), lax.axis_size("wide"), lax.axis_size("narrow")
    share, features = inputs.shape
    width = gate_weight.shape[1] // (strips * groups)
    half = share * wide
    tokens = half * groups
    f32, bf16 = jnp.float32, jnp.bfloat16
    slabs, side = 4 * share // 8, features // 2
    weights = tuple(
        pltpu.with_memory_space_constraint(weight, pltpu.HBM)
        for weight in (gate_weight, up_weight, down_weight)
    )
    weight_shapes = [
        pltpu.VMEM((features, width), bf16),
        pltpu.VMEM((features, width), bf16),
        pltpu.VMEM((width, features), bf16),
    ]
    kept = {}

    def load(name, pieces, after=()):
        args = weights + tuple(after)
        arrays = call(
            functools.partial(load_kernel, pieces, groups),
            name,
            [weight_shapes[kind] for kind, _ in pieces],
            args,
            {i: pltpu.HBM if i < 3 else pl.ANY for i in range(len(args))},
            [pltpu.SemaphoreType.DMA((len(pieces), CHUNKS))],
        )
        kept.update(zip(pieces, arrays))

    def call_loading(body, name, pieces, outs, args, scratch=(), spaces=None, own_copy=None):
        made = call(
            loading(body, pieces, groups, (len(outs), len(outs) + len(scratch)), own_copy),
            name,
            [weight_shapes[kind] for kind, _ in pieces] + outs,
            list(weights) + args,
            {**{i: pltpu.HBM for i in range(3)}, **(spaces or {})},
            list(scratch) + [pltpu.SemaphoreType.DMA((len(pieces), CHUNKS))],
        )
        kept.update(zip(pieces, made))
        return made[len(pieces) :]

    def hold(strip, kinds=WHOLE_STRIP):
        return [held(kept[kind, strip]) for kind in kinds]

    packed = call(
        pack_kernel,
        "pack",
        pltpu.VMEM((slabs, 8, features // 2), bf16),
        [pltpu.with_memory_space_constraint(array, pltpu.HBM) for array in (inputs, cotangent)],
        scratch=[pltpu.VMEM((4 * share, features // 2), f32)],
    )
    far = exchange(packed, "wide", FAR)
    (marks,) = call_loading(
        functools.partial(keys_kernel, share),
        "load_a",
        [(kind, 3) for kind in WHOLE_STRIP],
        [pltpu.VMEM((8, side), bf16)],
        [pltpu.with_memory_space_constraint(seq_ids[None, :], pltpu.HBM)],
        [pltpu.VMEM((1, half), jnp.int32), pltpu.SemaphoreType.DMA((1,))],
        {3: pltpu.HBM},
        fetch_ids,
    )
    pair, marked = call(
        relay_kernel,
        "relay",
        [pltpu.VMEM((2 * slabs, 8, side), bf16), pltpu.VMEM((2 * slabs + 1, 8, side), bf16)],
        [packed, far, marks],
    )
    diagonal = exchange(pair, ("groups", "wide"), WIDE + NEXT)
    other_marked = exchange(marked, "groups", 1)
    beside = exchange(pair, "wide", NEXT)
    load("load_b", [(kind, 2) for kind in WHOLE_STRIP], [pair])

    part = pltpu.VMEM((3, tokens, width), f32)
    near_shape = pltpu.VMEM((3, tokens, width), bf16)
    tokens_all, cotans_all, diagonal = call_loading(
        functools.partial(first_kernel, share),
        "forward_3",
        [(GATE, 1), (DOWN, 1)],
        [pltpu.VMEM((tokens, features), bf16)] * 2 + [part],
        [marked, beside, other_marked, diagonal] + hold(3) + hold(2, [GATE]),
        [pltpu.VMEM((tokens, features), f32)] * 2,
    )
    panel = [tokens_all, cotans_all]
    diagonal = exchange(diagonal, "narrow", 1)
    (second,) = call_loading(forward_kernel, "forward_2", [(UP, 1)], [part], panel + hold(2))
    crossing = call(join_kernel, "join", near_shape, [held(second), diagonal])
    crossed = exchange(crossing, "narrow", 2)
    (near,) = call_loading(
        forward_kernel, "forward_1", [(UP, 0), (DOWN, 0)], [near_shape], panel + hold(1) + [held(crossing)]
    )
    near = exchange(near, "narrow", 1)
    own_part, kept[GATE, 0] = call(
        functools.partial(own_strip_kernel, groups),
        "forward_0",
        [part, weight_shapes[GATE]],
        list(weights) + panel + hold(0, [UP, DOWN]),
        {i: pltpu.HBM for i in range(3)},
        [pltpu.SemaphoreType.DMA((1, CHUNKS))],
    )

    resident = [array for s in range(strips) for array in hold(s, [GATE, UP])]
    message, tiles, near_tiles, grads, other_grads = call(
        functools.partial(middle_kernel, groups),
        "middle",
        [
            pltpu.VMEM((2 * tokens + 16, width), bf16),
            pltpu.VMEM((2 * (tokens // 8) * (width // 128) + 3, 8, 128), bf16),
            pltpu.VMEM((2 * (tokens // 8) * (width // 128) + 2, 8, 128), bf16),
            pltpu.VMEM((SEQS, width), f32),
            pltpu.VMEM((SEQS, width), f32),
        ],
        [own_part, near, crossed, ia3_scale[None, :], marked, other_marked] + resident,
        scratch=[pltpu.VMEM((groups * SEQS, width), f32)],
    )

    total = pltpu.VMEM((features, tokens), f32)
    message_1 = exchange(near_tiles, "narrow", 1)
    message_2 = exchange(tiles, "narrow", 2)
    sums = call(backward_first_kernel, "backward_0", total, [message] + hold(0, [GATE, UP]))
    sums = call(backward_next_kernel, "backward_1", total, [message_1] + hold(1, [GATE, UP]) + [sums])
    message_2, sums = lax.optimization_barrier((message_2, sums))
    message_3 = exchange(message_2, "narrow", 1)
    sums = call(backward_next_kernel, "backward_2", total, [message_2] + hold(2, [GATE, UP]) + [sums])
    block = pltpu.VMEM((slabs, 8, side + 128), bf16)
    own, own_squares, *sends = call(
        functools.partial(backward_last_kernel, share),
        "backward_3",
        [
            pltpu.VMEM((4 * share, side), f32),
            pltpu.VMEM((8, 128), f32),
            block,
            pltpu.VMEM((slabs + 1, 8, side), bf16),
            block,
        ],
        [message_3] + hold(3, [GATE, UP]) + [sums, message, message_1, message_2, other_grads],
        scratch=[pltpu.VMEM((tokens, features), f32), pltpu.VMEM((4 * share, side), f32)],
    )
    across = exchange(sends[1], "groups", 1)
    beside = exchange(sends[0], "wide", NEXT)
    diagonal = exchange(sends[2], ("groups", "wide"), WIDE + NEXT)
    own, other_grads, send = call(
        functools.partial(combine_kernel, share),
        "combine",
        [pltpu.VMEM((16, side), f32), pltpu.VMEM((SEQS, width), f32), pltpu.VMEM((2, 8, side), bf16)],
        [own, own_squares, diagonal, across, beside],
        scratch=[pltpu.VMEM((4 * share, side), f32), pltpu.VMEM((16, side), f32)],
    )
    input_grad, example_grads, norms = call(
        functools.partial(last_kernel, share),
        "last",
        [
            jax.ShapeDtypeStruct((share, features), bf16),
            jax.ShapeDtypeStruct((SEQS, groups * width), f32),
            jax.ShapeDtypeStruct((SEQS,), f32),
        ],
        [own, exchange(send, "wide", FAR), grads, other_grads],
        scratch=[pltpu.VMEM((16, side), f32)],
        out_spaces={2: pltpu.SMEM},
    )
    return (example_grads, norms, input_grad)


def local(inputs, cotangent, gate_weight, up_weight, down_weight, ia3_scale, seq_ids):
    groups, wide, narrow = lax.axis_size("groups"), lax.axis_size("wide"), lax.axis_size("narrow")
    share, (features, hidden) = inputs.shape[0], gate_weight.shape
    width = hidden // (narrow * groups)
    fits = (
        groups == 2
        and narrow == 4
        and wide == WIDE
        and hidden % (narrow * groups * 256) == 0
        and features >= 2048
        and width <= features // 2 - 256
        and features % (2 * TILE) == 0
        and share in (4, 6)
        and (share * wide) % 8 == 0
        and share * wide <= 64
        and 3 * features * hidden // groups * 2 <= 40 << 20
    )
    plan = shared if fits else whole_block
    return plan(inputs, cotangent, gate_weight, up_weight, down_weight, ia3_scale, seq_ids)


def solution(mesh):
    return jax.shard_map(
        local,
        mesh=mesh,
        in_specs=(
            P(("groups", "wide"), "narrow"),
            P(("groups", "wide"), "narrow"),
            P("narrow", "wide"),
            P("narrow", "wide"),
            P("wide", "narrow"),
            P("wide"),
            P("groups"),
        ),
        out_specs=(P("groups", ("wide", "narrow")), P("groups"), P(("groups", "wide"), "narrow")),
        check_vma=False,
    )
```

```python
import functools
import math

import jax
import jax.numpy as jnp
from jax import lax
from jax.experimental import pallas as pl
from jax.experimental.pallas import tpu as pltpu
from jax.sharding import PartitionSpec as P

SEQS = 4
KERNEL_VMEM = 6 << 20


def contract_rows(left, right):
    return lax.dot_general(
        left, right, (((1,), (1,)), ((), ())), preferred_element_type=jnp.float32
    )


def local_grads(gate_pre, up_pre, mid_grad, scale_part):
    sigmoid_gate = jax.nn.sigmoid(gate_pre)
    activation = gate_pre * sigmoid_gate
    hidden = activation * up_pre
    scaled = scale_part * mid_grad
    d_up = (scaled * activation).astype(jnp.bfloat16)
    d_gate = (scaled * up_pre * sigmoid_gate * (1.0 + gate_pre * (1.0 - sigmoid_gate))).astype(
        jnp.bfloat16
    )
    return (hidden * mid_grad, d_gate, d_up)


def whole_block(inputs, cotangent, gate_weight, up_weight, down_weight, ia3_scale, seq_ids):
    panel_inputs = lax.all_gather(inputs, "wide", axis=0, tiled=True)
    panel_cotangent = lax.all_gather(cotangent, "wide", axis=0, tiled=True)
    gate_part = jnp.dot(panel_inputs, gate_weight, preferred_element_type=jnp.float32)
    up_part = jnp.dot(panel_inputs, up_weight, preferred_element_type=jnp.float32)
    mid_part = contract_rows(panel_cotangent, down_weight)
    quarter = gate_weight.shape[1] // lax.axis_size("narrow")
    position = lax.axis_index("narrow")
    onehot_full = (seq_ids[None, :] == jnp.arange(SEQS, dtype=jnp.int32)[:, None]).astype(
        jnp.float32
    )
    gate_pre, up_pre, mid_grad = (
        lax.psum_scatter(gate_part, "narrow", scatter_dimension=1, tiled=True),
        lax.psum_scatter(up_part, "narrow", scatter_dimension=1, tiled=True),
        lax.psum_scatter(mid_part, "narrow", scatter_dimension=1, tiled=True),
    )
    scale_part = lax.dynamic_slice_in_dim(ia3_scale, position * quarter, quarter, 0)
    product, d_gate, d_up = local_grads(gate_pre, up_pre, mid_grad, scale_part[None, :])
    example_grads = jnp.dot(onehot_full, product, precision=lax.Precision.HIGHEST)
    whole_gate, whole_up = (
        lax.all_gather(d_gate, "narrow", axis=1, tiled=True),
        lax.all_gather(d_up, "narrow", axis=1, tiled=True),
    )
    squares = lax.psum(jnp.sum(example_grads * example_grads, axis=1), ("wide", "narrow"))
    grad_norms = jnp.sqrt(squares)
    input_grad = lax.psum_scatter(
        contract_rows(whole_gate, gate_weight) + contract_rows(whole_up, up_weight),
        "wide",
        scatter_dimension=0,
        tiled=True,
    ).astype(jnp.bfloat16)
    return (example_grads, grad_norms, input_grad)


def exchange(array, axis, step):
    axes = axis if isinstance(axis, tuple) else (axis,)
    size = math.prod(lax.axis_size(name) for name in axes)
    return lax.ppermute(array, axes, [(i, i ^ step) for i in range(size)])


def held(array):
    return pltpu.with_memory_space_constraint(array, pltpu.VMEM)


def call(body, name, outs, args, spaces=None, scratch=(), out_spaces=None):
    spaces, out_spaces = spaces or {}, out_spaces or {}
    many = isinstance(outs, list)
    out_specs = [
        pl.BlockSpec(memory_space=out_spaces.get(i, pltpu.VMEM)) for i in range(len(outs) if many else 1)
    ]
    return pl.pallas_call(
        body,
        out_shape=outs,
        in_specs=[pl.BlockSpec(memory_space=spaces.get(i, pltpu.VMEM)) for i in range(len(args))],
        out_specs=out_specs if many else out_specs[0],
        scratch_shapes=list(scratch),
        compiler_params=pltpu.CompilerParams(vmem_limit_bytes=KERNEL_VMEM),
        cost_estimate=pl.CostEstimate(flops=1000, bytes_accessed=1000, transcendentals=0),
        name=name,
    )(*args)


def pack_kernel(inputs, cotangent, out, stage):
    share, features = inputs.shape
    half = features // 2
    for i, ref in enumerate((inputs, cotangent)):
        rows = ref[...].astype(jnp.float32)
        for j in range(2):
            stage[(2 * i + j) * share : (2 * i + j + 1) * share, :] = rows[:, j * half : (j + 1) * half]
    for k in range(out.shape[0]):
        out[k] = stage[8 * k : 8 * k + 8, :].astype(jnp.bfloat16)


def fetch_ids(ids_in, marks, ids, sem):
    return pltpu.make_async_copy(ids_in, ids, sem.at[0])


def keys_kernel(share, ids_in, marks, ids, sem):
    fetch_ids(ids_in, marks, ids, sem).wait()
    position, count = lax.axis_index("wide"), ids.shape[1]
    shape = (8, count)
    token, row = (lax.broadcasted_iota(jnp.int32, shape, axis) for axis in (1, 0))
    keys = []
    for base in range(0, WIDE * share, 8):
        at = row + base
        block = sum((at >= share * i).astype(jnp.int32) for i in range(1, WIDE))
        own = token == (position ^ block) * share + (at - block * share)
        key = jnp.sum(jnp.where(own, ids[...].astype(jnp.float32), 0.0), axis=1, keepdims=True)
        keys.append(jnp.broadcast_to(key, (8, 128)))
    keys.append(jnp.zeros((8, marks.shape[1] - 128 * len(keys)), jnp.float32))
    marks[...] = jnp.concatenate(keys, axis=1).astype(jnp.bfloat16)


def relay_kernel(own, far, marks, pair, marked):
    slabs, across = own.shape[0], own.shape[2] // 128
    pair[0:slabs] = own[...]
    pair[slabs : 2 * slabs] = far[...]
    for k in range(2 * slabs):
        rows = (own if k < slabs else far)[k % slabs]
        for j in range(across):
            marked[k * across + j] = rows[:, j * 128 : (j + 1) * 128]
    for k in range(marked.shape[0] - 2 * slabs * across):
        marked[2 * slabs * across + k] = marks[:, k * 128 : (k + 1) * 128]


WIDE, NEXT, FAR = 4, 1, 2
GATE, UP, DOWN = range(3)
WHOLE_STRIP = (GATE, UP, DOWN)
CHUNKS = 4


def start_loads(pieces, groups, sources, targets, sem):
    copies = []
    for i, (kind, strip) in enumerate(pieces):
        target = targets[i]
        width = target.shape[0 if kind == DOWN else 1]
        owner = lax.axis_index("narrow") ^ strip
        start = pl.multiple_of((owner * groups + lax.axis_index("groups")) * width, width)
        source = sources[kind]
        source = source.at[pl.ds(start, width), :] if kind == DOWN else source.at[:, pl.ds(start, width)]
        size = target.shape[0] // CHUNKS
        for c in range(CHUNKS):
            span = slice(c * size, (c + 1) * size)
            copies.append(pltpu.make_async_copy(source.at[span, :], target.at[span, :], sem.at[i, c]))
    for copy in copies:
        copy.start()
    return copies


def load_kernel(pieces, groups, *refs):
    count = len(pieces)
    for copy in start_loads(pieces, groups, refs[:3], refs[-1 - count : -1], refs[-1]):
        copy.wait()


def loading(body, pieces, groups, outs, own_copy=None):
    count = len(pieces)

    def kernel(*refs):
        sources, rest = refs[:3], refs[3:]
        at = len(rest) - outs[1] - 1 - count
        targets, sem = rest[at : at + count], rest[at + count + outs[1]]
        own = rest[:at] + rest[at + count : at + count + outs[1]]
        if own_copy is not None:
            own_copy(*own).start()
        copies = start_loads(pieces, groups, sources, targets, sem)

        @pl.when(lax.axis_index("narrow") >= 0)
        def _():
            body(*own)

        for copy in copies:
            copy.wait()

    return kernel


def strip_parts(tokens, cotans, gate, up, down, put):
    tile = 256
    for start in range(0, gate.shape[1], tile):
        span = slice(start, start + tile)
        put(GATE, span, jnp.dot(tokens[...], gate[:, span], preferred_element_type=jnp.float32))
        put(UP, span, jnp.dot(tokens[...], up[:, span], preferred_element_type=jnp.float32))
        put(DOWN, span, contract_rows(cotans[...], down[span, :]))


def forward_kernel(tokens, cotans, gate, up, down, *refs):
    out = refs[-1]

    def put(kind, span, part):
        out[kind, :, span] = part.astype(out.dtype)

    strip_parts(tokens, cotans, gate, up, down, put)


def join_kernel(own, arrived, out):
    out[...] = (own[...] + arrived[...]).astype(out.dtype)


def first_kernel(share, pair, beside, other, diagonal, gate, up, down, *refs):
    tokens, cotans, part, rows, cots = refs[-5:]
    slabs, half = 4 * share // 8, rows.shape[1] // 2
    for source, places in (
        (pair, (0, FAR)),
        (beside, (NEXT, FAR ^ NEXT)),
        (other, (WIDE, WIDE + FAR)),
        (diagonal, (WIDE + NEXT, WIDE + (FAR ^ NEXT))),
    ):
        for i, place in enumerate(places):
            if source is other:
                packed = from_tiles(source, i * slabs * (half // 128), 4 * share, half)
            else:
                packed = source[i * slabs : (i + 1) * slabs].astype(jnp.float32).reshape(4 * share, half)
            for j, target in enumerate((rows, rows, cots, cots)):
                span = slice((j % 2) * half, (j % 2 + 1) * half)
                target[place * share : (place + 1) * share, span] = packed[j * share : (j + 1) * share]
    tokens[...] = rows[...].astype(jnp.bfloat16)
    cotans[...] = cots[...].astype(jnp.bfloat16)
    forward_kernel(tokens, cotans, gate, up, down, part)


def own_strip_kernel(groups, *refs):
    sources, (tokens, cotans, up, down) = refs[:3], refs[3:7]
    out, gate, sem = refs[-3:]
    copies = start_loads([(GATE, 0)], groups, sources, [gate], sem)

    @pl.when(lax.axis_index("narrow") >= 0)
    def _():
        out[UP] = jnp.dot(tokens[...], up[...], preferred_element_type=jnp.float32)
        out[DOWN] = contract_rows(cotans[...], down[...])

    for copy in copies:
        copy.wait()
    out[GATE] = jnp.dot(tokens[...], gate[...], preferred_element_type=jnp.float32)


def to_tiles(values, tiles, first):
    rows, columns = values.shape
    values = values.astype(jnp.float32)
    for i in range(rows // 8):
        for j in range(columns // 128):
            tile = values[8 * i : 8 * i + 8, 128 * j : 128 * j + 128]
            tiles[first + i * (columns // 128) + j] = tile.astype(tiles.dtype)


def from_tiles(tiles, first, rows, columns):
    across = columns // 128
    parts = [
        jnp.concatenate([tiles[first + i * across + j].astype(jnp.float32) for j in range(across)], axis=1)
        for i in range(rows // 8)
    ]
    return jnp.concatenate(parts, axis=0)


def middle_kernel(groups, *refs):
    own, arrived, crossed, scale, relayed, other_relayed = refs[:6]
    message, tiles, near_tiles, grads, other_grads, stage = refs[-6:]
    _, tokens, width = own.shape
    narrow, group = lax.axis_index("narrow"), lax.axis_index("groups")
    sums = [own[i] + arrived[i].astype(jnp.float32) + crossed[i].astype(jnp.float32) for i in range(3)]
    start = pl.multiple_of((narrow * groups + group) * width, width)
    product, d_gate, d_up = local_grads(*sums, scale[:, pl.ds(start, width)])
    message[0:tokens, :] = d_gate
    message[tokens : 2 * tokens, :] = d_up
    count = tokens // 8 * (width // 128)
    for target in (tiles, near_tiles):
        to_tiles(d_gate, target, 0)
        to_tiles(d_up, target, count)
    half = tokens // groups
    first = other_relayed.shape[0] - half // 8
    own_marks = relayed[...].astype(jnp.float32)
    other_marks = jnp.concatenate([other_relayed[first + k].astype(jnp.float32) for k in range(half // 8)], axis=1)
    for side, (marks, target) in enumerate(((own_marks, grads), (other_marks, other_grads))):
        seq = jnp.concatenate(
            [
                jnp.concatenate([marks[:, k * 128 : (k + 1) * 128]] * (width // 128), axis=1)
                for k in range(half // 8)
            ],
            axis=0,
        )
        part = product[side * half : (side + 1) * half]
        for e in range(SEQS):
            total = jnp.sum(jnp.where(seq == float(e), part, 0.0), axis=0, keepdims=True)
            target[e : e + 1, :] = total
            stage[side * SEQS + e : side * SEQS + e + 1, :] = total
    every = stage[...]
    squares = jnp.broadcast_to(jnp.sum(every * every, axis=1, keepdims=True), every.shape)
    tail = jnp.concatenate(split_high(squares), axis=0).astype(jnp.bfloat16)
    message[2 * tokens :, :] = tail
    for i, rows in enumerate(split_high(squares)):
        for target in (tiles, near_tiles):
            target[2 * count + i] = rows[:, 0:128].astype(jnp.bfloat16)
    tiles[2 * count + 2] = jnp.zeros((8, 128), jnp.bfloat16)


TILE = 512


def backward_part(grads, gate, up, start):
    d_gate, d_up = grads
    gate_term = contract_rows(gate[start : start + TILE, :], d_gate)
    return gate_term + contract_rows(up[start : start + TILE, :], d_up)


def halves(message):
    tokens = (message.shape[0] - 16) // 2
    return message[0:tokens, :], message[tokens : 2 * tokens, :]


def halves_of_tiles(tiles, width):
    count = (tiles.shape[0] - 2) // 2
    rows = count // (width // 128) * 8
    return tuple(from_tiles(tiles, first, rows, width).astype(tiles.dtype) for first in (0, count))


def squares_of(message):
    if len(message.shape) == 3:
        first = (message.shape[0] - 2) // 2 * 2
        return message[first].astype(jnp.float32) + message[first + 1].astype(jnp.float32)
    rows = message[message.shape[0] - 16 :, 0:128].astype(jnp.float32)
    return rows[0:8] + rows[8:16]


def backward_first_kernel(message, gate, up, total):
    for start in range(0, total.shape[0], TILE):
        total[start : start + TILE, :] = backward_part(halves(message), gate, up, start)


def backward_next_kernel(tiles, gate, up, before, total):
    grads = halves_of_tiles(tiles, gate.shape[1])
    for start in range(0, total.shape[0], TILE):
        part = backward_part(grads, gate, up, start)
        total[start : start + TILE, :] = before[start : start + TILE, :] + part


def split_high(values):
    high = values.astype(jnp.bfloat16).astype(jnp.float32)
    return high, values - high


def backward_last_kernel(share, tiles, gate, up, before, *refs):
    others, other_grads, (own, own_squares), sends, (total, stage) = refs[:3], refs[3], refs[4:6], refs[6:9], refs[9:]
    tokens, features = total.shape
    side = features // 2
    grads = halves_of_tiles(tiles, gate.shape[1])
    for start in range(0, features, TILE):
        part = before[start : start + TILE, :] + backward_part(grads, gate, up, start)
        total[:, start : start + TILE] = part.T
    squares = sum(squares_of(ref) for ref in (tiles,) + others)
    own_squares[...] = squares
    tails = split_high(squares)
    slabs = 4 * share // 8
    for target, group, nearby in zip((own,) + tuple(sends), (0, 0, 1, 1), (0, NEXT, 0, NEXT)):
        rows = own if target is own else stage
        for i, place in enumerate((nearby, nearby ^ FAR)):
            at = (group * WIDE + place) * share
            for j in range(2):
                to = (2 * i + j) * share
                rows[to : to + share, :] = total[at : at + share, j * side : (j + 1) * side]
        if target is not own:
            for k in range(slabs):
                target[k, :, 0:side] = stage[8 * k : 8 * k + 8, :].astype(jnp.bfloat16)
                if target.shape[2] > side:
                    tail = tails[k] if k < 2 else jnp.zeros_like(squares)
                    target[k, :, side:] = tail.astype(jnp.bfloat16)
    width = other_grads.shape[1]
    stage[0:8, :] = jnp.zeros((8, side), jnp.float32)
    for i, rows in enumerate(split_high(other_grads[...])):
        stage[i * SEQS : (i + 1) * SEQS, 0:width] = rows
    for i, rows in enumerate(tails):
        stage[0:8, width + i * 128 : width + (i + 1) * 128] = rows
    sends[1][slabs] = stage[0:8, :].astype(jnp.bfloat16)


def combine_kernel(share, own, own_squares, diagonal, across, beside, *refs):
    kept_rows, other_grads, send, total, stage = refs
    slabs, side = beside.shape[0], own.shape[1]
    width = other_grads.shape[1]
    for k in range(slabs):
        rows = own[8 * k : 8 * k + 8, :] + across[k].astype(jnp.float32)
        for ref in (beside, diagonal):
            rows = rows + ref[k, :, 0:side].astype(jnp.float32)
        total[8 * k : 8 * k + 8, :] = rows
    tail = across[slabs].astype(jnp.float32)
    other_grads[...] = tail[0:SEQS, 0:width] + tail[SEQS : 2 * SEQS, 0:width]
    same, turned = own_squares[...], tail[:, width : width + 128] + tail[:, width + 128 : width + 256]
    for k in range(2):
        same = same + beside[k, :, side:].astype(jnp.float32)
        turned = turned + diagonal[k, :, side:].astype(jnp.float32)
    squares = same[0:SEQS] + turned[SEQS : 2 * SEQS]
    count = 2 * share
    kept_rows[...] = jnp.zeros_like(kept_rows)
    stage[...] = jnp.zeros_like(stage)
    kept_rows[0:count, :] = total[0:count, :]
    stage[0:count, :] = total[count : 2 * count, :]
    high, low = split_high(squares)
    for e in range(SEQS):
        span = slice(e * 128, (e + 1) * 128)
        for ref in (kept_rows, stage):
            ref[count : count + 1, span] = high[e : e + 1]
            ref[count + 1 : count + 2, span] = low[e : e + 1]
    for k in range(2):
        send[k] = stage[8 * k : 8 * k + 8, :].astype(jnp.bfloat16)


def last_kernel(share, own, arrived, grads, other_grads, input_grad, example_grads, norms, stage):
    side, width = own.shape[1], grads.shape[1]
    group = lax.axis_index("groups")
    for k in range(2):
        stage[8 * k : 8 * k + 8, :] = own[8 * k : 8 * k + 8, :] + arrived[k].astype(jnp.float32)
    for j in range(2):
        rows = stage[j * share : (j + 1) * share, :]
        input_grad[:, j * side : (j + 1) * side] = rows.astype(jnp.bfloat16)
    example_grads[:, pl.ds(pl.multiple_of(group * width, width), width)] = grads[...]
    example_grads[:, pl.ds(pl.multiple_of((1 - group) * width, width), width)] = other_grads[...]
    count = 2 * share
    squares = stage[count : count + 1, 0 : SEQS * 128] + stage[count + 1 : count + 2, 0 : SEQS * 128]
    roots = jnp.sqrt(squares)
    for e in range(SEQS):
        norms[e] = jnp.max(roots[:, e * 128 : (e + 1) * 128])


def shared(inputs, cotangent, gate_weight, up_weight, down_weight, ia3_scale, seq_ids):
    groups, wide, strips = lax.axis_size("groups"), lax.axis_size("wide"), lax.axis_size("narrow")
    share, features = inputs.shape
    width = gate_weight.shape[1] // (strips * groups)
    half = share * wide
    tokens = half * groups
    f32, bf16 = jnp.float32, jnp.bfloat16
    slabs, side = 4 * share // 8, features // 2
    weights = tuple(
        pltpu.with_memory_space_constraint(weight, pltpu.HBM)
        for weight in (gate_weight, up_weight, down_weight)
    )
    weight_shapes = [
        pltpu.VMEM((features, width), bf16),
        pltpu.VMEM((features, width), bf16),
        pltpu.VMEM((width, features), bf16),
    ]
    kept = {}

    def load(name, pieces, after=()):
        args = weights + tuple(after)
        arrays = call(
            functools.partial(load_kernel, pieces, groups),
            name,
            [weight_shapes[kind] for kind, _ in pieces],
            args,
            {i: pltpu.HBM if i < 3 else pl.ANY for i in range(len(args))},
            [pltpu.SemaphoreType.DMA((len(pieces), CHUNKS))],
        )
        kept.update(zip(pieces, arrays))

    def call_loading(body, name, pieces, outs, args, scratch=(), spaces=None, own_copy=None):
        made = call(
            loading(body, pieces, groups, (len(outs), len(outs) + len(scratch)), own_copy),
            name,
            [weight_shapes[kind] for kind, _ in pieces] + outs,
            list(weights) + args,
            {**{i: pltpu.HBM for i in range(3)}, **(spaces or {})},
            list(scratch) + [pltpu.SemaphoreType.DMA((len(pieces), CHUNKS))],
        )
        kept.update(zip(pieces, made))
        return made[len(pieces) :]

    def hold(strip, kinds=WHOLE_STRIP):
        return [held(kept[kind, strip]) for kind in kinds]

    packed = call(
        pack_kernel,
        "pack",
        pltpu.VMEM((slabs, 8, features // 2), bf16),
        [pltpu.with_memory_space_constraint(array, pltpu.HBM) for array in (inputs, cotangent)],
        scratch=[pltpu.VMEM((4 * share, features // 2), f32)],
    )
    far = exchange(packed, "wide", FAR)
    (marks,) = call_loading(
        functools.partial(keys_kernel, share),
        "load_a",
        [(kind, 3) for kind in WHOLE_STRIP],
        [pltpu.VMEM((8, side), bf16)],
        [pltpu.with_memory_space_constraint(seq_ids[None, :], pltpu.HBM)],
        [pltpu.VMEM((1, half), jnp.int32), pltpu.SemaphoreType.DMA((1,))],
        {3: pltpu.HBM},
        fetch_ids,
    )
    pair, marked = call(
        relay_kernel,
        "relay",
        [pltpu.VMEM((2 * slabs, 8, side), bf16), pltpu.VMEM((2 * slabs * (side // 128) + half // 8, 8, 128), bf16)],
        [packed, far, marks],
    )
    diagonal = exchange(pair, ("groups", "wide"), WIDE + NEXT)
    other_marked = exchange(marked, "groups", 1)
    beside = exchange(pair, "wide", NEXT)
    load("load_b", [(kind, 2) for kind in WHOLE_STRIP], [pair])

    part = pltpu.VMEM((3, tokens, width), f32)
    near_shape = pltpu.VMEM((3, tokens, width), bf16)
    tokens_all, cotans_all, diagonal = call_loading(
        functools.partial(first_kernel, share),
        "forward_3",
        [(GATE, 1), (DOWN, 1)],
        [pltpu.VMEM((tokens, features), bf16)] * 2 + [part],
        [pair, beside, other_marked, diagonal] + hold(3) + hold(2, [GATE]),
        [pltpu.VMEM((tokens, features), f32)] * 2,
    )
    panel = [tokens_all, cotans_all]
    diagonal = exchange(diagonal, "narrow", 1)
    (second,) = call_loading(forward_kernel, "forward_2", [(UP, 1)], [part], panel + hold(2))
    crossing = call(join_kernel, "join", near_shape, [held(second), diagonal])
    crossed = exchange(crossing, "narrow", 2)
    (near,) = call_loading(
        forward_kernel, "forward_1", [(UP, 0), (DOWN, 0)], [near_shape], panel + hold(1) + [held(crossing)]
    )
    near = exchange(near, "narrow", 1)
    own_part, kept[GATE, 0] = call(
        functools.partial(own_strip_kernel, groups),
        "forward_0",
        [part, weight_shapes[GATE]],
        list(weights) + panel + hold(0, [UP, DOWN]),
        {i: pltpu.HBM for i in range(3)},
        [pltpu.SemaphoreType.DMA((1, CHUNKS))],
    )

    resident = [array for s in range(strips) for array in hold(s, [GATE, UP])]
    message, tiles, near_tiles, grads, other_grads = call(
        functools.partial(middle_kernel, groups),
        "middle",
        [
            pltpu.VMEM((2 * tokens + 16, width), bf16),
            pltpu.VMEM((2 * (tokens // 8) * (width // 128) + 3, 8, 128), bf16),
            pltpu.VMEM((2 * (tokens // 8) * (width // 128) + 2, 8, 128), bf16),
            pltpu.VMEM((SEQS, width), f32),
            pltpu.VMEM((SEQS, width), f32),
        ],
        [own_part, near, crossed, ia3_scale[None, :], marks, other_marked] + resident,
        scratch=[pltpu.VMEM((groups * SEQS, width), f32)],
    )

    total = pltpu.VMEM((features, tokens), f32)
    message_1 = exchange(near_tiles, "narrow", 1)
    message_2 = exchange(tiles, "narrow", 2)
    sums = call(backward_first_kernel, "backward_0", total, [message] + hold(0, [GATE, UP]))
    sums = call(backward_next_kernel, "backward_1", total, [message_1] + hold(1, [GATE, UP]) + [sums])
    message_2, sums = lax.optimization_barrier((message_2, sums))
    message_3 = exchange(message_2, "narrow", 1)
    sums = call(backward_next_kernel, "backward_2", total, [message_2] + hold(2, [GATE, UP]) + [sums])
    block = pltpu.VMEM((slabs, 8, side + 128), bf16)
    own, own_squares, *sends = call(
        functools.partial(backward_last_kernel, share),
        "backward_3",
        [
            pltpu.VMEM((4 * share, side), f32),
            pltpu.VMEM((8, 128), f32),
            block,
            pltpu.VMEM((slabs + 1, 8, side), bf16),
            block,
        ],
        [message_3] + hold(3, [GATE, UP]) + [sums, message, message_1, message_2, other_grads],
        scratch=[pltpu.VMEM((tokens, features), f32), pltpu.VMEM((4 * share, side), f32)],
    )
    across = exchange(sends[1], "groups", 1)
    beside = exchange(sends[0], "wide", NEXT)
    diagonal = exchange(sends[2], ("groups", "wide"), WIDE + NEXT)
    own, other_grads, send = call(
        functools.partial(combine_kernel, share),
        "combine",
        [pltpu.VMEM((16, side), f32), pltpu.VMEM((SEQS, width), f32), pltpu.VMEM((2, 8, side), bf16)],
        [own, own_squares, diagonal, across, beside],
        scratch=[pltpu.VMEM((4 * share, side), f32), pltpu.VMEM((16, side), f32)],
    )
    input_grad, example_grads, norms = call(
        functools.partial(last_kernel, share),
        "last",
        [
            jax.ShapeDtypeStruct((share, features), bf16),
            jax.ShapeDtypeStruct((SEQS, groups * width), f32),
            jax.ShapeDtypeStruct((SEQS,), f32),
        ],
        [own, exchange(send, "wide", FAR), grads, other_grads],
        scratch=[pltpu.VMEM((16, side), f32)],
        out_spaces={2: pltpu.SMEM},
    )
    return (example_grads, norms, input_grad)


def local(inputs, cotangent, gate_weight, up_weight, down_weight, ia3_scale, seq_ids):
    groups, wide, narrow = lax.axis_size("groups"), lax.axis_size("wide"), lax.axis_size("narrow")
    share, (features, hidden) = inputs.shape[0], gate_weight.shape
    width = hidden // (narrow * groups)
    fits = (
        groups == 2
        and narrow == 4
        and wide == WIDE
        and hidden % (narrow * groups * 256) == 0
        and features >= 2048
        and width <= features // 2 - 256
        and features % (2 * TILE) == 0
        and share in (4, 6)
        and (share * wide) % 8 == 0
        and share * wide <= 64
        and 3 * features * hidden // groups * 2 <= 40 << 20
    )
    plan = shared if fits else whole_block
    return plan(inputs, cotangent, gate_weight, up_weight, down_weight, ia3_scale, seq_ids)


def solution(mesh):
    return jax.shard_map(
        local,
        mesh=mesh,
        in_specs=(
            P(("groups", "wide"), "narrow"),
            P(("groups", "wide"), "narrow"),
            P("narrow", "wide"),
            P("narrow", "wide"),
            P("wide", "narrow"),
            P("wide"),
            P("groups"),
        ),
        out_specs=(P("groups", ("wide", "narrow")), P("groups"), P(("groups", "wide"), "narrow")),
        check_vma=False,
    )
```

```python
import functools
import math

import jax
import jax.numpy as jnp
from jax import lax
from jax.experimental import pallas as pl
from jax.experimental.pallas import tpu as pltpu
from jax.sharding import PartitionSpec as P

SEQS = 4
KERNEL_VMEM = 6 << 20


def contract_rows(left, right):
    return lax.dot_general(
        left, right, (((1,), (1,)), ((), ())), preferred_element_type=jnp.float32
    )


def local_grads(gate_pre, up_pre, mid_grad, scale_part):
    sigmoid_gate = jax.nn.sigmoid(gate_pre)
    activation = gate_pre * sigmoid_gate
    hidden = activation * up_pre
    scaled = scale_part * mid_grad
    d_up = (scaled * activation).astype(jnp.bfloat16)
    d_gate = (scaled * up_pre * sigmoid_gate * (1.0 + gate_pre * (1.0 - sigmoid_gate))).astype(
        jnp.bfloat16
    )
    return (hidden * mid_grad, d_gate, d_up)


def whole_block(inputs, cotangent, gate_weight, up_weight, down_weight, ia3_scale, seq_ids):
    panel_inputs = lax.all_gather(inputs, "wide", axis=0, tiled=True)
    panel_cotangent = lax.all_gather(cotangent, "wide", axis=0, tiled=True)
    gate_part = jnp.dot(panel_inputs, gate_weight, preferred_element_type=jnp.float32)
    up_part = jnp.dot(panel_inputs, up_weight, preferred_element_type=jnp.float32)
    mid_part = contract_rows(panel_cotangent, down_weight)
    quarter = gate_weight.shape[1] // lax.axis_size("narrow")
    position = lax.axis_index("narrow")
    onehot_full = (seq_ids[None, :] == jnp.arange(SEQS, dtype=jnp.int32)[:, None]).astype(
        jnp.float32
    )
    gate_pre, up_pre, mid_grad = (
        lax.psum_scatter(gate_part, "narrow", scatter_dimension=1, tiled=True),
        lax.psum_scatter(up_part, "narrow", scatter_dimension=1, tiled=True),
        lax.psum_scatter(mid_part, "narrow", scatter_dimension=1, tiled=True),
    )
    scale_part = lax.dynamic_slice_in_dim(ia3_scale, position * quarter, quarter, 0)
    product, d_gate, d_up = local_grads(gate_pre, up_pre, mid_grad, scale_part[None, :])
    example_grads = jnp.dot(onehot_full, product, precision=lax.Precision.HIGHEST)
    whole_gate, whole_up = (
        lax.all_gather(d_gate, "narrow", axis=1, tiled=True),
        lax.all_gather(d_up, "narrow", axis=1, tiled=True),
    )
    squares = lax.psum(jnp.sum(example_grads * example_grads, axis=1), ("wide", "narrow"))
    grad_norms = jnp.sqrt(squares)
    input_grad = lax.psum_scatter(
        contract_rows(whole_gate, gate_weight) + contract_rows(whole_up, up_weight),
        "wide",
        scatter_dimension=0,
        tiled=True,
    ).astype(jnp.bfloat16)
    return (example_grads, grad_norms, input_grad)


def exchange(array, axis, step):
    axes = axis if isinstance(axis, tuple) else (axis,)
    size = math.prod(lax.axis_size(name) for name in axes)
    return lax.ppermute(array, axes, [(i, i ^ step) for i in range(size)])


def held(array):
    return pltpu.with_memory_space_constraint(array, pltpu.VMEM)


def call(body, name, outs, args, spaces=None, scratch=(), out_spaces=None):
    spaces, out_spaces = spaces or {}, out_spaces or {}
    many = isinstance(outs, list)
    out_specs = [
        pl.BlockSpec(memory_space=out_spaces.get(i, pltpu.VMEM)) for i in range(len(outs) if many else 1)
    ]
    return pl.pallas_call(
        body,
        out_shape=outs,
        in_specs=[pl.BlockSpec(memory_space=spaces.get(i, pltpu.VMEM)) for i in range(len(args))],
        out_specs=out_specs if many else out_specs[0],
        scratch_shapes=list(scratch),
        compiler_params=pltpu.CompilerParams(vmem_limit_bytes=KERNEL_VMEM),
        cost_estimate=pl.CostEstimate(flops=1000, bytes_accessed=1000, transcendentals=0),
        name=name,
    )(*args)


def pack_kernel(inputs, cotangent, out, stage):
    share, features = inputs.shape
    half = features // 2
    for i, ref in enumerate((inputs, cotangent)):
        rows = ref[...].astype(jnp.float32)
        for j in range(2):
            stage[(2 * i + j) * share : (2 * i + j + 1) * share, :] = rows[:, j * half : (j + 1) * half]
    for k in range(out.shape[0]):
        out[k] = stage[8 * k : 8 * k + 8, :].astype(jnp.bfloat16)


def fetch_ids(ids_in, marks, ids, sem):
    return pltpu.make_async_copy(ids_in, ids, sem.at[0])


def keys_kernel(share, ids_in, marks, ids, sem):
    fetch_ids(ids_in, marks, ids, sem).wait()
    position, count = lax.axis_index("wide"), ids.shape[1]
    shape = (8, count)
    token, row = (lax.broadcasted_iota(jnp.int32, shape, axis) for axis in (1, 0))
    keys = []
    for base in range(0, WIDE * share, 8):
        at = row + base
        block = sum((at >= share * i).astype(jnp.int32) for i in range(1, WIDE))
        own = token == (position ^ block) * share + (at - block * share)
        key = jnp.sum(jnp.where(own, ids[...].astype(jnp.float32), 0.0), axis=1, keepdims=True)
        keys.append(jnp.broadcast_to(key, (8, 128)))
    keys.append(jnp.zeros((8, marks.shape[1] - 128 * len(keys)), jnp.float32))
    marks[...] = jnp.concatenate(keys, axis=1).astype(jnp.bfloat16)


def relay_kernel(own, far, marks, pair, marked):
    slabs = own.shape[0]
    for target in (pair, marked):
        target[0:slabs] = own[...]
        target[slabs : 2 * slabs] = far[...]
    marked[2 * slabs] = marks[...]


WIDE, NEXT, FAR = 4, 1, 2
GATE, UP, DOWN = range(3)
WHOLE_STRIP = (GATE, UP, DOWN)
CHUNKS = 2


def start_loads(pieces, groups, sources, targets, sem):
    copies = []
    for i, (kind, strip) in enumerate(pieces):
        target = targets[i]
        width = target.shape[0 if kind == DOWN else 1]
        owner = lax.axis_index("narrow") ^ strip
        start = pl.multiple_of((owner * groups + lax.axis_index("groups")) * width, width)
        source = sources[kind]
        source = source.at[pl.ds(start, width), :] if kind == DOWN else source.at[:, pl.ds(start, width)]
        size = target.shape[0] // CHUNKS
        for c in range(CHUNKS):
            span = slice(c * size, (c + 1) * size)
            copies.append(pltpu.make_async_copy(source.at[span, :], target.at[span, :], sem.at[i, c]))
    for copy in copies:
        copy.start()
    return copies


def load_kernel(pieces, groups, *refs):
    count = len(pieces)
    for copy in start_loads(pieces, groups, refs[:3], refs[-1 - count : -1], refs[-1]):
        copy.wait()


def loading(body, pieces, groups, outs, own_copy=None):
    count = len(pieces)

    def kernel(*refs):
        sources, rest = refs[:3], refs[3:]
        at = len(rest) - outs[1] - 1 - count
        targets, sem = rest[at : at + count], rest[at + count + outs[1]]
        own = rest[:at] + rest[at + count : at + count + outs[1]]
        if own_copy is not None:
            own_copy(*own).start()
        copies = start_loads(pieces, groups, sources, targets, sem)

        @pl.when(lax.axis_index("narrow") >= 0)
        def _():
            body(*own)

        for copy in copies:
            copy.wait()

    return kernel


def strip_parts(tokens, cotans, gate, up, down, put):
    tile = 256
    for start in range(0, gate.shape[1], tile):
        span = slice(start, start + tile)
        put(GATE, span, jnp.dot(tokens[...], gate[:, span], preferred_element_type=jnp.float32))
        put(UP, span, jnp.dot(tokens[...], up[:, span], preferred_element_type=jnp.float32))
        put(DOWN, span, contract_rows(cotans[...], down[span, :]))


def forward_kernel(tokens, cotans, gate, up, down, *refs):
    out = refs[-1]

    def put(kind, span, part):
        out[kind, :, span] = part.astype(out.dtype)

    strip_parts(tokens, cotans, gate, up, down, put)


def join_kernel(own, arrived, out):
    out[...] = (own[...] + arrived[...]).astype(out.dtype)


def first_kernel(share, marked, beside, other, diagonal, gate, up, down, *refs):
    tokens, cotans, part, rows, cots = refs[-5:]
    slabs, half = 4 * share // 8, rows.shape[1] // 2
    for source, places in (
        (marked, (0, FAR)),
        (beside, (NEXT, FAR ^ NEXT)),
        (other, (WIDE, WIDE + FAR)),
        (diagonal, (WIDE + NEXT, WIDE + (FAR ^ NEXT))),
    ):
        for i, place in enumerate(places):
            packed = source[i * slabs : (i + 1) * slabs].astype(jnp.float32).reshape(4 * share, half)
            for j, target in enumerate((rows, rows, cots, cots)):
                span = slice((j % 2) * half, (j % 2 + 1) * half)
                target[place * share : (place + 1) * share, span] = packed[j * share : (j + 1) * share]
    tokens[...] = rows[...].astype(jnp.bfloat16)
    cotans[...] = cots[...].astype(jnp.bfloat16)
    forward_kernel(tokens, cotans, gate, up, down, part)


def own_strip_kernel(groups, *refs):
    sources, (tokens, cotans, up, down) = refs[:3], refs[3:7]
    out, gate, sem = refs[-3:]
    copies = start_loads([(GATE, 0)], groups, sources, [gate], sem)

    @pl.when(lax.axis_index("narrow") >= 0)
    def _():
        out[UP] = jnp.dot(tokens[...], up[...], preferred_element_type=jnp.float32)
        out[DOWN] = contract_rows(cotans[...], down[...])

    for copy in copies:
        copy.wait()
    out[GATE] = jnp.dot(tokens[...], gate[...], preferred_element_type=jnp.float32)


def to_tiles(values, tiles, first):
    rows, columns = values.shape
    values = values.astype(jnp.float32)
    for i in range(rows // 8):
        for j in range(columns // 128):
            tile = values[8 * i : 8 * i + 8, 128 * j : 128 * j + 128]
            tiles[first + i * (columns // 128) + j] = tile.astype(tiles.dtype)


def from_tiles(tiles, first, rows, columns):
    across = columns // 128
    parts = [
        jnp.concatenate([tiles[first + i * across + j].astype(jnp.float32) for j in range(across)], axis=1)
        for i in range(rows // 8)
    ]
    return jnp.concatenate(parts, axis=0).astype(tiles.dtype)


def middle_kernel(groups, *refs):
    own, arrived, crossed, scale, relayed, other_relayed = refs[:6]
    message, tiles, near_tiles, grads, other_grads, stage = refs[-6:]
    _, tokens, width = own.shape
    narrow, group = lax.axis_index("narrow"), lax.axis_index("groups")
    sums = [own[i] + arrived[i].astype(jnp.float32) + crossed[i].astype(jnp.float32) for i in range(3)]
    start = pl.multiple_of((narrow * groups + group) * width, width)
    product, d_gate, d_up = local_grads(*sums, scale[:, pl.ds(start, width)])
    message[0:tokens, :] = d_gate
    message[tokens : 2 * tokens, :] = d_up
    count = tokens // 8 * (width // 128)
    for target in (tiles, near_tiles):
        to_tiles(d_gate, target, 0)
        to_tiles(d_up, target, count)
    half = tokens // groups
    for side, (source, target) in enumerate(((relayed, grads), (other_relayed, other_grads))):
        marks = source[source.shape[0] - 1].astype(jnp.float32)
        seq = jnp.concatenate(
            [
                jnp.concatenate([marks[:, k * 128 : (k + 1) * 128]] * (width // 128), axis=1)
                for k in range(half // 8)
            ],
            axis=0,
        )
        part = product[side * half : (side + 1) * half]
        for e in range(SEQS):
            total = jnp.sum(jnp.where(seq == float(e), part, 0.0), axis=0, keepdims=True)
            target[e : e + 1, :] = total
            stage[side * SEQS + e : side * SEQS + e + 1, :] = total
    every = stage[...]
    squares = jnp.broadcast_to(jnp.sum(every * every, axis=1, keepdims=True), every.shape)
    tail = jnp.concatenate(split_high(squares), axis=0).astype(jnp.bfloat16)
    message[2 * tokens :, :] = tail
    for i, rows in enumerate(split_high(squares)):
        for target in (tiles, near_tiles):
            target[2 * count + i] = rows[:, 0:128].astype(jnp.bfloat16)
    tiles[2 * count + 2] = jnp.zeros((8, 128), jnp.bfloat16)


TILE = 512


def backward_part(grads, gate, up, start):
    d_gate, d_up = grads
    gate_term = contract_rows(gate[start : start + TILE, :], d_gate)
    return gate_term + contract_rows(up[start : start + TILE, :], d_up)


def halves(message):
    tokens = (message.shape[0] - 16) // 2
    return message[0:tokens, :], message[tokens : 2 * tokens, :]


def halves_of_tiles(tiles, width):
    count = (tiles.shape[0] - 2) // 2
    rows = count // (width // 128) * 8
    return from_tiles(tiles, 0, rows, width), from_tiles(tiles, count, rows, width)


def squares_of(message):
    if len(message.shape) == 3:
        first = (message.shape[0] - 2) // 2 * 2
        return message[first].astype(jnp.float32) + message[first + 1].astype(jnp.float32)
    rows = message[message.shape[0] - 16 :, 0:128].astype(jnp.float32)
    return rows[0:8] + rows[8:16]


def backward_first_kernel(message, gate, up, total):
    for start in range(0, total.shape[0], TILE):
        total[start : start + TILE, :] = backward_part(halves(message), gate, up, start)


def backward_next_kernel(tiles, gate, up, before, total):
    grads = halves_of_tiles(tiles, gate.shape[1])
    for start in range(0, total.shape[0], TILE):
        part = backward_part(grads, gate, up, start)
        total[start : start + TILE, :] = before[start : start + TILE, :] + part


def split_high(values):
    high = values.astype(jnp.bfloat16).astype(jnp.float32)
    return high, values - high


def backward_last_kernel(share, tiles, gate, up, before, *refs):
    others, other_grads, (own, own_squares), sends, (total, stage) = refs[:3], refs[3], refs[4:6], refs[6:9], refs[9:]
    tokens, features = total.shape
    side = features // 2
    grads = halves_of_tiles(tiles, gate.shape[1])
    for start in range(0, features, TILE):
        part = before[start : start + TILE, :] + backward_part(grads, gate, up, start)
        total[:, start : start + TILE] = part.T
    squares = sum(squares_of(ref) for ref in (tiles,) + others)
    own_squares[...] = squares
    tails = split_high(squares)
    slabs = 4 * share // 8
    for target, group, nearby in zip((own,) + tuple(sends), (0, 0, 1, 1), (0, NEXT, 0, NEXT)):
        rows = own if target is own else stage
        for i, place in enumerate((nearby, nearby ^ FAR)):
            at = (group * WIDE + place) * share
            for j in range(2):
                to = (2 * i + j) * share
                rows[to : to + share, :] = total[at : at + share, j * side : (j + 1) * side]
        if target is not own:
            for k in range(slabs):
                target[k, :, 0:side] = stage[8 * k : 8 * k + 8, :].astype(jnp.bfloat16)
                if target.shape[2] > side:
                    tail = tails[k] if k < 2 else jnp.zeros_like(squares)
                    target[k, :, side:] = tail.astype(jnp.bfloat16)
    width = other_grads.shape[1]
    stage[0:8, :] = jnp.zeros((8, side), jnp.float32)
    for i, rows in enumerate(split_high(other_grads[...])):
        stage[i * SEQS : (i + 1) * SEQS, 0:width] = rows
    for i, rows in enumerate(tails):
        stage[0:8, width + i * 128 : width + (i + 1) * 128] = rows
    sends[1][slabs] = stage[0:8, :].astype(jnp.bfloat16)


def combine_kernel(share, own, own_squares, diagonal, across, beside, *refs):
    kept_rows, other_grads, send, total, stage = refs
    slabs, side = beside.shape[0], own.shape[1]
    width = other_grads.shape[1]
    for k in range(slabs):
        rows = own[8 * k : 8 * k + 8, :] + across[k].astype(jnp.float32)
        for ref in (beside, diagonal):
            rows = rows + ref[k, :, 0:side].astype(jnp.float32)
        total[8 * k : 8 * k + 8, :] = rows
    tail = across[slabs].astype(jnp.float32)
    other_grads[...] = tail[0:SEQS, 0:width] + tail[SEQS : 2 * SEQS, 0:width]
    same, turned = own_squares[...], tail[:, width : width + 128] + tail[:, width + 128 : width + 256]
    for k in range(2):
        same = same + beside[k, :, side:].astype(jnp.float32)
        turned = turned + diagonal[k, :, side:].astype(jnp.float32)
    squares = same[0:SEQS] + turned[SEQS : 2 * SEQS]
    count = 2 * share
    kept_rows[...] = jnp.zeros_like(kept_rows)
    stage[...] = jnp.zeros_like(stage)
    kept_rows[0:count, :] = total[0:count, :]
    stage[0:count, :] = total[count : 2 * count, :]
    high, low = split_high(squares)
    for e in range(SEQS):
        span = slice(e * 128, (e + 1) * 128)
        for ref in (kept_rows, stage):
            ref[count : count + 1, span] = high[e : e + 1]
            ref[count + 1 : count + 2, span] = low[e : e + 1]
    for k in range(2):
        send[k] = stage[8 * k : 8 * k + 8, :].astype(jnp.bfloat16)


def last_kernel(share, own, arrived, grads, other_grads, input_grad, example_grads, norms, stage):
    side, width = own.shape[1], grads.shape[1]
    group = lax.axis_index("groups")
    for k in range(2):
        stage[8 * k : 8 * k + 8, :] = own[8 * k : 8 * k + 8, :] + arrived[k].astype(jnp.float32)
    for j in range(2):
        rows = stage[j * share : (j + 1) * share, :]
        input_grad[:, j * side : (j + 1) * side] = rows.astype(jnp.bfloat16)
    example_grads[:, pl.ds(pl.multiple_of(group * width, width), width)] = grads[...]
    example_grads[:, pl.ds(pl.multiple_of((1 - group) * width, width), width)] = other_grads[...]
    count = 2 * share
    squares = stage[count : count + 1, 0 : SEQS * 128] + stage[count + 1 : count + 2, 0 : SEQS * 128]
    roots = jnp.sqrt(squares)
    for e in range(SEQS):
        norms[e] = jnp.max(roots[:, e * 128 : (e + 1) * 128])


def shared(inputs, cotangent, gate_weight, up_weight, down_weight, ia3_scale, seq_ids):
    groups, wide, strips = lax.axis_size("groups"), lax.axis_size("wide"), lax.axis_size("narrow")
    share, features = inputs.shape
    width = gate_weight.shape[1] // (strips * groups)
    half = share * wide
    tokens = half * groups
    f32, bf16 = jnp.float32, jnp.bfloat16
    slabs, side = 4 * share // 8, features // 2
    weights = tuple(
        pltpu.with_memory_space_constraint(weight, pltpu.HBM)
        for weight in (gate_weight, up_weight, down_weight)
    )
    weight_shapes = [
        pltpu.VMEM((features, width), bf16),
        pltpu.VMEM((features, width), bf16),
        pltpu.VMEM((width, features), bf16),
    ]
    kept = {}

    def load(name, pieces, after=()):
        args = weights + tuple(after)
        arrays = call(
            functools.partial(load_kernel, pieces, groups),
            name,
            [weight_shapes[kind] for kind, _ in pieces],
            args,
            {i: pltpu.HBM if i < 3 else pl.ANY for i in range(len(args))},
            [pltpu.SemaphoreType.DMA((len(pieces), CHUNKS))],
        )
        kept.update(zip(pieces, arrays))

    def call_loading(body, name, pieces, outs, args, scratch=(), spaces=None, own_copy=None):
        made = call(
            loading(body, pieces, groups, (len(outs), len(outs) + len(scratch)), own_copy),
            name,
            [weight_shapes[kind] for kind, _ in pieces] + outs,
            list(weights) + args,
            {**{i: pltpu.HBM for i in range(3)}, **(spaces or {})},
            list(scratch) + [pltpu.SemaphoreType.DMA((len(pieces), CHUNKS))],
        )
        kept.update(zip(pieces, made))
        return made[len(pieces) :]

    def hold(strip, kinds=WHOLE_STRIP):
        return [held(kept[kind, strip]) for kind in kinds]

    packed = call(
        pack_kernel,
        "pack",
        pltpu.VMEM((slabs, 8, features // 2), bf16),
        [pltpu.with_memory_space_constraint(array, pltpu.HBM) for array in (inputs, cotangent)],
        scratch=[pltpu.VMEM((4 * share, features // 2), f32)],
    )
    far = exchange(packed, "wide", FAR)
    (marks,) = call_loading(
        functools.partial(keys_kernel, share),
        "load_a",
        [(kind, 3) for kind in WHOLE_STRIP],
        [pltpu.VMEM((8, side), bf16)],
        [pltpu.with_memory_space_constraint(seq_ids[None, :], pltpu.HBM)],
        [pltpu.VMEM((1, half), jnp.int32), pltpu.SemaphoreType.DMA((1,))],
        {3: pltpu.HBM},
        fetch_ids,
    )
    pair, marked = call(
        relay_kernel,
        "relay",
        [pltpu.VMEM((2 * slabs, 8, side), bf16), pltpu.VMEM((2 * slabs + 1, 8, side), bf16)],
        [packed, far, marks],
    )
    diagonal = exchange(pair, ("groups", "wide"), WIDE + NEXT)
    other_marked = exchange(marked, "groups", 1)
    beside = exchange(pair, "wide", NEXT)
    load("load_b", [(kind, 2) for kind in WHOLE_STRIP], [pair])

    part = pltpu.VMEM((3, tokens, width), f32)
    near_shape = pltpu.VMEM((3, tokens, width), bf16)
    tokens_all, cotans_all, diagonal = call_loading(
        functools.partial(first_kernel, share),
        "forward_3",
        [(GATE, 1), (DOWN, 1)],
        [pltpu.VMEM((tokens, features), bf16)] * 2 + [part],
        [marked, beside, other_marked, diagonal] + hold(3) + hold(2, [GATE]),
        [pltpu.VMEM((tokens, features), f32)] * 2,
    )
    panel = [tokens_all, cotans_all]
    diagonal = exchange(diagonal, "narrow", 1)
    (second,) = call_loading(forward_kernel, "forward_2", [(UP, 1)], [part], panel + hold(2))
    crossing = call(join_kernel, "join", near_shape, [held(second), diagonal])
    crossed = exchange(crossing, "narrow", 2)
    (near,) = call_loading(
        forward_kernel, "forward_1", [(UP, 0), (DOWN, 0)], [near_shape], panel + hold(1) + [held(crossing)]
    )
    near = exchange(near, "narrow", 1)
    own_part, kept[GATE, 0] = call(
        functools.partial(own_strip_kernel, groups),
        "forward_0",
        [part, weight_shapes[GATE]],
        list(weights) + panel + hold(0, [UP, DOWN]),
        {i: pltpu.HBM for i in range(3)},
        [pltpu.SemaphoreType.DMA((1, CHUNKS))],
    )

    resident = [array for s in range(strips) for array in hold(s, [GATE, UP])]
    message, tiles, near_tiles, grads, other_grads = call(
        functools.partial(middle_kernel, groups),
        "middle",
        [
            pltpu.VMEM((2 * tokens + 16, width), bf16),
            pltpu.VMEM((2 * (tokens // 8) * (width // 128) + 3, 8, 128), bf16),
            pltpu.VMEM((2 * (tokens // 8) * (width // 128) + 2, 8, 128), bf16),
            pltpu.VMEM((SEQS, width), f32),
            pltpu.VMEM((SEQS, width), f32),
        ],
        [own_part, near, crossed, ia3_scale[None, :], marked, other_marked] + resident,
        scratch=[pltpu.VMEM((groups * SEQS, width), f32)],
    )

    total = pltpu.VMEM((features, tokens), f32)
    message_1 = exchange(near_tiles, "narrow", 1)
    message_2 = exchange(tiles, "narrow", 2)
    sums = call(backward_first_kernel, "backward_0", total, [message] + hold(0, [GATE, UP]))
    sums = call(backward_next_kernel, "backward_1", total, [message_1] + hold(1, [GATE, UP]) + [sums])
    message_2, sums = lax.optimization_barrier((message_2, sums))
    message_3 = exchange(message_2, "narrow", 1)
    sums = call(backward_next_kernel, "backward_2", total, [message_2] + hold(2, [GATE, UP]) + [sums])
    block = pltpu.VMEM((slabs, 8, side + 128), bf16)
    own, own_squares, *sends = call(
        functools.partial(backward_last_kernel, share),
        "backward_3",
        [
            pltpu.VMEM((4 * share, side), f32),
            pltpu.VMEM((8, 128), f32),
            block,
            pltpu.VMEM((slabs + 1, 8, side), bf16),
            block,
        ],
        [message_3] + hold(3, [GATE, UP]) + [sums, message, message_1, message_2, other_grads],
        scratch=[pltpu.VMEM((tokens, features), f32), pltpu.VMEM((4 * share, side), f32)],
    )
    across = exchange(sends[1], "groups", 1)
    beside = exchange(sends[0], "wide", NEXT)
    diagonal = exchange(sends[2], ("groups", "wide"), WIDE + NEXT)
    own, other_grads, send = call(
        functools.partial(combine_kernel, share),
        "combine",
        [pltpu.VMEM((16, side), f32), pltpu.VMEM((SEQS, width), f32), pltpu.VMEM((2, 8, side), bf16)],
        [own, own_squares, diagonal, across, beside],
        scratch=[pltpu.VMEM((4 * share, side), f32), pltpu.VMEM((16, side), f32)],
    )
    input_grad, example_grads, norms = call(
        functools.partial(last_kernel, share),
        "last",
        [
            jax.ShapeDtypeStruct((share, features), bf16),
            jax.ShapeDtypeStruct((SEQS, groups * width), f32),
            jax.ShapeDtypeStruct((SEQS,), f32),
        ],
        [own, exchange(send, "wide", FAR), grads, other_grads],
        scratch=[pltpu.VMEM((16, side), f32)],
        out_spaces={2: pltpu.SMEM},
    )
    return (example_grads, norms, input_grad)


def local(inputs, cotangent, gate_weight, up_weight, down_weight, ia3_scale, seq_ids):
    groups, wide, narrow = lax.axis_size("groups"), lax.axis_size("wide"), lax.axis_size("narrow")
    share, (features, hidden) = inputs.shape[0], gate_weight.shape
    width = hidden // (narrow * groups)
    fits = (
        groups == 2
        and narrow == 4
        and wide == WIDE
        and hidden % (narrow * groups * 256) == 0
        and features >= 2048
        and width <= features // 2 - 256
        and features % (2 * TILE) == 0
        and share in (4, 6)
        and (share * wide) % 8 == 0
        and share * wide <= 64
        and 3 * features * hidden // groups * 2 <= 40 << 20
    )
    plan = shared if fits else whole_block
    return plan(inputs, cotangent, gate_weight, up_weight, down_weight, ia3_scale, seq_ids)


def solution(mesh):
    return jax.shard_map(
        local,
        mesh=mesh,
        in_specs=(
            P(("groups", "wide"), "narrow"),
            P(("groups", "wide"), "narrow"),
            P("narrow", "wide"),
            P("narrow", "wide"),
            P("wide", "narrow"),
            P("wide"),
            P("groups"),
        ),
        out_specs=(P("groups", ("wide", "narrow")), P("groups"), P(("groups", "wide"), "narrow")),
        check_vma=False,
    )
```
